32 devices in a mesh: grp: 2 (over y), seq: 16 (over z, x, core).
Axes of the slice: x: 2, y: 2, z: 4, core: 2. Of those that a mesh axis runs over, the one named last changes fastest.
Arguments:
- streams: bfloat16 [3, 4096, 4096], P(None, ('grp', 'seq')), parts along dimension 1, may hold values from -12 to 12
- long_filter: bfloat16 [4096, 2048], P('seq'), may hold values from -1 to 1
- gain: bfloat16 [4096], replicated, may hold values from 0.099609375 to 1.8984375
- unembed: bfloat16 [4096, 512], P('seq'), may hold values from -8 to 8
- offsets: int32 [32], P('grp'), parts along dimension 0, may hold values from 0 to 127
- ref_ids: int32 [32], P(('grp', 'seq')), parts along dimension 0, may hold values from 0 to 511
- alt_ids: int32 [32], P(('grp', 'seq')), parts along dimension 0, may hold values from 0 to 511
Outputs:
- mixed: bfloat16 [4096, 4096], P(('grp', 'seq')), parts along dimension 0
- scores: float32 [2, 32], P(None, ('grp', 'seq')), parts along dimension 1
The draws below stay inside these ranges and needn't reach their ends.
There are 2 independent parts, one for each index of `grp`. The reference program is written for one: setup_inputs(seed, part) draws one part's arguments, and reference() takes and returns one part's arrays. A program takes and returns all parts, laid end to end along the dimension named above; an argument that names none is the same for every part. Nothing has to cross between parts.
All inputs are finite; a program needn't handle non-finite values.
Results may differ from the reference program's by a relative error of at most 0.0057.
Values may be sent and summed in bfloat16 or wider, within the bound.
No kernel may reach another device: no remote copies, remote signals or barrier semaphores. Data moves between devices by JAX's collectives and lax.ppermute only.
A program may use at most 128 MiB of HBM per device.

```python
import math
import jax
import jax.numpy as jnp
from jax import lax

D = 4096
V = 512
TOK_DEV = 128
VARS_DEV = 1
WINDOW_LENGTH = 2048
NVAR = 16


def draw_streams(key, part):
    random_subkey_list = jax.random.split(key, 1)
    noise_all = jnp.clip(jax.random.normal(random_subkey_list[0], (3, WINDOW_LENGTH, D), jnp.float32), -4.0, 4.0)
    channel_ramp = jnp.arange(D, dtype=jnp.float32) / max(D - 1, 1)
    gate_scale = 1.0 + 2.0 * channel_ramp
    gate_part = noise_all[0] * gate_scale[None, :]
    stacked = jnp.stack([gate_part, noise_all[1], noise_all[2]])
    return jnp.clip(stacked, -12.0, 12.0).astype(jnp.bfloat16)


def draw_long_filter(key, part):
    random_subkey_list = jax.random.split(key, 6)
    noise_part = jnp.clip(jax.random.normal(random_subkey_list[0], (D, WINDOW_LENGTH), jnp.float32), -4.0, 4.0)
    chooser = jax.random.uniform(random_subkey_list[1], (D,), jnp.float32)
    fast_share = 0.5
    fast_tau = jax.random.uniform(random_subkey_list[2], (D,), jnp.float32, minval=10.0, maxval=17.0)
    slow_tau = WINDOW_LENGTH * jax.random.uniform(random_subkey_list[3], (D,), jnp.float32, minval=2.0, maxval=4.0)
    decay_constant = jnp.where(chooser < fast_share, fast_tau, slow_tau)
    step_positions = jnp.arange(WINDOW_LENGTH, dtype=jnp.float32)
    spike_position = jax.random.randint(random_subkey_list[4], (3,), 1, WINDOW_LENGTH).astype(jnp.float32)
    spike_retained = jax.random.uniform(random_subkey_list[5], (3,), jnp.float32, minval=0.55, maxval=0.8)
    spike_multiplier = jnp.prod(jnp.where(step_positions[None, :] >= spike_position[:, None], spike_retained[:, None], 1.0), axis=0)
    decay_envelope = jnp.exp(-step_positions[None, :] / decay_constant[:, None]) * spike_multiplier[None, :]
    scaled = decay_envelope / jnp.sqrt(jnp.sum(decay_envelope * decay_envelope, axis=1, keepdims=True))
    return jnp.clip(noise_part * scaled, -1.0, 1.0).astype(jnp.bfloat16)


def draw_unembed(key, part):
    random_subkey_list = jax.random.split(key, 1)
    drawn_part = jnp.clip(jax.random.normal(random_subkey_list[0], (D, V), jnp.float32), -5.0, 5.0) * (3.0 / math.sqrt(D))
    table = drawn_part
    return jnp.clip(table, -8.0, 8.0).astype(jnp.bfloat16)


def place_ends(entries, rng, low, high):
    spot = [jax.random.randint(jax.random.fold_in(rng, axis), (), 0, length) for axis, length in enumerate(entries.shape)]
    longest = entries.shape.index(max(entries.shape))
    neighbour = spot[:longest] + [(spot[longest] + 1) % entries.shape[longest]] + spot[longest + 1:]
    return entries.at[tuple(spot)].set(low).at[tuple(neighbour)].set(high)


def setup_inputs(seed: int = 0, part: int = 0) -> dict:
    arg_keys = jax.random.split(jax.random.key(seed), 8)
    part_keys = jax.random.split(jax.random.fold_in(arg_keys[7], part), 8)
    streams = draw_streams(jax.random.fold_in(jax.random.fold_in(arg_keys[7], part), 71), part)
    long_filter = draw_long_filter(jax.random.fold_in(arg_keys[7], 71), part)
    gain = jnp.clip(1.0 + 0.18 * jax.random.normal(arg_keys[2], (D,), jnp.float32), 0.099609375, 1.8984375).astype(jnp.bfloat16)
    unembed = draw_unembed(jax.random.fold_in(arg_keys[7], 71), part)
    offsets = place_ends(jax.random.randint(part_keys[4], (NVAR,), 0, TOK_DEV // VARS_DEV), jax.random.fold_in(part_keys[4], 1), 0, (TOK_DEV // VARS_DEV) - 1).astype(jnp.int32)
    ref_ids = place_ends(jax.random.randint(part_keys[5], (NVAR,), 0, V), jax.random.fold_in(part_keys[5], 1), 0, V - 1).astype(jnp.int32)
    alt_ids = place_ends(jax.random.randint(part_keys[6], (NVAR,), 0, V), jax.random.fold_in(part_keys[6], 1), 0, V - 1).astype(jnp.int32)
    return dict(streams=streams, long_filter=long_filter, gain=gain, unembed=unembed, offsets=offsets, ref_ids=ref_ids, alt_ids=alt_ids)


norm_eps = 1e-06

def filter_block(pair):
    signal, kernel = pair
    padded_len = 2 * signal.shape[1]
    spectrum = jnp.fft.rfft(signal, n=padded_len, axis=1) * jnp.fft.rfft(kernel, n=padded_len, axis=1)
    return jnp.fft.irfft(spectrum, n=padded_len, axis=1)[:, :signal.shape[1]]

def reference(streams, long_filter, gain, unembed, offsets, ref_ids, alt_ids):
    products = (streams[1].astype(jnp.float32) * streams[2].astype(jnp.float32)).astype(jnp.bfloat16)
    blocks = D // 128
    signal = products.astype(jnp.float32).T.reshape(blocks, 128, WINDOW_LENGTH)
    kernel = long_filter.astype(jnp.float32).reshape(blocks, 128, WINDOW_LENGTH)
    convolved = lax.map(filter_block, (signal, kernel)).reshape(D, WINDOW_LENGTH).T
    filtered = convolved.astype(jnp.bfloat16)
    mixed = (streams[0].astype(jnp.float32) * filtered.astype(jnp.float32)).astype(jnp.bfloat16)
    positions = jnp.arange(NVAR, dtype=jnp.int32) * (WINDOW_LENGTH // NVAR) + offsets.astype(jnp.int32)
    rows = mixed[positions]
    weighted = (rows.astype(jnp.float32) * gain.astype(jnp.float32)[None, :]).astype(jnp.bfloat16)
    raw = jnp.dot(weighted, unembed, preferred_element_type=jnp.float32)
    squares = lax.optimization_barrier(jnp.sum(jnp.square(rows.astype(jnp.float32)), axis=1))
    logits = raw * lax.rsqrt(squares / D + norm_eps)[:, None]
    largest = lax.optimization_barrier(jnp.max(logits, axis=1))
    log_total = largest + jnp.log(lax.optimization_barrier(jnp.sum(jnp.exp(logits - largest[:, None]), axis=1)))
    vocab_ids = jnp.arange(V, dtype=jnp.int32)
    ref_logit = lax.optimization_barrier(jnp.sum(jnp.where(vocab_ids[None, :] == ref_ids[:, None], logits, 0.0), axis=1))
    alt_logit = lax.optimization_barrier(jnp.sum(jnp.where(vocab_ids[None, :] == alt_ids[:, None], logits, 0.0), axis=1))
    scores = jnp.stack([ref_logit - log_total, alt_logit - ref_logit])
    return (mixed, scores)
```

```python
import functools
import math

import jax
import jax.numpy as jnp
import numpy as np
from jax import lax
from jax.experimental import pallas as pl
from jax.experimental.pallas import tpu as pltpu
from jax.sharding import PartitionSpec as P

norm_eps = 1e-06
f32 = jnp.float32
bf16 = jnp.bfloat16
row_tile = 16
lane_tile = 128
max_chunks = 2
MIB = 1 << 20


def round_up(value, step):
    return -(-value // step) * step


def split_bf16(values):
    high = values.astype(bf16)
    low = (values - high.astype(f32)).astype(bf16)
    return high, low


def block_tables(block):
    turns = (4 * np.arange(block)[:, None] + 1) * np.arange(block)[None, :] % (4 * block)
    theta = turns * (math.pi / (2 * block))
    table = np.concatenate([np.cos(theta), np.sin(theta)], axis=0)
    parts = []
    for matrix in (table, table.T / block):
        high = matrix.astype(bf16)
        low = (matrix - high.astype(np.float64)).astype(bf16)
        parts.append(np.concatenate([high, low], axis=0))
    return parts


def block_devices(n_devices, tok_rows):
    target = math.isqrt(32 * n_devices * tok_rows)
    count = 1
    while n_devices % (2 * count) == 0 and 2 * count * tok_rows <= target:
        count *= 2
    return count


def whole_spec():
    return pl.BlockSpec(memory_space=pltpu.VMEM)


def product_kernel(chunks, width, vars_dev, rows_ref, streams_ref, *out_refs):
    tok_rows = streams_ref.shape[1]
    n_owners = out_refs[0].shape[0]
    extra = out_refs[0].shape[1] - tok_rows
    place = lax.broadcasted_iota(jnp.int32, (extra, tok_rows), 0)
    column = lax.broadcasted_iota(jnp.int32, (extra, tok_rows), 1)
    for owner in range(n_owners):
        gates = jnp.zeros((extra, width), f32)
        for chunk in range(chunks):
            lanes = pl.ds((owner * chunks + chunk) * width, width)
            left = streams_ref[1, :, lanes].astype(f32)
            right = streams_ref[2, :, lanes].astype(f32)
            out_refs[chunk][owner, :tok_rows, :] = (left * right).astype(bf16)
            picker = jnp.zeros((extra, tok_rows), jnp.bool_)
            for var in range(vars_dev):
                picker |= (place == chunk * vars_dev + var) & (column == rows_ref[var])
            gates += jnp.dot(
                picker.astype(f32).astype(bf16),
                streams_ref[0, :, lanes],
                preferred_element_type=f32,
            )
        out_refs[0][owner, tok_rows:, :] = gates.astype(bf16)


def make_products(streams, local_rows, n_devices, chunks, extra):
    _, tok_rows, model_width = streams.shape
    vars_dev = local_rows.shape[0]
    group_width = model_width // n_devices
    width = group_width // chunks
    owners = max(1, n_devices // 4)
    while owners * group_width % lane_tile:
        owners *= 2
    steps = n_devices // owners
    rows_out = [tok_rows + extra] + [tok_rows] * (chunks - 1)
    return pl.pallas_call(
        functools.partial(product_kernel, chunks, width, vars_dev),
        grid=(steps,),
        in_specs=[
            pl.BlockSpec(memory_space=pltpu.SMEM),
            pl.BlockSpec((3, tok_rows, owners * group_width), lambda i: (0, 0, i)),
        ],
        out_specs=[pl.BlockSpec((owners, rows, width), lambda i: (i, 0, 0)) for rows in rows_out],
        out_shape=[jax.ShapeDtypeStruct((n_devices, rows, width), bf16) for rows in rows_out],
        compiler_params=pltpu.CompilerParams(vmem_limit_bytes=24 * MIB),
        name="products",
    )(local_rows, streams)


def spectrum_kernel(block, filter_ref, forward_ref, out_ref):
    n_blocks = out_ref.shape[0]
    for index in range(n_blocks):
        taps = filter_ref[:, index * block : (index + 1) * block]
        both = lax.dot_general(
            forward_ref[...], taps, (((1,), (1,)), ((), ())), preferred_element_type=f32
        )
        out_ref[index] = both[: 2 * block] + both[2 * block :]


def filter_spectrum(taps, forward, block):
    width, length = taps.shape
    n_blocks = length // block
    return pl.pallas_call(
        functools.partial(spectrum_kernel, block),
        in_specs=[whole_spec(), whole_spec()],
        out_specs=whole_spec(),
        out_shape=jax.ShapeDtypeStruct((n_blocks, 2 * block, width), f32),
        compiler_params=pltpu.CompilerParams(vmem_limit_bytes=40 * MIB),
        cost_estimate=pl.CostEstimate(
            flops=8 * block * length * width, bytes_accessed=4 * MIB, transcendentals=0
        ),
        name="filter_spectrum",
    )(taps, forward)


def convolve(chunk_ref, spectrum_ref, forward_ref, inverse_ref, out_ref, points, tok_rows):
    n_blocks, double, width = points.shape
    block = double // 2
    per_block = block // tok_rows
    group = max(1, min(n_blocks, 256 // width)) if width % lane_tile == 0 else 1

    def forward_step(step, carry):
        pieces = []
        for member in range(group):
            start = (step * group + member) * per_block
            rows = chunk_ref[pl.ds(start, per_block), :tok_rows, :]
            pieces.append(rows.reshape(block, width))
        signal = pieces[0] if group == 1 else jnp.concatenate(pieces, axis=1)
        both = jnp.dot(forward_ref[...], signal, preferred_element_type=f32)
        total = both[:double] + both[double:]
        for member in range(group):
            points[step * group + member] = total[:, member * width : (member + 1) * width]
        return carry

    lax.fori_loop(0, n_blocks // group, forward_step, 0)

    def multiply_step(step, carry):
        start = pl.multiple_of(step * row_tile, row_tile)
        upper = pl.ds(start, row_tile)
        lower = pl.ds(pl.multiple_of(block + start, row_tile), row_tile)

        def block_sum(total):
            sum_re = jnp.zeros((row_tile, width), f32)
            sum_im = jnp.zeros((row_tile, width), f32)
            for delay in range(total + 1):
                a_re = points[total - delay, upper, :]
                a_im = points[total - delay, lower, :]
                b_re = spectrum_ref[delay, upper, :]
                b_im = spectrum_ref[delay, lower, :]
                sum_re += a_re * b_re - a_im * b_im
                sum_im += a_re * b_im + a_im * b_re
            return sum_re, sum_im

        after_re, after_im = block_sum(n_blocks - 1)
        for total in range(n_blocks - 1, 0, -1):
            sum_re, sum_im = block_sum(total - 1)
            points[total, upper, :] = after_re + sum_im
            points[total, lower, :] = after_im - sum_re
            after_re, after_im = sum_re, sum_im
        points[0, upper, :] = after_re
        points[0, lower, :] = after_im
        return carry

    lax.fori_loop(0, block // row_tile, multiply_step, 0)

    def inverse_step(step, carry):
        first = step * group
        pieces = [points[first + member] for member in range(group)]
        highs, lows = split_bf16(pieces[0] if group == 1 else jnp.concatenate(pieces, axis=1))
        both = jnp.dot(inverse_ref[...], highs, preferred_element_type=f32)
        rest = jnp.dot(inverse_ref[:block, :], lows, preferred_element_type=f32)
        result = (both[:block] + both[block:] + rest).astype(bf16)
        for member in range(group):
            piece = result[:, member * width : (member + 1) * width]
            out_ref[pl.ds((first + member) * per_block, per_block), :tok_rows, :] = piece.reshape(
                per_block, tok_rows, width
            )
        return carry

    lax.fori_loop(0, n_blocks // group, inverse_step, 0)


def score_rows(index, vars_dev, tok_rows, positions, gate_block, out_ref, gain_row, unembed):
    n_devices, extra, width = gate_block.shape
    gates = gate_block.astype(f32)
    place = lax.broadcasted_iota(jnp.int32, (n_devices, extra, width), 1)
    picked = [
        jnp.sum(jnp.where(place == index * vars_dev + var, gates, 0.0), axis=1)
        for var in range(vars_dev)
    ]
    gate_rows = picked[0] if vars_dev == 1 else jnp.concatenate(picked, axis=0)
    length = n_devices * tok_rows
    column = lax.broadcasted_iota(jnp.int32, (positions.shape[0], length), 1)
    picker = (column == positions).astype(f32).astype(bf16)
    filtered = jnp.dot(
        picker, out_ref[:, :tok_rows, :].reshape(length, width), preferred_element_type=f32
    )
    rows = (gate_rows * filtered).astype(bf16).astype(f32)
    weighted = (rows * gain_row).astype(bf16)
    return jnp.dot(weighted, unembed, preferred_element_type=f32), rows * rows


def chunk_kernel(index, chunks, vars_dev, tok_rows, *refs):
    refs = list(refs)
    chunk_ref, spectrum_ref, forward_ref, inverse_ref = refs[:4]
    positions_ref, gain_ref, unembed_ref = refs[4:7]
    refs = refs[7:]
    first, last = index == 0, index == chunks - 1
    gates_ref = None if first else refs.pop(0)
    raw_before, square_before = (None, None) if first else (refs.pop(0), refs.pop(0))
    out_ref = refs.pop(0)
    raw_out, square_out = (None, None) if last else (refs.pop(0), refs.pop(0))
    gates_out = refs.pop(0) if first and not last else None
    points = refs[0]
    convolve(chunk_ref, spectrum_ref, forward_ref, inverse_ref, out_ref, points, tok_rows)
    gate_block = chunk_ref[:, tok_rows:, :] if first else gates_ref[...]
    raw, squares = score_rows(
        index, vars_dev, tok_rows, positions_ref[...], gate_block, out_ref, gain_ref[...], unembed_ref[...]
    )
    if not first:
        raw = raw + raw_before[...]
        squares = squares + square_before[...]
    if gates_out is not None:
        gates_out[...] = gate_block
    if not last:
        raw_out[...] = raw
        square_out[...] = squares
        return
    packed = refs[1]
    n_devices, _, width = out_ref.shape
    extra = out_ref.shape[1] - tok_rows
    per_row = raw.shape[1] // width
    packed[...] = jnp.zeros_like(packed)
    for var in range(vars_dev):
        mine = slice(var * n_devices, (var + 1) * n_devices)
        pieces = [raw[mine, r * width : (r + 1) * width] for r in range(per_row)] + [squares[mine]]
        for row, piece in enumerate(pieces):
            rounded = piece.astype(bf16).astype(f32)
            base = var * 2 * (per_row + 1) + row
            packed[pl.ds(base, n_devices, stride=extra), :] = rounded
            packed[pl.ds(base + per_row + 1, n_devices, stride=extra), :] = piece - rounded
    out_ref[:, tok_rows:, :] = packed[...].reshape(n_devices, extra, width).astype(bf16)


def filter_chunk(index, chunks, vars_dev, tok_rows, extra, operands, carried):
    moved, spectrum = operands[:2]
    n_devices, _, width = moved.shape
    n_blocks, double, _ = spectrum.shape
    vocab = operands[6].shape[1]
    n_vars = operands[4].shape[0]
    first, last = index == 0, index == chunks - 1
    rows_out = tok_rows + (extra if last else 0)
    out_shape = [jax.ShapeDtypeStruct((n_devices, rows_out, width), bf16)]
    scratch = [pltpu.VMEM((n_blocks, double, width), f32)]
    if last:
        scratch.append(pltpu.VMEM((n_devices * extra, width), f32))
    else:
        out_shape.append(jax.ShapeDtypeStruct((n_vars, vocab), f32))
        out_shape.append(jax.ShapeDtypeStruct((n_vars, width), f32))
    if first and not last:
        out_shape.append(jax.ShapeDtypeStruct((n_devices, moved.shape[1] - tok_rows, width), bf16))
    flops = 2 * width * n_blocks * (double * double * 5 // 2 + 4 * n_blocks * double)
    return pl.pallas_call(
        functools.partial(chunk_kernel, index, chunks, vars_dev, tok_rows),
        in_specs=[whole_spec()] * (len(operands) + len(carried)),
        out_specs=[whole_spec()] * len(out_shape),
        out_shape=out_shape,
        scratch_shapes=scratch,
        compiler_params=pltpu.CompilerParams(vmem_limit_bytes=(20 if n_blocks <= 8 else 58) * MIB),
        cost_estimate=pl.CostEstimate(flops=flops, bytes_accessed=8 * MIB, transcendentals=0),
        name="filter_chunk",
    )(*operands, *carried)


def finish_kernel(chunks, vars_dev, vocab, ref_ref, alt_ref, streams_ref, *refs):
    back_refs, mixed_ref, scores_ref, sums = refs[:chunks], refs[chunks], refs[chunks + 1], refs[chunks + 2]
    tok_rows = streams_ref.shape[1]
    owners, _, width = back_refs[0].shape
    step = pl.program_id(0)
    for owner in range(owners):
        for chunk in range(chunks):
            lanes = pl.ds((owner * chunks + chunk) * width, width)
            gate = streams_ref[0, :, lanes].astype(f32)
            filtered = back_refs[chunk][owner, :tok_rows, :].astype(f32)
            mixed_ref[:, lanes] = (gate * filtered).astype(bf16)
    part = jnp.sum(back_refs[-1][:, tok_rows:, :].astype(f32), axis=0)

    @pl.when(step == 0)
    def _():
        sums[...] = part

    @pl.when(step > 0)
    def _():
        sums[...] += part

    @pl.when(step == pl.num_programs(0) - 1)
    def _():
        per_row = vocab // width
        model_width = pl.num_programs(0) * owners * chunks * width
        ids = lax.broadcasted_iota(jnp.int32, (per_row, width), 0) * width
        ids += lax.broadcasted_iota(jnp.int32, (per_row, width), 1)
        row = lax.broadcasted_iota(jnp.int32, (2, vars_dev), 0)
        column = lax.broadcasted_iota(jnp.int32, (2, vars_dev), 1)
        scores = jnp.zeros((2, vars_dev), f32)
        for var in range(vars_dev):
            base = var * 2 * (per_row + 1)
            both = sums[base : base + per_row + 1, :]
            both = both + sums[base + per_row + 1 : base + 2 * (per_row + 1), :]
            square = jnp.sum(both[per_row:, :], axis=1, keepdims=True)
            logits = both[:per_row, :] * lax.rsqrt(square / model_width + norm_eps)

            def whole_sum(values):
                return jnp.sum(jnp.sum(values, axis=1, keepdims=True), axis=0, keepdims=True)

            largest = jnp.max(jnp.max(logits, axis=1, keepdims=True), axis=0, keepdims=True)
            log_total = largest + jnp.log(whole_sum(jnp.exp(logits - largest)))
            ref_logit = whole_sum(jnp.where(ids == ref_ref[var], logits, 0.0))
            alt_logit = whole_sum(jnp.where(ids == alt_ref[var], logits, 0.0))
            pair = jnp.where(row == 0, ref_logit - log_total, alt_logit - ref_logit)
            scores = jnp.where(column == var, pair, scores)
        scores_ref[...] = scores


def finish(streams, backs, ref_ids, alt_ids, vocab):
    _, tok_rows, model_width = streams.shape
    chunks = len(backs)
    n_devices, _, width = backs[0].shape
    vars_dev = ref_ids.shape[0]
    owners = max(1, n_devices // 4)
    while owners * chunks * width % lane_tile:
        owners *= 2
    extra = backs[-1].shape[1] - tok_rows
    return pl.pallas_call(
        functools.partial(finish_kernel, chunks, vars_dev, vocab),
        grid=(n_devices // owners,),
        in_specs=[
            pl.BlockSpec(memory_space=pltpu.SMEM),
            pl.BlockSpec(memory_space=pltpu.SMEM),
            pl.BlockSpec((1, tok_rows, owners * chunks * width), lambda i: (0, 0, i)),
        ]
        + [pl.BlockSpec((owners, back.shape[1], width), lambda i: (i, 0, 0)) for back in backs],
        out_specs=[
            pl.BlockSpec((tok_rows, owners * chunks * width), lambda i: (0, i)),
            pl.BlockSpec((2, vars_dev), lambda i: (0, 0)),
        ],
        out_shape=[
            jax.ShapeDtypeStruct((tok_rows, model_width), bf16),
            jax.ShapeDtypeStruct((2, vars_dev), f32),
        ],
        scratch_shapes=[pltpu.VMEM((extra, width), f32)],
        compiler_params=pltpu.CompilerParams(vmem_limit_bytes=24 * MIB),
        name="finish",
    )(ref_ids, alt_ids, streams, *backs)


def shards(streams, long_filter, gain, unembed, offsets, ref_ids, alt_ids):
    n_devices = lax.axis_size("seq")
    my_index = lax.axis_index("seq")
    _, tok_rows, model_width = streams.shape
    group_width = model_width // n_devices
    vars_dev = ref_ids.shape[0]
    vocab = unembed.shape[1]
    chunks = max(1, min(max_chunks, group_width // lane_tile))
    width = group_width // chunks
    block = tok_rows * block_devices(n_devices, tok_rows)
    forward, inverse = (jnp.asarray(table) for table in block_tables(block))

    slot = tok_rows // vars_dev
    starts = jnp.arange(vars_dev, dtype=jnp.int32) * slot
    local_rows = starts + lax.dynamic_slice_in_dim(offsets, my_index * vars_dev, vars_dev)
    by_device = offsets.reshape(n_devices, vars_dev)
    positions = by_device + starts[None, :]
    positions += jnp.arange(n_devices, dtype=jnp.int32)[:, None] * tok_rows
    positions = positions.T.reshape(n_devices * vars_dev, 1)
    my_gain = lax.dynamic_slice_in_dim(gain, my_index * group_width, group_width).astype(f32)

    gate_extra = round_up(chunks * vars_dev, row_tile)
    score_extra = round_up(vars_dev * 2 * (vocab // width + 1), row_tile)
    products = make_products(streams, local_rows, n_devices, chunks, gate_extra)
    moved = [lax.all_to_all(part, "seq", split_axis=0, concat_axis=0, tiled=True) for part in products]
    carried = ()
    backs = []
    for chunk in range(chunks):
        mine = slice(chunk * width, (chunk + 1) * width)
        spectrum = filter_spectrum(long_filter[mine], forward, block)
        operands = (
            moved[chunk], spectrum, forward, inverse, positions,
            my_gain[None, mine], unembed[mine],
        )
        if chunk > 0:
            carried = (gates,) + tuple(carried)
        results = filter_chunk(chunk, chunks, vars_dev, tok_rows, score_extra, operands, carried)
        carried = results[1:3]
        if chunk == 0 and chunks > 1:
            gates = results[3]
        backs.append(lax.all_to_all(results[0], "seq", split_axis=0, concat_axis=0, tiled=True))
    mixed, scores = finish(streams, backs, ref_ids, alt_ids, vocab)
    return (mixed, scores)


def solution(mesh):
    placed = (
        P(None, ("grp", "seq"), None),
        P("seq", None),
        P(),
        P("seq", None),
        P("grp"),
        P(("grp", "seq")),
        P(("grp", "seq")),
    )
    return jax.shard_map(
        shards,
        mesh=mesh,
        in_specs=placed,
        out_specs=(P(("grp", "seq"), None), P(None, ("grp", "seq"))),
        check_vma=False,
    )
```

```python
import functools
import math

import jax
import jax.numpy as jnp
import numpy as np
from jax import lax
from jax.experimental import pallas as pl
from jax.experimental.pallas import tpu as pltpu
from jax.sharding import PartitionSpec as P

norm_eps = 1e-06
f32 = jnp.float32
bf16 = jnp.bfloat16
row_tile = 16
lane_tile = 128
MIB = 1 << 20


def round_up(value, step):
    return -(-value // step) * step


def split_bf16(values):
    high = values.astype(bf16)
    low = (values - high.astype(f32)).astype(bf16)
    return high, low


def block_tables(block):
    turns = (4 * np.arange(block)[:, None] + 1) * np.arange(block)[None, :] % (4 * block)
    theta = turns * (math.pi / (2 * block))
    table = np.concatenate([np.cos(theta), np.sin(theta)], axis=0)
    parts = []
    for matrix in (table, table.T / block):
        high = matrix.astype(bf16)
        low = (matrix - high.astype(np.float64)).astype(bf16)
        parts.append(np.concatenate([high, low], axis=0))
    return parts


def block_devices(n_devices, tok_rows):
    target = math.isqrt(32 * n_devices * tok_rows)
    count = 1
    while n_devices % (2 * count) == 0 and 2 * count * tok_rows <= target:
        count *= 2
    return count


def whole_spec():
    return pl.BlockSpec(memory_space=pltpu.VMEM)


def product_kernel(chunks, width, vars_dev, rows_ref, streams_ref, *out_refs):
    tok_rows = streams_ref.shape[1]
    n_owners = out_refs[0].shape[0]
    extra = out_refs[0].shape[1] - tok_rows
    place = lax.broadcasted_iota(jnp.int32, (extra, tok_rows), 0)
    column = lax.broadcasted_iota(jnp.int32, (extra, tok_rows), 1)
    for owner in range(n_owners):
        gates = jnp.zeros((extra, width), f32)
        for chunk in range(chunks):
            lanes = pl.ds((owner * chunks + chunk) * width, width)
            left = streams_ref[1, :, lanes].astype(f32)
            right = streams_ref[2, :, lanes].astype(f32)
            out_refs[chunk][owner, :tok_rows, :] = (left * right).astype(bf16)
            picker = jnp.zeros((extra, tok_rows), jnp.bool_)
            for var in range(vars_dev):
                picker |= (place == chunk * vars_dev + var) & (column == rows_ref[var])
            gates += jnp.dot(
                picker.astype(f32).astype(bf16),
                streams_ref[0, :, lanes],
                preferred_element_type=f32,
            )
        out_refs[0][owner, tok_rows:, :] = gates.astype(bf16)


def make_products(streams, local_rows, n_devices, chunks, extra):
    _, tok_rows, model_width = streams.shape
    vars_dev = local_rows.shape[0]
    group_width = model_width // n_devices
    width = group_width // chunks
    owners = max(1, n_devices // 4)
    while owners * group_width % lane_tile:
        owners *= 2
    steps = n_devices // owners
    rows_out = [tok_rows + extra] + [tok_rows] * (chunks - 1)
    return pl.pallas_call(
        functools.partial(product_kernel, chunks, width, vars_dev),
        grid=(steps,),
        in_specs=[
            pl.BlockSpec(memory_space=pltpu.SMEM),
            pl.BlockSpec((3, tok_rows, owners * group_width), lambda i: (0, 0, i)),
        ],
        out_specs=[pl.BlockSpec((owners, rows, width), lambda i: (i, 0, 0)) for rows in rows_out],
        out_shape=[jax.ShapeDtypeStruct((n_devices, rows, width), bf16) for rows in rows_out],
        compiler_params=pltpu.CompilerParams(vmem_limit_bytes=24 * MIB),
        name="products",
    )(local_rows, streams)


def spectrum_kernel(block, filter_ref, forward_ref, out_ref):
    n_blocks = out_ref.shape[0]
    for index in range(n_blocks):
        taps = filter_ref[:, index * block : (index + 1) * block]
        both = lax.dot_general(
            forward_ref[...], taps, (((1,), (1,)), ((), ())), preferred_element_type=f32
        )
        out_ref[index] = both[: 2 * block] + both[2 * block :]


def filter_spectrum(taps, forward, block):
    width, length = taps.shape
    n_blocks = length // block
    return pl.pallas_call(
        functools.partial(spectrum_kernel, block),
        in_specs=[whole_spec(), whole_spec()],
        out_specs=whole_spec(),
        out_shape=jax.ShapeDtypeStruct((n_blocks, 2 * block, width), f32),
        compiler_params=pltpu.CompilerParams(vmem_limit_bytes=40 * MIB),
        cost_estimate=pl.CostEstimate(
            flops=8 * block * length * width, bytes_accessed=4 * MIB, transcendentals=0
        ),
        name="filter_spectrum",
    )(taps, forward)


def multiply_points(points, spectrum_ref):
    n_blocks, double, width = points.shape
    block = double // 2

    def multiply_step(step, carry):
        start = pl.multiple_of(step * row_tile, row_tile)
        upper = pl.ds(start, row_tile)
        lower = pl.ds(pl.multiple_of(block + start, row_tile), row_tile)

        def block_sum(total):
            sum_re = jnp.zeros((row_tile, width), f32)
            sum_im = jnp.zeros((row_tile, width), f32)
            for delay in range(total + 1):
                a_re = points[total - delay, upper, :]
                a_im = points[total - delay, lower, :]
                b_re = spectrum_ref[delay, upper, :]
                b_im = spectrum_ref[delay, lower, :]
                sum_re += a_re * b_re - a_im * b_im
                sum_im += a_re * b_im + a_im * b_re
            return sum_re, sum_im

        after_re, after_im = block_sum(n_blocks - 1)
        for total in range(n_blocks - 1, 0, -1):
            sum_re, sum_im = block_sum(total - 1)
            points[total, upper, :] = after_re + sum_im
            points[total, lower, :] = after_im - sum_re
            after_re, after_im = sum_re, sum_im
        points[0, upper, :] = after_re
        points[0, lower, :] = after_im
        return carry

    lax.fori_loop(0, block // row_tile, multiply_step, 0)


def convolve(chunk_ref, spectrum_ref, forward_ref, inverse_ref, out_ref, points, tok_rows):
    n_blocks, double, width = points.shape
    block = double // 2
    per_block = block // tok_rows
    group = max(1, min(n_blocks, 256 // width)) if width % lane_tile == 0 else 1

    def forward_step(step, carry):
        pieces = []
        for member in range(group):
            start = (step * group + member) * per_block
            rows = chunk_ref[pl.ds(start, per_block), :tok_rows, :]
            pieces.append(rows.reshape(block, width))
        signal = pieces[0] if group == 1 else jnp.concatenate(pieces, axis=1)
        both = jnp.dot(forward_ref[...], signal, preferred_element_type=f32)
        total = both[:double] + both[double:]
        for member in range(group):
            points[step * group + member] = total[:, member * width : (member + 1) * width]
        return carry

    lax.fori_loop(0, n_blocks // group, forward_step, 0)

    multiply_points(points, spectrum_ref)

    def inverse_step(step, carry):
        first = step * group
        pieces = [points[first + member] for member in range(group)]
        highs, lows = split_bf16(pieces[0] if group == 1 else jnp.concatenate(pieces, axis=1))
        both = jnp.dot(inverse_ref[...], highs, preferred_element_type=f32)
        rest = jnp.dot(inverse_ref[:block, :], lows, preferred_element_type=f32)
        result = (both[:block] + both[block:] + rest).astype(bf16)
        for member in range(group):
            piece = result[:, member * width : (member + 1) * width]
            out_ref[pl.ds((first + member) * per_block, per_block), :tok_rows, :] = piece.reshape(
                per_block, tok_rows, width
            )
        return carry

    lax.fori_loop(0, n_blocks // group, inverse_step, 0)


def score_rows(index, vars_dev, tok_rows, positions, gate_block, out_ref, gain_row, unembed):
    n_devices, extra, width = gate_block.shape
    gates = gate_block.astype(f32)
    place = lax.broadcasted_iota(jnp.int32, (n_devices, extra, width), 1)
    picked = [
        jnp.sum(jnp.where(place == index * vars_dev + var, gates, 0.0), axis=1)
        for var in range(vars_dev)
    ]
    gate_rows = picked[0] if vars_dev == 1 else jnp.concatenate(picked, axis=0)
    length = n_devices * tok_rows
    column = lax.broadcasted_iota(jnp.int32, (positions.shape[0], length), 1)
    picker = (column == positions).astype(f32).astype(bf16)
    filtered = jnp.dot(
        picker, out_ref[:, :tok_rows, :].reshape(length, width), preferred_element_type=f32
    )
    rows = (gate_rows * filtered).astype(bf16).astype(f32)
    weighted = (rows * gain_row).astype(bf16)
    return jnp.dot(weighted, unembed, preferred_element_type=f32), rows * rows


def pack_scores(raw, squares, vars_dev, packed, n_devices):
    total, width = packed.shape
    extra = total // n_devices
    per_row = raw.shape[1] // width
    packed[...] = jnp.zeros_like(packed)
    for var in range(vars_dev):
        mine = slice(var * n_devices, (var + 1) * n_devices)
        pieces = [raw[mine, r * width : (r + 1) * width] for r in range(per_row)] + [squares[mine]]
        for row, piece in enumerate(pieces):
            rounded = piece.astype(bf16).astype(f32)
            base = var * 2 * (per_row + 1) + row
            packed[pl.ds(base, n_devices, stride=extra), :] = rounded
            packed[pl.ds(base + per_row + 1, n_devices, stride=extra), :] = piece - rounded


def chunk_kernel(index, chunks, vars_dev, tok_rows, *refs):
    refs = list(refs)
    chunk_ref, spectrum_ref, forward_ref, inverse_ref = refs[:4]
    positions_ref, gain_ref, unembed_ref = refs[4:7]
    refs = refs[7:]
    first, last = index == 0, index == chunks - 1
    gates_ref = None if first else refs.pop(0)
    raw_before, square_before = (None, None) if first else (refs.pop(0), refs.pop(0))
    out_ref = refs.pop(0)
    raw_out, square_out = (None, None) if last else (refs.pop(0), refs.pop(0))
    gates_out = refs.pop(0) if first and not last else None
    points = refs[0]
    convolve(chunk_ref, spectrum_ref, forward_ref, inverse_ref, out_ref, points, tok_rows)
    gate_block = chunk_ref[:, tok_rows:, :] if first else gates_ref[...]
    raw, squares = score_rows(
        index, vars_dev, tok_rows, positions_ref[...], gate_block, out_ref, gain_ref[...], unembed_ref[...]
    )
    if not first:
        raw = raw + raw_before[...]
        squares = squares + square_before[...]
    if gates_out is not None:
        gates_out[...] = gate_block
    if not last:
        raw_out[...] = raw
        square_out[...] = squares
        return
    packed = refs[1]
    n_devices, _, width = out_ref.shape
    extra = out_ref.shape[1] - tok_rows
    pack_scores(raw, squares, vars_dev, packed, n_devices)
    out_ref[:, tok_rows:, :] = packed[...].reshape(n_devices, extra, width).astype(bf16)


def filter_chunk(index, chunks, vars_dev, tok_rows, extra, operands, carried):
    moved, spectrum = operands[:2]
    n_devices, _, width = moved.shape
    n_blocks, double, _ = spectrum.shape
    vocab = operands[6].shape[1]
    n_vars = operands[4].shape[0]
    first, last = index == 0, index == chunks - 1
    rows_out = tok_rows + (extra if last else 0)
    out_shape = [jax.ShapeDtypeStruct((n_devices, rows_out, width), bf16)]
    scratch = [pltpu.VMEM((n_blocks, double, width), f32)]
    if last:
        scratch.append(pltpu.VMEM((n_devices * extra, width), f32))
    else:
        out_shape.append(jax.ShapeDtypeStruct((n_vars, vocab), f32))
        out_shape.append(jax.ShapeDtypeStruct((n_vars, width), f32))
    if first and not last:
        out_shape.append(jax.ShapeDtypeStruct((n_devices, moved.shape[1] - tok_rows, width), bf16))
    flops = 2 * width * n_blocks * (double * double * 5 // 2 + 4 * n_blocks * double)
    return pl.pallas_call(
        functools.partial(chunk_kernel, index, chunks, vars_dev, tok_rows),
        in_specs=[whole_spec()] * (len(operands) + len(carried)),
        out_specs=[whole_spec()] * len(out_shape),
        out_shape=out_shape,
        scratch_shapes=scratch,
        compiler_params=pltpu.CompilerParams(vmem_limit_bytes=(20 if n_blocks <= 8 else 58) * MIB),
        cost_estimate=pl.CostEstimate(flops=flops, bytes_accessed=8 * MIB, transcendentals=0),
        name="filter_chunk",
    )(*operands, *carried)


def final_scores(sums, vars_dev, vocab, model_width, ref_ref, alt_ref):
    width = sums.shape[1]
    per_row = vocab // width
    ids = lax.broadcasted_iota(jnp.int32, (per_row, width), 0) * width
    ids += lax.broadcasted_iota(jnp.int32, (per_row, width), 1)
    row = lax.broadcasted_iota(jnp.int32, (2, vars_dev), 0)
    column = lax.broadcasted_iota(jnp.int32, (2, vars_dev), 1)
    scores = jnp.zeros((2, vars_dev), f32)

    def whole_sum(values):
        return jnp.sum(jnp.sum(values, axis=1, keepdims=True), axis=0, keepdims=True)

    for var in range(vars_dev):
        base = var * 2 * (per_row + 1)
        both = sums[base : base + per_row + 1, :]
        both = both + sums[base + per_row + 1 : base + 2 * (per_row + 1), :]
        square = jnp.sum(both[per_row:, :], axis=1, keepdims=True)
        logits = both[:per_row, :] * lax.rsqrt(square / model_width + norm_eps)
        largest = jnp.max(jnp.max(logits, axis=1, keepdims=True), axis=0, keepdims=True)
        log_total = largest + jnp.log(whole_sum(jnp.exp(logits - largest)))
        ref_logit = whole_sum(jnp.where(ids == ref_ref[var], logits, 0.0))
        alt_logit = whole_sum(jnp.where(ids == alt_ref[var], logits, 0.0))
        pair = jnp.where(row == 0, ref_logit - log_total, alt_logit - ref_logit)
        scores = jnp.where(column == var, pair, scores)
    return scores


def finish_kernel(chunks, vars_dev, vocab, ref_ref, alt_ref, streams_ref, *refs):
    back_refs, mixed_ref, scores_ref, sums = refs[:chunks], refs[chunks], refs[chunks + 1], refs[chunks + 2]
    tok_rows = streams_ref.shape[1]
    owners, _, width = back_refs[0].shape
    step = pl.program_id(0)
    for owner in range(owners):
        for chunk in range(chunks):
            lanes = pl.ds((owner * chunks + chunk) * width, width)
            gate = streams_ref[0, :, lanes].astype(f32)
            filtered = back_refs[chunk][owner, :tok_rows, :].astype(f32)
            mixed_ref[:, lanes] = (gate * filtered).astype(bf16)
    part = jnp.sum(back_refs[-1][:, tok_rows:, :].astype(f32), axis=0)

    @pl.when(step == 0)
    def _():
        sums[...] = part

    @pl.when(step > 0)
    def _():
        sums[...] += part

    @pl.when(step == pl.num_programs(0) - 1)
    def _():
        model_width = pl.num_programs(0) * owners * chunks * width
        scores_ref[...] = final_scores(sums[...], vars_dev, vocab, model_width, ref_ref, alt_ref)


def finish(streams, backs, ref_ids, alt_ids, vocab):
    _, tok_rows, model_width = streams.shape
    chunks = len(backs)
    n_devices, _, width = backs[0].shape
    vars_dev = ref_ids.shape[0]
    owners = max(1, n_devices // 4)
    while owners * chunks * width % lane_tile:
        owners *= 2
    extra = backs[-1].shape[1] - tok_rows
    return pl.pallas_call(
        functools.partial(finish_kernel, chunks, vars_dev, vocab),
        grid=(n_devices // owners,),
        in_specs=[
            pl.BlockSpec(memory_space=pltpu.SMEM),
            pl.BlockSpec(memory_space=pltpu.SMEM),
            pl.BlockSpec((1, tok_rows, owners * chunks * width), lambda i: (0, 0, i)),
        ]
        + [pl.BlockSpec((owners, back.shape[1], width), lambda i: (i, 0, 0)) for back in backs],
        out_specs=[
            pl.BlockSpec((tok_rows, owners * chunks * width), lambda i: (0, i)),
            pl.BlockSpec((2, vars_dev), lambda i: (0, 0)),
        ],
        out_shape=[
            jax.ShapeDtypeStruct((tok_rows, model_width), bf16),
            jax.ShapeDtypeStruct((2, vars_dev), f32),
        ],
        scratch_shapes=[pltpu.VMEM((extra, width), f32)],
        compiler_params=pltpu.CompilerParams(vmem_limit_bytes=24 * MIB),
        name="finish",
    )(ref_ids, alt_ids, streams, *backs)

def stacked(buffer, device, half, tok_rows):
    return buffer[device, half * tok_rows : (half + 1) * tok_rows, :]


def send_products_kernel(halves, vars_dev, me_ref, rows_ref, streams_ref, *refs):
    n_devices = len(refs) - 4
    out_refs = refs[:n_devices]
    pairs, gates, pair_sems, gate_sems = refs[n_devices:]
    tok_rows = streams_ref.shape[1]
    width = halves * lane_tile
    me = me_ref[0]

    def pair_copy(step):
        start = pl.multiple_of((me ^ step) * width, lane_tile)
        return pltpu.make_async_copy(
            streams_ref.at[pl.ds(1, 2), :, pl.ds(start, width)], pairs.at[step], pair_sems.at[step]
        )

    def gate_copy(var):
        start = pl.multiple_of(rows_ref[var] // row_tile * row_tile, row_tile)
        return pltpu.make_async_copy(
            streams_ref.at[0, pl.ds(start, row_tile), :], gates.at[var], gate_sems.at[var]
        )

    for var in range(vars_dev):
        gate_copy(var).start()
    for step in range(n_devices):
        pair_copy(step).start()
    for var in range(vars_dev):
        gate_copy(var).wait()
    extra = out_refs[0].shape[0] - halves * tok_rows
    row = lax.broadcasted_iota(jnp.int32, (row_tile, lane_tile), 0)
    place = lax.broadcasted_iota(jnp.int32, (extra, lane_tile), 0)
    for step in range(n_devices):
        pair_copy(step).wait()
        tail = jnp.zeros((extra, lane_tile), f32)
        for half in range(halves):
            lanes = slice(half * lane_tile, (half + 1) * lane_tile)
            left = pairs[step, 0, :, lanes].astype(f32)
            right = pairs[step, 1, :, lanes].astype(f32)
            rows = slice(half * tok_rows, (half + 1) * tok_rows)
            out_refs[step][rows, :] = (left * right).astype(bf16)
            start = pl.multiple_of((me ^ step) * width + half * lane_tile, lane_tile)
            for var in range(vars_dev):
                tile = gates[var, :, pl.ds(start, lane_tile)].astype(f32)
                mine = jnp.where(row == rows_ref[var] % row_tile, tile, 0.0)
                mine = jnp.sum(mine, axis=0, keepdims=True)
                tail = jnp.where(place == half * vars_dev + var, mine, tail)
        out_refs[step][halves * tok_rows :, :] = tail.astype(bf16)


def send_products(me, local_rows, streams, n_devices, extra):
    _, tok_rows, model_width = streams.shape
    vars_dev = local_rows.shape[0]
    halves = model_width // n_devices // lane_tile
    rows_out = halves * tok_rows + extra
    return pl.pallas_call(
        functools.partial(send_products_kernel, halves, vars_dev),
        in_specs=[
            pl.BlockSpec(memory_space=pltpu.SMEM),
            pl.BlockSpec(memory_space=pltpu.SMEM),
            pl.BlockSpec(memory_space=pltpu.HBM),
        ],
        out_specs=[whole_spec()] * n_devices,
        out_shape=[jax.ShapeDtypeStruct((rows_out, lane_tile), bf16)] * n_devices,
        scratch_shapes=[
            pltpu.VMEM((n_devices, 2, tok_rows, halves * lane_tile), bf16),
            pltpu.VMEM((vars_dev, row_tile, model_width), bf16),
            pltpu.SemaphoreType.DMA((n_devices,)),
            pltpu.SemaphoreType.DMA((vars_dev,)),
        ],
        compiler_params=pltpu.CompilerParams(vmem_limit_bytes=60 * MIB),
        cost_estimate=pl.CostEstimate(
            flops=tok_rows * model_width, bytes_accessed=6 * tok_rows * model_width, transcendentals=0
        ),
        name="send_products",
    )(me, local_rows, streams)


def direct_filter_kernel(vars_dev, halves, tok_rows, me_ref, *refs):
    spectrum_ref, forward_ref, inverse_ref, positions_ref, gain_ref, unembed_ref = refs[:6]
    points, arrived, leaving, packed = refs[-4:]
    n_devices = arrived.shape[0]
    in_refs, out_refs = refs[6 : 6 + n_devices], refs[6 + n_devices : 6 + 2 * n_devices]
    me = me_ref[0]
    for step in range(n_devices):
        arrived[me ^ step] = in_refs[step][...]

    n_blocks, double, width = points.shape
    block = double // 2
    per_block = block // tok_rows

    def forward_step(step, carry):
        pieces = []
        for half in range(halves):
            parts = [stacked(arrived, step * per_block + m, half, tok_rows) for m in range(per_block)]
            pieces.append(jnp.concatenate(parts, axis=0))
        signal = jnp.concatenate(pieces, axis=1)
        both = jnp.dot(forward_ref[...], signal, preferred_element_type=f32)
        points[step] = both[:double] + both[double:]
        return carry

    lax.fori_loop(0, n_blocks, forward_step, 0)
    multiply_points(points, spectrum_ref)

    def inverse_step(step, carry):
        highs, lows = split_bf16(points[step])
        both = jnp.dot(inverse_ref[...], highs, preferred_element_type=f32)
        rest = jnp.dot(inverse_ref[:block, :], lows, preferred_element_type=f32)
        result = (both[:block] + both[block:] + rest).astype(bf16)
        for member in range(per_block):
            for half in range(halves):
                leaving[step * per_block + member, half * tok_rows : (half + 1) * tok_rows, :] = result[
                    member * tok_rows : (member + 1) * tok_rows,
                    half * lane_tile : (half + 1) * lane_tile,
                ]
        return carry

    lax.fori_loop(0, n_blocks, inverse_step, 0)

    length = n_devices * tok_rows
    column = lax.broadcasted_iota(jnp.int32, (positions_ref.shape[0], length), 1)
    picker = (column == positions_ref[...]).astype(f32).astype(bf16)
    tails = arrived[:, halves * tok_rows :, :].astype(f32)
    place = lax.broadcasted_iota(jnp.int32, tails.shape, 1)
    raw = None
    squares = None
    for half in range(halves):
        lanes = slice(half * lane_tile, (half + 1) * lane_tile)
        picked = [
            jnp.sum(jnp.where(place == half * vars_dev + var, tails, 0.0), axis=1)
            for var in range(vars_dev)
        ]
        gate_rows = picked[0] if vars_dev == 1 else jnp.concatenate(picked, axis=0)
        filtered = leaving[:, half * tok_rows : (half + 1) * tok_rows, :].reshape(length, lane_tile)
        filtered = jnp.dot(picker, filtered, preferred_element_type=f32)
        rows = (gate_rows * filtered).astype(bf16).astype(f32)
        weighted = (rows * gain_ref[:, lanes]).astype(bf16)
        part = jnp.dot(weighted, unembed_ref[lanes, :], preferred_element_type=f32)
        raw = part if raw is None else raw + part
        squares = rows * rows if squares is None else squares + rows * rows
    pack_scores(raw, squares, vars_dev, packed, n_devices)
    extra = packed.shape[0] // n_devices
    leaving[:, halves * tok_rows :, :] = packed[...].reshape(n_devices, extra, lane_tile).astype(bf16)
    for step in range(n_devices):
        out_refs[step][...] = leaving[me ^ step]


def direct_filter(me, operands, arrivals, vars_dev, tok_rows, extra):
    n_devices = len(arrivals)
    n_blocks, double, width = operands[0].shape
    halves = width // lane_tile
    rows_out = halves * tok_rows + extra
    flops = 2 * width * n_blocks * (double * double * 5 // 2 + 4 * n_blocks * double)
    return pl.pallas_call(
        functools.partial(direct_filter_kernel, vars_dev, halves, tok_rows),
        in_specs=[pl.BlockSpec(memory_space=pltpu.SMEM)]
        + [whole_spec()] * (len(operands) + n_devices),
        out_specs=[whole_spec()] * n_devices,
        out_shape=[jax.ShapeDtypeStruct((rows_out, lane_tile), bf16)] * n_devices,
        scratch_shapes=[
            pltpu.VMEM((n_blocks, double, width), f32),
            pltpu.VMEM((n_devices, arrivals[0].shape[0], lane_tile), bf16),
            pltpu.VMEM((n_devices, rows_out, lane_tile), bf16),
            pltpu.VMEM((n_devices * extra, lane_tile), f32),
        ],
        compiler_params=pltpu.CompilerParams(vmem_limit_bytes=32 * MIB),
        cost_estimate=pl.CostEstimate(flops=flops, bytes_accessed=8 * MIB, transcendentals=0),
        name="direct_filter",
    )(me, *operands, *arrivals)


def direct_finish_kernel(halves, vars_dev, vocab, me_ref, ref_ref, alt_ref, streams_ref, *refs):
    gates, results, gate_sems, out_sems = refs[-4:]
    n_devices = gates.shape[0]
    back_refs, mixed_ref, scores_ref = refs[:n_devices], refs[n_devices], refs[n_devices + 1]
    tok_rows = streams_ref.shape[1]
    width = halves * lane_tile
    me = me_ref[0]

    def lanes_of(step):
        return pl.ds(pl.multiple_of((me ^ step) * width, lane_tile), width)

    def gate_copy(step):
        return pltpu.make_async_copy(
            streams_ref.at[0, :, lanes_of(step)], gates.at[step], gate_sems.at[step]
        )

    def out_copy(step):
        return pltpu.make_async_copy(
            results.at[step], mixed_ref.at[:, lanes_of(step)], out_sems.at[step]
        )

    for step in range(n_devices):
        gate_copy(step).start()
    sums = None
    for step in range(n_devices):
        gate_copy(step).wait()
        for half in range(halves):
            lanes = slice(half * lane_tile, (half + 1) * lane_tile)
            filtered = back_refs[step][half * tok_rows : (half + 1) * tok_rows, :].astype(f32)
            results[step, :, lanes] = (gates[step, :, lanes].astype(f32) * filtered).astype(bf16)
        out_copy(step).start()
        tail = back_refs[step][halves * tok_rows :, :].astype(f32)
        sums = tail if sums is None else sums + tail
    model_width = n_devices * width
    scores_ref[...] = final_scores(sums, vars_dev, vocab, model_width, ref_ref, alt_ref)
    for step in range(n_devices):
        out_copy(step).wait()


def direct_finish(me, ref_ids, alt_ids, streams, backs, vocab):
    _, tok_rows, model_width = streams.shape
    n_devices = len(backs)
    vars_dev = ref_ids.shape[0]
    width = model_width // n_devices
    return pl.pallas_call(
        functools.partial(direct_finish_kernel, width // lane_tile, vars_dev, vocab),
        in_specs=[pl.BlockSpec(memory_space=pltpu.SMEM)] * 3
        + [pl.BlockSpec(memory_space=pltpu.HBM)]
        + [whole_spec()] * n_devices,
        out_specs=[pl.BlockSpec(memory_space=pltpu.HBM), whole_spec()],
        out_shape=[
            jax.ShapeDtypeStruct((tok_rows, model_width), bf16),
            jax.ShapeDtypeStruct((2, vars_dev), f32),
        ],
        scratch_shapes=[
            pltpu.VMEM((n_devices, tok_rows, width), bf16),
            pltpu.VMEM((n_devices, tok_rows, width), bf16),
            pltpu.SemaphoreType.DMA((n_devices,)),
            pltpu.SemaphoreType.DMA((n_devices,)),
        ],
        compiler_params=pltpu.CompilerParams(vmem_limit_bytes=12 * MIB),
        cost_estimate=pl.CostEstimate(
            flops=tok_rows * model_width, bytes_accessed=6 * tok_rows * model_width, transcendentals=0
        ),
        name="direct_finish",
    )(me, ref_ids, alt_ids, streams, *backs)


def exchange(parts):
    n_devices = len(parts)
    moved = [parts[0]] + [None] * (n_devices - 1)
    for step in range(n_devices - 1, 0, -1):
        pairs = [(device, device ^ step) for device in range(n_devices)]
        moved[step] = lax.ppermute(parts[step], "seq", pairs)
    return moved


def shards(streams, long_filter, gain, unembed, offsets, ref_ids, alt_ids):
    n_devices = lax.axis_size("seq")
    my_index = lax.axis_index("seq")
    _, tok_rows, model_width = streams.shape
    group_width = model_width // n_devices
    vars_dev = ref_ids.shape[0]
    vocab = unembed.shape[1]
    chunks = max(1, group_width // lane_tile)
    width = group_width // chunks
    block = tok_rows * block_devices(n_devices, tok_rows)
    forward, inverse = (jnp.asarray(table) for table in block_tables(block))

    slot = tok_rows // vars_dev
    starts = jnp.arange(vars_dev, dtype=jnp.int32) * slot
    local_rows = starts + lax.dynamic_slice_in_dim(offsets, my_index * vars_dev, vars_dev)
    by_device = offsets.reshape(n_devices, vars_dev)
    positions = by_device + starts[None, :]
    positions += jnp.arange(n_devices, dtype=jnp.int32)[:, None] * tok_rows
    positions = positions.T.reshape(n_devices * vars_dev, 1)
    my_gain = lax.dynamic_slice_in_dim(gain, my_index * group_width, group_width).astype(f32)

    if chunks * lane_tile == group_width and n_devices & (n_devices - 1) == 0:
        me = jnp.reshape(my_index, (1,)).astype(jnp.int32)
        gate_extra = round_up(chunks * vars_dev, row_tile)
        score_extra = round_up(vars_dev * 2 * (vocab // lane_tile + 1), row_tile)
        arrivals = exchange(send_products(me, local_rows, streams, n_devices, gate_extra))
        spectrum = filter_spectrum(long_filter, forward, block)
        operands = (spectrum, forward, inverse, positions, my_gain[None, :], unembed)
        leaving = direct_filter(me, operands, arrivals, vars_dev, tok_rows, score_extra)
        mixed, scores = direct_finish(me, ref_ids, alt_ids, streams, exchange(leaving), vocab)
        return (mixed, scores)

    gate_extra = round_up(chunks * vars_dev, row_tile)
    score_extra = round_up(vars_dev * 2 * (vocab // width + 1), row_tile)
    products = make_products(streams, local_rows, n_devices, chunks, gate_extra)
    moved = [lax.all_to_all(part, "seq", split_axis=0, concat_axis=0, tiled=True) for part in products]
    carried = ()
    backs = []
    for chunk in range(chunks):
        mine = slice(chunk * width, (chunk + 1) * width)
        spectrum = filter_spectrum(long_filter[mine], forward, block)
        operands = (
            moved[chunk], spectrum, forward, inverse, positions,
            my_gain[None, mine], unembed[mine],
        )
        if chunk > 0:
            carried = (gates,) + tuple(carried)
        results = filter_chunk(chunk, chunks, vars_dev, tok_rows, score_extra, operands, carried)
        carried = results[1:3]
        if chunk == 0 and chunks > 1:
            gates = results[3]
        backs.append(lax.all_to_all(results[0], "seq", split_axis=0, concat_axis=0, tiled=True))
    mixed, scores = finish(streams, backs, ref_ids, alt_ids, vocab)
    return (mixed, scores)


def solution(mesh):
    placed = (
        P(None, ("grp", "seq"), None),
        P("seq", None),
        P(),
        P("seq", None),
        P("grp"),
        P(("grp", "seq")),
        P(("grp", "seq")),
    )
    return jax.shard_map(
        shards,
        mesh=mesh,
        in_specs=placed,
        out_specs=(P(("grp", "seq"), None), P(None, ("grp", "seq"))),
        check_vma=False,
    )
```

```python
import functools
import math

import jax
import jax.numpy as jnp
import numpy as np
from jax import lax
from jax.experimental import pallas as pl
from jax.experimental.pallas import tpu as pltpu
from jax.sharding import PartitionSpec as P

norm_eps = 1e-06
f32 = jnp.float32
bf16 = jnp.bfloat16
row_tile = 16
half_tile = 8
lane_tile = 128
MIB = 1 << 20


def round_up(value, step):
    return -(-value // step) * step


def split_bf16(values):
    high = values.astype(bf16)
    low = (values - high.astype(f32)).astype(bf16)
    return high, low


def block_tables(block):
    turns = (4 * np.arange(block)[:, None] + 1) * np.arange(block)[None, :] % (4 * block)
    theta = turns * (math.pi / (2 * block))
    table = np.concatenate([np.cos(theta), np.sin(theta)], axis=0)
    parts = []
    for matrix in (table, table.T / block):
        high = matrix.astype(bf16)
        low = (matrix - high.astype(np.float64)).astype(bf16)
        parts.append(np.concatenate([high, low], axis=0))
    return parts


def block_devices(n_devices, tok_rows):
    target = math.isqrt(32 * n_devices * tok_rows)
    count = 1
    while n_devices % (2 * count) == 0 and 2 * count * tok_rows <= target:
        count *= 2
    return count


def whole_spec():
    return pl.BlockSpec(memory_space=pltpu.VMEM)


def product_kernel(chunks, width, vars_dev, rows_ref, streams_ref, *out_refs):
    tok_rows = streams_ref.shape[1]
    n_owners = out_refs[0].shape[0]
    extra = out_refs[0].shape[1] - tok_rows
    place = lax.broadcasted_iota(jnp.int32, (extra, tok_rows), 0)
    column = lax.broadcasted_iota(jnp.int32, (extra, tok_rows), 1)
    for owner in range(n_owners):
        gates = jnp.zeros((extra, width), f32)
        for chunk in range(chunks):
            lanes = pl.ds((owner * chunks + chunk) * width, width)
            left = streams_ref[1, :, lanes].astype(f32)
            right = streams_ref[2, :, lanes].astype(f32)
            out_refs[chunk][owner, :tok_rows, :] = (left * right).astype(bf16)
            picker = jnp.zeros((extra, tok_rows), jnp.bool_)
            for var in range(vars_dev):
                picker |= (place == chunk * vars_dev + var) & (column == rows_ref[var])
            gates += jnp.dot(
                picker.astype(f32).astype(bf16),
                streams_ref[0, :, lanes],
                preferred_element_type=f32,
            )
        out_refs[0][owner, tok_rows:, :] = gates.astype(bf16)


def make_products(streams, local_rows, n_devices, chunks, extra):
    _, tok_rows, model_width = streams.shape
    vars_dev = local_rows.shape[0]
    group_width = model_width // n_devices
    width = group_width // chunks
    owners = max(1, n_devices // 4)
    while owners * group_width % lane_tile:
        owners *= 2
    steps = n_devices // owners
    rows_out = [tok_rows + extra] + [tok_rows] * (chunks - 1)
    return pl.pallas_call(
        functools.partial(product_kernel, chunks, width, vars_dev),
        grid=(steps,),
        in_specs=[
            pl.BlockSpec(memory_space=pltpu.SMEM),
            pl.BlockSpec((3, tok_rows, owners * group_width), lambda i: (0, 0, i)),
        ],
        out_specs=[pl.BlockSpec((owners, rows, width), lambda i: (i, 0, 0)) for rows in rows_out],
        out_shape=[jax.ShapeDtypeStruct((n_devices, rows, width), bf16) for rows in rows_out],
        compiler_params=pltpu.CompilerParams(vmem_limit_bytes=24 * MIB),
        name="products",
    )(local_rows, streams)


def spectrum_kernel(block, filter_ref, forward_ref, out_ref):
    n_blocks = out_ref.shape[0]
    for index in range(n_blocks):
        taps = filter_ref[:, index * block : (index + 1) * block]
        both = lax.dot_general(
            forward_ref[...], taps, (((1,), (1,)), ((), ())), preferred_element_type=f32
        )
        out_ref[index] = both[: 2 * block] + both[2 * block :]


def filter_spectrum(taps, forward, block):
    width, length = taps.shape
    n_blocks = length // block
    return pl.pallas_call(
        functools.partial(spectrum_kernel, block),
        in_specs=[whole_spec(), whole_spec()],
        out_specs=whole_spec(),
        out_shape=jax.ShapeDtypeStruct((n_blocks, 2 * block, width), f32),
        compiler_params=pltpu.CompilerParams(vmem_limit_bytes=40 * MIB),
        cost_estimate=pl.CostEstimate(
            flops=8 * block * length * width, bytes_accessed=4 * MIB, transcendentals=0
        ),
        name="filter_spectrum",
    )(taps, forward)


def multiply_points(points, spectrum_ref):
    n_blocks, double, width = points.shape
    block = double // 2
    lanes_step = min(width, lane_tile)

    def multiply_step(step, carry):
        start = pl.multiple_of(step * half_tile, half_tile)
        upper = pl.ds(start, half_tile)
        lower = pl.ds(pl.multiple_of(block + start, half_tile), half_tile)
        for first in range(0, width, lanes_step):
            lanes = slice(first, first + lanes_step)

            def block_sum(total):
                sum_re = jnp.zeros((half_tile, lanes_step), f32)
                sum_im = jnp.zeros((half_tile, lanes_step), f32)
                for delay in range(total + 1):
                    a_re = points[total - delay, upper, lanes]
                    a_im = points[total - delay, lower, lanes]
                    b_re = spectrum_ref[delay, upper, lanes]
                    b_im = spectrum_ref[delay, lower, lanes]
                    sum_re += a_re * b_re - a_im * b_im
                    sum_im += a_re * b_im + a_im * b_re
                return sum_re, sum_im

            after_re, after_im = block_sum(n_blocks - 1)
            for total in range(n_blocks - 1, 0, -1):
                sum_re, sum_im = block_sum(total - 1)
                points[total, upper, lanes] = after_re + sum_im
                points[total, lower, lanes] = after_im - sum_re
                after_re, after_im = sum_re, sum_im
            points[0, upper, lanes] = after_re
            points[0, lower, lanes] = after_im
        return carry

    lax.fori_loop(0, block // half_tile, multiply_step, 0)


def convolve(chunk_ref, spectrum_ref, forward_ref, inverse_ref, out_ref, points, tok_rows):
    n_blocks, double, width = points.shape
    block = double // 2
    per_block = block // tok_rows
    group = max(1, min(n_blocks, 256 // width)) if width % lane_tile == 0 else 1

    def forward_step(step, carry):
        pieces = []
        for member in range(group):
            start = (step * group + member) * per_block
            rows = chunk_ref[pl.ds(start, per_block), :tok_rows, :]
            pieces.append(rows.reshape(block, width))
        signal = pieces[0] if group == 1 else jnp.concatenate(pieces, axis=1)
        both = jnp.dot(forward_ref[...], signal, preferred_element_type=f32)
        total = both[:double] + both[double:]
        for member in range(group):
            points[step * group + member] = total[:, member * width : (member + 1) * width]
        return carry

    lax.fori_loop(0, n_blocks // group, forward_step, 0)

    multiply_points(points, spectrum_ref)

    def inverse_step(step, carry):
        first = step * group
        pieces = [points[first + member] for member in range(group)]
        highs, lows = split_bf16(pieces[0] if group == 1 else jnp.concatenate(pieces, axis=1))
        both = jnp.dot(inverse_ref[...], highs, preferred_element_type=f32)
        rest = jnp.dot(inverse_ref[:block, :], lows, preferred_element_type=f32)
        result = (both[:block] + both[block:] + rest).astype(bf16)
        for member in range(group):
            piece = result[:, member * width : (member + 1) * width]
            out_ref[pl.ds((first + member) * per_block, per_block), :tok_rows, :] = piece.reshape(
                per_block, tok_rows, width
            )
        return carry

    lax.fori_loop(0, n_blocks // group, inverse_step, 0)


def score_rows(index, vars_dev, tok_rows, positions, gate_block, out_ref, gain_row, unembed):
    n_devices, extra, width = gate_block.shape
    gates = gate_block.astype(f32)
    place = lax.broadcasted_iota(jnp.int32, (n_devices, extra, width), 1)
    picked = [
        jnp.sum(jnp.where(place == index * vars_dev + var, gates, 0.0), axis=1)
        for var in range(vars_dev)
    ]
    gate_rows = picked[0] if vars_dev == 1 else jnp.concatenate(picked, axis=0)
    length = n_devices * tok_rows
    column = lax.broadcasted_iota(jnp.int32, (positions.shape[0], length), 1)
    picker = (column == positions).astype(f32).astype(bf16)
    filtered = jnp.dot(
        picker, out_ref[:, :tok_rows, :].reshape(length, width), preferred_element_type=f32
    )
    rows = (gate_rows * filtered).astype(bf16).astype(f32)
    weighted = (rows * gain_row).astype(bf16)
    return jnp.dot(weighted, unembed, preferred_element_type=f32), rows * rows


def pack_scores(raw, squares, vars_dev, packed, n_devices):
    total, width = packed.shape
    extra = total // n_devices
    per_row = raw.shape[1] // width
    packed[...] = jnp.zeros_like(packed)
    for var in range(vars_dev):
        mine = slice(var * n_devices, (var + 1) * n_devices)
        pieces = [raw[mine, r * width : (r + 1) * width] for r in range(per_row)] + [squares[mine]]
        for row, piece in enumerate(pieces):
            rounded = piece.astype(bf16).astype(f32)
            base = var * 2 * (per_row + 1) + row
            packed[pl.ds(base, n_devices, stride=extra), :] = rounded
            packed[pl.ds(base + per_row + 1, n_devices, stride=extra), :] = piece - rounded


def chunk_kernel(index, chunks, vars_dev, tok_rows, *refs):
    refs = list(refs)
    chunk_ref, spectrum_ref, forward_ref, inverse_ref = refs[:4]
    positions_ref, gain_ref, unembed_ref = refs[4:7]
    refs = refs[7:]
    first, last = index == 0, index == chunks - 1
    gates_ref = None if first else refs.pop(0)
    raw_before, square_before = (None, None) if first else (refs.pop(0), refs.pop(0))
    out_ref = refs.pop(0)
    raw_out, square_out = (None, None) if last else (refs.pop(0), refs.pop(0))
    gates_out = refs.pop(0) if first and not last else None
    points = refs[0]
    convolve(chunk_ref, spectrum_ref, forward_ref, inverse_ref, out_ref, points, tok_rows)
    gate_block = chunk_ref[:, tok_rows:, :] if first else gates_ref[...]
    raw, squares = score_rows(
        index, vars_dev, tok_rows, positions_ref[...], gate_block, out_ref, gain_ref[...], unembed_ref[...]
    )
    if not first:
        raw = raw + raw_before[...]
        squares = squares + square_before[...]
    if gates_out is not None:
        gates_out[...] = gate_block
    if not last:
        raw_out[...] = raw
        square_out[...] = squares
        return
    packed = refs[1]
    n_devices, _, width = out_ref.shape
    extra = out_ref.shape[1] - tok_rows
    pack_scores(raw, squares, vars_dev, packed, n_devices)
    out_ref[:, tok_rows:, :] = packed[...].reshape(n_devices, extra, width).astype(bf16)


def filter_chunk(index, chunks, vars_dev, tok_rows, extra, operands, carried):
    moved, spectrum = operands[:2]
    n_devices, _, width = moved.shape
    n_blocks, double, _ = spectrum.shape
    vocab = operands[6].shape[1]
    n_vars = operands[4].shape[0]
    first, last = index == 0, index == chunks - 1
    rows_out = tok_rows + (extra if last else 0)
    out_shape = [jax.ShapeDtypeStruct((n_devices, rows_out, width), bf16)]
    scratch = [pltpu.VMEM((n_blocks, double, width), f32)]
    if last:
        scratch.append(pltpu.VMEM((n_devices * extra, width), f32))
    else:
        out_shape.append(jax.ShapeDtypeStruct((n_vars, vocab), f32))
        out_shape.append(jax.ShapeDtypeStruct((n_vars, width), f32))
    if first and not last:
        out_shape.append(jax.ShapeDtypeStruct((n_devices, moved.shape[1] - tok_rows, width), bf16))
    flops = 2 * width * n_blocks * (double * double * 5 // 2 + 4 * n_blocks * double)
    return pl.pallas_call(
        functools.partial(chunk_kernel, index, chunks, vars_dev, tok_rows),
        in_specs=[whole_spec()] * (len(operands) + len(carried)),
        out_specs=[whole_spec()] * len(out_shape),
        out_shape=out_shape,
        scratch_shapes=scratch,
        compiler_params=pltpu.CompilerParams(vmem_limit_bytes=(20 if n_blocks <= 8 else 58) * MIB),
        cost_estimate=pl.CostEstimate(flops=flops, bytes_accessed=8 * MIB, transcendentals=0),
        name="filter_chunk",
    )(*operands, *carried)


def final_scores(sums, vars_dev, vocab, model_width, ref_ref, alt_ref):
    width = sums.shape[1]
    per_row = vocab // width
    ids = lax.broadcasted_iota(jnp.int32, (per_row, width), 0) * width
    ids += lax.broadcasted_iota(jnp.int32, (per_row, width), 1)
    row = lax.broadcasted_iota(jnp.int32, (2, vars_dev), 0)
    column = lax.broadcasted_iota(jnp.int32, (2, vars_dev), 1)
    scores = jnp.zeros((2, vars_dev), f32)

    def whole_sum(values):
        return jnp.sum(jnp.sum(values, axis=1, keepdims=True), axis=0, keepdims=True)

    for var in range(vars_dev):
        base = var * 2 * (per_row + 1)
        both = sums[base : base + per_row + 1, :]
        both = both + sums[base + per_row + 1 : base + 2 * (per_row + 1), :]
        square = jnp.sum(both[per_row:, :], axis=1, keepdims=True)
        logits = both[:per_row, :] * lax.rsqrt(square / model_width + norm_eps)
        largest = jnp.max(jnp.max(logits, axis=1, keepdims=True), axis=0, keepdims=True)
        log_total = largest + jnp.log(whole_sum(jnp.exp(logits - largest)))
        ref_logit = whole_sum(jnp.where(ids == ref_ref[var], logits, 0.0))
        alt_logit = whole_sum(jnp.where(ids == alt_ref[var], logits, 0.0))
        pair = jnp.where(row == 0, ref_logit - log_total, alt_logit - ref_logit)
        scores = jnp.where(column == var, pair, scores)
    return scores


def finish_kernel(chunks, vars_dev, vocab, ref_ref, alt_ref, streams_ref, *refs):
    back_refs, mixed_ref, scores_ref, sums = refs[:chunks], refs[chunks], refs[chunks + 1], refs[chunks + 2]
    tok_rows = streams_ref.shape[1]
    owners, _, width = back_refs[0].shape
    step = pl.program_id(0)
    for owner in range(owners):
        for chunk in range(chunks):
            lanes = pl.ds((owner * chunks + chunk) * width, width)
            gate = streams_ref[0, :, lanes].astype(f32)
            filtered = back_refs[chunk][owner, :tok_rows, :].astype(f32)
            mixed_ref[:, lanes] = (gate * filtered).astype(bf16)
    part = jnp.sum(back_refs[-1][:, tok_rows:, :].astype(f32), axis=0)

    @pl.when(step == 0)
    def _():
        sums[...] = part

    @pl.when(step > 0)
    def _():
        sums[...] += part

    @pl.when(step == pl.num_programs(0) - 1)
    def _():
        model_width = pl.num_programs(0) * owners * chunks * width
        scores_ref[...] = final_scores(sums[...], vars_dev, vocab, model_width, ref_ref, alt_ref)


def finish(streams, backs, ref_ids, alt_ids, vocab):
    _, tok_rows, model_width = streams.shape
    chunks = len(backs)
    n_devices, _, width = backs[0].shape
    vars_dev = ref_ids.shape[0]
    owners = max(1, n_devices // 4)
    while owners * chunks * width % lane_tile:
        owners *= 2
    extra = backs[-1].shape[1] - tok_rows
    return pl.pallas_call(
        functools.partial(finish_kernel, chunks, vars_dev, vocab),
        grid=(n_devices // owners,),
        in_specs=[
            pl.BlockSpec(memory_space=pltpu.SMEM),
            pl.BlockSpec(memory_space=pltpu.SMEM),
            pl.BlockSpec((1, tok_rows, owners * chunks * width), lambda i: (0, 0, i)),
        ]
        + [pl.BlockSpec((owners, back.shape[1], width), lambda i: (i, 0, 0)) for back in backs],
        out_specs=[
            pl.BlockSpec((tok_rows, owners * chunks * width), lambda i: (0, i)),
            pl.BlockSpec((2, vars_dev), lambda i: (0, 0)),
        ],
        out_shape=[
            jax.ShapeDtypeStruct((tok_rows, model_width), bf16),
            jax.ShapeDtypeStruct((2, vars_dev), f32),
        ],
        scratch_shapes=[pltpu.VMEM((extra, width), f32)],
        compiler_params=pltpu.CompilerParams(vmem_limit_bytes=24 * MIB),
        name="finish",
    )(ref_ids, alt_ids, streams, *backs)

def send_products_kernel(first, together, halves, vars_dev, me_ref, offsets_ref, streams_ref, *refs):
    built, pairs, gates, pair_sems, gate_sems, out_sems = refs[-6:]
    out_refs = refs[:-6]
    count, _, tok_rows, width = pairs.shape
    me = me_ref[0]
    slot = tok_rows // vars_dev
    local_rows = [var * slot + offsets_ref[me * vars_dev + var] for var in range(vars_dev)]
    base = me // count * count

    def partner(step):
        return base + step if together else me ^ (first + step)

    def pair_copy(step):
        start = pl.multiple_of(partner(step) * width, lane_tile)
        return pltpu.make_async_copy(
            streams_ref.at[pl.ds(1, 2), :, pl.ds(start, width)], pairs.at[step], pair_sems.at[step]
        )

    def gate_copy(var):
        start = pl.multiple_of(local_rows[var] // row_tile * row_tile, row_tile)
        return pltpu.make_async_copy(
            streams_ref.at[0, pl.ds(start, row_tile), :], gates.at[var], gate_sems.at[var]
        )

    def out_copy(step):
        target = out_refs[0].at[step] if together else out_refs[step]
        return pltpu.make_async_copy(built.at[step], target, out_sems.at[step])

    for var in range(vars_dev):
        gate_copy(var).start()
    for step in range(count):
        pair_copy(step).start()
    for var in range(vars_dev):
        gate_copy(var).wait()
    extra = built.shape[1] - halves * tok_rows
    row = lax.broadcasted_iota(jnp.int32, (row_tile, lane_tile), 0)
    place = lax.broadcasted_iota(jnp.int32, (extra, lane_tile), 0)
    for step in range(count):
        pair_copy(step).wait()
        tail = jnp.zeros((extra, lane_tile), f32)
        for half in range(halves):
            lanes = slice(half * lane_tile, (half + 1) * lane_tile)
            rows = slice(half * tok_rows, (half + 1) * tok_rows)
            built[step, rows, :] = pairs[step, 0, :, lanes] * pairs[step, 1, :, lanes]
            start = pl.multiple_of(partner(step) * width + half * lane_tile, lane_tile)
            for var in range(vars_dev):
                tile = gates[var, :, pl.ds(start, lane_tile)].astype(f32)
                mine = jnp.where(row == local_rows[var] % row_tile, tile, 0.0)
                mine = jnp.sum(mine, axis=0, keepdims=True)
                tail = jnp.where(place == half * vars_dev + var, mine, tail)
        built[step, halves * tok_rows :, :] = tail.astype(bf16)
        out_copy(step).start()
    for step in range(count):
        out_copy(step).wait()


def send_products(me, offsets, streams, first, count, together, vars_dev, n_devices, extra):
    _, tok_rows, model_width = streams.shape
    width = model_width // n_devices
    halves = width // lane_tile
    rows_out = halves * tok_rows + extra
    if together:
        out_shape = [jax.ShapeDtypeStruct((count, rows_out, lane_tile), bf16)]
    else:
        out_shape = [jax.ShapeDtypeStruct((rows_out, lane_tile), bf16)] * count
    return pl.pallas_call(
        functools.partial(send_products_kernel, first, together, halves, vars_dev),
        in_specs=[
            pl.BlockSpec(memory_space=pltpu.SMEM),
            pl.BlockSpec(memory_space=pltpu.SMEM),
            pl.BlockSpec(memory_space=pltpu.HBM),
        ],
        out_specs=[pl.BlockSpec(memory_space=pltpu.HBM)] * len(out_shape),
        out_shape=out_shape,
        scratch_shapes=[
            pltpu.VMEM((count, rows_out, lane_tile), bf16),
            pltpu.VMEM((count, 2, tok_rows, width), bf16),
            pltpu.VMEM((vars_dev, row_tile, model_width), bf16),
            pltpu.SemaphoreType.DMA((count,)),
            pltpu.SemaphoreType.DMA((vars_dev,)),
            pltpu.SemaphoreType.DMA((count,)),
        ],
        compiler_params=pltpu.CompilerParams(vmem_limit_bytes=60 * MIB),
        cost_estimate=pl.CostEstimate(
            flops=tok_rows * count * width, bytes_accessed=6 * tok_rows * count * width, transcendentals=0
        ),
        name="send_products",
    )(me, offsets, streams)


def direct_filter_kernel(vars_dev, halves, tok_rows, me_ref, *refs):
    positions_ref, gain_ref, unembed_ref, forward_ref, inverse_hbm, spectrum_hbm = refs[:6]
    points, arrived, leaving, packed, spectrum, inverse = refs[-11:-5]
    in_sems, out_sems, tail_sems, spectrum_sem, inverse_sem = refs[-5:]
    n_devices = arrived.shape[0]
    near = n_devices // 2
    far = n_devices - near
    in_refs = refs[6 : 7 + far]
    out_refs = refs[7 + far : 8 + 2 * far]
    me = me_ref[0]
    base = me // near * near
    body = halves * tok_rows

    def in_copy(index):
        target = arrived.at[pl.ds(base, near)] if index == 0 else arrived.at[me ^ (near + index - 1)]
        return pltpu.make_async_copy(in_refs[index], target, in_sems.at[index])

    def out_copy(index, start, size, sems):
        rows = pl.ds(start, size)
        if index == 0:
            source, target = leaving.at[pl.ds(base, near), rows], out_refs[0].at[:, rows]
        else:
            source, target = leaving.at[me ^ (near + index - 1), rows], out_refs[index].at[rows]
        return pltpu.make_async_copy(source, target, sems.at[index])

    spectrum_copy = pltpu.make_async_copy(spectrum_hbm, spectrum, spectrum_sem.at[0])
    inverse_copy = pltpu.make_async_copy(inverse_hbm, inverse, inverse_sem.at[0])
    for index in range(far + 1):
        in_copy(index).start()
    spectrum_copy.start()
    inverse_copy.start()
    for index in range(far + 1):
        in_copy(index).wait()

    n_blocks, double, width = points.shape
    block = double // 2
    per_block = block // tok_rows

    def forward_step(step, carry):
        pieces = []
        for half in range(halves):
            rows = slice(half * tok_rows, (half + 1) * tok_rows)
            parts = [arrived[step * per_block + m, rows, :] for m in range(per_block)]
            pieces.append(jnp.concatenate(parts + parts, axis=0))
        signal = jnp.concatenate(pieces, axis=1)
        points[step] = jnp.dot(forward_ref[...], signal, preferred_element_type=f32)
        return carry

    lax.fori_loop(0, n_blocks, forward_step, 0)
    spectrum_copy.wait()
    multiply_points(points, spectrum)
    inverse_copy.wait()

    def inverse_step(step, carry):
        highs, lows = split_bf16(points[step])
        terms = jnp.concatenate([highs, highs, lows], axis=0)
        result = jnp.dot(inverse[...], terms, preferred_element_type=f32).astype(bf16)
        for member in range(per_block):
            for half in range(halves):
                leaving[step * per_block + member, half * tok_rows : (half + 1) * tok_rows, :] = result[
                    member * tok_rows : (member + 1) * tok_rows,
                    half * lane_tile : (half + 1) * lane_tile,
                ]
        return carry

    lax.fori_loop(0, n_blocks, inverse_step, 0)
    for index in range(far, -1, -1):
        out_copy(index, 0, body, out_sems).start()

    length = n_devices * tok_rows
    column = lax.broadcasted_iota(jnp.int32, (positions_ref.shape[0], length), 1)
    picker = (column == positions_ref[...]).astype(f32).astype(bf16)
    tails = arrived[:, body:, :].astype(f32)
    place = lax.broadcasted_iota(jnp.int32, tails.shape, 1)
    raw = None
    squares = None
    for half in range(halves):
        lanes = slice(half * lane_tile, (half + 1) * lane_tile)
        picked = [
            jnp.sum(jnp.where(place == half * vars_dev + var, tails, 0.0), axis=1)
            for var in range(vars_dev)
        ]
        gate_rows = picked[0] if vars_dev == 1 else jnp.concatenate(picked, axis=0)
        filtered = leaving[:, half * tok_rows : (half + 1) * tok_rows, :].reshape(length, lane_tile)
        filtered = jnp.dot(picker, filtered, preferred_element_type=f32)
        rows = (gate_rows * filtered).astype(bf16).astype(f32)
        weighted = (rows * gain_ref[:, lanes]).astype(bf16)
        part = jnp.dot(weighted, unembed_ref[lanes, :], preferred_element_type=f32)
        raw = part if raw is None else raw + part
        squares = rows * rows if squares is None else squares + rows * rows
    pack_scores(raw, squares, vars_dev, packed, n_devices)
    extra = packed.shape[0] // n_devices
    leaving[:, body:, :] = packed[...].reshape(n_devices, extra, lane_tile).astype(bf16)
    for index in range(far, -1, -1):
        out_copy(index, body, extra, tail_sems).start()
    for index in range(far + 1):
        out_copy(index, 0, body, out_sems).wait()
        out_copy(index, body, extra, tail_sems).wait()


def direct_filter(me, operands, arrivals, vars_dev, tok_rows, extra):
    near = arrivals[0].shape[0]
    far = len(arrivals) - 1
    n_devices = near + far
    forward, inverse, spectrum = operands[3:]
    n_blocks, double, width = spectrum.shape
    halves = width // lane_tile
    rows_out = halves * tok_rows + extra
    flops = 2 * width * n_blocks * (double * double * 5 // 2 + 4 * n_blocks * double)
    in_hbm = pl.BlockSpec(memory_space=pltpu.HBM)
    return pl.pallas_call(
        functools.partial(direct_filter_kernel, vars_dev, halves, tok_rows),
        in_specs=[pl.BlockSpec(memory_space=pltpu.SMEM)]
        + [whole_spec()] * 4
        + [in_hbm] * (2 + len(arrivals)),
        out_specs=[in_hbm] * len(arrivals),
        out_shape=[jax.ShapeDtypeStruct((near, rows_out, lane_tile), bf16)]
        + [jax.ShapeDtypeStruct((rows_out, lane_tile), bf16)] * far,
        scratch_shapes=[
            pltpu.VMEM((n_blocks, double, width), f32),
            pltpu.VMEM((n_devices, arrivals[0].shape[1], lane_tile), bf16),
            pltpu.VMEM((n_devices, rows_out, lane_tile), bf16),
            pltpu.VMEM((n_devices * extra, lane_tile), f32),
            pltpu.VMEM(spectrum.shape, f32),
            pltpu.VMEM(inverse.shape, bf16),
            pltpu.SemaphoreType.DMA((far + 1,)),
            pltpu.SemaphoreType.DMA((far + 1,)),
            pltpu.SemaphoreType.DMA((far + 1,)),
            pltpu.SemaphoreType.DMA((1,)),
            pltpu.SemaphoreType.DMA((1,)),
        ],
        compiler_params=pltpu.CompilerParams(vmem_limit_bytes=32 * MIB),
        cost_estimate=pl.CostEstimate(flops=flops, bytes_accessed=8 * MIB, transcendentals=0),
        name="direct_filter",
    )(me, *operands, *arrivals)


def direct_finish_kernel(halves, vars_dev, vocab, me_ref, ref_ref, alt_ref, streams_ref, *refs):
    gates, results, gate_sems, out_sems = refs[-4:]
    n_devices, tok_rows, width = gates.shape
    near = n_devices // 2
    near_ref, far_refs = refs[0], refs[1 : 1 + n_devices - near]
    mixed_ref, scores_ref = refs[-6:-4]
    me = me_ref[0]
    base = me // near * near

    def lanes_of(step):
        owner = base + step if step < near else me ^ step
        return pl.ds(pl.multiple_of(owner * width, lane_tile), width)

    def gate_copy(step):
        return pltpu.make_async_copy(
            streams_ref.at[0, :, lanes_of(step)], gates.at[step], gate_sems.at[step]
        )

    def out_copy(step):
        return pltpu.make_async_copy(
            results.at[step], mixed_ref.at[:, lanes_of(step)], out_sems.at[step]
        )

    for step in range(n_devices):
        gate_copy(step).start()
    sums = None
    for step in range(n_devices):
        gate_copy(step).wait()
        block_ref = near_ref.at[step] if step < near else far_refs[step - near]
        for half in range(halves):
            lanes = slice(half * lane_tile, (half + 1) * lane_tile)
            filtered = block_ref[half * tok_rows : (half + 1) * tok_rows, :]
            results[step, :, lanes] = gates[step, :, lanes] * filtered
        out_copy(step).start()
        tail = block_ref[halves * tok_rows :, :].astype(f32)
        sums = tail if sums is None else sums + tail
    model_width = n_devices * width
    scores_ref[...] = final_scores(sums, vars_dev, vocab, model_width, ref_ref, alt_ref)
    for step in range(n_devices):
        out_copy(step).wait()


def direct_finish(me, ref_ids, alt_ids, streams, backs, vocab, n_devices):
    _, tok_rows, model_width = streams.shape
    vars_dev = ref_ids.shape[0]
    width = model_width // n_devices
    return pl.pallas_call(
        functools.partial(direct_finish_kernel, width // lane_tile, vars_dev, vocab),
        in_specs=[pl.BlockSpec(memory_space=pltpu.SMEM)] * 3
        + [pl.BlockSpec(memory_space=pltpu.HBM)]
        + [whole_spec()] * len(backs),
        out_specs=[pl.BlockSpec(memory_space=pltpu.HBM), whole_spec()],
        out_shape=[
            jax.ShapeDtypeStruct((tok_rows, model_width), bf16),
            jax.ShapeDtypeStruct((2, vars_dev), f32),
        ],
        scratch_shapes=[
            pltpu.VMEM((n_devices, tok_rows, width), bf16),
            pltpu.VMEM((n_devices, tok_rows, width), bf16),
            pltpu.SemaphoreType.DMA((n_devices,)),
            pltpu.SemaphoreType.DMA((n_devices,)),
        ],
        compiler_params=pltpu.CompilerParams(vmem_limit_bytes=12 * MIB),
        cost_estimate=pl.CostEstimate(
            flops=tok_rows * model_width, bytes_accessed=6 * tok_rows * model_width, transcendentals=0
        ),
        name="direct_finish",
    )(me, ref_ids, alt_ids, streams, *backs)


def exchange_near(part, n_devices):
    near = n_devices // 2
    groups = [list(range(near)), list(range(near, n_devices))]
    return lax.all_to_all(
        part, "seq", split_axis=0, concat_axis=0, axis_index_groups=groups, tiled=True
    )


def exchange_far(parts, n_devices):
    near = n_devices // 2
    moved = []
    for step, part in enumerate(parts):
        pairs = [(device, device ^ (near + step)) for device in range(n_devices)]
        moved.append(lax.ppermute(part, "seq", pairs))
    return moved


def shards(streams, long_filter, gain, unembed, offsets, ref_ids, alt_ids):
    n_devices = lax.axis_size("seq")
    my_index = lax.axis_index("seq")
    _, tok_rows, model_width = streams.shape
    group_width = model_width // n_devices
    vars_dev = ref_ids.shape[0]
    vocab = unembed.shape[1]
    chunks = max(1, group_width // lane_tile)
    width = group_width // chunks
    block = tok_rows * block_devices(n_devices, tok_rows)
    forward_np, inverse_np = block_tables(block)
    forward, inverse = jnp.asarray(forward_np), jnp.asarray(inverse_np)

    slot = tok_rows // vars_dev
    starts = jnp.arange(vars_dev, dtype=jnp.int32) * slot
    local_rows = starts + lax.dynamic_slice_in_dim(offsets, my_index * vars_dev, vars_dev)
    by_device = offsets.reshape(n_devices, vars_dev)
    positions = by_device + starts[None, :]
    positions += jnp.arange(n_devices, dtype=jnp.int32)[:, None] * tok_rows
    positions = positions.T.reshape(n_devices * vars_dev, 1)
    my_gain = lax.dynamic_slice_in_dim(gain, my_index * group_width, group_width).astype(f32)

    if chunks * lane_tile == group_width and n_devices & (n_devices - 1) == 0:
        me = jnp.reshape(my_index, (1,)).astype(jnp.int32)
        gate_extra = round_up(chunks * vars_dev, row_tile)
        score_extra = round_up(vars_dev * 2 * (vocab // lane_tile + 1), row_tile)
        near = n_devices // 2
        streams_args = (vars_dev, n_devices, gate_extra)
        far_parts = send_products(me, offsets, streams, near, n_devices - near, False, *streams_args)
        near_part = send_products(me, offsets, streams, 0, near, True, *streams_args)
        arrivals = [exchange_near(near_part[0], n_devices), *exchange_far(far_parts, n_devices)]
        spectrum = filter_spectrum(long_filter, forward, block)
        joined_forward = jnp.asarray(np.concatenate(np.split(forward_np, 2, axis=0), axis=1))
        joined_inverse = np.split(inverse_np, 2, axis=0)
        joined_inverse = jnp.asarray(np.concatenate(joined_inverse + joined_inverse[:1], axis=1))
        operands = (positions, my_gain[None, :], unembed, joined_forward, joined_inverse, spectrum)
        leaving = direct_filter(me, operands, arrivals, vars_dev, tok_rows, score_extra)
        backs = [exchange_near(leaving[0], n_devices), *exchange_far(leaving[1:], n_devices)]
        mixed, scores = direct_finish(me, ref_ids, alt_ids, streams, backs, vocab, n_devices)
        return (mixed, scores)

    gate_extra = round_up(chunks * vars_dev, row_tile)
    score_extra = round_up(vars_dev * 2 * (vocab // width + 1), row_tile)
    products = make_products(streams, local_rows, n_devices, chunks, gate_extra)
    moved = [lax.all_to_all(part, "seq", split_axis=0, concat_axis=0, tiled=True) for part in products]
    carried = ()
    backs = []
    for chunk in range(chunks):
        mine = slice(chunk * width, (chunk + 1) * width)
        spectrum = filter_spectrum(long_filter[mine], forward, block)
        operands = (
            moved[chunk], spectrum, forward, inverse, positions,
            my_gain[None, mine], unembed[mine],
        )
        if chunk > 0:
            carried = (gates,) + tuple(carried)
        results = filter_chunk(chunk, chunks, vars_dev, tok_rows, score_extra, operands, carried)
        carried = results[1:3]
        if chunk == 0 and chunks > 1:
            gates = results[3]
        backs.append(lax.all_to_all(results[0], "seq", split_axis=0, concat_axis=0, tiled=True))
    mixed, scores = finish(streams, backs, ref_ids, alt_ids, vocab)
    return (mixed, scores)


def solution(mesh):
    placed = (
        P(None, ("grp", "seq"), None),
        P("seq", None),
        P(),
        P("seq", None),
        P("grp"),
        P(("grp", "seq")),
        P(("grp", "seq")),
    )
    return jax.shard_map(
        shards,
        mesh=mesh,
        in_specs=placed,
        out_specs=(P(("grp", "seq"), None), P(None, ("grp", "seq"))),
        check_vma=False,
    )
```

```python
import functools
import math

import jax
import jax.numpy as jnp
import numpy as np
from jax import lax
from jax.experimental import pallas as pl
from jax.experimental.pallas import tpu as pltpu
from jax.sharding import PartitionSpec as P

norm_eps = 1e-06
f32 = jnp.float32
bf16 = jnp.bfloat16
row_tile = 16
half_tile = 8
lane_tile = 128
MIB = 1 << 20


def round_up(value, step):
    return -(-value // step) * step


def split_bf16(values):
    high = values.astype(bf16)
    low = (values - high.astype(f32)).astype(bf16)
    return high, low


def block_tables(block):
    turns = (4 * np.arange(block)[:, None] + 1) * np.arange(block)[None, :] % (4 * block)
    theta = turns * (math.pi / (2 * block))
    table = np.concatenate([np.cos(theta), np.sin(theta)], axis=0)
    parts = []
    for matrix in (table, table.T / block):
        high = matrix.astype(bf16)
        low = (matrix - high.astype(np.float64)).astype(bf16)
        parts.append(np.concatenate([high, low], axis=0))
    return parts


def block_devices(n_devices, tok_rows):
    target = math.isqrt(32 * n_devices * tok_rows)
    count = 1
    while n_devices % (2 * count) == 0 and 2 * count * tok_rows <= target:
        count *= 2
    return count


def whole_spec():
    return pl.BlockSpec(memory_space=pltpu.VMEM)


def product_kernel(chunks, width, vars_dev, rows_ref, streams_ref, *out_refs):
    tok_rows = streams_ref.shape[1]
    n_owners = out_refs[0].shape[0]
    extra = out_refs[0].shape[1] - tok_rows
    place = lax.broadcasted_iota(jnp.int32, (extra, tok_rows), 0)
    column = lax.broadcasted_iota(jnp.int32, (extra, tok_rows), 1)
    for owner in range(n_owners):
        gates = jnp.zeros((extra, width), f32)
        for chunk in range(chunks):
            lanes = pl.ds((owner * chunks + chunk) * width, width)
            left = streams_ref[1, :, lanes].astype(f32)
            right = streams_ref[2, :, lanes].astype(f32)
            out_refs[chunk][owner, :tok_rows, :] = (left * right).astype(bf16)
            picker = jnp.zeros((extra, tok_rows), jnp.bool_)
            for var in range(vars_dev):
                picker |= (place == chunk * vars_dev + var) & (column == rows_ref[var])
            gates += jnp.dot(
                picker.astype(f32).astype(bf16),
                streams_ref[0, :, lanes],
                preferred_element_type=f32,
            )
        out_refs[0][owner, tok_rows:, :] = gates.astype(bf16)


def make_products(streams, local_rows, n_devices, chunks, extra):
    _, tok_rows, model_width = streams.shape
    vars_dev = local_rows.shape[0]
    group_width = model_width // n_devices
    width = group_width // chunks
    owners = max(1, n_devices // 4)
    while owners * group_width % lane_tile:
        owners *= 2
    steps = n_devices // owners
    rows_out = [tok_rows + extra] + [tok_rows] * (chunks - 1)
    return pl.pallas_call(
        functools.partial(product_kernel, chunks, width, vars_dev),
        grid=(steps,),
        in_specs=[
            pl.BlockSpec(memory_space=pltpu.SMEM),
            pl.BlockSpec((3, tok_rows, owners * group_width), lambda i: (0, 0, i)),
        ],
        out_specs=[pl.BlockSpec((owners, rows, width), lambda i: (i, 0, 0)) for rows in rows_out],
        out_shape=[jax.ShapeDtypeStruct((n_devices, rows, width), bf16) for rows in rows_out],
        compiler_params=pltpu.CompilerParams(vmem_limit_bytes=24 * MIB),
        name="products",
    )(local_rows, streams)


def spectrum_kernel(block, filter_ref, forward_ref, out_ref):
    n_blocks = out_ref.shape[0]
    for index in range(n_blocks):
        taps = filter_ref[:, index * block : (index + 1) * block]
        both = lax.dot_general(
            forward_ref[...], taps, (((1,), (1,)), ((), ())), preferred_element_type=f32
        )
        out_ref[index] = both[: 2 * block] + both[2 * block :]


def filter_spectrum(taps, forward, block):
    width, length = taps.shape
    n_blocks = length // block
    return pl.pallas_call(
        functools.partial(spectrum_kernel, block),
        in_specs=[whole_spec(), whole_spec()],
        out_specs=whole_spec(),
        out_shape=jax.ShapeDtypeStruct((n_blocks, 2 * block, width), f32),
        compiler_params=pltpu.CompilerParams(vmem_limit_bytes=40 * MIB),
        cost_estimate=pl.CostEstimate(
            flops=8 * block * length * width, bytes_accessed=4 * MIB, transcendentals=0
        ),
        name="filter_spectrum",
    )(taps, forward)


def multiply_points(points, spectrum_ref, joint):
    n_blocks, double, width = points.shape
    block = double // 2
    lanes_step = min(width, lane_tile)

    def multiply_step(step, carry):
        start = pl.multiple_of(step * half_tile, half_tile)
        upper = pl.ds(start, half_tile)
        lower = pl.ds(pl.multiple_of(block + start, half_tile), half_tile)
        for first in range(0, width, lanes_step):
            lanes = slice(first, first + lanes_step)
            signal = [(points[k, upper, lanes], points[k, lower, lanes]) for k in range(n_blocks)]
            taps = [
                (spectrum_ref[k, upper, lanes], spectrum_ref[k, lower, lanes]) for k in range(n_blocks)
            ]
            before_re = jnp.zeros((half_tile, lanes_step), f32)
            before_im = jnp.zeros((half_tile, lanes_step), f32)
            for total in range(n_blocks):
                sum_re = jnp.zeros((half_tile, lanes_step), f32)
                sum_im = jnp.zeros((half_tile, lanes_step), f32)
                for delay in range(total + 1):
                    a_re, a_im = signal[total - delay]
                    b_re, b_im = taps[delay]
                    sum_re += a_re * b_re - a_im * b_im
                    sum_im += a_re * b_im + a_im * b_re
                joint[total, upper, lanes] = sum_re + before_im
                joint[total, lower, lanes] = sum_im - before_re
                before_re, before_im = sum_re, sum_im
        return carry

    lax.fori_loop(0, block // half_tile, multiply_step, 0)


def convolve(chunk_ref, spectrum_ref, forward_ref, inverse_ref, out_ref, points, tok_rows):
    n_blocks, double, width = points.shape
    block = double // 2
    per_block = block // tok_rows
    group = max(1, min(n_blocks, 256 // width)) if width % lane_tile == 0 else 1

    def forward_step(step, carry):
        pieces = []
        for member in range(group):
            start = (step * group + member) * per_block
            rows = chunk_ref[pl.ds(start, per_block), :tok_rows, :]
            pieces.append(rows.reshape(block, width))
        signal = pieces[0] if group == 1 else jnp.concatenate(pieces, axis=1)
        both = jnp.dot(forward_ref[...], signal, preferred_element_type=f32)
        total = both[:double] + both[double:]
        for member in range(group):
            points[step * group + member] = total[:, member * width : (member + 1) * width]
        return carry

    lax.fori_loop(0, n_blocks // group, forward_step, 0)

    multiply_points(points, spectrum_ref, points)

    def inverse_step(step, carry):
        first = step * group
        pieces = [points[first + member] for member in range(group)]
        highs, lows = split_bf16(pieces[0] if group == 1 else jnp.concatenate(pieces, axis=1))
        both = jnp.dot(inverse_ref[...], highs, preferred_element_type=f32)
        rest = jnp.dot(inverse_ref[:block, :], lows, preferred_element_type=f32)
        result = (both[:block] + both[block:] + rest).astype(bf16)
        for member in range(group):
            piece = result[:, member * width : (member + 1) * width]
            out_ref[pl.ds((first + member) * per_block, per_block), :tok_rows, :] = piece.reshape(
                per_block, tok_rows, width
            )
        return carry

    lax.fori_loop(0, n_blocks // group, inverse_step, 0)


def score_rows(index, vars_dev, tok_rows, positions, gate_block, out_ref, gain_row, unembed):
    n_devices, extra, width = gate_block.shape
    gates = gate_block.astype(f32)
    place = lax.broadcasted_iota(jnp.int32, (n_devices, extra, width), 1)
    picked = [
        jnp.sum(jnp.where(place == index * vars_dev + var, gates, 0.0), axis=1)
        for var in range(vars_dev)
    ]
    gate_rows = picked[0] if vars_dev == 1 else jnp.concatenate(picked, axis=0)
    length = n_devices * tok_rows
    column = lax.broadcasted_iota(jnp.int32, (positions.shape[0], length), 1)
    picker = (column == positions).astype(f32).astype(bf16)
    filtered = jnp.dot(
        picker, out_ref[:, :tok_rows, :].reshape(length, width), preferred_element_type=f32
    )
    rows = (gate_rows * filtered).astype(bf16).astype(f32)
    weighted = (rows * gain_row).astype(bf16)
    return jnp.dot(weighted, unembed, preferred_element_type=f32), rows * rows


def pack_scores(raw, squares, vars_dev, packed, n_devices):
    total, width = packed.shape
    extra = total // n_devices
    per_row = raw.shape[1] // width
    packed[...] = jnp.zeros_like(packed)
    for var in range(vars_dev):
        mine = slice(var * n_devices, (var + 1) * n_devices)
        pieces = [raw[mine, r * width : (r + 1) * width] for r in range(per_row)] + [squares[mine]]
        for row, piece in enumerate(pieces):
            rounded = piece.astype(bf16).astype(f32)
            base = var * 2 * (per_row + 1) + row
            packed[pl.ds(base, n_devices, stride=extra), :] = rounded
            packed[pl.ds(base + per_row + 1, n_devices, stride=extra), :] = piece - rounded


def chunk_kernel(index, chunks, vars_dev, tok_rows, *refs):
    refs = list(refs)
    chunk_ref, spectrum_ref, forward_ref, inverse_ref = refs[:4]
    positions_ref, gain_ref, unembed_ref = refs[4:7]
    refs = refs[7:]
    first, last = index == 0, index == chunks - 1
    gates_ref = None if first else refs.pop(0)
    raw_before, square_before = (None, None) if first else (refs.pop(0), refs.pop(0))
    out_ref = refs.pop(0)
    raw_out, square_out = (None, None) if last else (refs.pop(0), refs.pop(0))
    gates_out = refs.pop(0) if first and not last else None
    points = refs[0]
    convolve(chunk_ref, spectrum_ref, forward_ref, inverse_ref, out_ref, points, tok_rows)
    gate_block = chunk_ref[:, tok_rows:, :] if first else gates_ref[...]
    raw, squares = score_rows(
        index, vars_dev, tok_rows, positions_ref[...], gate_block, out_ref, gain_ref[...], unembed_ref[...]
    )
    if not first:
        raw = raw + raw_before[...]
        squares = squares + square_before[...]
    if gates_out is not None:
        gates_out[...] = gate_block
    if not last:
        raw_out[...] = raw
        square_out[...] = squares
        return
    packed = refs[1]
    n_devices, _, width = out_ref.shape
    extra = out_ref.shape[1] - tok_rows
    pack_scores(raw, squares, vars_dev, packed, n_devices)
    out_ref[:, tok_rows:, :] = packed[...].reshape(n_devices, extra, width).astype(bf16)


def filter_chunk(index, chunks, vars_dev, tok_rows, extra, operands, carried):
    moved, spectrum = operands[:2]
    n_devices, _, width = moved.shape
    n_blocks, double, _ = spectrum.shape
    vocab = operands[6].shape[1]
    n_vars = operands[4].shape[0]
    first, last = index == 0, index == chunks - 1
    rows_out = tok_rows + (extra if last else 0)
    out_shape = [jax.ShapeDtypeStruct((n_devices, rows_out, width), bf16)]
    scratch = [pltpu.VMEM((n_blocks, double, width), f32)]
    if last:
        scratch.append(pltpu.VMEM((n_devices * extra, width), f32))
    else:
        out_shape.append(jax.ShapeDtypeStruct((n_vars, vocab), f32))
        out_shape.append(jax.ShapeDtypeStruct((n_vars, width), f32))
    if first and not last:
        out_shape.append(jax.ShapeDtypeStruct((n_devices, moved.shape[1] - tok_rows, width), bf16))
    flops = 2 * width * n_blocks * (double * double * 5 // 2 + 4 * n_blocks * double)
    return pl.pallas_call(
        functools.partial(chunk_kernel, index, chunks, vars_dev, tok_rows),
        in_specs=[whole_spec()] * (len(operands) + len(carried)),
        out_specs=[whole_spec()] * len(out_shape),
        out_shape=out_shape,
        scratch_shapes=scratch,
        compiler_params=pltpu.CompilerParams(vmem_limit_bytes=(20 if n_blocks <= 8 else 58) * MIB),
        cost_estimate=pl.CostEstimate(flops=flops, bytes_accessed=8 * MIB, transcendentals=0),
        name="filter_chunk",
    )(*operands, *carried)


def final_scores(sums, vars_dev, vocab, model_width, ref_ref, alt_ref):
    width = sums.shape[1]
    per_row = vocab // width
    ids = lax.broadcasted_iota(jnp.int32, (per_row, width), 0) * width
    ids += lax.broadcasted_iota(jnp.int32, (per_row, width), 1)
    row = lax.broadcasted_iota(jnp.int32, (2, vars_dev), 0)
    column = lax.broadcasted_iota(jnp.int32, (2, vars_dev), 1)
    scores = jnp.zeros((2, vars_dev), f32)

    def whole_sum(values):
        return jnp.sum(jnp.sum(values, axis=1, keepdims=True), axis=0, keepdims=True)

    for var in range(vars_dev):
        base = var * 2 * (per_row + 1)
        both = sums[base : base + per_row + 1, :]
        both = both + sums[base + per_row + 1 : base + 2 * (per_row + 1), :]
        square = jnp.sum(both[per_row:, :], axis=1, keepdims=True)
        logits = both[:per_row, :] * lax.rsqrt(square / model_width + norm_eps)
        largest = jnp.max(jnp.max(logits, axis=1, keepdims=True), axis=0, keepdims=True)
        log_total = largest + jnp.log(whole_sum(jnp.exp(logits - largest)))
        ref_logit = whole_sum(jnp.where(ids == ref_ref[var], logits, 0.0))
        alt_logit = whole_sum(jnp.where(ids == alt_ref[var], logits, 0.0))
        pair = jnp.where(row == 0, ref_logit - log_total, alt_logit - ref_logit)
        scores = jnp.where(column == var, pair, scores)
    return scores


def finish_kernel(chunks, vars_dev, vocab, ref_ref, alt_ref, streams_ref, *refs):
    back_refs, mixed_ref, scores_ref, sums = refs[:chunks], refs[chunks], refs[chunks + 1], refs[chunks + 2]
    tok_rows = streams_ref.shape[1]
    owners, _, width = back_refs[0].shape
    step = pl.program_id(0)
    for owner in range(owners):
        for chunk in range(chunks):
            lanes = pl.ds((owner * chunks + chunk) * width, width)
            gate = streams_ref[0, :, lanes].astype(f32)
            filtered = back_refs[chunk][owner, :tok_rows, :].astype(f32)
            mixed_ref[:, lanes] = (gate * filtered).astype(bf16)
    part = jnp.sum(back_refs[-1][:, tok_rows:, :].astype(f32), axis=0)

    @pl.when(step == 0)
    def _():
        sums[...] = part

    @pl.when(step > 0)
    def _():
        sums[...] += part

    @pl.when(step == pl.num_programs(0) - 1)
    def _():
        model_width = pl.num_programs(0) * owners * chunks * width
        scores_ref[...] = final_scores(sums[...], vars_dev, vocab, model_width, ref_ref, alt_ref)


def finish(streams, backs, ref_ids, alt_ids, vocab):
    _, tok_rows, model_width = streams.shape
    chunks = len(backs)
    n_devices, _, width = backs[0].shape
    vars_dev = ref_ids.shape[0]
    owners = max(1, n_devices // 4)
    while owners * chunks * width % lane_tile:
        owners *= 2
    extra = backs[-1].shape[1] - tok_rows
    return pl.pallas_call(
        functools.partial(finish_kernel, chunks, vars_dev, vocab),
        grid=(n_devices // owners,),
        in_specs=[
            pl.BlockSpec(memory_space=pltpu.SMEM),
            pl.BlockSpec(memory_space=pltpu.SMEM),
            pl.BlockSpec((1, tok_rows, owners * chunks * width), lambda i: (0, 0, i)),
        ]
        + [pl.BlockSpec((owners, back.shape[1], width), lambda i: (i, 0, 0)) for back in backs],
        out_specs=[
            pl.BlockSpec((tok_rows, owners * chunks * width), lambda i: (0, i)),
            pl.BlockSpec((2, vars_dev), lambda i: (0, 0)),
        ],
        out_shape=[
            jax.ShapeDtypeStruct((tok_rows, model_width), bf16),
            jax.ShapeDtypeStruct((2, vars_dev), f32),
        ],
        scratch_shapes=[pltpu.VMEM((extra, width), f32)],
        compiler_params=pltpu.CompilerParams(vmem_limit_bytes=24 * MIB),
        name="finish",
    )(ref_ids, alt_ids, streams, *backs)

def send_products_kernel(halves, vars_dev, me_ref, offsets_ref, streams_ref, *refs):
    built, pairs, gates, pair_sems, gate_sems, out_sems = refs[-6:]
    out_refs = refs[:-6]
    n_devices, _, tok_rows, width = pairs.shape
    me = me_ref[0]
    slot = tok_rows // vars_dev
    local_rows = [var * slot + offsets_ref[me * vars_dev + var] for var in range(vars_dev)]

    def pair_copy(step):
        start = pl.multiple_of((me ^ step) * width, lane_tile)
        return pltpu.make_async_copy(
            streams_ref.at[pl.ds(1, 2), :, pl.ds(start, width)], pairs.at[step], pair_sems.at[step]
        )

    def gate_copy(var):
        start = pl.multiple_of(local_rows[var] // row_tile * row_tile, row_tile)
        return pltpu.make_async_copy(
            streams_ref.at[0, pl.ds(start, row_tile), :], gates.at[var], gate_sems.at[var]
        )

    def out_copy(step):
        return pltpu.make_async_copy(built.at[step], out_refs[step], out_sems.at[step])

    for var in range(vars_dev):
        gate_copy(var).start()
    for step in range(n_devices):
        pair_copy(step).start()
    for var in range(vars_dev):
        gate_copy(var).wait()
    extra = built.shape[1] - halves * tok_rows
    row = lax.broadcasted_iota(jnp.int32, (row_tile, lane_tile), 0)
    place = lax.broadcasted_iota(jnp.int32, (extra, lane_tile), 0)
    for step in range(n_devices):
        pair_copy(step).wait()
        tail = jnp.zeros((extra, lane_tile), f32)
        for half in range(halves):
            lanes = slice(half * lane_tile, (half + 1) * lane_tile)
            rows = slice(half * tok_rows, (half + 1) * tok_rows)
            built[step, rows, :] = pairs[step, 0, :, lanes] * pairs[step, 1, :, lanes]
            start = pl.multiple_of((me ^ step) * width + half * lane_tile, lane_tile)
            for var in range(vars_dev):
                tile = gates[var, :, pl.ds(start, lane_tile)].astype(f32)
                mine = jnp.where(row == local_rows[var] % row_tile, tile, 0.0)
                mine = jnp.sum(mine, axis=0, keepdims=True)
                tail = jnp.where(place == half * vars_dev + var, mine, tail)
        built[step, halves * tok_rows :, :] = tail.astype(bf16)
        out_copy(step).start()
    for step in range(n_devices):
        out_copy(step).wait()


def send_products(me, offsets, streams, vars_dev, n_devices, extra):
    _, tok_rows, model_width = streams.shape
    width = model_width // n_devices
    halves = width // lane_tile
    rows_out = halves * tok_rows + extra
    return pl.pallas_call(
        functools.partial(send_products_kernel, halves, vars_dev),
        in_specs=[
            pl.BlockSpec(memory_space=pltpu.SMEM),
            pl.BlockSpec(memory_space=pltpu.SMEM),
            pl.BlockSpec(memory_space=pl.ANY),
        ],
        out_specs=[pl.BlockSpec(memory_space=pl.ANY)] * n_devices,
        out_shape=[jax.ShapeDtypeStruct((rows_out, lane_tile), bf16)] * n_devices,
        scratch_shapes=[
            pltpu.VMEM((n_devices, rows_out, lane_tile), bf16),
            pltpu.VMEM((n_devices, 2, tok_rows, width), bf16),
            pltpu.VMEM((vars_dev, row_tile, model_width), bf16),
            pltpu.SemaphoreType.DMA((n_devices,)),
            pltpu.SemaphoreType.DMA((vars_dev,)),
            pltpu.SemaphoreType.DMA((n_devices,)),
        ],
        compiler_params=pltpu.CompilerParams(vmem_limit_bytes=60 * MIB),
        cost_estimate=pl.CostEstimate(
            flops=tok_rows * model_width, bytes_accessed=6 * tok_rows * model_width, transcendentals=0
        ),
        name="send_products",
    )(me, offsets, streams)


def direct_filter_kernel(steps, vars_dev, halves, tok_rows, me_ref, *refs):
    positions_ref, gain_ref, unembed_ref, forward_ref, inverse_hbm, spectrum_hbm = refs[:6]
    points, joint, arrived, leaving, packed, spectrum, inverse = refs[-12:-5]
    in_sems, out_sems, tail_sems, spectrum_sem, inverse_sem = refs[-5:]
    n_devices = arrived.shape[0]
    in_refs = refs[6 : 6 + n_devices]
    out_refs = refs[6 + n_devices : 6 + 2 * n_devices]
    me = me_ref[0]
    body = halves * tok_rows

    def in_copy(index):
        return pltpu.make_async_copy(
            in_refs[index], arrived.at[me ^ steps[index]], in_sems.at[index]
        )

    def out_copy(step, start, size, sems):
        rows = pl.ds(start, size)
        return pltpu.make_async_copy(
            leaving.at[me ^ step, rows], out_refs[step].at[rows], sems.at[step]
        )

    spectrum_copy = pltpu.make_async_copy(spectrum_hbm, spectrum, spectrum_sem.at[0])
    inverse_copy = pltpu.make_async_copy(inverse_hbm, inverse, inverse_sem.at[0])
    for index in range(n_devices):
        in_copy(index).start()
    spectrum_copy.start()
    inverse_copy.start()
    for index in range(n_devices):
        in_copy(index).wait()

    n_blocks, double, width = points.shape
    block = double // 2
    per_block = block // tok_rows

    def forward_step(step, carry):
        pieces = []
        for half in range(halves):
            rows = slice(half * tok_rows, (half + 1) * tok_rows)
            parts = [arrived[step * per_block + m, rows, :] for m in range(per_block)]
            pieces.append(jnp.concatenate(parts, axis=0))
        signal = jnp.concatenate(pieces, axis=1)
        both = jnp.dot(forward_ref[...], signal, preferred_element_type=f32)
        points[step] = both[:double] + both[double:]
        return carry

    lax.fori_loop(0, n_blocks, forward_step, 0)
    spectrum_copy.wait()
    multiply_points(points, spectrum, joint)
    inverse_copy.wait()

    def inverse_step(step, carry):
        highs, lows = split_bf16(joint[step])
        both = jnp.dot(inverse[...], highs, preferred_element_type=f32)
        rest = jnp.dot(inverse[:block, :], lows, preferred_element_type=f32)
        result = (both[:block] + both[block:] + rest).astype(bf16)
        for member in range(per_block):
            for half in range(halves):
                leaving[step * per_block + member, half * tok_rows : (half + 1) * tok_rows, :] = result[
                    member * tok_rows : (member + 1) * tok_rows,
                    half * lane_tile : (half + 1) * lane_tile,
                ]
        return carry

    lax.fori_loop(0, n_blocks, inverse_step, 0)
    for step in range(n_devices):
        out_copy(step, 0, body, out_sems).start()

    length = n_devices * tok_rows
    column = lax.broadcasted_iota(jnp.int32, (positions_ref.shape[0], length), 1)
    picker = (column == positions_ref[...]).astype(f32).astype(bf16)
    tails = arrived[:, body:, :].astype(f32)
    place = lax.broadcasted_iota(jnp.int32, tails.shape, 1)
    raw = None
    squares = None
    for half in range(halves):
        lanes = slice(half * lane_tile, (half + 1) * lane_tile)
        picked = [
            jnp.sum(jnp.where(place == half * vars_dev + var, tails, 0.0), axis=1)
            for var in range(vars_dev)
        ]
        gate_rows = picked[0] if vars_dev == 1 else jnp.concatenate(picked, axis=0)
        filtered = leaving[:, half * tok_rows : (half + 1) * tok_rows, :].reshape(length, lane_tile)
        filtered = jnp.dot(picker, filtered, preferred_element_type=f32)
        rows = (gate_rows * filtered).astype(bf16).astype(f32)
        weighted = (rows * gain_ref[:, lanes]).astype(bf16)
        part = jnp.dot(weighted, unembed_ref[lanes, :], preferred_element_type=f32)
        raw = part if raw is None else raw + part
        squares = rows * rows if squares is None else squares + rows * rows
    pack_scores(raw, squares, vars_dev, packed, n_devices)
    extra = packed.shape[0] // n_devices
    leaving[:, body:, :] = packed[...].reshape(n_devices, extra, lane_tile).astype(bf16)
    for step in range(n_devices):
        out_copy(step, body, extra, tail_sems).start()
    for step in range(n_devices):
        out_copy(step, 0, body, out_sems).wait()
        out_copy(step, body, extra, tail_sems).wait()


def direct_filter(me, operands, steps, arrivals, vars_dev, tok_rows, extra):
    n_devices = len(arrivals)
    forward, inverse, spectrum = operands[3:]
    n_blocks, double, width = spectrum.shape
    halves = width // lane_tile
    rows_out = halves * tok_rows + extra
    flops = 2 * width * n_blocks * (double * double * 5 // 2 + 4 * n_blocks * double)
    anywhere = pl.BlockSpec(memory_space=pl.ANY)
    return pl.pallas_call(
        functools.partial(direct_filter_kernel, steps, vars_dev, halves, tok_rows),
        in_specs=[pl.BlockSpec(memory_space=pltpu.SMEM)]
        + [whole_spec()] * 4
        + [anywhere] * (2 + n_devices),
        out_specs=[anywhere] * n_devices,
        out_shape=[jax.ShapeDtypeStruct((rows_out, lane_tile), bf16)] * n_devices,
        scratch_shapes=[
            pltpu.VMEM((n_blocks, double, width), f32),
            pltpu.VMEM((n_blocks, double, width), f32),
            pltpu.VMEM((n_devices,) + arrivals[0].shape, bf16),
            pltpu.VMEM((n_devices, rows_out, lane_tile), bf16),
            pltpu.VMEM((n_devices * extra, lane_tile), f32),
            pltpu.VMEM(spectrum.shape, f32),
            pltpu.VMEM(inverse.shape, bf16),
            pltpu.SemaphoreType.DMA((n_devices,)),
            pltpu.SemaphoreType.DMA((n_devices,)),
            pltpu.SemaphoreType.DMA((n_devices,)),
            pltpu.SemaphoreType.DMA((1,)),
            pltpu.SemaphoreType.DMA((1,)),
        ],
        compiler_params=pltpu.CompilerParams(vmem_limit_bytes=32 * MIB),
        cost_estimate=pl.CostEstimate(flops=flops, bytes_accessed=8 * MIB, transcendentals=0),
        name="direct_filter",
    )(me, *operands, *arrivals)


def direct_finish_kernel(steps, halves, vars_dev, vocab, me_ref, ref_ref, alt_ref, streams_ref, *refs):
    gates, results, gate_sems, out_sems = refs[-4:]
    n_devices, tok_rows, width = gates.shape
    mixed_ref, scores_ref = refs[-6:-4]
    me = me_ref[0]

    def lanes_of(index):
        return pl.ds(pl.multiple_of((me ^ steps[index]) * width, lane_tile), width)

    def gate_copy(step):
        return pltpu.make_async_copy(
            streams_ref.at[0, :, lanes_of(step)], gates.at[step], gate_sems.at[step]
        )

    def out_copy(step):
        return pltpu.make_async_copy(
            results.at[step], mixed_ref.at[:, lanes_of(step)], out_sems.at[step]
        )

    for step in range(n_devices):
        gate_copy(step).start()
    sums = None
    for step in range(n_devices):
        gate_copy(step).wait()
        block_ref = refs[step]
        for half in range(halves):
            lanes = slice(half * lane_tile, (half + 1) * lane_tile)
            filtered = block_ref[half * tok_rows : (half + 1) * tok_rows, :]
            results[step, :, lanes] = gates[step, :, lanes] * filtered
        out_copy(step).start()
        tail = block_ref[halves * tok_rows :, :].astype(f32)
        sums = tail if sums is None else sums + tail
    model_width = n_devices * width
    scores_ref[...] = final_scores(sums, vars_dev, vocab, model_width, ref_ref, alt_ref)
    for step in range(n_devices):
        out_copy(step).wait()


def direct_finish(me, ref_ids, alt_ids, streams, steps, backs, vocab):
    _, tok_rows, model_width = streams.shape
    n_devices = len(backs)
    vars_dev = ref_ids.shape[0]
    width = model_width // n_devices
    return pl.pallas_call(
        functools.partial(direct_finish_kernel, steps, width // lane_tile, vars_dev, vocab),
        in_specs=[pl.BlockSpec(memory_space=pltpu.SMEM)] * 3
        + [pl.BlockSpec(memory_space=pl.ANY)]
        + [whole_spec()] * len(backs),
        out_specs=[pl.BlockSpec(memory_space=pl.ANY), whole_spec()],
        out_shape=[
            jax.ShapeDtypeStruct((tok_rows, model_width), bf16),
            jax.ShapeDtypeStruct((2, vars_dev), f32),
        ],
        scratch_shapes=[
            pltpu.VMEM((n_devices, tok_rows, width), bf16),
            pltpu.VMEM((n_devices, tok_rows, width), bf16),
            pltpu.SemaphoreType.DMA((n_devices,)),
            pltpu.SemaphoreType.DMA((n_devices,)),
        ],
        compiler_params=pltpu.CompilerParams(vmem_limit_bytes=12 * MIB),
        cost_estimate=pl.CostEstimate(
            flops=tok_rows * model_width, bytes_accessed=6 * tok_rows * model_width, transcendentals=0
        ),
        name="direct_finish",
    )(me, ref_ids, alt_ids, streams, *backs)


def partner_order(n_devices):
    half = n_devices // 2
    far, near = list(range(half, n_devices)), list(range(1, half))
    lead = len(far) // 2
    order = far[:lead]
    rest = far[lead:]
    while rest or near:
        order += near[:1] + rest[:1]
        rest, near = rest[1:], near[1:]
    return order


def exchange(parts, order):
    n_devices = len(parts)
    moved = {0: parts[0]}
    for step in order:
        pairs = [(device, device ^ step) for device in range(n_devices)]
        moved[step] = lax.ppermute(parts[step], "seq", pairs)
    return moved


def shards(streams, long_filter, gain, unembed, offsets, ref_ids, alt_ids):
    n_devices = lax.axis_size("seq")
    my_index = lax.axis_index("seq")
    _, tok_rows, model_width = streams.shape
    group_width = model_width // n_devices
    vars_dev = ref_ids.shape[0]
    vocab = unembed.shape[1]
    chunks = max(1, group_width // lane_tile)
    width = group_width // chunks
    block = tok_rows * block_devices(n_devices, tok_rows)
    forward_np, inverse_np = block_tables(block)
    forward, inverse = jnp.asarray(forward_np), jnp.asarray(inverse_np)

    slot = tok_rows // vars_dev
    starts = jnp.arange(vars_dev, dtype=jnp.int32) * slot
    local_rows = starts + lax.dynamic_slice_in_dim(offsets, my_index * vars_dev, vars_dev)
    by_device = offsets.reshape(n_devices, vars_dev)
    positions = by_device + starts[None, :]
    positions += jnp.arange(n_devices, dtype=jnp.int32)[:, None] * tok_rows
    positions = positions.T.reshape(n_devices * vars_dev, 1)
    my_gain = lax.dynamic_slice_in_dim(gain, my_index * group_width, group_width).astype(f32)

    if chunks * lane_tile == group_width and n_devices & (n_devices - 1) == 0:
        me = jnp.reshape(my_index, (1,)).astype(jnp.int32)
        gate_extra = round_up(chunks * vars_dev, row_tile)
        score_extra = round_up(vars_dev * 2 * (vocab // lane_tile + 1), row_tile)
        parts = send_products(me, offsets, streams, vars_dev, n_devices, gate_extra)
        order = partner_order(n_devices)
        slots = sorted(range(len(order)), key=str)
        steps = [0] + [order[slots.index(place)] for place in range(len(order))]
        moved = exchange(parts, steps[1:])
        spectrum = filter_spectrum(long_filter, forward, block)
        operands = (positions, my_gain[None, :], unembed, forward, inverse, spectrum)
        arrivals = [moved[step] for step in steps]
        leaving = direct_filter(me, operands, steps, arrivals, vars_dev, tok_rows, score_extra)
        steps = [0] + order
        returned = exchange(leaving, order)
        backs = [returned[step] for step in steps]
        mixed, scores = direct_finish(me, ref_ids, alt_ids, streams, steps, backs, vocab)
        return (mixed, scores)

    gate_extra = round_up(chunks * vars_dev, row_tile)
    score_extra = round_up(vars_dev * 2 * (vocab // width + 1), row_tile)
    products = make_products(streams, local_rows, n_devices, chunks, gate_extra)
    moved = [lax.all_to_all(part, "seq", split_axis=0, concat_axis=0, tiled=True) for part in products]
    carried = ()
    backs = []
    for chunk in range(chunks):
        mine = slice(chunk * width, (chunk + 1) * width)
        spectrum = filter_spectrum(long_filter[mine], forward, block)
        operands = (
            moved[chunk], spectrum, forward, inverse, positions,
            my_gain[None, mine], unembed[mine],
        )
        if chunk > 0:
            carried = (gates,) + tuple(carried)
        results = filter_chunk(chunk, chunks, vars_dev, tok_rows, score_extra, operands, carried)
        carried = results[1:3]
        if chunk == 0 and chunks > 1:
            gates = results[3]
        backs.append(lax.all_to_all(results[0], "seq", split_axis=0, concat_axis=0, tiled=True))
    mixed, scores = finish(streams, backs, ref_ids, alt_ids, vocab)
    return (mixed, scores)


def solution(mesh):
    placed = (
        P(None, ("grp", "seq"), None),
        P("seq", None),
        P(),
        P("seq", None),
        P("grp"),
        P(("grp", "seq")),
        P(("grp", "seq")),
    )
    return jax.shard_map(
        shards,
        mesh=mesh,
        in_specs=placed,
        out_specs=(P(("grp", "seq"), None), P(None, ("grp", "seq"))),
        check_vma=False,
    )
```

```python
import functools
import math

import jax
import jax.numpy as jnp
import numpy as np
from jax import lax
from jax.experimental import pallas as pl
from jax.experimental.pallas import tpu as pltpu
from jax.sharding import PartitionSpec as P

norm_eps = 1e-06
f32 = jnp.float32
bf16 = jnp.bfloat16
row_tile = 16
half_tile = 8
lane_tile = 128
MIB = 1 << 20


def round_up(value, step):
    return -(-value // step) * step


def split_bf16(values):
    high = values.astype(bf16)
    low = (values - high.astype(f32)).astype(bf16)
    return high, low


def block_tables(block):
    turns = (4 * np.arange(block)[:, None] + 1) * np.arange(block)[None, :] % (4 * block)
    theta = turns * (math.pi / (2 * block))
    table = np.concatenate([np.cos(theta), np.sin(theta)], axis=0)
    parts = []
    for matrix in (table, table.T / block):
        high = matrix.astype(bf16)
        low = (matrix - high.astype(np.float64)).astype(bf16)
        parts.append(np.concatenate([high, low], axis=0))
    return parts


def block_devices(n_devices, tok_rows):
    target = math.isqrt(32 * n_devices * tok_rows)
    count = 1
    while n_devices % (2 * count) == 0 and 2 * count * tok_rows <= target:
        count *= 2
    return count


def whole_spec():
    return pl.BlockSpec(memory_space=pltpu.VMEM)


def product_kernel(chunks, width, vars_dev, rows_ref, streams_ref, *out_refs):
    tok_rows = streams_ref.shape[1]
    n_owners = out_refs[0].shape[0]
    extra = out_refs[0].shape[1] - tok_rows
    place = lax.broadcasted_iota(jnp.int32, (extra, tok_rows), 0)
    column = lax.broadcasted_iota(jnp.int32, (extra, tok_rows), 1)
    for owner in range(n_owners):
        gates = jnp.zeros((extra, width), f32)
        for chunk in range(chunks):
            lanes = pl.ds((owner * chunks + chunk) * width, width)
            left = streams_ref[1, :, lanes].astype(f32)
            right = streams_ref[2, :, lanes].astype(f32)
            out_refs[chunk][owner, :tok_rows, :] = (left * right).astype(bf16)
            picker = jnp.zeros((extra, tok_rows), jnp.bool_)
            for var in range(vars_dev):
                picker |= (place == chunk * vars_dev + var) & (column == rows_ref[var])
            gates += jnp.dot(
                picker.astype(f32).astype(bf16),
                streams_ref[0, :, lanes],
                preferred_element_type=f32,
            )
        out_refs[0][owner, tok_rows:, :] = gates.astype(bf16)


def make_products(streams, local_rows, n_devices, chunks, extra):
    _, tok_rows, model_width = streams.shape
    vars_dev = local_rows.shape[0]
    group_width = model_width // n_devices
    width = group_width // chunks
    owners = max(1, n_devices // 4)
    while owners * group_width % lane_tile:
        owners *= 2
    steps = n_devices // owners
    rows_out = [tok_rows + extra] + [tok_rows] * (chunks - 1)
    return pl.pallas_call(
        functools.partial(product_kernel, chunks, width, vars_dev),
        grid=(steps,),
        in_specs=[
            pl.BlockSpec(memory_space=pltpu.SMEM),
            pl.BlockSpec((3, tok_rows, owners * group_width), lambda i: (0, 0, i)),
        ],
        out_specs=[pl.BlockSpec((owners, rows, width), lambda i: (i, 0, 0)) for rows in rows_out],
        out_shape=[jax.ShapeDtypeStruct((n_devices, rows, width), bf16) for rows in rows_out],
        compiler_params=pltpu.CompilerParams(vmem_limit_bytes=24 * MIB),
        name="products",
    )(local_rows, streams)


def spectrum_kernel(block, filter_ref, forward_ref, *refs):
    out_ref = refs[-1]
    n_blocks = out_ref.shape[0]
    for index in range(n_blocks):
        taps = filter_ref[:, index * block : (index + 1) * block]
        both = lax.dot_general(
            forward_ref[...], taps, (((1,), (1,)), ((), ())), preferred_element_type=f32
        )
        out_ref[index] = both[: 2 * block] + both[2 * block :]


def filter_spectrum(taps, forward, block, *earlier):
    width, length = taps.shape
    n_blocks = length // block
    return pl.pallas_call(
        functools.partial(spectrum_kernel, block),
        in_specs=[whole_spec(), whole_spec()] + [pl.BlockSpec(memory_space=pl.ANY)] * len(earlier),
        out_specs=whole_spec(),
        out_shape=jax.ShapeDtypeStruct((n_blocks, 2 * block, width), f32),
        compiler_params=pltpu.CompilerParams(vmem_limit_bytes=40 * MIB),
        cost_estimate=pl.CostEstimate(
            flops=8 * block * length * width, bytes_accessed=4 * MIB, transcendentals=0
        ),
        name="filter_spectrum",
    )(taps, forward, *earlier)


def multiply_points(points, spectrum_ref, joint):
    n_blocks, double, width = points.shape
    block = double // 2
    lanes_step = min(width, lane_tile)

    def multiply_step(step, carry):
        start = pl.multiple_of(step * half_tile, half_tile)
        upper = pl.ds(start, half_tile)
        lower = pl.ds(pl.multiple_of(block + start, half_tile), half_tile)
        for first in range(0, width, lanes_step):
            lanes = slice(first, first + lanes_step)
            signal = [(points[k, upper, lanes], points[k, lower, lanes]) for k in range(n_blocks)]
            taps = [
                (spectrum_ref[k, upper, lanes], spectrum_ref[k, lower, lanes]) for k in range(n_blocks)
            ]
            before_re = jnp.zeros((half_tile, lanes_step), f32)
            before_im = jnp.zeros((half_tile, lanes_step), f32)
            for total in range(n_blocks):
                sum_re = jnp.zeros((half_tile, lanes_step), f32)
                sum_im = jnp.zeros((half_tile, lanes_step), f32)
                for delay in range(total + 1):
                    a_re, a_im = signal[total - delay]
                    b_re, b_im = taps[delay]
                    sum_re += a_re * b_re - a_im * b_im
                    sum_im += a_re * b_im + a_im * b_re
                joint[total, upper, lanes] = sum_re + before_im
                joint[total, lower, lanes] = sum_im - before_re
                before_re, before_im = sum_re, sum_im
        return carry

    lax.fori_loop(0, block // half_tile, multiply_step, 0)


def convolve(chunk_ref, spectrum_ref, forward_ref, inverse_ref, out_ref, points, tok_rows):
    n_blocks, double, width = points.shape
    block = double // 2
    per_block = block // tok_rows
    group = max(1, min(n_blocks, 256 // width)) if width % lane_tile == 0 else 1

    def forward_step(step, carry):
        pieces = []
        for member in range(group):
            start = (step * group + member) * per_block
            rows = chunk_ref[pl.ds(start, per_block), :tok_rows, :]
            pieces.append(rows.reshape(block, width))
        signal = pieces[0] if group == 1 else jnp.concatenate(pieces, axis=1)
        both = jnp.dot(forward_ref[...], signal, preferred_element_type=f32)
        total = both[:double] + both[double:]
        for member in range(group):
            points[step * group + member] = total[:, member * width : (member + 1) * width]
        return carry

    lax.fori_loop(0, n_blocks // group, forward_step, 0)

    multiply_points(points, spectrum_ref, points)

    def inverse_step(step, carry):
        first = step * group
        pieces = [points[first + member] for member in range(group)]
        highs, lows = split_bf16(pieces[0] if group == 1 else jnp.concatenate(pieces, axis=1))
        both = jnp.dot(inverse_ref[...], highs, preferred_element_type=f32)
        rest = jnp.dot(inverse_ref[:block, :], lows, preferred_element_type=f32)
        result = (both[:block] + both[block:] + rest).astype(bf16)
        for member in range(group):
            piece = result[:, member * width : (member + 1) * width]
            out_ref[pl.ds((first + member) * per_block, per_block), :tok_rows, :] = piece.reshape(
                per_block, tok_rows, width
            )
        return carry

    lax.fori_loop(0, n_blocks // group, inverse_step, 0)


def score_rows(index, vars_dev, tok_rows, positions, gate_block, out_ref, gain_row, unembed):
    n_devices, extra, width = gate_block.shape
    gates = gate_block.astype(f32)
    place = lax.broadcasted_iota(jnp.int32, (n_devices, extra, width), 1)
    picked = [
        jnp.sum(jnp.where(place == index * vars_dev + var, gates, 0.0), axis=1)
        for var in range(vars_dev)
    ]
    gate_rows = picked[0] if vars_dev == 1 else jnp.concatenate(picked, axis=0)
    length = n_devices * tok_rows
    column = lax.broadcasted_iota(jnp.int32, (positions.shape[0], length), 1)
    picker = (column == positions).astype(f32).astype(bf16)
    filtered = jnp.dot(
        picker, out_ref[:, :tok_rows, :].reshape(length, width), preferred_element_type=f32
    )
    rows = (gate_rows * filtered).astype(bf16).astype(f32)
    weighted = (rows * gain_row).astype(bf16)
    return jnp.dot(weighted, unembed, preferred_element_type=f32), rows * rows


def pack_scores(raw, squares, vars_dev, packed, n_devices):
    total, width = packed.shape
    extra = total // n_devices
    per_row = raw.shape[1] // width
    packed[...] = jnp.zeros_like(packed)
    for var in range(vars_dev):
        mine = slice(var * n_devices, (var + 1) * n_devices)
        pieces = [raw[mine, r * width : (r + 1) * width] for r in range(per_row)] + [squares[mine]]
        for row, piece in enumerate(pieces):
            rounded = piece.astype(bf16).astype(f32)
            base = var * 2 * (per_row + 1) + row
            packed[pl.ds(base, n_devices, stride=extra), :] = rounded
            packed[pl.ds(base + per_row + 1, n_devices, stride=extra), :] = piece - rounded


def chunk_kernel(index, chunks, vars_dev, tok_rows, *refs):
    refs = list(refs)
    chunk_ref, spectrum_ref, forward_ref, inverse_ref = refs[:4]
    positions_ref, gain_ref, unembed_ref = refs[4:7]
    refs = refs[7:]
    first, last = index == 0, index == chunks - 1
    gates_ref = None if first else refs.pop(0)
    raw_before, square_before = (None, None) if first else (refs.pop(0), refs.pop(0))
    out_ref = refs.pop(0)
    raw_out, square_out = (None, None) if last else (refs.pop(0), refs.pop(0))
    gates_out = refs.pop(0) if first and not last else None
    points = refs[0]
    convolve(chunk_ref, spectrum_ref, forward_ref, inverse_ref, out_ref, points, tok_rows)
    gate_block = chunk_ref[:, tok_rows:, :] if first else gates_ref[...]
    raw, squares = score_rows(
        index, vars_dev, tok_rows, positions_ref[...], gate_block, out_ref, gain_ref[...], unembed_ref[...]
    )
    if not first:
        raw = raw + raw_before[...]
        squares = squares + square_before[...]
    if gates_out is not None:
        gates_out[...] = gate_block
    if not last:
        raw_out[...] = raw
        square_out[...] = squares
        return
    packed = refs[1]
    n_devices, _, width = out_ref.shape
    extra = out_ref.shape[1] - tok_rows
    pack_scores(raw, squares, vars_dev, packed, n_devices)
    out_ref[:, tok_rows:, :] = packed[...].reshape(n_devices, extra, width).astype(bf16)


def filter_chunk(index, chunks, vars_dev, tok_rows, extra, operands, carried):
    moved, spectrum = operands[:2]
    n_devices, _, width = moved.shape
    n_blocks, double, _ = spectrum.shape
    vocab = operands[6].shape[1]
    n_vars = operands[4].shape[0]
    first, last = index == 0, index == chunks - 1
    rows_out = tok_rows + (extra if last else 0)
    out_shape = [jax.ShapeDtypeStruct((n_devices, rows_out, width), bf16)]
    scratch = [pltpu.VMEM((n_blocks, double, width), f32)]
    if last:
        scratch.append(pltpu.VMEM((n_devices * extra, width), f32))
    else:
        out_shape.append(jax.ShapeDtypeStruct((n_vars, vocab), f32))
        out_shape.append(jax.ShapeDtypeStruct((n_vars, width), f32))
    if first and not last:
        out_shape.append(jax.ShapeDtypeStruct((n_devices, moved.shape[1] - tok_rows, width), bf16))
    flops = 2 * width * n_blocks * (double * double * 5 // 2 + 4 * n_blocks * double)
    return pl.pallas_call(
        functools.partial(chunk_kernel, index, chunks, vars_dev, tok_rows),
        in_specs=[whole_spec()] * (len(operands) + len(carried)),
        out_specs=[whole_spec()] * len(out_shape),
        out_shape=out_shape,
        scratch_shapes=scratch,
        compiler_params=pltpu.CompilerParams(vmem_limit_bytes=(20 if n_blocks <= 8 else 58) * MIB),
        cost_estimate=pl.CostEstimate(flops=flops, bytes_accessed=8 * MIB, transcendentals=0),
        name="filter_chunk",
    )(*operands, *carried)


def final_scores(sums, vars_dev, vocab, model_width, ref_ref, alt_ref):
    width = sums.shape[1]
    per_row = vocab // width
    ids = lax.broadcasted_iota(jnp.int32, (per_row, width), 0) * width
    ids += lax.broadcasted_iota(jnp.int32, (per_row, width), 1)
    row = lax.broadcasted_iota(jnp.int32, (2, vars_dev), 0)
    column = lax.broadcasted_iota(jnp.int32, (2, vars_dev), 1)
    scores = jnp.zeros((2, vars_dev), f32)

    def whole_sum(values):
        return jnp.sum(jnp.sum(values, axis=1, keepdims=True), axis=0, keepdims=True)

    for var in range(vars_dev):
        base = var * 2 * (per_row + 1)
        both = sums[base : base + per_row + 1, :]
        both = both + sums[base + per_row + 1 : base + 2 * (per_row + 1), :]
        square = jnp.sum(both[per_row:, :], axis=1, keepdims=True)
        logits = both[:per_row, :] * lax.rsqrt(square / model_width + norm_eps)
        largest = jnp.max(jnp.max(logits, axis=1, keepdims=True), axis=0, keepdims=True)
        log_total = largest + jnp.log(whole_sum(jnp.exp(logits - largest)))
        ref_logit = whole_sum(jnp.where(ids == ref_ref[var], logits, 0.0))
        alt_logit = whole_sum(jnp.where(ids == alt_ref[var], logits, 0.0))
        pair = jnp.where(row == 0, ref_logit - log_total, alt_logit - ref_logit)
        scores = jnp.where(column == var, pair, scores)
    return scores


def finish_kernel(chunks, vars_dev, vocab, ref_ref, alt_ref, streams_ref, *refs):
    back_refs, mixed_ref, scores_ref, sums = refs[:chunks], refs[chunks], refs[chunks + 1], refs[chunks + 2]
    tok_rows = streams_ref.shape[1]
    owners, _, width = back_refs[0].shape
    step = pl.program_id(0)
    for owner in range(owners):
        for chunk in range(chunks):
            lanes = pl.ds((owner * chunks + chunk) * width, width)
            gate = streams_ref[0, :, lanes].astype(f32)
            filtered = back_refs[chunk][owner, :tok_rows, :].astype(f32)
            mixed_ref[:, lanes] = (gate * filtered).astype(bf16)
    part = jnp.sum(back_refs[-1][:, tok_rows:, :].astype(f32), axis=0)

    @pl.when(step == 0)
    def _():
        sums[...] = part

    @pl.when(step > 0)
    def _():
        sums[...] += part

    @pl.when(step == pl.num_programs(0) - 1)
    def _():
        model_width = pl.num_programs(0) * owners * chunks * width
        scores_ref[...] = final_scores(sums[...], vars_dev, vocab, model_width, ref_ref, alt_ref)


def finish(streams, backs, ref_ids, alt_ids, vocab):
    _, tok_rows, model_width = streams.shape
    chunks = len(backs)
    n_devices, _, width = backs[0].shape
    vars_dev = ref_ids.shape[0]
    owners = max(1, n_devices // 4)
    while owners * chunks * width % lane_tile:
        owners *= 2
    extra = backs[-1].shape[1] - tok_rows
    return pl.pallas_call(
        functools.partial(finish_kernel, chunks, vars_dev, vocab),
        grid=(n_devices // owners,),
        in_specs=[
            pl.BlockSpec(memory_space=pltpu.SMEM),
            pl.BlockSpec(memory_space=pltpu.SMEM),
            pl.BlockSpec((1, tok_rows, owners * chunks * width), lambda i: (0, 0, i)),
        ]
        + [pl.BlockSpec((owners, back.shape[1], width), lambda i: (i, 0, 0)) for back in backs],
        out_specs=[
            pl.BlockSpec((tok_rows, owners * chunks * width), lambda i: (0, i)),
            pl.BlockSpec((2, vars_dev), lambda i: (0, 0)),
        ],
        out_shape=[
            jax.ShapeDtypeStruct((tok_rows, model_width), bf16),
            jax.ShapeDtypeStruct((2, vars_dev), f32),
        ],
        scratch_shapes=[pltpu.VMEM((extra, width), f32)],
        compiler_params=pltpu.CompilerParams(vmem_limit_bytes=24 * MIB),
        name="finish",
    )(ref_ids, alt_ids, streams, *backs)

def send_products_kernel(halves, vars_dev, me_ref, offsets_ref, streams_ref, out_ref, *scratch):
    built, pairs, gates, gate_rows, pair_sems, gate_sems, out_sems = scratch
    n_devices, _, tok_rows, width = pairs.shape
    me = me_ref[0]
    slot = tok_rows // vars_dev
    local_rows = [var * slot + offsets_ref[me * vars_dev + var] for var in range(vars_dev)]

    def pair_copy(owner):
        return pltpu.make_async_copy(
            streams_ref.at[pl.ds(1, 2), :, pl.ds(owner * width, width)],
            pairs.at[owner],
            pair_sems.at[owner],
        )

    def gate_copy(var):
        start = pl.multiple_of(local_rows[var] // row_tile * row_tile, row_tile)
        return pltpu.make_async_copy(
            streams_ref.at[0, pl.ds(start, row_tile), :], gates.at[var], gate_sems.at[var]
        )

    def out_copy(owner):
        return pltpu.make_async_copy(built.at[owner], out_ref.at[owner], out_sems.at[owner])

    for var in range(vars_dev):
        gate_copy(var).start()
    for owner in range(n_devices):
        pair_copy(owner).start()
    row = lax.broadcasted_iota(jnp.int32, gates.shape[1:], 0)
    for var in range(vars_dev):
        gate_copy(var).wait()
        mine = jnp.where(row == local_rows[var] % row_tile, gates[var].astype(f32), 0.0)
        gate_rows[var : var + 1, :] = jnp.sum(mine, axis=0, keepdims=True)
    extra = built.shape[1] - halves * tok_rows
    place = lax.broadcasted_iota(jnp.int32, (extra, lane_tile), 0)
    for owner in range(n_devices):
        pair_copy(owner).wait()
        tail = jnp.zeros((extra, lane_tile), f32)
        for half in range(halves):
            lanes = slice(half * lane_tile, (half + 1) * lane_tile)
            rows = slice(half * tok_rows, (half + 1) * tok_rows)
            built[owner, rows, :] = pairs[owner, 0, :, lanes] * pairs[owner, 1, :, lanes]
            start = owner * width + half * lane_tile
            for var in range(vars_dev):
                mine = gate_rows[var : var + 1, start : start + lane_tile]
                tail = jnp.where(place == half * vars_dev + var, mine, tail)
        built[owner, halves * tok_rows :, :] = tail.astype(bf16)
        out_copy(owner).start()
    for owner in range(n_devices):
        out_copy(owner).wait()


def send_products(me, offsets, streams, vars_dev, n_devices, extra):
    _, tok_rows, model_width = streams.shape
    width = model_width // n_devices
    halves = width // lane_tile
    rows_out = halves * tok_rows + extra
    return pl.pallas_call(
        functools.partial(send_products_kernel, halves, vars_dev),
        in_specs=[
            pl.BlockSpec(memory_space=pltpu.SMEM),
            pl.BlockSpec(memory_space=pltpu.SMEM),
            pl.BlockSpec(memory_space=pl.ANY),
        ],
        out_specs=pl.BlockSpec(memory_space=pl.ANY),
        out_shape=jax.ShapeDtypeStruct((n_devices, rows_out, lane_tile), bf16),
        scratch_shapes=[
            pltpu.VMEM((n_devices, rows_out, lane_tile), bf16),
            pltpu.VMEM((n_devices, 2, tok_rows, width), bf16),
            pltpu.VMEM((vars_dev, row_tile, model_width), bf16),
            pltpu.VMEM((round_up(vars_dev, half_tile), model_width), f32),
            pltpu.SemaphoreType.DMA((n_devices,)),
            pltpu.SemaphoreType.DMA((vars_dev,)),
            pltpu.SemaphoreType.DMA((n_devices,)),
        ],
        compiler_params=pltpu.CompilerParams(vmem_limit_bytes=60 * MIB),
        cost_estimate=pl.CostEstimate(
            flops=tok_rows * model_width, bytes_accessed=6 * tok_rows * model_width, transcendentals=0
        ),
        name="send_products",
    )(me, offsets, streams)


def stacked_filter_kernel(vars_dev, halves, tok_rows, *refs):
    positions_ref, gain_ref, unembed_ref, forward_ref, inverse_ref, spectrum_ref = refs[:6]
    arrived, leaving, points, joint, packed = refs[6:]
    n_devices = arrived.shape[0]
    body = halves * tok_rows
    n_blocks, double, width = points.shape
    block = double // 2
    per_block = block // tok_rows

    def forward_step(step, carry):
        pieces = []
        for half in range(halves):
            rows = slice(half * tok_rows, (half + 1) * tok_rows)
            parts = [arrived[step * per_block + m, rows, :] for m in range(per_block)]
            pieces.append(jnp.concatenate(parts, axis=0))
        signal = jnp.concatenate(pieces, axis=1)
        both = jnp.dot(forward_ref[...], signal, preferred_element_type=f32)
        points[step] = both[:double] + both[double:]
        return carry

    lax.fori_loop(0, n_blocks, forward_step, 0)
    multiply_points(points, spectrum_ref, joint)

    def inverse_step(step, carry):
        highs, lows = split_bf16(joint[step])
        both = jnp.dot(inverse_ref[...], highs, preferred_element_type=f32)
        rest = jnp.dot(inverse_ref[:block, :], lows, preferred_element_type=f32)
        result = (both[:block] + both[block:] + rest).astype(bf16)
        for member in range(per_block):
            for half in range(halves):
                leaving[step * per_block + member, half * tok_rows : (half + 1) * tok_rows, :] = result[
                    member * tok_rows : (member + 1) * tok_rows,
                    half * lane_tile : (half + 1) * lane_tile,
                ]
        return carry

    lax.fori_loop(0, n_blocks, inverse_step, 0)

    length = n_devices * tok_rows
    column = lax.broadcasted_iota(jnp.int32, (positions_ref.shape[0], length), 1)
    picker = (column == positions_ref[...]).astype(f32).astype(bf16)
    tails = arrived[:, body:, :].astype(f32)
    place = lax.broadcasted_iota(jnp.int32, tails.shape, 1)
    raw = None
    squares = None
    for half in range(halves):
        lanes = slice(half * lane_tile, (half + 1) * lane_tile)
        picked = [
            jnp.sum(jnp.where(place == half * vars_dev + var, tails, 0.0), axis=1)
            for var in range(vars_dev)
        ]
        gate_rows = picked[0] if vars_dev == 1 else jnp.concatenate(picked, axis=0)
        filtered = leaving[:, half * tok_rows : (half + 1) * tok_rows, :].reshape(length, lane_tile)
        filtered = jnp.dot(picker, filtered, preferred_element_type=f32)
        rows = (gate_rows * filtered).astype(bf16).astype(f32)
        weighted = (rows * gain_ref[:, lanes]).astype(bf16)
        part = jnp.dot(weighted, unembed_ref[lanes, :], preferred_element_type=f32)
        raw = part if raw is None else raw + part
        squares = rows * rows if squares is None else squares + rows * rows
    pack_scores(raw, squares, vars_dev, packed, n_devices)
    extra = packed.shape[0] // n_devices
    leaving[:, body:, :] = packed[...].reshape(n_devices, extra, lane_tile).astype(bf16)


def stacked_filter(operands, arrived, vars_dev, tok_rows, extra):
    n_devices = arrived.shape[0]
    n_blocks, double, width = operands[-1].shape
    halves = width // lane_tile
    rows_out = halves * tok_rows + extra
    flops = 2 * width * n_blocks * (double * double * 5 // 2 + 4 * n_blocks * double)
    return pl.pallas_call(
        functools.partial(stacked_filter_kernel, vars_dev, halves, tok_rows),
        in_specs=[whole_spec()] * (len(operands) + 1),
        out_specs=whole_spec(),
        out_shape=jax.ShapeDtypeStruct((n_devices, rows_out, lane_tile), bf16),
        scratch_shapes=[
            pltpu.VMEM((n_blocks, double, width), f32),
            pltpu.VMEM((n_blocks, double, width), f32),
            pltpu.VMEM((n_devices * extra, lane_tile), f32),
        ],
        compiler_params=pltpu.CompilerParams(vmem_limit_bytes=32 * MIB),
        cost_estimate=pl.CostEstimate(flops=flops, bytes_accessed=8 * MIB, transcendentals=0),
        name="stacked_filter",
    )(*operands, arrived)


def stacked_finish_kernel(halves, vars_dev, vocab, ref_ref, alt_ref, streams_ref, back_ref, *refs):
    mixed_ref, scores_ref, gates, results, gate_sems, out_sems = refs
    n_devices, tok_rows, width = gates.shape

    def gate_copy(owner):
        return pltpu.make_async_copy(
            streams_ref.at[0, :, pl.ds(owner * width, width)], gates.at[owner], gate_sems.at[owner]
        )

    def out_copy(owner):
        return pltpu.make_async_copy(
            results.at[owner], mixed_ref.at[:, pl.ds(owner * width, width)], out_sems.at[owner]
        )

    for owner in range(n_devices):
        gate_copy(owner).start()
    sums = None
    for owner in range(n_devices):
        gate_copy(owner).wait()
        for half in range(halves):
            lanes = slice(half * lane_tile, (half + 1) * lane_tile)
            filtered = back_ref[owner, half * tok_rows : (half + 1) * tok_rows, :]
            results[owner, :, lanes] = gates[owner, :, lanes] * filtered
        out_copy(owner).start()
        tail = back_ref[owner, halves * tok_rows :, :].astype(f32)
        sums = tail if sums is None else sums + tail
    model_width = n_devices * width
    scores_ref[...] = final_scores(sums, vars_dev, vocab, model_width, ref_ref, alt_ref)
    for owner in range(n_devices):
        out_copy(owner).wait()


def stacked_finish(ref_ids, alt_ids, streams, back, vocab):
    _, tok_rows, model_width = streams.shape
    n_devices = back.shape[0]
    vars_dev = ref_ids.shape[0]
    width = model_width // n_devices
    return pl.pallas_call(
        functools.partial(stacked_finish_kernel, width // lane_tile, vars_dev, vocab),
        in_specs=[pl.BlockSpec(memory_space=pltpu.SMEM)] * 2
        + [pl.BlockSpec(memory_space=pl.ANY), whole_spec()],
        out_specs=[pl.BlockSpec(memory_space=pl.ANY), whole_spec()],
        out_shape=[
            jax.ShapeDtypeStruct((tok_rows, model_width), bf16),
            jax.ShapeDtypeStruct((2, vars_dev), f32),
        ],
        scratch_shapes=[
            pltpu.VMEM((n_devices, tok_rows, width), bf16),
            pltpu.VMEM((n_devices, tok_rows, width), bf16),
            pltpu.SemaphoreType.DMA((n_devices,)),
            pltpu.SemaphoreType.DMA((n_devices,)),
        ],
        compiler_params=pltpu.CompilerParams(vmem_limit_bytes=12 * MIB),
        cost_estimate=pl.CostEstimate(
            flops=tok_rows * model_width, bytes_accessed=6 * tok_rows * model_width, transcendentals=0
        ),
        name="stacked_finish",
    )(ref_ids, alt_ids, streams, back)


def transposed(blocks):
    return lax.all_to_all(blocks, "seq", split_axis=0, concat_axis=0, tiled=True)


def shards(streams, long_filter, gain, unembed, offsets, ref_ids, alt_ids):
    n_devices = lax.axis_size("seq")
    my_index = lax.axis_index("seq")
    _, tok_rows, model_width = streams.shape
    group_width = model_width // n_devices
    vars_dev = ref_ids.shape[0]
    vocab = unembed.shape[1]
    chunks = max(1, group_width // lane_tile)
    width = group_width // chunks
    block = tok_rows * block_devices(n_devices, tok_rows)
    forward_np, inverse_np = block_tables(block)
    forward, inverse = jnp.asarray(forward_np), jnp.asarray(inverse_np)

    slot = tok_rows // vars_dev
    starts = jnp.arange(vars_dev, dtype=jnp.int32) * slot
    local_rows = starts + lax.dynamic_slice_in_dim(offsets, my_index * vars_dev, vars_dev)
    by_device = offsets.reshape(n_devices, vars_dev)
    positions = by_device + starts[None, :]
    positions += jnp.arange(n_devices, dtype=jnp.int32)[:, None] * tok_rows
    positions = positions.T.reshape(n_devices * vars_dev, 1)
    my_gain = lax.dynamic_slice_in_dim(gain, my_index * group_width, group_width).astype(f32)

    if chunks * lane_tile == group_width:
        me = jnp.reshape(my_index, (1,)).astype(jnp.int32)
        gate_extra = round_up(chunks * vars_dev, row_tile)
        score_extra = round_up(vars_dev * 2 * (vocab // lane_tile + 1), row_tile)
        blocks = send_products(me, offsets, streams, vars_dev, n_devices, gate_extra)
        arrived = transposed(blocks)
        spectrum = filter_spectrum(long_filter, forward, block, blocks)
        operands = (positions, my_gain[None, :], unembed, forward, inverse, spectrum)
        leaving = stacked_filter(operands, arrived, vars_dev, tok_rows, score_extra)
        mixed, scores = stacked_finish(ref_ids, alt_ids, streams, transposed(leaving), vocab)
        return (mixed, scores)

    gate_extra = round_up(chunks * vars_dev, row_tile)
    score_extra = round_up(vars_dev * 2 * (vocab // width + 1), row_tile)
    products = make_products(streams, local_rows, n_devices, chunks, gate_extra)
    moved = [lax.all_to_all(part, "seq", split_axis=0, concat_axis=0, tiled=True) for part in products]
    carried = ()
    backs = []
    for chunk in range(chunks):
        mine = slice(chunk * width, (chunk + 1) * width)
        spectrum = filter_spectrum(long_filter[mine], forward, block)
        operands = (
            moved[chunk], spectrum, forward, inverse, positions,
            my_gain[None, mine], unembed[mine],
        )
        if chunk > 0:
            carried = (gates,) + tuple(carried)
        results = filter_chunk(chunk, chunks, vars_dev, tok_rows, score_extra, operands, carried)
        carried = results[1:3]
        if chunk == 0 and chunks > 1:
            gates = results[3]
        backs.append(lax.all_to_all(results[0], "seq", split_axis=0, concat_axis=0, tiled=True))
    mixed, scores = finish(streams, backs, ref_ids, alt_ids, vocab)
    return (mixed, scores)


def solution(mesh):
    placed = (
        P(None, ("grp", "seq"), None),
        P("seq", None),
        P(),
        P("seq", None),
        P("grp"),
        P(("grp", "seq")),
        P(("grp", "seq")),
    )
    return jax.shard_map(
        shards,
        mesh=mesh,
        in_specs=placed,
        out_specs=(P(("grp", "seq"), None), P(None, ("grp", "seq"))),
        check_vma=False,
    )
```

```python
import functools
import math

import jax
import jax.numpy as jnp
import numpy as np
from jax import lax
from jax.experimental import pallas as pl
from jax.experimental.pallas import tpu as pltpu
from jax.sharding import PartitionSpec as P

norm_eps = 1e-06
f32 = jnp.float32
bf16 = jnp.bfloat16
row_tile = 16
half_tile = 8
lane_tile = 128
MIB = 1 << 20


def round_up(value, step):
    return -(-value // step) * step


def split_bf16(values):
    high = values.astype(bf16)
    low = (values - high.astype(f32)).astype(bf16)
    return high, low


def block_tables(block):
    turns = (4 * np.arange(block)[:, None] + 1) * np.arange(block)[None, :] % (4 * block)
    theta = turns * (math.pi / (2 * block))
    table = np.concatenate([np.cos(theta), np.sin(theta)], axis=0)
    parts = []
    for matrix in (table, table.T / block):
        high = matrix.astype(bf16)
        low = (matrix - high.astype(np.float64)).astype(bf16)
        parts.append(np.concatenate([high, low], axis=0))
    return parts


def block_devices(n_devices, tok_rows):
    target = math.isqrt(32 * n_devices * tok_rows)
    count = 1
    while n_devices % (2 * count) == 0 and 2 * count * tok_rows <= target:
        count *= 2
    return count


def whole_spec():
    return pl.BlockSpec(memory_space=pltpu.VMEM)


anywhere = pl.BlockSpec(memory_space=pl.ANY)
in_hbm = pl.BlockSpec(memory_space=pltpu.HBM)


def product_kernel(chunks, width, vars_dev, rows_ref, streams_ref, *out_refs):
    tok_rows = streams_ref.shape[1]
    n_owners = out_refs[0].shape[0]
    extra = out_refs[0].shape[1] - tok_rows
    place = lax.broadcasted_iota(jnp.int32, (extra, tok_rows), 0)
    column = lax.broadcasted_iota(jnp.int32, (extra, tok_rows), 1)
    for owner in range(n_owners):
        gates = jnp.zeros((extra, width), f32)
        for chunk in range(chunks):
            lanes = pl.ds((owner * chunks + chunk) * width, width)
            left = streams_ref[1, :, lanes].astype(f32)
            right = streams_ref[2, :, lanes].astype(f32)
            out_refs[chunk][owner, :tok_rows, :] = (left * right).astype(bf16)
            picker = jnp.zeros((extra, tok_rows), jnp.bool_)
            for var in range(vars_dev):
                picker |= (place == chunk * vars_dev + var) & (column == rows_ref[var])
            gates += jnp.dot(
                picker.astype(f32).astype(bf16),
                streams_ref[0, :, lanes],
                preferred_element_type=f32,
            )
        out_refs[0][owner, tok_rows:, :] = gates.astype(bf16)


def make_products(streams, local_rows, n_devices, chunks, extra):
    _, tok_rows, model_width = streams.shape
    vars_dev = local_rows.shape[0]
    group_width = model_width // n_devices
    width = group_width // chunks
    owners = max(1, n_devices // 4)
    while owners * group_width % lane_tile:
        owners *= 2
    steps = n_devices // owners
    rows_out = [tok_rows + extra] + [tok_rows] * (chunks - 1)
    return pl.pallas_call(
        functools.partial(product_kernel, chunks, width, vars_dev),
        grid=(steps,),
        in_specs=[
            pl.BlockSpec(memory_space=pltpu.SMEM),
            pl.BlockSpec((3, tok_rows, owners * group_width), lambda i: (0, 0, i)),
        ],
        out_specs=[pl.BlockSpec((owners, rows, width), lambda i: (i, 0, 0)) for rows in rows_out],
        out_shape=[jax.ShapeDtypeStruct((n_devices, rows, width), bf16) for rows in rows_out],
        compiler_params=pltpu.CompilerParams(vmem_limit_bytes=24 * MIB),
        name="products",
    )(local_rows, streams)


def spectrum_kernel(block, filter_ref, forward_ref, out_ref):
    n_blocks = out_ref.shape[0]
    for index in range(n_blocks):
        taps = filter_ref[:, index * block : (index + 1) * block]
        both = lax.dot_general(
            forward_ref[...], taps, (((1,), (1,)), ((), ())), preferred_element_type=f32
        )
        out_ref[index] = both[: 2 * block] + both[2 * block :]


def filter_spectrum(taps, forward, block):
    width, length = taps.shape
    n_blocks = length // block
    return pl.pallas_call(
        functools.partial(spectrum_kernel, block),
        in_specs=[whole_spec()] * 2,
        out_specs=whole_spec(),
        out_shape=jax.ShapeDtypeStruct((n_blocks, 2 * block, width), f32),
        compiler_params=pltpu.CompilerParams(vmem_limit_bytes=40 * MIB),
        cost_estimate=pl.CostEstimate(
            flops=8 * block * length * width, bytes_accessed=4 * MIB, transcendentals=0
        ),
        name="filter_spectrum",
    )(taps, forward)


def multiply_points(points, spectrum_ref, joint):
    n_blocks, double, width = points.shape
    block = double // 2
    lanes_step = min(width, lane_tile)

    def multiply_step(step, carry):
        start = pl.multiple_of(step * half_tile, half_tile)
        upper = pl.ds(start, half_tile)
        lower = pl.ds(pl.multiple_of(block + start, half_tile), half_tile)
        for first in range(0, width, lanes_step):
            lanes = slice(first, first + lanes_step)
            signal = [(points[k, upper, lanes], points[k, lower, lanes]) for k in range(n_blocks)]
            taps = [
                (spectrum_ref[k, upper, lanes], spectrum_ref[k, lower, lanes]) for k in range(n_blocks)
            ]
            before_re = jnp.zeros((half_tile, lanes_step), f32)
            before_im = jnp.zeros((half_tile, lanes_step), f32)
            for total in range(n_blocks):
                sum_re = jnp.zeros((half_tile, lanes_step), f32)
                sum_im = jnp.zeros((half_tile, lanes_step), f32)
                for delay in range(total + 1):
                    a_re, a_im = signal[total - delay]
                    b_re, b_im = taps[delay]
                    sum_re += a_re * b_re - a_im * b_im
                    sum_im += a_re * b_im + a_im * b_re
                joint[total, upper, lanes] = sum_re + before_im
                joint[total, lower, lanes] = sum_im - before_re
                before_re, before_im = sum_re, sum_im
        return carry

    lax.fori_loop(0, block // half_tile, multiply_step, 0)


def convolve(chunk_ref, spectrum_ref, forward_ref, inverse_ref, out_ref, points, tok_rows):
    n_blocks, double, width = points.shape
    block = double // 2
    per_block = block // tok_rows
    group = max(1, min(n_blocks, 256 // width)) if width % lane_tile == 0 else 1

    def forward_step(step, carry):
        pieces = []
        for member in range(group):
            start = (step * group + member) * per_block
            rows = chunk_ref[pl.ds(start, per_block), :tok_rows, :]
            pieces.append(rows.reshape(block, width))
        signal = pieces[0] if group == 1 else jnp.concatenate(pieces, axis=1)
        both = jnp.dot(forward_ref[...], signal, preferred_element_type=f32)
        total = both[:double] + both[double:]
        for member in range(group):
            points[step * group + member] = total[:, member * width : (member + 1) * width]
        return carry

    lax.fori_loop(0, n_blocks // group, forward_step, 0)

    multiply_points(points, spectrum_ref, points)

    def inverse_step(step, carry):
        first = step * group
        pieces = [points[first + member] for member in range(group)]
        highs, lows = split_bf16(pieces[0] if group == 1 else jnp.concatenate(pieces, axis=1))
        both = jnp.dot(inverse_ref[...], highs, preferred_element_type=f32)
        rest = jnp.dot(inverse_ref[:block, :], lows, preferred_element_type=f32)
        result = (both[:block] + both[block:] + rest).astype(bf16)
        for member in range(group):
            piece = result[:, member * width : (member + 1) * width]
            out_ref[pl.ds((first + member) * per_block, per_block), :tok_rows, :] = piece.reshape(
                per_block, tok_rows, width
            )
        return carry

    lax.fori_loop(0, n_blocks // group, inverse_step, 0)


def score_rows(index, vars_dev, tok_rows, positions, gate_block, out_ref, gain_row, unembed):
    n_devices, extra, width = gate_block.shape
    gates = gate_block.astype(f32)
    place = lax.broadcasted_iota(jnp.int32, (n_devices, extra, width), 1)
    picked = [
        jnp.sum(jnp.where(place == index * vars_dev + var, gates, 0.0), axis=1)
        for var in range(vars_dev)
    ]
    gate_rows = picked[0] if vars_dev == 1 else jnp.concatenate(picked, axis=0)
    length = n_devices * tok_rows
    column = lax.broadcasted_iota(jnp.int32, (positions.shape[0], length), 1)
    picker = (column == positions).astype(f32).astype(bf16)
    filtered = jnp.dot(
        picker, out_ref[:, :tok_rows, :].reshape(length, width), preferred_element_type=f32
    )
    rows = (gate_rows * filtered).astype(bf16).astype(f32)
    weighted = (rows * gain_row).astype(bf16)
    return jnp.dot(weighted, unembed, preferred_element_type=f32), rows * rows


def pack_scores(raw, squares, vars_dev, packed, n_devices):
    total, width = packed.shape
    extra = total // n_devices
    per_row = raw.shape[1] // width
    packed[...] = jnp.zeros_like(packed)
    for var in range(vars_dev):
        mine = slice(var * n_devices, (var + 1) * n_devices)
        pieces = [raw[mine, r * width : (r + 1) * width] for r in range(per_row)] + [squares[mine]]
        for row, piece in enumerate(pieces):
            rounded = piece.astype(bf16).astype(f32)
            base = var * 2 * (per_row + 1) + row
            packed[pl.ds(base, n_devices, stride=extra), :] = rounded
            packed[pl.ds(base + per_row + 1, n_devices, stride=extra), :] = piece - rounded


def chunk_kernel(index, chunks, vars_dev, tok_rows, *refs):
    refs = list(refs)
    chunk_ref, spectrum_ref, forward_ref, inverse_ref = refs[:4]
    positions_ref, gain_ref, unembed_ref = refs[4:7]
    refs = refs[7:]
    first, last = index == 0, index == chunks - 1
    gates_ref = None if first else refs.pop(0)
    raw_before, square_before = (None, None) if first else (refs.pop(0), refs.pop(0))
    out_ref = refs.pop(0)
    raw_out, square_out = (None, None) if last else (refs.pop(0), refs.pop(0))
    gates_out = refs.pop(0) if first and not last else None
    points = refs[0]
    convolve(chunk_ref, spectrum_ref, forward_ref, inverse_ref, out_ref, points, tok_rows)
    gate_block = chunk_ref[:, tok_rows:, :] if first else gates_ref[...]
    raw, squares = score_rows(
        index, vars_dev, tok_rows, positions_ref[...], gate_block, out_ref, gain_ref[...], unembed_ref[...]
    )
    if not first:
        raw = raw + raw_before[...]
        squares = squares + square_before[...]
    if gates_out is not None:
        gates_out[...] = gate_block
    if not last:
        raw_out[...] = raw
        square_out[...] = squares
        return
    packed = refs[1]
    n_devices, _, width = out_ref.shape
    extra = out_ref.shape[1] - tok_rows
    pack_scores(raw, squares, vars_dev, packed, n_devices)
    out_ref[:, tok_rows:, :] = packed[...].reshape(n_devices, extra, width).astype(bf16)


def filter_chunk(index, chunks, vars_dev, tok_rows, extra, operands, carried):
    moved, spectrum = operands[:2]
    n_devices, _, width = moved.shape
    n_blocks, double, _ = spectrum.shape
    vocab = operands[6].shape[1]
    n_vars = operands[4].shape[0]
    first, last = index == 0, index == chunks - 1
    rows_out = tok_rows + (extra if last else 0)
    out_shape = [jax.ShapeDtypeStruct((n_devices, rows_out, width), bf16)]
    scratch = [pltpu.VMEM((n_blocks, double, width), f32)]
    if last:
        scratch.append(pltpu.VMEM((n_devices * extra, width), f32))
    else:
        out_shape.append(jax.ShapeDtypeStruct((n_vars, vocab), f32))
        out_shape.append(jax.ShapeDtypeStruct((n_vars, width), f32))
    if first and not last:
        out_shape.append(jax.ShapeDtypeStruct((n_devices, moved.shape[1] - tok_rows, width), bf16))
    flops = 2 * width * n_blocks * (double * double * 5 // 2 + 4 * n_blocks * double)
    return pl.pallas_call(
        functools.partial(chunk_kernel, index, chunks, vars_dev, tok_rows),
        in_specs=[whole_spec()] * (len(operands) + len(carried)),
        out_specs=[whole_spec()] * len(out_shape),
        out_shape=out_shape,
        scratch_shapes=scratch,
        compiler_params=pltpu.CompilerParams(vmem_limit_bytes=(20 if n_blocks <= 8 else 58) * MIB),
        cost_estimate=pl.CostEstimate(flops=flops, bytes_accessed=8 * MIB, transcendentals=0),
        name="filter_chunk",
    )(*operands, *carried)


def final_scores(sums, vars_dev, vocab, model_width, ref_ref, alt_ref):
    width = sums.shape[1]
    per_row = vocab // width
    ids = lax.broadcasted_iota(jnp.int32, (per_row, width), 0) * width
    ids += lax.broadcasted_iota(jnp.int32, (per_row, width), 1)
    row = lax.broadcasted_iota(jnp.int32, (2, vars_dev), 0)
    column = lax.broadcasted_iota(jnp.int32, (2, vars_dev), 1)
    scores = jnp.zeros((2, vars_dev), f32)

    def whole_sum(values):
        return jnp.sum(jnp.sum(values, axis=1, keepdims=True), axis=0, keepdims=True)

    for var in range(vars_dev):
        base = var * 2 * (per_row + 1)
        both = sums[base : base + per_row + 1, :]
        both = both + sums[base + per_row + 1 : base + 2 * (per_row + 1), :]
        square = jnp.sum(both[per_row:, :], axis=1, keepdims=True)
        logits = both[:per_row, :] * lax.rsqrt(square / model_width + norm_eps)
        largest = jnp.max(jnp.max(logits, axis=1, keepdims=True), axis=0, keepdims=True)
        log_total = largest + jnp.log(whole_sum(jnp.exp(logits - largest)))
        ref_logit = whole_sum(jnp.where(ids == ref_ref[var], logits, 0.0))
        alt_logit = whole_sum(jnp.where(ids == alt_ref[var], logits, 0.0))
        pair = jnp.where(row == 0, ref_logit - log_total, alt_logit - ref_logit)
        scores = jnp.where(column == var, pair, scores)
    return scores


def finish_kernel(chunks, vars_dev, vocab, ref_ref, alt_ref, streams_ref, *refs):
    back_refs, mixed_ref, scores_ref, sums = refs[:chunks], refs[chunks], refs[chunks + 1], refs[chunks + 2]
    tok_rows = streams_ref.shape[1]
    owners, _, width = back_refs[0].shape
    step = pl.program_id(0)
    for owner in range(owners):
        for chunk in range(chunks):
            lanes = pl.ds((owner * chunks + chunk) * width, width)
            gate = streams_ref[0, :, lanes].astype(f32)
            filtered = back_refs[chunk][owner, :tok_rows, :].astype(f32)
            mixed_ref[:, lanes] = (gate * filtered).astype(bf16)
    part = jnp.sum(back_refs[-1][:, tok_rows:, :].astype(f32), axis=0)

    @pl.when(step == 0)
    def _():
        sums[...] = part

    @pl.when(step > 0)
    def _():
        sums[...] += part

    @pl.when(step == pl.num_programs(0) - 1)
    def _():
        model_width = pl.num_programs(0) * owners * chunks * width
        scores_ref[...] = final_scores(sums[...], vars_dev, vocab, model_width, ref_ref, alt_ref)


def finish(streams, backs, ref_ids, alt_ids, vocab):
    _, tok_rows, model_width = streams.shape
    chunks = len(backs)
    n_devices, _, width = backs[0].shape
    vars_dev = ref_ids.shape[0]
    owners = max(1, n_devices // 4)
    while owners * chunks * width % lane_tile:
        owners *= 2
    extra = backs[-1].shape[1] - tok_rows
    return pl.pallas_call(
        functools.partial(finish_kernel, chunks, vars_dev, vocab),
        grid=(n_devices // owners,),
        in_specs=[
            pl.BlockSpec(memory_space=pltpu.SMEM),
            pl.BlockSpec(memory_space=pltpu.SMEM),
            pl.BlockSpec((1, tok_rows, owners * chunks * width), lambda i: (0, 0, i)),
        ]
        + [pl.BlockSpec((owners, back.shape[1], width), lambda i: (i, 0, 0)) for back in backs],
        out_specs=[
            pl.BlockSpec((tok_rows, owners * chunks * width), lambda i: (0, i)),
            pl.BlockSpec((2, vars_dev), lambda i: (0, 0)),
        ],
        out_shape=[
            jax.ShapeDtypeStruct((tok_rows, model_width), bf16),
            jax.ShapeDtypeStruct((2, vars_dev), f32),
        ],
        scratch_shapes=[pltpu.VMEM((extra, width), f32)],
        compiler_params=pltpu.CompilerParams(vmem_limit_bytes=24 * MIB),
        name="finish",
    )(ref_ids, alt_ids, streams, *backs)

def send_products_kernel(first, together, halves, vars_dev, me_ref, offsets_ref, streams_ref, *refs):
    built, pairs, gates, gate_rows, pair_sems, gate_sems, out_sems = refs[-7:]
    count, _, tok_rows, width = pairs.shape
    out_refs = refs[-8:-7] if together else refs[-7 - count : -7]
    me = me_ref[0]
    slot = tok_rows // vars_dev
    local_rows = [var * slot + offsets_ref[me * vars_dev + var] for var in range(vars_dev)]
    base = me // count * count

    def lanes_from(step, offset):
        owner = base + step if together else me ^ (first + step)
        return pl.multiple_of(owner * width + offset, lane_tile)

    def pair_copy(step):
        return pltpu.make_async_copy(
            streams_ref.at[pl.ds(1, 2), :, pl.ds(lanes_from(step, 0), width)],
            pairs.at[step],
            pair_sems.at[step],
        )

    def gate_copy(var):
        start = pl.multiple_of(local_rows[var] // row_tile * row_tile, row_tile)
        return pltpu.make_async_copy(
            streams_ref.at[0, pl.ds(start, row_tile), :], gates.at[var], gate_sems.at[var]
        )

    def out_copy(step):
        target = out_refs[0].at[step] if together else out_refs[step]
        return pltpu.make_async_copy(built.at[step], target, out_sems.at[step])

    for var in range(vars_dev):
        gate_copy(var).start()
    for step in range(count):
        pair_copy(step).start()
    row = lax.broadcasted_iota(jnp.int32, gates.shape[1:], 0)
    for var in range(vars_dev):
        gate_copy(var).wait()
        mine = jnp.where(row == local_rows[var] % row_tile, gates[var].astype(f32), 0.0)
        gate_rows[var : var + 1, :] = jnp.sum(mine, axis=0, keepdims=True)
    extra = built.shape[1] - halves * tok_rows
    place = lax.broadcasted_iota(jnp.int32, (extra, lane_tile), 0)
    for step in range(count):
        pair_copy(step).wait()
        tail = jnp.zeros((extra, lane_tile), f32)
        for half in range(halves):
            lanes = slice(half * lane_tile, (half + 1) * lane_tile)
            rows = slice(half * tok_rows, (half + 1) * tok_rows)
            built[step, rows, :] = pairs[step, 0, :, lanes] * pairs[step, 1, :, lanes]
            for var in range(vars_dev):
                mine = gate_rows[var : var + 1, pl.ds(lanes_from(step, half * lane_tile), lane_tile)]
                tail = jnp.where(place == half * vars_dev + var, mine, tail)
        built[step, halves * tok_rows :, :] = tail.astype(bf16)
        out_copy(step).start()
    for step in range(count):
        out_copy(step).wait()


def send_products(me, offsets, streams, first, count, together, vars_dev, n_devices, extra, *earlier):
    _, tok_rows, model_width = streams.shape
    width = model_width // n_devices
    halves = width // lane_tile
    rows_out = halves * tok_rows + extra
    if together:
        out_shape = [jax.ShapeDtypeStruct((count, rows_out, lane_tile), bf16)]
    else:
        out_shape = [jax.ShapeDtypeStruct((rows_out, lane_tile), bf16)] * count
    return pl.pallas_call(
        functools.partial(send_products_kernel, first, together, halves, vars_dev),
        in_specs=[pl.BlockSpec(memory_space=pltpu.SMEM)] * 2 + [in_hbm] + [anywhere] * len(earlier),
        out_specs=[anywhere] * len(out_shape),
        out_shape=out_shape,
        scratch_shapes=[
            pltpu.VMEM((count, rows_out, lane_tile), bf16),
            pltpu.VMEM((count, 2, tok_rows, width), bf16),
            pltpu.VMEM((vars_dev, row_tile, model_width), bf16),
            pltpu.VMEM((round_up(vars_dev, half_tile), model_width), f32),
            pltpu.SemaphoreType.DMA((count,)),
            pltpu.SemaphoreType.DMA((vars_dev,)),
            pltpu.SemaphoreType.DMA((count,)),
        ],
        compiler_params=pltpu.CompilerParams(vmem_limit_bytes=60 * MIB),
        cost_estimate=pl.CostEstimate(
            flops=tok_rows * count * width, bytes_accessed=6 * tok_rows * count * width, transcendentals=0
        ),
        name="send_products",
    )(me, offsets, streams, *earlier)


def split_filter_kernel(steps, vars_dev, halves, tok_rows, me_ref, positions_ref, gain_ref, *refs):
    forward, inverse, unembed, taps = refs[:4]
    points, joint, spectrum, packed, arrived, leaving = refs[-6:]
    n_devices = arrived.shape[0]
    near = n_devices // 2
    count = 1 + len(steps)
    in_refs, out_refs = refs[4 : 4 + count], refs[4 + count : 4 + 2 * count]
    me = me_ref[0]
    base = me // near * near
    body = halves * tok_rows
    n_blocks, double, width = points.shape
    block = double // 2
    per_block = block // tok_rows
    group = 2 if n_blocks % 2 == 0 else 1

    for index in range(near):
        arrived[base + index] = in_refs[0][index]
    for index, step in enumerate(steps):
        arrived[me ^ step] = in_refs[1 + index][...]
    for index in range(n_blocks):
        both = lax.dot_general(
            forward[...],
            taps[:, index * block : (index + 1) * block],
            (((1,), (1,)), ((), ())),
            preferred_element_type=f32,
        )
        spectrum[index] = both[:double] + both[double:]

    for step in range(0, n_blocks, group):
        pieces = []
        for index in range(step, step + group):
            for half in range(halves):
                rows = slice(half * tok_rows, (half + 1) * tok_rows)
                parts = [arrived[index * per_block + m, rows, :] for m in range(per_block)]
                pieces.append(jnp.concatenate(parts, axis=0))
        signal = jnp.concatenate(pieces, axis=1)
        both = jnp.dot(forward[...], signal, preferred_element_type=f32)
        total = both[:double] + both[double:]
        for member in range(group):
            points[step + member] = total[:, member * width : (member + 1) * width]
    multiply_points(points, spectrum, joint)

    for step in range(0, n_blocks, group):
        highs, lows = split_bf16(jnp.concatenate([joint[step + m] for m in range(group)], axis=1))
        both = jnp.dot(inverse[...], highs, preferred_element_type=f32)
        rest = jnp.dot(inverse[:block, :], lows, preferred_element_type=f32)
        result = (both[:block] + both[block:] + rest).astype(bf16)
        for index in range(group):
            for member in range(per_block):
                for half in range(halves):
                    start = index * width + half * lane_tile
                    leaving[
                        (step + index) * per_block + member, half * tok_rows : (half + 1) * tok_rows, :
                    ] = result[member * tok_rows : (member + 1) * tok_rows, start : start + lane_tile]

    length = n_devices * tok_rows
    column = lax.broadcasted_iota(jnp.int32, (positions_ref.shape[0], length), 1)
    picker = (column == positions_ref[...]).astype(f32).astype(bf16)
    tails = arrived[:, body:, :].astype(f32)
    place = lax.broadcasted_iota(jnp.int32, tails.shape, 1)
    raw = None
    squares = None
    for half in range(halves):
        lanes = slice(half * lane_tile, (half + 1) * lane_tile)
        picked = [
            jnp.sum(jnp.where(place == half * vars_dev + var, tails, 0.0), axis=1)
            for var in range(vars_dev)
        ]
        gate_rows = picked[0] if vars_dev == 1 else jnp.concatenate(picked, axis=0)
        filtered = leaving[:, half * tok_rows : (half + 1) * tok_rows, :].reshape(length, lane_tile)
        filtered = jnp.dot(picker, filtered, preferred_element_type=f32)
        rows = (gate_rows * filtered).astype(bf16).astype(f32)
        weighted = (rows * gain_ref[:, lanes]).astype(bf16)
        part = jnp.dot(weighted, unembed[lanes, :], preferred_element_type=f32)
        raw = part if raw is None else raw + part
        squares = rows * rows if squares is None else squares + rows * rows
    pack_scores(raw, squares, vars_dev, packed, n_devices)
    extra = packed.shape[0] // n_devices
    leaving[:, body:, :] = packed[...].reshape(n_devices, extra, lane_tile).astype(bf16)
    for index, step in enumerate(steps):
        out_refs[1 + index][...] = leaving[me ^ step]
    for index in range(near):
        out_refs[0][index] = leaving[base + index]


def split_filter(me, positions, gain_row, tables, steps, arrivals, vars_dev, tok_rows, extra):
    width, length = tables[3].shape
    near = arrivals[0].shape[0]
    n_devices = 2 * near
    double = tables[0].shape[0] // 2
    n_blocks = 2 * length // double
    halves = width // lane_tile
    rows_out = halves * tok_rows + extra
    count = len(arrivals)
    flops = 2 * width * n_blocks * (double * double * 5 // 2 + 4 * n_blocks * double)
    return pl.pallas_call(
        functools.partial(split_filter_kernel, steps, vars_dev, halves, tok_rows),
        in_specs=[pl.BlockSpec(memory_space=pltpu.SMEM)] + [whole_spec()] * (6 + count),
        out_specs=[whole_spec()] * count,
        out_shape=[jax.ShapeDtypeStruct((near, rows_out, lane_tile), bf16)]
        + [jax.ShapeDtypeStruct((rows_out, lane_tile), bf16)] * (count - 1),
        scratch_shapes=[
            pltpu.VMEM((n_blocks, double, width), f32),
            pltpu.VMEM((n_blocks, double, width), f32),
            pltpu.VMEM((n_blocks, double, width), f32),
            pltpu.VMEM((n_devices * extra, lane_tile), f32),
            pltpu.VMEM((n_devices,) + arrivals[1].shape, bf16),
            pltpu.VMEM((n_devices, rows_out, lane_tile), bf16),
        ],
        compiler_params=pltpu.CompilerParams(vmem_limit_bytes=24 * MIB),
        cost_estimate=pl.CostEstimate(flops=flops, bytes_accessed=8 * MIB, transcendentals=0),
        name="split_filter",
    )(me, positions, gain_row, *tables, *arrivals)


def split_finish_kernel(steps, halves, vars_dev, vocab, me_ref, ref_ref, alt_ref, gates_ref, *refs):
    mixed_ref, scores_ref, results, out_sems = refs[-4:]
    n_devices, tok_rows, width = results.shape
    near = n_devices // 2
    me = me_ref[0]
    base = me // near * near

    def lanes_of(index, offset=0, size=width):
        owner = base + index if index < near else me ^ steps[index - near]
        return pl.ds(pl.multiple_of(owner * width + offset, lane_tile), size)

    def out_copy(index):
        return pltpu.make_async_copy(
            results.at[index], mixed_ref.at[:, lanes_of(index)], out_sems.at[index]
        )

    sums = None
    for index in range(n_devices):
        back_ref = refs[0].at[index] if index < near else refs[1 + index - near]
        for half in range(halves):
            lanes = slice(half * lane_tile, (half + 1) * lane_tile)
            filtered = back_ref[half * tok_rows : (half + 1) * tok_rows, :]
            gate = gates_ref[:, lanes_of(index, half * lane_tile, lane_tile)]
            results[index, :, lanes] = gate * filtered
        out_copy(index).start()
        tail = back_ref[halves * tok_rows :, :].astype(f32)
        sums = tail if sums is None else sums + tail
    model_width = n_devices * width
    scores_ref[...] = final_scores(sums, vars_dev, vocab, model_width, ref_ref, alt_ref)
    for index in range(n_devices):
        out_copy(index).wait()


def split_finish(me, ref_ids, alt_ids, gates, steps, backs, vocab):
    tok_rows, model_width = gates.shape
    n_devices = 2 * backs[0].shape[0]
    vars_dev = ref_ids.shape[0]
    width = model_width // n_devices
    return pl.pallas_call(
        functools.partial(split_finish_kernel, steps, width // lane_tile, vars_dev, vocab),
        in_specs=[pl.BlockSpec(memory_space=pltpu.SMEM)] * 3 + [whole_spec()] * (1 + len(backs)),
        out_specs=[anywhere, whole_spec()],
        out_shape=[
            jax.ShapeDtypeStruct((tok_rows, model_width), bf16),
            jax.ShapeDtypeStruct((2, vars_dev), f32),
        ],
        scratch_shapes=[
            pltpu.VMEM((n_devices, tok_rows, width), bf16),
            pltpu.SemaphoreType.DMA((n_devices,)),
        ],
        compiler_params=pltpu.CompilerParams(vmem_limit_bytes=16 * MIB),
        cost_estimate=pl.CostEstimate(
            flops=tok_rows * model_width, bytes_accessed=6 * tok_rows * model_width, transcendentals=0
        ),
        name="split_finish",
    )(me, ref_ids, alt_ids, gates, *backs)


def hold_kernel(part_ref, earlier_ref, out_ref):
    pass


def held_until(part, earlier):
    return pl.pallas_call(
        hold_kernel,
        in_specs=[anywhere, anywhere],
        out_specs=anywhere,
        out_shape=jax.ShapeDtypeStruct(part.shape, part.dtype),
        input_output_aliases={0: 0},
        compiler_params=pltpu.CompilerParams(vmem_limit_bytes=16 * MIB),
        name="hold",
    )(part, earlier)


def exchange_near(part, n_devices):
    near = n_devices // 2
    groups = [list(range(near)), list(range(near, n_devices))]
    return lax.all_to_all(
        part, "seq", split_axis=0, concat_axis=0, axis_index_groups=groups, tiled=True
    )


def exchange_far(parts, steps, n_devices):
    moved = []
    for step, part in zip(steps, parts):
        pairs = [(device, device ^ step) for device in range(n_devices)]
        moved.append(lax.ppermute(part, "seq", pairs))
    return moved


def shards(streams, long_filter, gain, unembed, offsets, ref_ids, alt_ids):
    n_devices = lax.axis_size("seq")
    my_index = lax.axis_index("seq")
    _, tok_rows, model_width = streams.shape
    group_width = model_width // n_devices
    vars_dev = ref_ids.shape[0]
    vocab = unembed.shape[1]
    chunks = max(1, group_width // lane_tile)
    width = group_width // chunks
    block = tok_rows * block_devices(n_devices, tok_rows)
    forward_np, inverse_np = block_tables(block)
    forward, inverse = jnp.asarray(forward_np), jnp.asarray(inverse_np)

    slot = tok_rows // vars_dev
    starts = jnp.arange(vars_dev, dtype=jnp.int32) * slot
    local_rows = starts + lax.dynamic_slice_in_dim(offsets, my_index * vars_dev, vars_dev)
    by_device = offsets.reshape(n_devices, vars_dev)
    positions = by_device + starts[None, :]
    positions += jnp.arange(n_devices, dtype=jnp.int32)[:, None] * tok_rows
    positions = positions.T.reshape(n_devices * vars_dev, 1)
    my_gain = lax.dynamic_slice_in_dim(gain, my_index * group_width, group_width).astype(f32)

    if chunks * lane_tile == group_width and n_devices & (n_devices - 1) == 0:
        me = jnp.reshape(my_index, (1,)).astype(jnp.int32)
        gate_extra = round_up(chunks * vars_dev, row_tile)
        score_extra = round_up(vars_dev * 2 * (vocab // lane_tile + 1), row_tile)
        near = n_devices // 2
        steps = list(range(near, n_devices))
        sizes = (vars_dev, n_devices, gate_extra)
        far_parts = send_products(me, offsets, streams, near, near, False, *sizes)
        far_moved = exchange_far(far_parts, steps, n_devices)
        near_part = send_products(me, offsets, streams, 0, near, True, *sizes, far_moved[0])[0]
        arrivals = [exchange_near(near_part, n_devices)] + far_moved
        tables = (forward, inverse, unembed, long_filter)
        leaving = split_filter(
            me, positions, my_gain[None, :], tables, steps, arrivals, vars_dev, tok_rows, score_extra
        )
        returned = exchange_far(leaving[1:], steps, n_devices)
        near_back = exchange_near(held_until(leaving[0], returned[0]), n_devices)
        backs = [near_back] + returned
        mixed, scores = split_finish(me, ref_ids, alt_ids, streams[0], steps, backs, vocab)
        return (mixed, scores)

    gate_extra = round_up(chunks * vars_dev, row_tile)
    score_extra = round_up(vars_dev * 2 * (vocab // width + 1), row_tile)
    products = make_products(streams, local_rows, n_devices, chunks, gate_extra)
    moved = [lax.all_to_all(part, "seq", split_axis=0, concat_axis=0, tiled=True) for part in products]
    carried = ()
    backs = []
    for chunk in range(chunks):
        mine = slice(chunk * width, (chunk + 1) * width)
        spectrum = filter_spectrum(long_filter[mine], forward, block)
        operands = (
            moved[chunk], spectrum, forward, inverse, positions,
            my_gain[None, mine], unembed[mine],
        )
        if chunk > 0:
            carried = (gates,) + tuple(carried)
        results = filter_chunk(chunk, chunks, vars_dev, tok_rows, score_extra, operands, carried)
        carried = results[1:3]
        if chunk == 0 and chunks > 1:
            gates = results[3]
        backs.append(lax.all_to_all(results[0], "seq", split_axis=0, concat_axis=0, tiled=True))
    mixed, scores = finish(streams, backs, ref_ids, alt_ids, vocab)
    return (mixed, scores)


def solution(mesh):
    placed = (
        P(None, ("grp", "seq"), None),
        P("seq", None),
        P(),
        P("seq", None),
        P("grp"),
        P(("grp", "seq")),
        P(("grp", "seq")),
    )
    return jax.shard_map(
        shards,
        mesh=mesh,
        in_specs=placed,
        out_specs=(P(("grp", "seq"), None), P(None, ("grp", "seq"))),
        check_vma=False,
    )
```

```python
import functools
import math

import jax
import jax.numpy as jnp
import numpy as np
from jax import lax
from jax.experimental import pallas as pl
from jax.experimental.pallas import tpu as pltpu
from jax.sharding import PartitionSpec as P

norm_eps = 1e-06
f32 = jnp.float32
bf16 = jnp.bfloat16
row_tile = 16
half_tile = 8
lane_tile = 128
MIB = 1 << 20


def round_up(value, step):
    return -(-value // step) * step


def split_bf16(values):
    high = values.astype(bf16)
    low = (values - high.astype(f32)).astype(bf16)
    return high, low


def block_tables(block):
    turns = (4 * np.arange(block)[:, None] + 1) * np.arange(block)[None, :] % (4 * block)
    theta = turns * (math.pi / (2 * block))
    table = np.concatenate([np.cos(theta), np.sin(theta)], axis=0)
    parts = []
    for matrix in (table, table.T / block):
        high = matrix.astype(bf16)
        low = (matrix - high.astype(np.float64)).astype(bf16)
        parts.append(np.concatenate([high, low], axis=0))
    return parts


def block_devices(n_devices, tok_rows):
    target = math.isqrt(32 * n_devices * tok_rows)
    count = 1
    while n_devices % (2 * count) == 0 and 2 * count * tok_rows <= target:
        count *= 2
    return count


def whole_spec():
    return pl.BlockSpec(memory_space=pltpu.VMEM)


def product_kernel(chunks, width, vars_dev, rows_ref, streams_ref, *out_refs):
    tok_rows = streams_ref.shape[1]
    n_owners = out_refs[0].shape[0]
    extra = out_refs[0].shape[1] - tok_rows
    place = lax.broadcasted_iota(jnp.int32, (extra, tok_rows), 0)
    column = lax.broadcasted_iota(jnp.int32, (extra, tok_rows), 1)
    for owner in range(n_owners):
        gates = jnp.zeros((extra, width), f32)
        for chunk in range(chunks):
            lanes = pl.ds((owner * chunks + chunk) * width, width)
            left = streams_ref[1, :, lanes].astype(f32)
            right = streams_ref[2, :, lanes].astype(f32)
            out_refs[chunk][owner, :tok_rows, :] = (left * right).astype(bf16)
            picker = jnp.zeros((extra, tok_rows), jnp.bool_)
            for var in range(vars_dev):
                picker |= (place == chunk * vars_dev + var) & (column == rows_ref[var])
            gates += jnp.dot(
                picker.astype(f32).astype(bf16),
                streams_ref[0, :, lanes],
                preferred_element_type=f32,
            )
        out_refs[0][owner, tok_rows:, :] = gates.astype(bf16)


def make_products(streams, local_rows, n_devices, chunks, extra):
    _, tok_rows, model_width = streams.shape
    vars_dev = local_rows.shape[0]
    group_width = model_width // n_devices
    width = group_width // chunks
    owners = max(1, n_devices // 4)
    while owners * group_width % lane_tile:
        owners *= 2
    steps = n_devices // owners
    rows_out = [tok_rows + extra] + [tok_rows] * (chunks - 1)
    return pl.pallas_call(
        functools.partial(product_kernel, chunks, width, vars_dev),
        grid=(steps,),
        in_specs=[
            pl.BlockSpec(memory_space=pltpu.SMEM),
            pl.BlockSpec((3, tok_rows, owners * group_width), lambda i: (0, 0, i)),
        ],
        out_specs=[pl.BlockSpec((owners, rows, width), lambda i: (i, 0, 0)) for rows in rows_out],
        out_shape=[jax.ShapeDtypeStruct((n_devices, rows, width), bf16) for rows in rows_out],
        compiler_params=pltpu.CompilerParams(vmem_limit_bytes=24 * MIB),
        name="products",
    )(local_rows, streams)


def spectrum_kernel(block, filter_ref, forward_ref, out_ref):
    n_blocks = out_ref.shape[0]
    for index in range(n_blocks):
        taps = filter_ref[:, index * block : (index + 1) * block]
        both = lax.dot_general(
            forward_ref[...], taps, (((1,), (1,)), ((), ())), preferred_element_type=f32
        )
        out_ref[index] = both[: 2 * block] + both[2 * block :]


def filter_spectrum(taps, forward, block):
    width, length = taps.shape
    n_blocks = length // block
    return pl.pallas_call(
        functools.partial(spectrum_kernel, block),
        in_specs=[whole_spec()] * 2,
        out_specs=whole_spec(),
        out_shape=jax.ShapeDtypeStruct((n_blocks, 2 * block, width), f32),
        compiler_params=pltpu.CompilerParams(vmem_limit_bytes=40 * MIB),
        cost_estimate=pl.CostEstimate(
            flops=8 * block * length * width, bytes_accessed=4 * MIB, transcendentals=0
        ),
        name="filter_spectrum",
    )(taps, forward)


def multiply_points(points, spectrum_ref, joint):
    n_blocks, double, width = points.shape
    block = double // 2
    lanes_step = min(width, lane_tile)

    def multiply_step(step, carry):
        start = pl.multiple_of(step * half_tile, half_tile)
        upper = pl.ds(start, half_tile)
        lower = pl.ds(pl.multiple_of(block + start, half_tile), half_tile)
        for first in range(0, width, lanes_step):
            lanes = slice(first, first + lanes_step)
            signal = [(points[k, upper, lanes], points[k, lower, lanes]) for k in range(n_blocks)]
            taps = [
                (spectrum_ref[k, upper, lanes], spectrum_ref[k, lower, lanes]) for k in range(n_blocks)
            ]
            before_re = jnp.zeros((half_tile, lanes_step), f32)
            before_im = jnp.zeros((half_tile, lanes_step), f32)
            for total in range(n_blocks):
                sum_re = jnp.zeros((half_tile, lanes_step), f32)
                sum_im = jnp.zeros((half_tile, lanes_step), f32)
                for delay in range(total + 1):
                    a_re, a_im = signal[total - delay]
                    b_re, b_im = taps[delay]
                    sum_re += a_re * b_re - a_im * b_im
                    sum_im += a_re * b_im + a_im * b_re
                joint[total, upper, lanes] = sum_re + before_im
                joint[total, lower, lanes] = sum_im - before_re
                before_re, before_im = sum_re, sum_im
        return carry

    lax.fori_loop(0, block // half_tile, multiply_step, 0)


def convolve(chunk_ref, spectrum_ref, forward_ref, inverse_ref, out_ref, points, tok_rows):
    n_blocks, double, width = points.shape
    block = double // 2
    per_block = block // tok_rows
    group = max(1, min(n_blocks, 256 // width)) if width % lane_tile == 0 else 1

    def forward_step(step, carry):
        pieces = []
        for member in range(group):
            start = (step * group + member) * per_block
            rows = chunk_ref[pl.ds(start, per_block), :tok_rows, :]
            pieces.append(rows.reshape(block, width))
        signal = pieces[0] if group == 1 else jnp.concatenate(pieces, axis=1)
        both = jnp.dot(forward_ref[...], signal, preferred_element_type=f32)
        total = both[:double] + both[double:]
        for member in range(group):
            points[step * group + member] = total[:, member * width : (member + 1) * width]
        return carry

    lax.fori_loop(0, n_blocks // group, forward_step, 0)

    multiply_points(points, spectrum_ref, points)

    def inverse_step(step, carry):
        first = step * group
        pieces = [points[first + member] for member in range(group)]
        highs, lows = split_bf16(pieces[0] if group == 1 else jnp.concatenate(pieces, axis=1))
        both = jnp.dot(inverse_ref[...], highs, preferred_element_type=f32)
        rest = jnp.dot(inverse_ref[:block, :], lows, preferred_element_type=f32)
        result = (both[:block] + both[block:] + rest).astype(bf16)
        for member in range(group):
            piece = result[:, member * width : (member + 1) * width]
            out_ref[pl.ds((first + member) * per_block, per_block), :tok_rows, :] = piece.reshape(
                per_block, tok_rows, width
            )
        return carry

    lax.fori_loop(0, n_blocks // group, inverse_step, 0)


def score_rows(index, vars_dev, tok_rows, positions, gate_block, out_ref, gain_row, unembed):
    n_devices, extra, width = gate_block.shape
    gates = gate_block.astype(f32)
    place = lax.broadcasted_iota(jnp.int32, (n_devices, extra, width), 1)
    picked = [
        jnp.sum(jnp.where(place == index * vars_dev + var, gates, 0.0), axis=1)
        for var in range(vars_dev)
    ]
    gate_rows = picked[0] if vars_dev == 1 else jnp.concatenate(picked, axis=0)
    length = n_devices * tok_rows
    column = lax.broadcasted_iota(jnp.int32, (positions.shape[0], length), 1)
    picker = (column == positions).astype(f32).astype(bf16)
    filtered = jnp.dot(
        picker, out_ref[:, :tok_rows, :].reshape(length, width), preferred_element_type=f32
    )
    rows = (gate_rows * filtered).astype(bf16).astype(f32)
    weighted = (rows * gain_row).astype(bf16)
    return jnp.dot(weighted, unembed, preferred_element_type=f32), rows * rows


def pack_scores(raw, squares, raw_parts, vars_dev, packed, n_devices):
    total, width = packed.shape
    extra = total // n_devices
    per_row = raw.shape[1] // width
    count = raw_parts * per_row + 2
    packed[...] = jnp.zeros_like(packed)
    for var in range(vars_dev):
        mine = slice(var * n_devices, (var + 1) * n_devices)
        pieces = [raw[mine, r * width : (r + 1) * width] for r in range(per_row)]
        rounded = [piece.astype(bf16).astype(f32) for piece in pieces]
        rows = rounded + [piece - high for piece, high in zip(pieces, rounded)][: (raw_parts - 1) * per_row]
        high = squares[mine].astype(bf16).astype(f32)
        rows += [high, squares[mine] - high]
        for row, piece in enumerate(rows):
            packed[pl.ds(var * count + row, n_devices, stride=extra), :] = piece


def chunk_kernel(index, chunks, vars_dev, tok_rows, *refs):
    refs = list(refs)
    chunk_ref, spectrum_ref, forward_ref, inverse_ref = refs[:4]
    positions_ref, gain_ref, unembed_ref = refs[4:7]
    refs = refs[7:]
    first, last = index == 0, index == chunks - 1
    gates_ref = None if first else refs.pop(0)
    raw_before, square_before = (None, None) if first else (refs.pop(0), refs.pop(0))
    out_ref = refs.pop(0)
    raw_out, square_out = (None, None) if last else (refs.pop(0), refs.pop(0))
    gates_out = refs.pop(0) if first and not last else None
    points = refs[0]
    convolve(chunk_ref, spectrum_ref, forward_ref, inverse_ref, out_ref, points, tok_rows)
    gate_block = chunk_ref[:, tok_rows:, :] if first else gates_ref[...]
    raw, squares = score_rows(
        index, vars_dev, tok_rows, positions_ref[...], gate_block, out_ref, gain_ref[...], unembed_ref[...]
    )
    if not first:
        raw = raw + raw_before[...]
        squares = squares + square_before[...]
    if gates_out is not None:
        gates_out[...] = gate_block
    if not last:
        raw_out[...] = raw
        square_out[...] = squares
        return
    packed = refs[1]
    n_devices, _, width = out_ref.shape
    extra = out_ref.shape[1] - tok_rows
    pack_scores(raw, squares, 2, vars_dev, packed, n_devices)
    out_ref[:, tok_rows:, :] = packed[...].reshape(n_devices, extra, width).astype(bf16)


def filter_chunk(index, chunks, vars_dev, tok_rows, extra, operands, carried):
    moved, spectrum = operands[:2]
    n_devices, _, width = moved.shape
    n_blocks, double, _ = spectrum.shape
    vocab = operands[6].shape[1]
    n_vars = operands[4].shape[0]
    first, last = index == 0, index == chunks - 1
    rows_out = tok_rows + (extra if last else 0)
    out_shape = [jax.ShapeDtypeStruct((n_devices, rows_out, width), bf16)]
    scratch = [pltpu.VMEM((n_blocks, double, width), f32)]
    if last:
        scratch.append(pltpu.VMEM((n_devices * extra, width), f32))
    else:
        out_shape.append(jax.ShapeDtypeStruct((n_vars, vocab), f32))
        out_shape.append(jax.ShapeDtypeStruct((n_vars, width), f32))
    if first and not last:
        out_shape.append(jax.ShapeDtypeStruct((n_devices, moved.shape[1] - tok_rows, width), bf16))
    flops = 2 * width * n_blocks * (double * double * 5 // 2 + 4 * n_blocks * double)
    return pl.pallas_call(
        functools.partial(chunk_kernel, index, chunks, vars_dev, tok_rows),
        in_specs=[whole_spec()] * (len(operands) + len(carried)),
        out_specs=[whole_spec()] * len(out_shape),
        out_shape=out_shape,
        scratch_shapes=scratch,
        compiler_params=pltpu.CompilerParams(vmem_limit_bytes=(20 if n_blocks <= 8 else 58) * MIB),
        cost_estimate=pl.CostEstimate(flops=flops, bytes_accessed=8 * MIB, transcendentals=0),
        name="filter_chunk",
    )(*operands, *carried)


def final_scores(sums, raw_parts, vars_dev, vocab, model_width, ref_ref, alt_ref):
    width = sums.shape[1]
    per_row = vocab // width
    count = raw_parts * per_row + 2
    ids = lax.broadcasted_iota(jnp.int32, (per_row, width), 0) * width
    ids += lax.broadcasted_iota(jnp.int32, (per_row, width), 1)
    row = lax.broadcasted_iota(jnp.int32, (vars_dev, 2), 0)
    column = lax.broadcasted_iota(jnp.int32, (vars_dev, 2), 1)
    scores = jnp.zeros((vars_dev, 2), f32)

    def whole_sum(values):
        return jnp.sum(jnp.sum(values, axis=1, keepdims=True), axis=0, keepdims=True)

    for var in range(vars_dev):
        base = var * count
        raw = sums[base : base + per_row, :]
        if raw_parts == 2:
            raw = raw + sums[base + per_row : base + 2 * per_row, :]
        square = whole_sum(sums[base + count - 2 : base + count, :])
        logits = raw * lax.rsqrt(square / model_width + norm_eps)
        largest = jnp.max(jnp.max(logits, axis=1, keepdims=True), axis=0, keepdims=True)
        log_total = largest + jnp.log(whole_sum(jnp.exp(logits - largest)))
        ref_logit = whole_sum(jnp.where(ids == ref_ref[var], logits, 0.0))
        alt_logit = whole_sum(jnp.where(ids == alt_ref[var], logits, 0.0))
        pair = jnp.where(column == 0, ref_logit - log_total, alt_logit - ref_logit)
        scores = jnp.where(row == var, pair, scores)
    return scores


def finish_kernel(chunks, vars_dev, vocab, ref_ref, alt_ref, streams_ref, *refs):
    back_refs, mixed_ref, scores_ref, sums = refs[:chunks], refs[chunks], refs[chunks + 1], refs[chunks + 2]
    tok_rows = streams_ref.shape[1]
    owners, _, width = back_refs[0].shape
    step = pl.program_id(0)
    for owner in range(owners):
        for chunk in range(chunks):
            lanes = pl.ds((owner * chunks + chunk) * width, width)
            gate = streams_ref[0, :, lanes].astype(f32)
            filtered = back_refs[chunk][owner, :tok_rows, :].astype(f32)
            mixed_ref[:, lanes] = (gate * filtered).astype(bf16)
    part = jnp.sum(back_refs[-1][:, tok_rows:, :].astype(f32), axis=0)

    @pl.when(step == 0)
    def _():
        sums[...] = part

    @pl.when(step > 0)
    def _():
        sums[...] += part

    @pl.when(step == pl.num_programs(0) - 1)
    def _():
        model_width = pl.num_programs(0) * owners * chunks * width
        scores_ref[...] = final_scores(sums[...], 2, vars_dev, vocab, model_width, ref_ref, alt_ref)


def finish(streams, backs, ref_ids, alt_ids, vocab):
    _, tok_rows, model_width = streams.shape
    chunks = len(backs)
    n_devices, _, width = backs[0].shape
    vars_dev = ref_ids.shape[0]
    owners = max(1, n_devices // 4)
    while owners * chunks * width % lane_tile:
        owners *= 2
    extra = backs[-1].shape[1] - tok_rows
    return pl.pallas_call(
        functools.partial(finish_kernel, chunks, vars_dev, vocab),
        grid=(n_devices // owners,),
        in_specs=[
            pl.BlockSpec(memory_space=pltpu.SMEM),
            pl.BlockSpec(memory_space=pltpu.SMEM),
            pl.BlockSpec((1, tok_rows, owners * chunks * width), lambda i: (0, 0, i)),
        ]
        + [pl.BlockSpec((owners, back.shape[1], width), lambda i: (i, 0, 0)) for back in backs],
        out_specs=[
            pl.BlockSpec((tok_rows, owners * chunks * width), lambda i: (0, i)),
            pl.BlockSpec((vars_dev, 2), lambda i: (0, 0)),
        ],
        out_shape=[
            jax.ShapeDtypeStruct((tok_rows, model_width), bf16),
            jax.ShapeDtypeStruct((vars_dev, 2), f32),
        ],
        scratch_shapes=[pltpu.VMEM((extra, width), f32)],
        compiler_params=pltpu.CompilerParams(vmem_limit_bytes=24 * MIB),
        name="finish",
    )(ref_ids, alt_ids, streams, *backs)

def stacked_products_kernel(halves, vars_dev, me_ref, offsets_ref, streams_ref, out_ref):
    _, tok_rows, model_width = streams_ref.shape
    n_devices = out_ref.shape[0]
    extra = out_ref.shape[1] - halves * tok_rows
    me = me_ref[0]
    slot = tok_rows // vars_dev
    row = lax.broadcasted_iota(jnp.int32, (row_tile, model_width), 0)
    place = lax.broadcasted_iota(jnp.int32, (extra, lane_tile), 0)
    gate_rows = []
    for var in range(vars_dev):
        local = var * slot + offsets_ref[me * vars_dev + var]
        start = pl.multiple_of(local // row_tile * row_tile, row_tile)
        tile = streams_ref[0, pl.ds(start, row_tile), :].astype(f32)
        mine = jnp.where(row == local % row_tile, tile, 0.0)
        gate_rows.append(jnp.sum(mine, axis=0, keepdims=True))
    for owner in range(n_devices):
        tail = jnp.zeros((extra, lane_tile), f32)
        for half in range(halves):
            start = (owner * halves + half) * lane_tile
            lanes = slice(start, start + lane_tile)
            rows = slice(half * tok_rows, (half + 1) * tok_rows)
            out_ref[owner, rows, :] = streams_ref[1, :, lanes] * streams_ref[2, :, lanes]
            for var in range(vars_dev):
                tail = jnp.where(place == half * vars_dev + var, gate_rows[var][:, lanes], tail)
        out_ref[owner, halves * tok_rows :, :] = tail.astype(bf16)


def stacked_products(me, offsets, streams, vars_dev, n_devices, extra):
    _, tok_rows, model_width = streams.shape
    halves = model_width // n_devices // lane_tile
    rows_out = halves * tok_rows + extra
    return pl.pallas_call(
        functools.partial(stacked_products_kernel, halves, vars_dev),
        in_specs=[pl.BlockSpec(memory_space=pltpu.SMEM)] * 2 + [whole_spec()],
        out_specs=whole_spec(),
        out_shape=jax.ShapeDtypeStruct((n_devices, rows_out, lane_tile), bf16),
        compiler_params=pltpu.CompilerParams(vmem_limit_bytes=16 * MIB),
        cost_estimate=pl.CostEstimate(
            flops=tok_rows * model_width, bytes_accessed=6 * tok_rows * model_width, transcendentals=0
        ),
        name="stacked_products",
    )(me, offsets, streams)


def stacked_filter_kernel(vars_dev, halves, tok_rows, *refs):
    positions_ref, gain_ref, forward, inverse, unembed, taps, arrived = refs[:7]
    leaving, points, joint, spectrum, packed = refs[7:]
    n_devices = arrived.shape[0]
    body = halves * tok_rows
    n_blocks, double, width = points.shape
    block = double // 2
    per_block = block // tok_rows
    group = 2 if n_blocks % 2 == 0 else 1

    for index in range(n_blocks):
        both = lax.dot_general(
            forward[...],
            taps[:, index * block : (index + 1) * block],
            (((1,), (1,)), ((), ())),
            preferred_element_type=f32,
        )
        spectrum[index] = both[:double] + both[double:]

    for step in range(0, n_blocks, group):
        pieces = []
        for index in range(step, step + group):
            for half in range(halves):
                rows = slice(half * tok_rows, (half + 1) * tok_rows)
                parts = [arrived[index * per_block + m, rows, :] for m in range(per_block)]
                pieces.append(jnp.concatenate(parts, axis=0))
        signal = jnp.concatenate(pieces, axis=1)
        both = jnp.dot(forward[...], signal, preferred_element_type=f32)
        total = both[:double] + both[double:]
        for member in range(group):
            points[step + member] = total[:, member * width : (member + 1) * width]
    multiply_points(points, spectrum, joint)

    for step in range(0, n_blocks, group):
        highs, lows = split_bf16(jnp.concatenate([joint[step + m] for m in range(group)], axis=1))
        both = jnp.dot(inverse[...], highs, preferred_element_type=f32)
        rest = jnp.dot(inverse[:block, :], lows, preferred_element_type=f32)
        result = (both[:block] + both[block:] + rest).astype(bf16)
        for index in range(group):
            for member in range(per_block):
                for half in range(halves):
                    start = index * width + half * lane_tile
                    leaving[
                        (step + index) * per_block + member, half * tok_rows : (half + 1) * tok_rows, :
                    ] = result[member * tok_rows : (member + 1) * tok_rows, start : start + lane_tile]

    length = n_devices * tok_rows
    column = lax.broadcasted_iota(jnp.int32, (positions_ref.shape[0], length), 1)
    picker = (column == positions_ref[...]).astype(f32).astype(bf16)
    tails = arrived[:, body:, :].astype(f32)
    place = lax.broadcasted_iota(jnp.int32, tails.shape, 1)
    raw = None
    squares = None
    for half in range(halves):
        lanes = slice(half * lane_tile, (half + 1) * lane_tile)
        picked = [
            jnp.sum(jnp.where(place == half * vars_dev + var, tails, 0.0), axis=1)
            for var in range(vars_dev)
        ]
        gate_rows = picked[0] if vars_dev == 1 else jnp.concatenate(picked, axis=0)
        filtered = leaving[:, half * tok_rows : (half + 1) * tok_rows, :].reshape(length, lane_tile)
        filtered = jnp.dot(picker, filtered, preferred_element_type=f32)
        rows = (gate_rows * filtered).astype(bf16).astype(f32)
        weighted = (rows * gain_ref[:, lanes]).astype(bf16)
        part = jnp.dot(weighted, unembed[lanes, :], preferred_element_type=f32)
        raw = part if raw is None else raw + part
        squares = rows * rows if squares is None else squares + rows * rows
    pack_scores(raw, squares, 1, vars_dev, packed, n_devices)
    extra = packed.shape[0] // n_devices
    leaving[:, body:, :] = packed[...].reshape(n_devices, extra, lane_tile).astype(bf16)


def stacked_filter(positions, gain_row, tables, arrived, vars_dev, tok_rows, extra):
    width, length = tables[3].shape
    n_devices = arrived.shape[0]
    double = tables[0].shape[0] // 2
    n_blocks = 2 * length // double
    halves = width // lane_tile
    rows_out = halves * tok_rows + extra
    flops = 2 * width * n_blocks * (double * double * 5 // 2 + 4 * n_blocks * double)
    return pl.pallas_call(
        functools.partial(stacked_filter_kernel, vars_dev, halves, tok_rows),
        in_specs=[whole_spec()] * 7,
        out_specs=whole_spec(),
        out_shape=jax.ShapeDtypeStruct((n_devices, rows_out, lane_tile), bf16),
        scratch_shapes=[pltpu.VMEM((n_blocks, double, width), f32)] * 3
        + [pltpu.VMEM((n_devices * extra, lane_tile), f32)],
        compiler_params=pltpu.CompilerParams(vmem_limit_bytes=24 * MIB),
        cost_estimate=pl.CostEstimate(flops=flops, bytes_accessed=8 * MIB, transcendentals=0),
        name="stacked_filter",
    )(positions, gain_row, *tables, arrived)


def stacked_finish_kernel(halves, vars_dev, vocab, ref_ref, alt_ref, gates_ref, back_ref, *refs):
    mixed_ref, scores_ref, results, out_sems = refs
    n_devices, tok_rows, width = results.shape

    def out_copy(owner):
        return pltpu.make_async_copy(
            results.at[owner], mixed_ref.at[:, pl.ds(owner * width, width)], out_sems.at[owner]
        )

    sums = None
    for owner in range(n_devices):
        for half in range(halves):
            lanes = slice(half * lane_tile, (half + 1) * lane_tile)
            start = owner * width + half * lane_tile
            filtered = back_ref[owner, half * tok_rows : (half + 1) * tok_rows, :]
            results[owner, :, lanes] = gates_ref[:, start : start + lane_tile] * filtered
        out_copy(owner).start()
        tail = back_ref[owner, halves * tok_rows :, :].astype(f32)
        sums = tail if sums is None else sums + tail
    model_width = n_devices * width
    scores_ref[...] = final_scores(sums, 1, vars_dev, vocab, model_width, ref_ref, alt_ref)
    for owner in range(n_devices):
        out_copy(owner).wait()


def stacked_finish(ref_ids, alt_ids, gates, back, vocab):
    tok_rows, model_width = gates.shape
    n_devices = back.shape[0]
    vars_dev = ref_ids.shape[0]
    width = model_width // n_devices
    return pl.pallas_call(
        functools.partial(stacked_finish_kernel, width // lane_tile, vars_dev, vocab),
        in_specs=[pl.BlockSpec(memory_space=pltpu.SMEM)] * 2 + [whole_spec()] * 2,
        out_specs=[pl.BlockSpec(memory_space=pl.ANY), whole_spec()],
        out_shape=[
            jax.ShapeDtypeStruct((tok_rows, model_width), bf16),
            jax.ShapeDtypeStruct((vars_dev, 2), f32),
        ],
        scratch_shapes=[
            pltpu.VMEM((n_devices, tok_rows, width), bf16),
            pltpu.SemaphoreType.DMA((n_devices,)),
        ],
        compiler_params=pltpu.CompilerParams(vmem_limit_bytes=16 * MIB),
        cost_estimate=pl.CostEstimate(
            flops=tok_rows * model_width, bytes_accessed=6 * tok_rows * model_width, transcendentals=0
        ),
        name="stacked_finish",
    )(ref_ids, alt_ids, gates, back)


def transposed(blocks):
    return lax.all_to_all(blocks, "seq", split_axis=0, concat_axis=0, tiled=True)


def shards(streams, long_filter, gain, unembed, offsets, ref_ids, alt_ids):
    n_devices = lax.axis_size("seq")
    my_index = lax.axis_index("seq")
    _, tok_rows, model_width = streams.shape
    group_width = model_width // n_devices
    vars_dev = ref_ids.shape[0]
    vocab = unembed.shape[1]
    chunks = max(1, group_width // lane_tile)
    width = group_width // chunks
    block = tok_rows * block_devices(n_devices, tok_rows)
    forward_np, inverse_np = block_tables(block)
    forward, inverse = jnp.asarray(forward_np), jnp.asarray(inverse_np)

    slot = tok_rows // vars_dev
    starts = jnp.arange(vars_dev, dtype=jnp.int32) * slot
    local_rows = starts + lax.dynamic_slice_in_dim(offsets, my_index * vars_dev, vars_dev)
    by_device = offsets.reshape(n_devices, vars_dev)
    positions = by_device + starts[None, :]
    positions += jnp.arange(n_devices, dtype=jnp.int32)[:, None] * tok_rows
    positions = positions.T.reshape(n_devices * vars_dev, 1)
    my_gain = lax.dynamic_slice_in_dim(gain, my_index * group_width, group_width).astype(f32)

    if chunks * lane_tile == group_width:
        me = jnp.reshape(my_index, (1,)).astype(jnp.int32)
        gate_extra = round_up(chunks * vars_dev, half_tile)
        score_extra = round_up(vars_dev * (vocab // lane_tile + 2), half_tile)
        arrived = transposed(stacked_products(me, offsets, streams, vars_dev, n_devices, gate_extra))
        tables = (forward, inverse, unembed, long_filter)
        gain_row = my_gain[None, :]
        leaving = stacked_filter(positions, gain_row, tables, arrived, vars_dev, tok_rows, score_extra)
        back = transposed(leaving)
        mixed, scores = stacked_finish(ref_ids, alt_ids, streams[0], back, vocab)
        return (mixed, scores.T)

    gate_extra = round_up(chunks * vars_dev, row_tile)
    score_extra = round_up(vars_dev * 2 * (vocab // width + 1), row_tile)
    products = make_products(streams, local_rows, n_devices, chunks, gate_extra)
    moved = [lax.all_to_all(part, "seq", split_axis=0, concat_axis=0, tiled=True) for part in products]
    carried = ()
    backs = []
    for chunk in range(chunks):
        mine = slice(chunk * width, (chunk + 1) * width)
        spectrum = filter_spectrum(long_filter[mine], forward, block)
        operands = (
            moved[chunk], spectrum, forward, inverse, positions,
            my_gain[None, mine], unembed[mine],
        )
        if chunk > 0:
            carried = (gates,) + tuple(carried)
        results = filter_chunk(chunk, chunks, vars_dev, tok_rows, score_extra, operands, carried)
        carried = results[1:3]
        if chunk == 0 and chunks > 1:
            gates = results[3]
        backs.append(lax.all_to_all(results[0], "seq", split_axis=0, concat_axis=0, tiled=True))
    mixed, scores = finish(streams, backs, ref_ids, alt_ids, vocab)
    return (mixed, scores.T)


def solution(mesh):
    placed = (
        P(None, ("grp", "seq"), None),
        P("seq", None),
        P(),
        P("seq", None),
        P("grp"),
        P(("grp", "seq")),
        P(("grp", "seq")),
    )
    return jax.shard_map(
        shards,
        mesh=mesh,
        in_specs=placed,
        out_specs=(P(("grp", "seq"), None), P(None, ("grp", "seq"))),
        check_vma=False,
    )
```

```python
import functools
import math

import jax
import jax.numpy as jnp
import numpy as np
from jax import lax
from jax.experimental import pallas as pl
from jax.experimental.pallas import tpu as pltpu
from jax.sharding import PartitionSpec as P

norm_eps = 1e-06
f32 = jnp.float32
bf16 = jnp.bfloat16
row_tile = 16
half_tile = 8
lane_tile = 128
MIB = 1 << 20


def round_up(value, step):
    return -(-value // step) * step


def split_bf16(values):
    high = values.astype(bf16)
    low = (values - high.astype(f32)).astype(bf16)
    return high, low


def block_tables(block):
    turns = (4 * np.arange(block)[:, None] + 1) * np.arange(block)[None, :] % (4 * block)
    theta = turns * (math.pi / (2 * block))
    table = np.concatenate([np.cos(theta), np.sin(theta)], axis=0)
    parts = []
    for matrix in (table, table.T / block):
        high = matrix.astype(bf16)
        low = (matrix - high.astype(np.float64)).astype(bf16)
        parts.append(np.concatenate([high, low], axis=0))
    return parts


def block_devices(n_devices, tok_rows):
    target = math.isqrt(32 * n_devices * tok_rows)
    count = 1
    while n_devices % (2 * count) == 0 and 2 * count * tok_rows <= target:
        count *= 2
    return count


def whole_spec():
    return pl.BlockSpec(memory_space=pltpu.VMEM)


def product_kernel(chunks, width, vars_dev, rows_ref, streams_ref, *out_refs):
    tok_rows = streams_ref.shape[1]
    n_owners = out_refs[0].shape[0]
    extra = out_refs[0].shape[1] - tok_rows
    place = lax.broadcasted_iota(jnp.int32, (extra, tok_rows), 0)
    column = lax.broadcasted_iota(jnp.int32, (extra, tok_rows), 1)
    for owner in range(n_owners):
        gates = jnp.zeros((extra, width), f32)
        for chunk in range(chunks):
            lanes = pl.ds((owner * chunks + chunk) * width, width)
            left = streams_ref[1, :, lanes].astype(f32)
            right = streams_ref[2, :, lanes].astype(f32)
            out_refs[chunk][owner, :tok_rows, :] = (left * right).astype(bf16)
            picker = jnp.zeros((extra, tok_rows), jnp.bool_)
            for var in range(vars_dev):
                picker |= (place == chunk * vars_dev + var) & (column == rows_ref[var])
            gates += jnp.dot(
                picker.astype(f32).astype(bf16),
                streams_ref[0, :, lanes],
                preferred_element_type=f32,
            )
        out_refs[0][owner, tok_rows:, :] = gates.astype(bf16)


def make_products(streams, local_rows, n_devices, chunks, extra):
    _, tok_rows, model_width = streams.shape
    vars_dev = local_rows.shape[0]
    group_width = model_width // n_devices
    width = group_width // chunks
    owners = max(1, n_devices // 4)
    while owners * group_width % lane_tile:
        owners *= 2
    steps = n_devices // owners
    rows_out = [tok_rows + extra] + [tok_rows] * (chunks - 1)
    return pl.pallas_call(
        functools.partial(product_kernel, chunks, width, vars_dev),
        grid=(steps,),
        in_specs=[
            pl.BlockSpec(memory_space=pltpu.SMEM),
            pl.BlockSpec((3, tok_rows, owners * group_width), lambda i: (0, 0, i)),
        ],
        out_specs=[pl.BlockSpec((owners, rows, width), lambda i: (i, 0, 0)) for rows in rows_out],
        out_shape=[jax.ShapeDtypeStruct((n_devices, rows, width), bf16) for rows in rows_out],
        compiler_params=pltpu.CompilerParams(vmem_limit_bytes=24 * MIB),
        name="products",
    )(local_rows, streams)


def spectrum_kernel(block, filter_ref, forward_ref, out_ref):
    n_blocks = out_ref.shape[0]
    for index in range(n_blocks):
        taps = filter_ref[:, index * block : (index + 1) * block]
        both = lax.dot_general(
            forward_ref[...], taps, (((1,), (1,)), ((), ())), preferred_element_type=f32
        )
        out_ref[index] = both[: 2 * block] + both[2 * block :]


def filter_spectrum(taps, forward, block):
    width, length = taps.shape
    n_blocks = length // block
    return pl.pallas_call(
        functools.partial(spectrum_kernel, block),
        in_specs=[whole_spec()] * 2,
        out_specs=whole_spec(),
        out_shape=jax.ShapeDtypeStruct((n_blocks, 2 * block, width), f32),
        compiler_params=pltpu.CompilerParams(vmem_limit_bytes=40 * MIB),
        cost_estimate=pl.CostEstimate(
            flops=8 * block * length * width, bytes_accessed=4 * MIB, transcendentals=0
        ),
        name="filter_spectrum",
    )(taps, forward)


def multiply_points(points, spectrum_ref, joint):
    n_blocks, double, width = points.shape
    block = double // 2
    lanes_step = min(width, lane_tile)

    def multiply_step(step, carry):
        start = pl.multiple_of(step * half_tile, half_tile)
        upper = pl.ds(start, half_tile)
        lower = pl.ds(pl.multiple_of(block + start, half_tile), half_tile)
        for first in range(0, width, lanes_step):
            lanes = slice(first, first + lanes_step)
            signal = [(points[k, upper, lanes], points[k, lower, lanes]) for k in range(n_blocks)]
            taps = [
                (spectrum_ref[k, upper, lanes], spectrum_ref[k, lower, lanes]) for k in range(n_blocks)
            ]
            before_re = jnp.zeros((half_tile, lanes_step), f32)
            before_im = jnp.zeros((half_tile, lanes_step), f32)
            for total in range(n_blocks):
                sum_re = jnp.zeros((half_tile, lanes_step), f32)
                sum_im = jnp.zeros((half_tile, lanes_step), f32)
                for delay in range(total + 1):
                    a_re, a_im = signal[total - delay]
                    b_re, b_im = taps[delay]
                    sum_re += a_re * b_re - a_im * b_im
                    sum_im += a_re * b_im + a_im * b_re
                joint[total, upper, lanes] = sum_re + before_im
                joint[total, lower, lanes] = sum_im - before_re
                before_re, before_im = sum_re, sum_im
        return carry

    lax.fori_loop(0, block // half_tile, multiply_step, 0)


def convolve(chunk_ref, spectrum_ref, forward_ref, inverse_ref, out_ref, points, tok_rows):
    n_blocks, double, width = points.shape
    block = double // 2
    per_block = block // tok_rows
    group = max(1, min(n_blocks, 256 // width)) if width % lane_tile == 0 else 1

    def forward_step(step, carry):
        pieces = []
        for member in range(group):
            start = (step * group + member) * per_block
            rows = chunk_ref[pl.ds(start, per_block), :tok_rows, :]
            pieces.append(rows.reshape(block, width))
        signal = pieces[0] if group == 1 else jnp.concatenate(pieces, axis=1)
        both = jnp.dot(forward_ref[...], signal, preferred_element_type=f32)
        total = both[:double] + both[double:]
        for member in range(group):
            points[step * group + member] = total[:, member * width : (member + 1) * width]
        return carry

    lax.fori_loop(0, n_blocks // group, forward_step, 0)

    multiply_points(points, spectrum_ref, points)

    def inverse_step(step, carry):
        first = step * group
        pieces = [points[first + member] for member in range(group)]
        highs, lows = split_bf16(pieces[0] if group == 1 else jnp.concatenate(pieces, axis=1))
        both = jnp.dot(inverse_ref[...], highs, preferred_element_type=f32)
        rest = jnp.dot(inverse_ref[:block, :], lows, preferred_element_type=f32)
        result = (both[:block] + both[block:] + rest).astype(bf16)
        for member in range(group):
            piece = result[:, member * width : (member + 1) * width]
            out_ref[pl.ds((first + member) * per_block, per_block), :tok_rows, :] = piece.reshape(
                per_block, tok_rows, width
            )
        return carry

    lax.fori_loop(0, n_blocks // group, inverse_step, 0)


def score_rows(index, vars_dev, tok_rows, positions, gate_block, out_ref, gain_row, unembed):
    n_devices, extra, width = gate_block.shape
    gates = gate_block.astype(f32)
    place = lax.broadcasted_iota(jnp.int32, (n_devices, extra, width), 1)
    picked = [
        jnp.sum(jnp.where(place == index * vars_dev + var, gates, 0.0), axis=1)
        for var in range(vars_dev)
    ]
    gate_rows = picked[0] if vars_dev == 1 else jnp.concatenate(picked, axis=0)
    length = n_devices * tok_rows
    column = lax.broadcasted_iota(jnp.int32, (positions.shape[0], length), 1)
    picker = (column == positions).astype(f32).astype(bf16)
    filtered = jnp.dot(
        picker, out_ref[:, :tok_rows, :].reshape(length, width), preferred_element_type=f32
    )
    rows = (gate_rows * filtered).astype(bf16).astype(f32)
    weighted = (rows * gain_row).astype(bf16)
    return jnp.dot(weighted, unembed, preferred_element_type=f32), rows * rows


def pack_scores(raw, squares, raw_parts, vars_dev, packed, n_devices):
    total, width = packed.shape
    extra = total // n_devices
    per_row = raw.shape[1] // width
    count = raw_parts * per_row + 2
    packed[...] = jnp.zeros_like(packed)
    for var in range(vars_dev):
        mine = slice(var * n_devices, (var + 1) * n_devices)
        pieces = [raw[mine, r * width : (r + 1) * width] for r in range(per_row)]
        rounded = [piece.astype(bf16).astype(f32) for piece in pieces]
        rows = rounded + [piece - high for piece, high in zip(pieces, rounded)][: (raw_parts - 1) * per_row]
        high = squares[mine].astype(bf16).astype(f32)
        rows += [high, squares[mine] - high]
        for row, piece in enumerate(rows):
            packed[pl.ds(var * count + row, n_devices, stride=extra), :] = piece


def chunk_kernel(index, chunks, vars_dev, tok_rows, *refs):
    refs = list(refs)
    chunk_ref, spectrum_ref, forward_ref, inverse_ref = refs[:4]
    positions_ref, gain_ref, unembed_ref = refs[4:7]
    refs = refs[7:]
    first, last = index == 0, index == chunks - 1
    gates_ref = None if first else refs.pop(0)
    raw_before, square_before = (None, None) if first else (refs.pop(0), refs.pop(0))
    out_ref = refs.pop(0)
    raw_out, square_out = (None, None) if last else (refs.pop(0), refs.pop(0))
    gates_out = refs.pop(0) if first and not last else None
    points = refs[0]
    convolve(chunk_ref, spectrum_ref, forward_ref, inverse_ref, out_ref, points, tok_rows)
    gate_block = chunk_ref[:, tok_rows:, :] if first else gates_ref[...]
    raw, squares = score_rows(
        index, vars_dev, tok_rows, positions_ref[...], gate_block, out_ref, gain_ref[...], unembed_ref[...]
    )
    if not first:
        raw = raw + raw_before[...]
        squares = squares + square_before[...]
    if gates_out is not None:
        gates_out[...] = gate_block
    if not last:
        raw_out[...] = raw
        square_out[...] = squares
        return
    packed = refs[1]
    n_devices, _, width = out_ref.shape
    extra = out_ref.shape[1] - tok_rows
    pack_scores(raw, squares, 2, vars_dev, packed, n_devices)
    out_ref[:, tok_rows:, :] = packed[...].reshape(n_devices, extra, width).astype(bf16)


def filter_chunk(index, chunks, vars_dev, tok_rows, extra, operands, carried):
    moved, spectrum = operands[:2]
    n_devices, _, width = moved.shape
    n_blocks, double, _ = spectrum.shape
    vocab = operands[6].shape[1]
    n_vars = operands[4].shape[0]
    first, last = index == 0, index == chunks - 1
    rows_out = tok_rows + (extra if last else 0)
    out_shape = [jax.ShapeDtypeStruct((n_devices, rows_out, width), bf16)]
    scratch = [pltpu.VMEM((n_blocks, double, width), f32)]
    if last:
        scratch.append(pltpu.VMEM((n_devices * extra, width), f32))
    else:
        out_shape.append(jax.ShapeDtypeStruct((n_vars, vocab), f32))
        out_shape.append(jax.ShapeDtypeStruct((n_vars, width), f32))
    if first and not last:
        out_shape.append(jax.ShapeDtypeStruct((n_devices, moved.shape[1] - tok_rows, width), bf16))
    flops = 2 * width * n_blocks * (double * double * 5 // 2 + 4 * n_blocks * double)
    return pl.pallas_call(
        functools.partial(chunk_kernel, index, chunks, vars_dev, tok_rows),
        in_specs=[whole_spec()] * (len(operands) + len(carried)),
        out_specs=[whole_spec()] * len(out_shape),
        out_shape=out_shape,
        scratch_shapes=scratch,
        compiler_params=pltpu.CompilerParams(vmem_limit_bytes=(20 if n_blocks <= 8 else 58) * MIB),
        cost_estimate=pl.CostEstimate(flops=flops, bytes_accessed=8 * MIB, transcendentals=0),
        name="filter_chunk",
    )(*operands, *carried)


def final_scores(sums, raw_parts, vars_dev, vocab, model_width, ref_ref, alt_ref):
    width = sums.shape[1]
    per_row = vocab // width
    count = raw_parts * per_row + 2
    ids = lax.broadcasted_iota(jnp.int32, (per_row, width), 0) * width
    ids += lax.broadcasted_iota(jnp.int32, (per_row, width), 1)
    row = lax.broadcasted_iota(jnp.int32, (vars_dev, 2), 0)
    column = lax.broadcasted_iota(jnp.int32, (vars_dev, 2), 1)
    scores = jnp.zeros((vars_dev, 2), f32)

    def whole_sum(values):
        return jnp.sum(jnp.sum(values, axis=1, keepdims=True), axis=0, keepdims=True)

    for var in range(vars_dev):
        base = var * count
        raw = sums[base : base + per_row, :]
        if raw_parts == 2:
            raw = raw + sums[base + per_row : base + 2 * per_row, :]
        square = whole_sum(sums[base + count - 2 : base + count, :])
        logits = raw * lax.rsqrt(square / model_width + norm_eps)
        largest = jnp.max(jnp.max(logits, axis=1, keepdims=True), axis=0, keepdims=True)
        log_total = largest + jnp.log(whole_sum(jnp.exp(logits - largest)))
        ref_logit = whole_sum(jnp.where(ids == ref_ref[var], logits, 0.0))
        alt_logit = whole_sum(jnp.where(ids == alt_ref[var], logits, 0.0))
        pair = jnp.where(column == 0, ref_logit - log_total, alt_logit - ref_logit)
        scores = jnp.where(row == var, pair, scores)
    return scores


def finish_kernel(chunks, vars_dev, vocab, ref_ref, alt_ref, streams_ref, *refs):
    back_refs, mixed_ref, scores_ref, sums = refs[:chunks], refs[chunks], refs[chunks + 1], refs[chunks + 2]
    tok_rows = streams_ref.shape[1]
    owners, _, width = back_refs[0].shape
    step = pl.program_id(0)
    for owner in range(owners):
        for chunk in range(chunks):
            lanes = pl.ds((owner * chunks + chunk) * width, width)
            gate = streams_ref[0, :, lanes].astype(f32)
            filtered = back_refs[chunk][owner, :tok_rows, :].astype(f32)
            mixed_ref[:, lanes] = (gate * filtered).astype(bf16)
    part = jnp.sum(back_refs[-1][:, tok_rows:, :].astype(f32), axis=0)

    @pl.when(step == 0)
    def _():
        sums[...] = part

    @pl.when(step > 0)
    def _():
        sums[...] += part

    @pl.when(step == pl.num_programs(0) - 1)
    def _():
        model_width = pl.num_programs(0) * owners * chunks * width
        scores_ref[...] = final_scores(sums[...], 2, vars_dev, vocab, model_width, ref_ref, alt_ref)


def finish(streams, backs, ref_ids, alt_ids, vocab):
    _, tok_rows, model_width = streams.shape
    chunks = len(backs)
    n_devices, _, width = backs[0].shape
    vars_dev = ref_ids.shape[0]
    owners = max(1, n_devices // 4)
    while owners * chunks * width % lane_tile:
        owners *= 2
    extra = backs[-1].shape[1] - tok_rows
    return pl.pallas_call(
        functools.partial(finish_kernel, chunks, vars_dev, vocab),
        grid=(n_devices // owners,),
        in_specs=[
            pl.BlockSpec(memory_space=pltpu.SMEM),
            pl.BlockSpec(memory_space=pltpu.SMEM),
            pl.BlockSpec((1, tok_rows, owners * chunks * width), lambda i: (0, 0, i)),
        ]
        + [pl.BlockSpec((owners, back.shape[1], width), lambda i: (i, 0, 0)) for back in backs],
        out_specs=[
            pl.BlockSpec((tok_rows, owners * chunks * width), lambda i: (0, i)),
            pl.BlockSpec((vars_dev, 2), lambda i: (0, 0)),
        ],
        out_shape=[
            jax.ShapeDtypeStruct((tok_rows, model_width), bf16),
            jax.ShapeDtypeStruct((vars_dev, 2), f32),
        ],
        scratch_shapes=[pltpu.VMEM((extra, width), f32)],
        compiler_params=pltpu.CompilerParams(vmem_limit_bytes=24 * MIB),
        name="finish",
    )(ref_ids, alt_ids, streams, *backs)

def half_order(n_devices):
    half = n_devices // 2
    return [device for pair in zip(range(half), range(half, n_devices)) for device in pair]


def stacked_products_kernel(halves, vars_dev, order, me_ref, offsets_ref, streams_ref, out_ref, *scratch):
    gates, pairs, built, gate_sem, pair_sems, out_sems = scratch
    n_devices = len(order)
    pieces, _, tok_rows, lanes_each = pairs.shape
    body = halves * tok_rows
    width = halves * lane_tile
    owners = lanes_each // width
    me = me_ref[0]
    slot = tok_rows // vars_dev
    rank_of = {device: rank for rank, device in enumerate(order)}

    def pair_copy(piece):
        lanes = pl.ds(piece * lanes_each, lanes_each)
        return pltpu.make_async_copy(
            streams_ref.at[pl.ds(1, 2), :, lanes], pairs.at[piece], pair_sems.at[piece]
        )

    def out_copy(rank):
        return pltpu.make_async_copy(built.at[rank], out_ref.at[rank], out_sems.at[rank])

    gate_copy = pltpu.make_async_copy(streams_ref.at[0], gates, gate_sem.at[0])
    gate_copy.start()
    for piece in range(pieces):
        pair_copy(piece).start()
    extra = built.shape[1] - body
    row = lax.broadcasted_iota(jnp.int32, (row_tile, gates.shape[1]), 0)
    place = lax.broadcasted_iota(jnp.int32, (extra, lane_tile), 0)
    gate_copy.wait()
    gate_rows = []
    for var in range(vars_dev):
        local = var * slot + offsets_ref[me * vars_dev + var]
        start = pl.multiple_of(local // row_tile * row_tile, row_tile)
        tile = gates[pl.ds(start, row_tile), :].astype(f32)
        mine = jnp.where(row == local % row_tile, tile, 0.0)
        gate_rows.append(jnp.sum(mine, axis=0, keepdims=True))
    for piece in range(pieces):
        pair_copy(piece).wait()
        for member in range(owners):
            owner = piece * owners + member
            rank = rank_of[owner]
            tail = jnp.zeros((extra, lane_tile), f32)
            for half in range(halves):
                lanes = slice(member * width + half * lane_tile, member * width + (half + 1) * lane_tile)
                rows = slice(half * tok_rows, (half + 1) * tok_rows)
                built[rank, rows, :] = pairs[piece, 0, :, lanes] * pairs[piece, 1, :, lanes]
                start = owner * width + half * lane_tile
                for var in range(vars_dev):
                    mine = gate_rows[var][:, start : start + lane_tile]
                    tail = jnp.where(place == half * vars_dev + var, mine, tail)
            built[rank, body:, :] = tail.astype(bf16)
            out_copy(rank).start()
    for rank in range(n_devices):
        out_copy(rank).wait()


def stacked_products(me, offsets, streams, vars_dev, order, extra):
    _, tok_rows, model_width = streams.shape
    n_devices = len(order)
    halves = model_width // n_devices // lane_tile
    rows_out = halves * tok_rows + extra
    pieces = math.gcd(n_devices, 4)
    return pl.pallas_call(
        functools.partial(stacked_products_kernel, halves, vars_dev, order),
        in_specs=[pl.BlockSpec(memory_space=pltpu.SMEM)] * 2 + [pl.BlockSpec(memory_space=pl.ANY)],
        out_specs=pl.BlockSpec(memory_space=pl.ANY),
        out_shape=jax.ShapeDtypeStruct((n_devices, rows_out, lane_tile), bf16),
        scratch_shapes=[
            pltpu.VMEM((tok_rows, model_width), bf16),
            pltpu.VMEM((pieces, 2, tok_rows, model_width // pieces), bf16),
            pltpu.VMEM((n_devices, rows_out, lane_tile), bf16),
            pltpu.SemaphoreType.DMA((1,)),
            pltpu.SemaphoreType.DMA((pieces,)),
            pltpu.SemaphoreType.DMA((n_devices,)),
        ],
        compiler_params=pltpu.CompilerParams(vmem_limit_bytes=60 * MIB),
        cost_estimate=pl.CostEstimate(
            flops=tok_rows * model_width, bytes_accessed=6 * tok_rows * model_width, transcendentals=0
        ),
        name="stacked_products",
    )(me, offsets, streams)


def stacked_filter_kernel(vars_dev, halves, tok_rows, order, *refs):
    positions_ref, gain_ref, forward, inverse, unembed, taps, arrived = refs[:7]
    leaving, points, joint, spectrum, packed = refs[7:]
    n_devices = arrived.shape[0]
    rank_of = {device: rank for rank, device in enumerate(order)}
    body = halves * tok_rows
    n_blocks, double, width = points.shape
    block = double // 2
    per_block = block // tok_rows
    group = 2 if n_blocks % 2 == 0 else 1

    for index in range(n_blocks):
        part = taps[:, index * block : (index + 1) * block]
        spectrum[index] = lax.dot_general(
            forward[...],
            jnp.concatenate([part, part], axis=1),
            (((1,), (1,)), ((), ())),
            preferred_element_type=f32,
        )

    for step in range(0, n_blocks, group):
        pieces = []
        for index in range(step, step + group):
            for half in range(halves):
                rows = slice(half * tok_rows, (half + 1) * tok_rows)
                parts = [arrived[rank_of[index * per_block + m], rows, :] for m in range(per_block)]
                pieces.append(jnp.concatenate(parts + parts, axis=0))
        signal = jnp.concatenate(pieces, axis=1)
        total = jnp.dot(forward[...], signal, preferred_element_type=f32)
        for member in range(group):
            points[step + member] = total[:, member * width : (member + 1) * width]
    multiply_points(points, spectrum, joint)

    for step in range(0, n_blocks, group):
        highs, lows = split_bf16(jnp.concatenate([joint[step + m] for m in range(group)], axis=1))
        terms = jnp.concatenate([highs, highs, lows], axis=0)
        result = jnp.dot(inverse[...], terms, preferred_element_type=f32).astype(bf16)
        for index in range(group):
            for member in range(per_block):
                rank = rank_of[(step + index) * per_block + member]
                for half in range(halves):
                    start = index * width + half * lane_tile
                    leaving[rank, half * tok_rows : (half + 1) * tok_rows, :] = result[
                        member * tok_rows : (member + 1) * tok_rows, start : start + lane_tile
                    ]

    length = n_devices * tok_rows
    column = lax.broadcasted_iota(jnp.int32, (positions_ref.shape[0], length), 1)
    picker = (column == positions_ref[...]).astype(f32).astype(bf16)
    tails = arrived[:, body:, :].astype(f32)
    place = lax.broadcasted_iota(jnp.int32, tails.shape, 1)
    raw = None
    squares = None
    for half in range(halves):
        lanes = slice(half * lane_tile, (half + 1) * lane_tile)
        picked = [
            jnp.sum(jnp.where(place == half * vars_dev + var, tails, 0.0), axis=1)
            for var in range(vars_dev)
        ]
        gate_rows = picked[0] if vars_dev == 1 else jnp.concatenate(picked, axis=0)
        filtered = leaving[:, half * tok_rows : (half + 1) * tok_rows, :].reshape(length, lane_tile)
        filtered = jnp.dot(picker, filtered, preferred_element_type=f32)
        rows = (gate_rows * filtered).astype(bf16).astype(f32)
        weighted = (rows * gain_ref[:, lanes]).astype(bf16)
        part = jnp.dot(weighted, unembed[lanes, :], preferred_element_type=f32)
        raw = part if raw is None else raw + part
        squares = rows * rows if squares is None else squares + rows * rows
    pack_scores(raw, squares, 1, vars_dev, packed, n_devices)
    extra = packed.shape[0] // n_devices
    leaving[:, body:, :] = packed[...].reshape(n_devices, extra, lane_tile).astype(bf16)


def stacked_filter(positions, gain_row, tables, arrived, vars_dev, tok_rows, order, extra):
    width, length = tables[3].shape
    n_devices = arrived.shape[0]
    double = tables[0].shape[0]
    n_blocks = 2 * length // double
    halves = width // lane_tile
    rows_out = halves * tok_rows + extra
    flops = 2 * width * n_blocks * (double * double * 5 // 2 + 4 * n_blocks * double)
    return pl.pallas_call(
        functools.partial(stacked_filter_kernel, vars_dev, halves, tok_rows, order),
        in_specs=[whole_spec()] * 7,
        out_specs=whole_spec(),
        out_shape=jax.ShapeDtypeStruct((n_devices, rows_out, lane_tile), bf16),
        scratch_shapes=[pltpu.VMEM((n_blocks, double, width), f32)] * 3
        + [pltpu.VMEM((n_devices * extra, lane_tile), f32)],
        compiler_params=pltpu.CompilerParams(vmem_limit_bytes=24 * MIB),
        cost_estimate=pl.CostEstimate(flops=flops, bytes_accessed=8 * MIB, transcendentals=0),
        name="stacked_filter",
    )(positions, gain_row, *tables, arrived)


def stacked_finish_kernel(halves, vars_dev, vocab, order, ref_ref, alt_ref, gates_ref, back_ref, *refs):
    mixed_ref, scores_ref, results, out_sems = refs
    n_devices, tok_rows, width = results.shape

    def out_copy(owner):
        return pltpu.make_async_copy(
            results.at[owner], mixed_ref.at[:, pl.ds(owner * width, width)], out_sems.at[owner]
        )

    sums = None
    for rank, owner in enumerate(order):
        for half in range(halves):
            lanes = slice(half * lane_tile, (half + 1) * lane_tile)
            start = owner * width + half * lane_tile
            filtered = back_ref[rank, half * tok_rows : (half + 1) * tok_rows, :]
            results[owner, :, lanes] = gates_ref[:, start : start + lane_tile] * filtered
        out_copy(owner).start()
        tail = back_ref[rank, halves * tok_rows :, :].astype(f32)
        sums = tail if sums is None else sums + tail
    model_width = n_devices * width
    scores_ref[...] = final_scores(sums, 1, vars_dev, vocab, model_width, ref_ref, alt_ref)
    for owner in range(n_devices):
        out_copy(owner).wait()


def stacked_finish(ref_ids, alt_ids, gates, back, vocab, order):
    tok_rows, model_width = gates.shape
    n_devices = back.shape[0]
    vars_dev = ref_ids.shape[0]
    width = model_width // n_devices
    return pl.pallas_call(
        functools.partial(stacked_finish_kernel, width // lane_tile, vars_dev, vocab, order),
        in_specs=[pl.BlockSpec(memory_space=pltpu.SMEM)] * 2 + [whole_spec()] * 2,
        out_specs=[pl.BlockSpec(memory_space=pl.ANY), whole_spec()],
        out_shape=[
            jax.ShapeDtypeStruct((tok_rows, model_width), bf16),
            jax.ShapeDtypeStruct((vars_dev, 2), f32),
        ],
        scratch_shapes=[
            pltpu.VMEM((n_devices, tok_rows, width), bf16),
            pltpu.SemaphoreType.DMA((n_devices,)),
        ],
        compiler_params=pltpu.CompilerParams(vmem_limit_bytes=16 * MIB),
        cost_estimate=pl.CostEstimate(
            flops=tok_rows * model_width, bytes_accessed=6 * tok_rows * model_width, transcendentals=0
        ),
        name="stacked_finish",
    )(ref_ids, alt_ids, gates, back)


def transposed(blocks, order):
    return lax.all_to_all(
        blocks, "seq", split_axis=0, concat_axis=0, axis_index_groups=[order], tiled=True
    )


def shards(streams, long_filter, gain, unembed, offsets, ref_ids, alt_ids):
    n_devices = lax.axis_size("seq")
    my_index = lax.axis_index("seq")
    _, tok_rows, model_width = streams.shape
    group_width = model_width // n_devices
    vars_dev = ref_ids.shape[0]
    vocab = unembed.shape[1]
    chunks = max(1, group_width // lane_tile)
    width = group_width // chunks
    block = tok_rows * block_devices(n_devices, tok_rows)
    forward_np, inverse_np = block_tables(block)
    forward, inverse = jnp.asarray(forward_np), jnp.asarray(inverse_np)

    slot = tok_rows // vars_dev
    starts = jnp.arange(vars_dev, dtype=jnp.int32) * slot
    local_rows = starts + lax.dynamic_slice_in_dim(offsets, my_index * vars_dev, vars_dev)
    by_device = offsets.reshape(n_devices, vars_dev)
    positions = by_device + starts[None, :]
    positions += jnp.arange(n_devices, dtype=jnp.int32)[:, None] * tok_rows
    positions = positions.T.reshape(n_devices * vars_dev, 1)
    my_gain = lax.dynamic_slice_in_dim(gain, my_index * group_width, group_width).astype(f32)

    if chunks * lane_tile == group_width and n_devices % 2 == 0:
        me = jnp.reshape(my_index, (1,)).astype(jnp.int32)
        gate_extra = round_up(chunks * vars_dev, half_tile)
        score_extra = round_up(vars_dev * (vocab // lane_tile + 2), half_tile)
        order = half_order(n_devices)
        arrived = transposed(stacked_products(me, offsets, streams, vars_dev, order, gate_extra), order)
        joined_forward = jnp.asarray(np.concatenate(np.split(forward_np, 2, axis=0), axis=1))
        joined_inverse = np.split(inverse_np, 2, axis=0)
        joined_inverse = jnp.asarray(np.concatenate(joined_inverse + joined_inverse[:1], axis=1))
        tables = (joined_forward, joined_inverse, unembed, long_filter)
        places = by_device.reshape(2, n_devices // 2, vars_dev).transpose(1, 0, 2)
        places = places.reshape(n_devices, vars_dev) + starts[None, :]
        places += jnp.arange(n_devices, dtype=jnp.int32)[:, None] * tok_rows
        places = places.T.reshape(n_devices * vars_dev, 1)
        leaving = stacked_filter(
            places, my_gain[None, :], tables, arrived, vars_dev, tok_rows, order, score_extra
        )
        back = transposed(leaving, order)
        mixed, scores = stacked_finish(ref_ids, alt_ids, streams[0], back, vocab, order)
        return (mixed, scores.T)

    gate_extra = round_up(chunks * vars_dev, row_tile)
    score_extra = round_up(vars_dev * 2 * (vocab // width + 1), row_tile)
    products = make_products(streams, local_rows, n_devices, chunks, gate_extra)
    moved = [lax.all_to_all(part, "seq", split_axis=0, concat_axis=0, tiled=True) for part in products]
    carried = ()
    backs = []
    for chunk in range(chunks):
        mine = slice(chunk * width, (chunk + 1) * width)
        spectrum = filter_spectrum(long_filter[mine], forward, block)
        operands = (
            moved[chunk], spectrum, forward, inverse, positions,
            my_gain[None, mine], unembed[mine],
        )
        if chunk > 0:
            carried = (gates,) + tuple(carried)
        results = filter_chunk(chunk, chunks, vars_dev, tok_rows, score_extra, operands, carried)
        carried = results[1:3]
        if chunk == 0 and chunks > 1:
            gates = results[3]
        backs.append(lax.all_to_all(results[0], "seq", split_axis=0, concat_axis=0, tiled=True))
    mixed, scores = finish(streams, backs, ref_ids, alt_ids, vocab)
    return (mixed, scores.T)


def solution(mesh):
    placed = (
        P(None, ("grp", "seq"), None),
        P("seq", None),
        P(),
        P("seq", None),
        P("grp"),
        P(("grp", "seq")),
        P(("grp", "seq")),
    )
    return jax.shard_map(
        shards,
        mesh=mesh,
        in_specs=placed,
        out_specs=(P(("grp", "seq"), None), P(None, ("grp", "seq"))),
        check_vma=False,
    )
```

```python
import functools
import math

import jax
import jax.numpy as jnp
import numpy as np
from jax import lax
from jax.experimental import pallas as pl
from jax.experimental.pallas import tpu as pltpu
from jax.sharding import PartitionSpec as P

norm_eps = 1e-06
f32 = jnp.float32
bf16 = jnp.bfloat16
row_tile = 16
half_tile = 8
lane_tile = 128
MIB = 1 << 20


def round_up(value, step):
    return -(-value // step) * step


def split_bf16(values):
    high = values.astype(bf16)
    low = (values - high.astype(f32)).astype(bf16)
    return high, low


def block_tables(block):
    turns = (4 * np.arange(block)[:, None] + 1) * np.arange(block)[None, :] % (4 * block)
    theta = turns * (math.pi / (2 * block))
    table = np.concatenate([np.cos(theta), np.sin(theta)], axis=0)
    parts = []
    for matrix in (table, table.T / block):
        high = matrix.astype(bf16)
        low = (matrix - high.astype(np.float64)).astype(bf16)
        parts.append(np.concatenate([high, low], axis=0))
    return parts


def block_devices(n_devices, tok_rows):
    target = math.isqrt(32 * n_devices * tok_rows)
    count = 1
    while n_devices % (2 * count) == 0 and 2 * count * tok_rows <= target:
        count *= 2
    return count


def whole_spec():
    return pl.BlockSpec(memory_space=pltpu.VMEM)


def product_kernel(chunks, width, vars_dev, rows_ref, streams_ref, *out_refs):
    tok_rows = streams_ref.shape[1]
    n_owners = out_refs[0].shape[0]
    extra = out_refs[0].shape[1] - tok_rows
    place = lax.broadcasted_iota(jnp.int32, (extra, tok_rows), 0)
    column = lax.broadcasted_iota(jnp.int32, (extra, tok_rows), 1)
    for owner in range(n_owners):
        gates = jnp.zeros((extra, width), f32)
        for chunk in range(chunks):
            lanes = pl.ds((owner * chunks + chunk) * width, width)
            left = streams_ref[1, :, lanes].astype(f32)
            right = streams_ref[2, :, lanes].astype(f32)
            out_refs[chunk][owner, :tok_rows, :] = (left * right).astype(bf16)
            picker = jnp.zeros((extra, tok_rows), jnp.bool_)
            for var in range(vars_dev):
                picker |= (place == chunk * vars_dev + var) & (column == rows_ref[var])
            gates += jnp.dot(
                picker.astype(f32).astype(bf16),
                streams_ref[0, :, lanes],
                preferred_element_type=f32,
            )
        out_refs[0][owner, tok_rows:, :] = gates.astype(bf16)


def make_products(streams, local_rows, n_devices, chunks, extra):
    _, tok_rows, model_width = streams.shape
    vars_dev = local_rows.shape[0]
    group_width = model_width // n_devices
    width = group_width // chunks
    owners = max(1, n_devices // 4)
    while owners * group_width % lane_tile:
        owners *= 2
    steps = n_devices // owners
    rows_out = [tok_rows + extra] + [tok_rows] * (chunks - 1)
    return pl.pallas_call(
        functools.partial(product_kernel, chunks, width, vars_dev),
        grid=(steps,),
        in_specs=[
            pl.BlockSpec(memory_space=pltpu.SMEM),
            pl.BlockSpec((3, tok_rows, owners * group_width), lambda i: (0, 0, i)),
        ],
        out_specs=[pl.BlockSpec((owners, rows, width), lambda i: (i, 0, 0)) for rows in rows_out],
        out_shape=[jax.ShapeDtypeStruct((n_devices, rows, width), bf16) for rows in rows_out],
        compiler_params=pltpu.CompilerParams(vmem_limit_bytes=24 * MIB),
        name="products",
    )(local_rows, streams)


def spectrum_kernel(block, filter_ref, forward_ref, out_ref):
    n_blocks = out_ref.shape[0]
    for index in range(n_blocks):
        taps = filter_ref[:, index * block : (index + 1) * block]
        both = lax.dot_general(
            forward_ref[...], taps, (((1,), (1,)), ((), ())), preferred_element_type=f32
        )
        out_ref[index] = both[: 2 * block] + both[2 * block :]


def filter_spectrum(taps, forward, block):
    width, length = taps.shape
    n_blocks = length // block
    return pl.pallas_call(
        functools.partial(spectrum_kernel, block),
        in_specs=[whole_spec()] * 2,
        out_specs=whole_spec(),
        out_shape=jax.ShapeDtypeStruct((n_blocks, 2 * block, width), f32),
        compiler_params=pltpu.CompilerParams(vmem_limit_bytes=40 * MIB),
        cost_estimate=pl.CostEstimate(
            flops=8 * block * length * width, bytes_accessed=4 * MIB, transcendentals=0
        ),
        name="filter_spectrum",
    )(taps, forward)


def multiply_points(points, spectrum_ref, joint):
    n_blocks, double, width = points.shape
    block = double // 2
    lanes_step = min(width, lane_tile)

    def multiply_step(step, carry):
        start = pl.multiple_of(step * half_tile, half_tile)
        upper = pl.ds(start, half_tile)
        lower = pl.ds(pl.multiple_of(block + start, half_tile), half_tile)
        for first in range(0, width, lanes_step):
            lanes = slice(first, first + lanes_step)
            signal = [(points[k, upper, lanes], points[k, lower, lanes]) for k in range(n_blocks)]
            taps = [
                (spectrum_ref[k, upper, lanes], spectrum_ref[k, lower, lanes]) for k in range(n_blocks)
            ]
            before_re = jnp.zeros((half_tile, lanes_step), f32)
            before_im = jnp.zeros((half_tile, lanes_step), f32)
            for total in range(n_blocks):
                sum_re = jnp.zeros((half_tile, lanes_step), f32)
                sum_im = jnp.zeros((half_tile, lanes_step), f32)
                for delay in range(total + 1):
                    a_re, a_im = signal[total - delay]
                    b_re, b_im = taps[delay]
                    sum_re += a_re * b_re - a_im * b_im
                    sum_im += a_re * b_im + a_im * b_re
                joint[total, upper, lanes] = sum_re + before_im
                joint[total, lower, lanes] = sum_im - before_re
                before_re, before_im = sum_re, sum_im
        return carry

    lax.fori_loop(0, block // half_tile, multiply_step, 0)


def convolve(chunk_ref, spectrum_ref, forward_ref, inverse_ref, out_ref, points, tok_rows):
    n_blocks, double, width = points.shape
    block = double // 2
    per_block = block // tok_rows
    group = max(1, min(n_blocks, 256 // width)) if width % lane_tile == 0 else 1

    def forward_step(step, carry):
        pieces = []
        for member in range(group):
            start = (step * group + member) * per_block
            rows = chunk_ref[pl.ds(start, per_block), :tok_rows, :]
            pieces.append(rows.reshape(block, width))
        signal = pieces[0] if group == 1 else jnp.concatenate(pieces, axis=1)
        both = jnp.dot(forward_ref[...], signal, preferred_element_type=f32)
        total = both[:double] + both[double:]
        for member in range(group):
            points[step * group + member] = total[:, member * width : (member + 1) * width]
        return carry

    lax.fori_loop(0, n_blocks // group, forward_step, 0)

    multiply_points(points, spectrum_ref, points)

    def inverse_step(step, carry):
        first = step * group
        pieces = [points[first + member] for member in range(group)]
        highs, lows = split_bf16(pieces[0] if group == 1 else jnp.concatenate(pieces, axis=1))
        both = jnp.dot(inverse_ref[...], highs, preferred_element_type=f32)
        rest = jnp.dot(inverse_ref[:block, :], lows, preferred_element_type=f32)
        result = (both[:block] + both[block:] + rest).astype(bf16)
        for member in range(group):
            piece = result[:, member * width : (member + 1) * width]
            out_ref[pl.ds((first + member) * per_block, per_block), :tok_rows, :] = piece.reshape(
                per_block, tok_rows, width
            )
        return carry

    lax.fori_loop(0, n_blocks // group, inverse_step, 0)


def score_rows(index, vars_dev, tok_rows, positions, gate_block, out_ref, gain_row, unembed):
    n_devices, extra, width = gate_block.shape
    gates = gate_block.astype(f32)
    place = lax.broadcasted_iota(jnp.int32, (n_devices, extra, width), 1)
    picked = [
        jnp.sum(jnp.where(place == index * vars_dev + var, gates, 0.0), axis=1)
        for var in range(vars_dev)
    ]
    gate_rows = picked[0] if vars_dev == 1 else jnp.concatenate(picked, axis=0)
    length = n_devices * tok_rows
    column = lax.broadcasted_iota(jnp.int32, (positions.shape[0], length), 1)
    picker = (column == positions).astype(f32).astype(bf16)
    filtered = jnp.dot(
        picker, out_ref[:, :tok_rows, :].reshape(length, width), preferred_element_type=f32
    )
    rows = (gate_rows * filtered).astype(bf16).astype(f32)
    weighted = (rows * gain_row).astype(bf16)
    return jnp.dot(weighted, unembed, preferred_element_type=f32), rows * rows


def pack_scores(raw, squares, raw_parts, vars_dev, packed, n_devices):
    total, width = packed.shape
    extra = total // n_devices
    per_row = raw.shape[1] // width
    count = raw_parts * per_row + 2
    packed[...] = jnp.zeros_like(packed)
    for var in range(vars_dev):
        mine = slice(var * n_devices, (var + 1) * n_devices)
        pieces = [raw[mine, r * width : (r + 1) * width] for r in range(per_row)]
        rounded = [piece.astype(bf16).astype(f32) for piece in pieces]
        rows = rounded + [piece - high for piece, high in zip(pieces, rounded)][: (raw_parts - 1) * per_row]
        high = squares[mine].astype(bf16).astype(f32)
        rows += [high, squares[mine] - high]
        for row, piece in enumerate(rows):
            packed[pl.ds(var * count + row, n_devices, stride=extra), :] = piece


def chunk_kernel(index, chunks, vars_dev, tok_rows, *refs):
    refs = list(refs)
    chunk_ref, spectrum_ref, forward_ref, inverse_ref = refs[:4]
    positions_ref, gain_ref, unembed_ref = refs[4:7]
    refs = refs[7:]
    first, last = index == 0, index == chunks - 1
    gates_ref = None if first else refs.pop(0)
    raw_before, square_before = (None, None) if first else (refs.pop(0), refs.pop(0))
    out_ref = refs.pop(0)
    raw_out, square_out = (None, None) if last else (refs.pop(0), refs.pop(0))
    gates_out = refs.pop(0) if first and not last else None
    points = refs[0]
    convolve(chunk_ref, spectrum_ref, forward_ref, inverse_ref, out_ref, points, tok_rows)
    gate_block = chunk_ref[:, tok_rows:, :] if first else gates_ref[...]
    raw, squares = score_rows(
        index, vars_dev, tok_rows, positions_ref[...], gate_block, out_ref, gain_ref[...], unembed_ref[...]
    )
    if not first:
        raw = raw + raw_before[...]
        squares = squares + square_before[...]
    if gates_out is not None:
        gates_out[...] = gate_block
    if not last:
        raw_out[...] = raw
        square_out[...] = squares
        return
    packed = refs[1]
    n_devices, _, width = out_ref.shape
    extra = out_ref.shape[1] - tok_rows
    pack_scores(raw, squares, 2, vars_dev, packed, n_devices)
    out_ref[:, tok_rows:, :] = packed[...].reshape(n_devices, extra, width).astype(bf16)


def filter_chunk(index, chunks, vars_dev, tok_rows, extra, operands, carried):
    moved, spectrum = operands[:2]
    n_devices, _, width = moved.shape
    n_blocks, double, _ = spectrum.shape
    vocab = operands[6].shape[1]
    n_vars = operands[4].shape[0]
    first, last = index == 0, index == chunks - 1
    rows_out = tok_rows + (extra if last else 0)
    out_shape = [jax.ShapeDtypeStruct((n_devices, rows_out, width), bf16)]
    scratch = [pltpu.VMEM((n_blocks, double, width), f32)]
    if last:
        scratch.append(pltpu.VMEM((n_devices * extra, width), f32))
    else:
        out_shape.append(jax.ShapeDtypeStruct((n_vars, vocab), f32))
        out_shape.append(jax.ShapeDtypeStruct((n_vars, width), f32))
    if first and not last:
        out_shape.append(jax.ShapeDtypeStruct((n_devices, moved.shape[1] - tok_rows, width), bf16))
    flops = 2 * width * n_blocks * (double * double * 5 // 2 + 4 * n_blocks * double)
    return pl.pallas_call(
        functools.partial(chunk_kernel, index, chunks, vars_dev, tok_rows),
        in_specs=[whole_spec()] * (len(operands) + len(carried)),
        out_specs=[whole_spec()] * len(out_shape),
        out_shape=out_shape,
        scratch_shapes=scratch,
        compiler_params=pltpu.CompilerParams(vmem_limit_bytes=(20 if n_blocks <= 8 else 58) * MIB),
        cost_estimate=pl.CostEstimate(flops=flops, bytes_accessed=8 * MIB, transcendentals=0),
        name="filter_chunk",
    )(*operands, *carried)


def final_scores(sums, raw_parts, vars_dev, vocab, model_width, ref_ref, alt_ref):
    width = sums.shape[1]
    per_row = vocab // width
    count = raw_parts * per_row + 2
    ids = lax.broadcasted_iota(jnp.int32, (per_row, width), 0) * width
    ids += lax.broadcasted_iota(jnp.int32, (per_row, width), 1)
    row = lax.broadcasted_iota(jnp.int32, (vars_dev, 2), 0)
    column = lax.broadcasted_iota(jnp.int32, (vars_dev, 2), 1)
    scores = jnp.zeros((vars_dev, 2), f32)

    def whole_sum(values):
        return jnp.sum(jnp.sum(values, axis=1, keepdims=True), axis=0, keepdims=True)

    for var in range(vars_dev):
        base = var * count
        raw = sums[base : base + per_row, :]
        if raw_parts == 2:
            raw = raw + sums[base + per_row : base + 2 * per_row, :]
        square = whole_sum(sums[base + count - 2 : base + count, :])
        logits = raw * lax.rsqrt(square / model_width + norm_eps)
        largest = jnp.max(jnp.max(logits, axis=1, keepdims=True), axis=0, keepdims=True)
        log_total = largest + jnp.log(whole_sum(jnp.exp(logits - largest)))
        ref_logit = whole_sum(jnp.where(ids == ref_ref[var], logits, 0.0))
        alt_logit = whole_sum(jnp.where(ids == alt_ref[var], logits, 0.0))
        pair = jnp.where(column == 0, ref_logit - log_total, alt_logit - ref_logit)
        scores = jnp.where(row == var, pair, scores)
    return scores


def finish_kernel(chunks, vars_dev, vocab, ref_ref, alt_ref, streams_ref, *refs):
    back_refs, mixed_ref, scores_ref, sums = refs[:chunks], refs[chunks], refs[chunks + 1], refs[chunks + 2]
    tok_rows = streams_ref.shape[1]
    owners, _, width = back_refs[0].shape
    step = pl.program_id(0)
    for owner in range(owners):
        for chunk in range(chunks):
            lanes = pl.ds((owner * chunks + chunk) * width, width)
            gate = streams_ref[0, :, lanes].astype(f32)
            filtered = back_refs[chunk][owner, :tok_rows, :].astype(f32)
            mixed_ref[:, lanes] = (gate * filtered).astype(bf16)
    part = jnp.sum(back_refs[-1][:, tok_rows:, :].astype(f32), axis=0)

    @pl.when(step == 0)
    def _():
        sums[...] = part

    @pl.when(step > 0)
    def _():
        sums[...] += part

    @pl.when(step == pl.num_programs(0) - 1)
    def _():
        model_width = pl.num_programs(0) * owners * chunks * width
        scores_ref[...] = final_scores(sums[...], 2, vars_dev, vocab, model_width, ref_ref, alt_ref)


def finish(streams, backs, ref_ids, alt_ids, vocab):
    _, tok_rows, model_width = streams.shape
    chunks = len(backs)
    n_devices, _, width = backs[0].shape
    vars_dev = ref_ids.shape[0]
    owners = max(1, n_devices // 4)
    while owners * chunks * width % lane_tile:
        owners *= 2
    extra = backs[-1].shape[1] - tok_rows
    return pl.pallas_call(
        functools.partial(finish_kernel, chunks, vars_dev, vocab),
        grid=(n_devices // owners,),
        in_specs=[
            pl.BlockSpec(memory_space=pltpu.SMEM),
            pl.BlockSpec(memory_space=pltpu.SMEM),
            pl.BlockSpec((1, tok_rows, owners * chunks * width), lambda i: (0, 0, i)),
        ]
        + [pl.BlockSpec((owners, back.shape[1], width), lambda i: (i, 0, 0)) for back in backs],
        out_specs=[
            pl.BlockSpec((tok_rows, owners * chunks * width), lambda i: (0, i)),
            pl.BlockSpec((vars_dev, 2), lambda i: (0, 0)),
        ],
        out_shape=[
            jax.ShapeDtypeStruct((tok_rows, model_width), bf16),
            jax.ShapeDtypeStruct((vars_dev, 2), f32),
        ],
        scratch_shapes=[pltpu.VMEM((extra, width), f32)],
        compiler_params=pltpu.CompilerParams(vmem_limit_bytes=24 * MIB),
        name="finish",
    )(ref_ids, alt_ids, streams, *backs)

def stacked_products_kernel(halves, vars_dev, me_ref, offsets_ref, streams_ref, out_ref, *scratch):
    gates, pairs, built, gate_sem, pair_sems, body_sems, tail_sem = scratch
    n_devices = built.shape[0]
    pieces, _, tok_rows, lanes_each = pairs.shape
    body = halves * tok_rows
    width = halves * lane_tile
    owners = lanes_each // width
    me = me_ref[0]
    slot = tok_rows // vars_dev

    def pair_copy(piece):
        lanes = pl.ds(piece * lanes_each, lanes_each)
        return pltpu.make_async_copy(
            streams_ref.at[pl.ds(1, 2), :, lanes], pairs.at[piece], pair_sems.at[piece]
        )

    def body_copy(rank):
        rows = pl.ds(0, body)
        return pltpu.make_async_copy(built.at[rank, rows], out_ref.at[rank, rows], body_sems.at[rank])

    gate_copy = pltpu.make_async_copy(streams_ref.at[0], gates, gate_sem.at[0])
    for piece in range(pieces):
        pair_copy(piece).start()
    gate_copy.start()
    for piece in range(pieces):
        pair_copy(piece).wait()
        for member in range(owners):
            owner = piece * owners + member
            for half in range(halves):
                lanes = slice(member * width + half * lane_tile, member * width + (half + 1) * lane_tile)
                rows = slice(half * tok_rows, (half + 1) * tok_rows)
                built[owner, rows, :] = pairs[piece, 0, :, lanes] * pairs[piece, 1, :, lanes]
            body_copy(owner).start()

    extra = built.shape[1] - body
    row = lax.broadcasted_iota(jnp.int32, (row_tile, gates.shape[1]), 0)
    place = lax.broadcasted_iota(jnp.int32, (extra, lane_tile), 0)
    gate_copy.wait()
    gate_rows = []
    for var in range(vars_dev):
        local = var * slot + offsets_ref[me * vars_dev + var]
        start = pl.multiple_of(local // row_tile * row_tile, row_tile)
        tile = gates[pl.ds(start, row_tile), :].astype(f32)
        mine = jnp.where(row == local % row_tile, tile, 0.0)
        gate_rows.append(jnp.sum(mine, axis=0, keepdims=True))
    for owner in range(n_devices):
        tail = jnp.zeros((extra, lane_tile), f32)
        for half in range(halves):
            start = owner * width + half * lane_tile
            for var in range(vars_dev):
                mine = gate_rows[var][:, start : start + lane_tile]
                tail = jnp.where(place == half * vars_dev + var, mine, tail)
        built[owner, body:, :] = tail.astype(bf16)
    rows = pl.ds(body, extra)
    tail_copy = pltpu.make_async_copy(built.at[:, rows], out_ref.at[:, rows], tail_sem.at[0])
    tail_copy.start()
    for rank in range(n_devices):
        body_copy(rank).wait()
    tail_copy.wait()


def stacked_products(me, offsets, streams, vars_dev, n_devices, extra):
    _, tok_rows, model_width = streams.shape
    halves = model_width // n_devices // lane_tile
    rows_out = halves * tok_rows + extra
    pieces = math.gcd(n_devices, 4)
    return pl.pallas_call(
        functools.partial(stacked_products_kernel, halves, vars_dev),
        in_specs=[pl.BlockSpec(memory_space=pltpu.SMEM)] * 2 + [pl.BlockSpec(memory_space=pl.ANY)],
        out_specs=pl.BlockSpec(memory_space=pl.ANY),
        out_shape=jax.ShapeDtypeStruct((n_devices, rows_out, lane_tile), bf16),
        scratch_shapes=[
            pltpu.VMEM((tok_rows, model_width), bf16),
            pltpu.VMEM((pieces, 2, tok_rows, model_width // pieces), bf16),
            pltpu.VMEM((n_devices, rows_out, lane_tile), bf16),
            pltpu.SemaphoreType.DMA((1,)),
            pltpu.SemaphoreType.DMA((pieces,)),
            pltpu.SemaphoreType.DMA((n_devices,)),
            pltpu.SemaphoreType.DMA((1,)),
        ],
        compiler_params=pltpu.CompilerParams(vmem_limit_bytes=60 * MIB),
        cost_estimate=pl.CostEstimate(
            flops=tok_rows * model_width, bytes_accessed=6 * tok_rows * model_width, transcendentals=0
        ),
        name="stacked_products",
    )(me, offsets, streams)


def stacked_filter_kernel(vars_dev, halves, tok_rows, *refs):
    positions_ref, gain_ref, forward, inverse, unembed, taps, arrived = refs[:7]
    out_ref, points, joint, spectrum, packed, leaving, body_sems, tail_sem = refs[7:]
    n_devices = arrived.shape[0]
    body = halves * tok_rows
    n_blocks, double, width = points.shape
    block = double // 2
    per_block = block // tok_rows
    group = 2 if n_blocks % 2 == 0 else 1

    def body_copy(rank):
        rows = pl.ds(0, body)
        return pltpu.make_async_copy(leaving.at[rank, rows], out_ref.at[rank, rows], body_sems.at[rank])

    for index in range(n_blocks):
        both = lax.dot_general(
            forward[...],
            taps[:, index * block : (index + 1) * block],
            (((1,), (1,)), ((), ())),
            preferred_element_type=f32,
        )
        spectrum[index] = both[:double] + both[double:]

    for step in range(0, n_blocks, group):
        pieces = []
        for index in range(step, step + group):
            for half in range(halves):
                rows = slice(half * tok_rows, (half + 1) * tok_rows)
                parts = [arrived[index * per_block + m, rows, :] for m in range(per_block)]
                pieces.append(jnp.concatenate(parts, axis=0))
        signal = jnp.concatenate(pieces, axis=1)
        both = jnp.dot(forward[...], signal, preferred_element_type=f32)
        total = both[:double] + both[double:]
        for member in range(group):
            points[step + member] = total[:, member * width : (member + 1) * width]
    multiply_points(points, spectrum, joint)

    for step in range(0, n_blocks, group):
        highs, lows = split_bf16(jnp.concatenate([joint[step + m] for m in range(group)], axis=1))
        both = jnp.dot(inverse[...], highs, preferred_element_type=f32)
        rest = jnp.dot(inverse[:block, :], lows, preferred_element_type=f32)
        result = (both[:block] + both[block:] + rest).astype(bf16)
        for index in range(group):
            for member in range(per_block):
                rank = (step + index) * per_block + member
                for half in range(halves):
                    start = index * width + half * lane_tile
                    leaving[rank, half * tok_rows : (half + 1) * tok_rows, :] = result[
                        member * tok_rows : (member + 1) * tok_rows, start : start + lane_tile
                    ]
                body_copy(rank).start()

    length = n_devices * tok_rows
    column = lax.broadcasted_iota(jnp.int32, (positions_ref.shape[0], length), 1)
    picker = (column == positions_ref[...]).astype(f32).astype(bf16)
    tails = arrived[:, body:, :].astype(f32)
    place = lax.broadcasted_iota(jnp.int32, tails.shape, 1)
    raw = None
    squares = None
    for half in range(halves):
        lanes = slice(half * lane_tile, (half + 1) * lane_tile)
        picked = [
            jnp.sum(jnp.where(place == half * vars_dev + var, tails, 0.0), axis=1)
            for var in range(vars_dev)
        ]
        gate_rows = picked[0] if vars_dev == 1 else jnp.concatenate(picked, axis=0)
        filtered = leaving[:, half * tok_rows : (half + 1) * tok_rows, :].reshape(length, lane_tile)
        filtered = jnp.dot(picker, filtered, preferred_element_type=f32)
        rows = (gate_rows * filtered).astype(bf16).astype(f32)
        weighted = (rows * gain_ref[:, lanes]).astype(bf16)
        part = jnp.dot(weighted, unembed[lanes, :], preferred_element_type=f32)
        raw = part if raw is None else raw + part
        squares = rows * rows if squares is None else squares + rows * rows
    pack_scores(raw, squares, 2, vars_dev, packed, n_devices)
    extra = packed.shape[0] // n_devices
    leaving[:, body:, :] = packed[...].reshape(n_devices, extra, lane_tile).astype(bf16)
    rows = pl.ds(body, extra)
    tail_copy = pltpu.make_async_copy(leaving.at[:, rows], out_ref.at[:, rows], tail_sem.at[0])
    tail_copy.start()
    for rank in range(n_devices):
        body_copy(rank).wait()
    tail_copy.wait()


def stacked_filter(positions, gain_row, tables, arrived, vars_dev, tok_rows, extra):
    width, length = tables[3].shape
    n_devices = arrived.shape[0]
    double = tables[0].shape[0] // 2
    n_blocks = 2 * length // double
    halves = width // lane_tile
    rows_out = halves * tok_rows + extra
    flops = 2 * width * n_blocks * (double * double * 5 // 2 + 4 * n_blocks * double)
    return pl.pallas_call(
        functools.partial(stacked_filter_kernel, vars_dev, halves, tok_rows),
        in_specs=[whole_spec()] * 7,
        out_specs=pl.BlockSpec(memory_space=pl.ANY),
        out_shape=jax.ShapeDtypeStruct((n_devices, rows_out, lane_tile), bf16),
        scratch_shapes=[pltpu.VMEM((n_blocks, double, width), f32)] * 3
        + [
            pltpu.VMEM((n_devices * extra, lane_tile), f32),
            pltpu.VMEM((n_devices, rows_out, lane_tile), bf16),
            pltpu.SemaphoreType.DMA((n_devices,)),
            pltpu.SemaphoreType.DMA((1,)),
        ],
        compiler_params=pltpu.CompilerParams(vmem_limit_bytes=24 * MIB),
        cost_estimate=pl.CostEstimate(flops=flops, bytes_accessed=8 * MIB, transcendentals=0),
        name="stacked_filter",
    )(positions, gain_row, *tables, arrived)


def stacked_finish_kernel(halves, vars_dev, vocab, ref_ref, alt_ref, gates_ref, back_ref, *refs):
    mixed_ref, scores_ref, results, out_sems = refs
    n_devices, tok_rows, width = results.shape

    def out_copy(owner):
        return pltpu.make_async_copy(
            results.at[owner], mixed_ref.at[:, pl.ds(owner * width, width)], out_sems.at[owner]
        )

    sums = None
    for owner in range(n_devices):
        for half in range(halves):
            lanes = slice(half * lane_tile, (half + 1) * lane_tile)
            start = owner * width + half * lane_tile
            filtered = back_ref[owner, half * tok_rows : (half + 1) * tok_rows, :]
            results[owner, :, lanes] = gates_ref[:, start : start + lane_tile] * filtered
        out_copy(owner).start()
        tail = back_ref[owner, halves * tok_rows :, :].astype(f32)
        sums = tail if sums is None else sums + tail
    model_width = n_devices * width
    scores_ref[...] = final_scores(sums, 2, vars_dev, vocab, model_width, ref_ref, alt_ref)
    for owner in range(n_devices):
        out_copy(owner).wait()


def stacked_finish(ref_ids, alt_ids, gates, back, vocab):
    tok_rows, model_width = gates.shape
    n_devices = back.shape[0]
    vars_dev = ref_ids.shape[0]
    width = model_width // n_devices
    return pl.pallas_call(
        functools.partial(stacked_finish_kernel, width // lane_tile, vars_dev, vocab),
        in_specs=[pl.BlockSpec(memory_space=pltpu.SMEM)] * 2 + [whole_spec()] * 2,
        out_specs=[pl.BlockSpec(memory_space=pl.ANY), whole_spec()],
        out_shape=[
            jax.ShapeDtypeStruct((tok_rows, model_width), bf16),
            jax.ShapeDtypeStruct((vars_dev, 2), f32),
        ],
        scratch_shapes=[
            pltpu.VMEM((n_devices, tok_rows, width), bf16),
            pltpu.SemaphoreType.DMA((n_devices,)),
        ],
        compiler_params=pltpu.CompilerParams(vmem_limit_bytes=16 * MIB),
        cost_estimate=pl.CostEstimate(
            flops=tok_rows * model_width, bytes_accessed=6 * tok_rows * model_width, transcendentals=0
        ),
        name="stacked_finish",
    )(ref_ids, alt_ids, gates, back)


def transposed(blocks):
    return lax.all_to_all(blocks, "seq", split_axis=0, concat_axis=0, tiled=True)


def shards(streams, long_filter, gain, unembed, offsets, ref_ids, alt_ids):
    n_devices = lax.axis_size("seq")
    my_index = lax.axis_index("seq")
    _, tok_rows, model_width = streams.shape
    group_width = model_width // n_devices
    vars_dev = ref_ids.shape[0]
    vocab = unembed.shape[1]
    chunks = max(1, group_width // lane_tile)
    width = group_width // chunks
    block = tok_rows * block_devices(n_devices, tok_rows)
    forward_np, inverse_np = block_tables(block)
    forward, inverse = jnp.asarray(forward_np), jnp.asarray(inverse_np)

    slot = tok_rows // vars_dev
    starts = jnp.arange(vars_dev, dtype=jnp.int32) * slot
    local_rows = starts + lax.dynamic_slice_in_dim(offsets, my_index * vars_dev, vars_dev)
    by_device = offsets.reshape(n_devices, vars_dev)
    positions = by_device + starts[None, :]
    positions += jnp.arange(n_devices, dtype=jnp.int32)[:, None] * tok_rows
    positions = positions.T.reshape(n_devices * vars_dev, 1)
    my_gain = lax.dynamic_slice_in_dim(gain, my_index * group_width, group_width).astype(f32)

    if chunks * lane_tile == group_width:
        me = jnp.reshape(my_index, (1,)).astype(jnp.int32)
        gate_extra = round_up(chunks * vars_dev, row_tile)
        score_extra = round_up(2 * vars_dev * (vocab // lane_tile + 1), row_tile)
        arrived = transposed(stacked_products(me, offsets, streams, vars_dev, n_devices, gate_extra))
        tables = (forward, inverse, unembed, long_filter)
        gain_row = my_gain[None, :]
        leaving = stacked_filter(positions, gain_row, tables, arrived, vars_dev, tok_rows, score_extra)
        back = transposed(leaving)
        mixed, scores = stacked_finish(ref_ids, alt_ids, streams[0], back, vocab)
        return (mixed, scores.T)

    gate_extra = round_up(chunks * vars_dev, row_tile)
    score_extra = round_up(vars_dev * 2 * (vocab // width + 1), row_tile)
    products = make_products(streams, local_rows, n_devices, chunks, gate_extra)
    moved = [lax.all_to_all(part, "seq", split_axis=0, concat_axis=0, tiled=True) for part in products]
    carried = ()
    backs = []
    for chunk in range(chunks):
        mine = slice(chunk * width, (chunk + 1) * width)
        spectrum = filter_spectrum(long_filter[mine], forward, block)
        operands = (
            moved[chunk], spectrum, forward, inverse, positions,
            my_gain[None, mine], unembed[mine],
        )
        if chunk > 0:
            carried = (gates,) + tuple(carried)
        results = filter_chunk(chunk, chunks, vars_dev, tok_rows, score_extra, operands, carried)
        carried = results[1:3]
        if chunk == 0 and chunks > 1:
            gates = results[3]
        backs.append(lax.all_to_all(results[0], "seq", split_axis=0, concat_axis=0, tiled=True))
    mixed, scores = finish(streams, backs, ref_ids, alt_ids, vocab)
    return (mixed, scores.T)


def solution(mesh):
    placed = (
        P(None, ("grp", "seq"), None),
        P("seq", None),
        P(),
        P("seq", None),
        P("grp"),
        P(("grp", "seq")),
        P(("grp", "seq")),
    )
    return jax.shard_map(
        shards,
        mesh=mesh,
        in_specs=placed,
        out_specs=(P(("grp", "seq"), None), P(None, ("grp", "seq"))),
        check_vma=False,
    )
```

```python
import functools
import math

import jax
import jax.numpy as jnp
import numpy as np
from jax import lax
from jax.experimental import pallas as pl
from jax.experimental.pallas import tpu as pltpu
from jax.sharding import PartitionSpec as P

norm_eps = 1e-06
f32 = jnp.float32
bf16 = jnp.bfloat16
row_tile = 16
half_tile = 8
lane_tile = 128
MIB = 1 << 20


def round_up(value, step):
    return -(-value // step) * step


def split_bf16(values):
    high = values.astype(bf16)
    low = (values - high.astype(f32)).astype(bf16)
    return high, low


def block_tables(block):
    turns = (4 * np.arange(block)[:, None] + 1) * np.arange(block)[None, :] % (4 * block)
    theta = turns * (math.pi / (2 * block))
    table = np.concatenate([np.cos(theta), np.sin(theta)], axis=0)
    parts = []
    for matrix in (table, table.T / block):
        high = matrix.astype(bf16)
        low = (matrix - high.astype(np.float64)).astype(bf16)
        parts.append(np.concatenate([high, low], axis=0))
    return parts


def block_devices(n_devices, tok_rows):
    target = math.isqrt(32 * n_devices * tok_rows)
    count = 1
    while n_devices % (2 * count) == 0 and 2 * count * tok_rows <= target:
        count *= 2
    return count


def whole_spec():
    return pl.BlockSpec(memory_space=pltpu.VMEM)


def product_kernel(chunks, width, vars_dev, rows_ref, streams_ref, *out_refs):
    tok_rows = streams_ref.shape[1]
    n_owners = out_refs[0].shape[0]
    extra = out_refs[0].shape[1] - tok_rows
    place = lax.broadcasted_iota(jnp.int32, (extra, tok_rows), 0)
    column = lax.broadcasted_iota(jnp.int32, (extra, tok_rows), 1)
    for owner in range(n_owners):
        gates = jnp.zeros((extra, width), f32)
        for chunk in range(chunks):
            lanes = pl.ds((owner * chunks + chunk) * width, width)
            left = streams_ref[1, :, lanes].astype(f32)
            right = streams_ref[2, :, lanes].astype(f32)
            out_refs[chunk][owner, :tok_rows, :] = (left * right).astype(bf16)
            picker = jnp.zeros((extra, tok_rows), jnp.bool_)
            for var in range(vars_dev):
                picker |= (place == chunk * vars_dev + var) & (column == rows_ref[var])
            gates += jnp.dot(
                picker.astype(f32).astype(bf16),
                streams_ref[0, :, lanes],
                preferred_element_type=f32,
            )
        out_refs[0][owner, tok_rows:, :] = gates.astype(bf16)


def make_products(streams, local_rows, n_devices, chunks, extra):
    _, tok_rows, model_width = streams.shape
    vars_dev = local_rows.shape[0]
    group_width = model_width // n_devices
    width = group_width // chunks
    owners = max(1, n_devices // 4)
    while owners * group_width % lane_tile:
        owners *= 2
    steps = n_devices // owners
    rows_out = [tok_rows + extra] + [tok_rows] * (chunks - 1)
    return pl.pallas_call(
        functools.partial(product_kernel, chunks, width, vars_dev),
        grid=(steps,),
        in_specs=[
            pl.BlockSpec(memory_space=pltpu.SMEM),
            pl.BlockSpec((3, tok_rows, owners * group_width), lambda i: (0, 0, i)),
        ],
        out_specs=[pl.BlockSpec((owners, rows, width), lambda i: (i, 0, 0)) for rows in rows_out],
        out_shape=[jax.ShapeDtypeStruct((n_devices, rows, width), bf16) for rows in rows_out],
        compiler_params=pltpu.CompilerParams(vmem_limit_bytes=24 * MIB),
        name="products",
    )(local_rows, streams)


def spectrum_kernel(block, filter_ref, forward_ref, out_ref):
    n_blocks = out_ref.shape[0]
    for index in range(n_blocks):
        taps = filter_ref[:, index * block : (index + 1) * block]
        both = lax.dot_general(
            forward_ref[...], taps, (((1,), (1,)), ((), ())), preferred_element_type=f32
        )
        out_ref[index] = both[: 2 * block] + both[2 * block :]


def filter_spectrum(taps, forward, block):
    width, length = taps.shape
    n_blocks = length // block
    return pl.pallas_call(
        functools.partial(spectrum_kernel, block),
        in_specs=[whole_spec()] * 2,
        out_specs=whole_spec(),
        out_shape=jax.ShapeDtypeStruct((n_blocks, 2 * block, width), f32),
        compiler_params=pltpu.CompilerParams(vmem_limit_bytes=40 * MIB),
        cost_estimate=pl.CostEstimate(
            flops=8 * block * length * width, bytes_accessed=4 * MIB, transcendentals=0
        ),
        name="filter_spectrum",
    )(taps, forward)


def multiply_tile(points, spectrum_ref, joint, start, lanes):
    n_blocks, double, _ = points.shape
    upper = pl.ds(start, half_tile)
    lower = pl.ds(pl.multiple_of(double // 2 + start, half_tile), half_tile)
    signal = [(points[k, upper, lanes], points[k, lower, lanes]) for k in range(n_blocks)]
    taps = [(spectrum_ref[k, upper, lanes], spectrum_ref[k, lower, lanes]) for k in range(n_blocks)]
    before_re = jnp.zeros_like(signal[0][0])
    before_im = before_re
    for total in range(n_blocks):
        sum_re = jnp.zeros_like(before_re)
        sum_im = sum_re
        for delay in range(total + 1):
            a_re, a_im = signal[total - delay]
            b_re, b_im = taps[delay]
            sum_re += a_re * b_re - a_im * b_im
            sum_im += a_re * b_im + a_im * b_re
        joint[total, upper, lanes] = sum_re + before_im
        joint[total, lower, lanes] = sum_im - before_re
        before_re, before_im = sum_re, sum_im


def multiply_points(points, spectrum_ref, joint):
    n_blocks, double, width = points.shape
    lanes_step = min(width, lane_tile)

    def multiply_step(step, carry):
        start = pl.multiple_of(step * half_tile, half_tile)
        for first in range(0, width, lanes_step):
            multiply_tile(points, spectrum_ref, joint, start, slice(first, first + lanes_step))
        return carry

    lax.fori_loop(0, double // 2 // half_tile, multiply_step, 0)


def convolve(chunk_ref, spectrum_ref, forward_ref, inverse_ref, out_ref, points, tok_rows):
    n_blocks, double, width = points.shape
    block = double // 2
    per_block = block // tok_rows
    group = max(1, min(n_blocks, 256 // width)) if width % lane_tile == 0 else 1

    def forward_step(step, carry):
        pieces = []
        for member in range(group):
            start = (step * group + member) * per_block
            rows = chunk_ref[pl.ds(start, per_block), :tok_rows, :]
            pieces.append(rows.reshape(block, width))
        signal = pieces[0] if group == 1 else jnp.concatenate(pieces, axis=1)
        both = jnp.dot(forward_ref[...], signal, preferred_element_type=f32)
        total = both[:double] + both[double:]
        for member in range(group):
            points[step * group + member] = total[:, member * width : (member + 1) * width]
        return carry

    lax.fori_loop(0, n_blocks // group, forward_step, 0)

    multiply_points(points, spectrum_ref, points)

    def inverse_step(step, carry):
        first = step * group
        pieces = [points[first + member] for member in range(group)]
        highs, lows = split_bf16(pieces[0] if group == 1 else jnp.concatenate(pieces, axis=1))
        both = jnp.dot(inverse_ref[...], highs, preferred_element_type=f32)
        rest = jnp.dot(inverse_ref[:block, :], lows, preferred_element_type=f32)
        result = (both[:block] + both[block:] + rest).astype(bf16)
        for member in range(group):
            piece = result[:, member * width : (member + 1) * width]
            out_ref[pl.ds((first + member) * per_block, per_block), :tok_rows, :] = piece.reshape(
                per_block, tok_rows, width
            )
        return carry

    lax.fori_loop(0, n_blocks // group, inverse_step, 0)


def score_rows(index, vars_dev, tok_rows, positions, gate_block, out_ref, gain_row, unembed):
    n_devices, extra, width = gate_block.shape
    gates = gate_block.astype(f32)
    place = lax.broadcasted_iota(jnp.int32, (n_devices, extra, width), 1)
    picked = [
        jnp.sum(jnp.where(place == index * vars_dev + var, gates, 0.0), axis=1)
        for var in range(vars_dev)
    ]
    gate_rows = picked[0] if vars_dev == 1 else jnp.concatenate(picked, axis=0)
    length = n_devices * tok_rows
    column = lax.broadcasted_iota(jnp.int32, (positions.shape[0], length), 1)
    picker = (column == positions).astype(f32).astype(bf16)
    filtered = jnp.dot(
        picker, out_ref[:, :tok_rows, :].reshape(length, width), preferred_element_type=f32
    )
    rows = (gate_rows * filtered).astype(bf16).astype(f32)
    weighted = (rows * gain_row).astype(bf16)
    return jnp.dot(weighted, unembed, preferred_element_type=f32), rows * rows


def pack_scores(raw, squares, raw_parts, vars_dev, packed, n_devices):
    total, width = packed.shape
    extra = total // n_devices
    per_row = raw.shape[1] // width
    count = raw_parts * per_row + 2
    packed[...] = jnp.zeros_like(packed)
    for var in range(vars_dev):
        mine = slice(var * n_devices, (var + 1) * n_devices)
        pieces = [raw[mine, r * width : (r + 1) * width] for r in range(per_row)]
        rounded = [piece.astype(bf16).astype(f32) for piece in pieces]
        rows = rounded + [piece - high for piece, high in zip(pieces, rounded)][: (raw_parts - 1) * per_row]
        high = squares[mine].astype(bf16).astype(f32)
        rows += [high, squares[mine] - high]
        for row, piece in enumerate(rows):
            packed[pl.ds(var * count + row, n_devices, stride=extra), :] = piece


def chunk_kernel(index, chunks, vars_dev, tok_rows, *refs):
    refs = list(refs)
    chunk_ref, spectrum_ref, forward_ref, inverse_ref = refs[:4]
    positions_ref, gain_ref, unembed_ref = refs[4:7]
    refs = refs[7:]
    first, last = index == 0, index == chunks - 1
    gates_ref = None if first else refs.pop(0)
    raw_before, square_before = (None, None) if first else (refs.pop(0), refs.pop(0))
    out_ref = refs.pop(0)
    raw_out, square_out = (None, None) if last else (refs.pop(0), refs.pop(0))
    gates_out = refs.pop(0) if first and not last else None
    points = refs[0]
    convolve(chunk_ref, spectrum_ref, forward_ref, inverse_ref, out_ref, points, tok_rows)
    gate_block = chunk_ref[:, tok_rows:, :] if first else gates_ref[...]
    raw, squares = score_rows(
        index, vars_dev, tok_rows, positions_ref[...], gate_block, out_ref, gain_ref[...], unembed_ref[...]
    )
    if not first:
        raw = raw + raw_before[...]
        squares = squares + square_before[...]
    if gates_out is not None:
        gates_out[...] = gate_block
    if not last:
        raw_out[...] = raw
        square_out[...] = squares
        return
    packed = refs[1]
    n_devices, _, width = out_ref.shape
    extra = out_ref.shape[1] - tok_rows
    pack_scores(raw, squares, 2, vars_dev, packed, n_devices)
    out_ref[:, tok_rows:, :] = packed[...].reshape(n_devices, extra, width).astype(bf16)


def filter_chunk(index, chunks, vars_dev, tok_rows, extra, operands, carried):
    moved, spectrum = operands[:2]
    n_devices, _, width = moved.shape
    n_blocks, double, _ = spectrum.shape
    vocab = operands[6].shape[1]
    n_vars = operands[4].shape[0]
    first, last = index == 0, index == chunks - 1
    rows_out = tok_rows + (extra if last else 0)
    out_shape = [jax.ShapeDtypeStruct((n_devices, rows_out, width), bf16)]
    scratch = [pltpu.VMEM((n_blocks, double, width), f32)]
    if last:
        scratch.append(pltpu.VMEM((n_devices * extra, width), f32))
    else:
        out_shape.append(jax.ShapeDtypeStruct((n_vars, vocab), f32))
        out_shape.append(jax.ShapeDtypeStruct((n_vars, width), f32))
    if first and not last:
        out_shape.append(jax.ShapeDtypeStruct((n_devices, moved.shape[1] - tok_rows, width), bf16))
    flops = 2 * width * n_blocks * (double * double * 5 // 2 + 4 * n_blocks * double)
    return pl.pallas_call(
        functools.partial(chunk_kernel, index, chunks, vars_dev, tok_rows),
        in_specs=[whole_spec()] * (len(operands) + len(carried)),
        out_specs=[whole_spec()] * len(out_shape),
        out_shape=out_shape,
        scratch_shapes=scratch,
        compiler_params=pltpu.CompilerParams(vmem_limit_bytes=(20 if n_blocks <= 8 else 58) * MIB),
        cost_estimate=pl.CostEstimate(flops=flops, bytes_accessed=8 * MIB, transcendentals=0),
        name="filter_chunk",
    )(*operands, *carried)


def final_scores(sums, raw_parts, vars_dev, vocab, model_width, ref_ref, alt_ref):
    width = sums.shape[1]
    per_row = vocab // width
    count = raw_parts * per_row + 2
    ids = lax.broadcasted_iota(jnp.int32, (per_row, width), 0) * width
    ids += lax.broadcasted_iota(jnp.int32, (per_row, width), 1)
    row = lax.broadcasted_iota(jnp.int32, (vars_dev, 2), 0)
    column = lax.broadcasted_iota(jnp.int32, (vars_dev, 2), 1)
    scores = jnp.zeros((vars_dev, 2), f32)

    def whole_sum(values):
        return jnp.sum(jnp.sum(values, axis=1, keepdims=True), axis=0, keepdims=True)

    for var in range(vars_dev):
        base = var * count
        raw = sums[base : base + per_row, :]
        if raw_parts == 2:
            raw = raw + sums[base + per_row : base + 2 * per_row, :]
        square = whole_sum(sums[base + count - 2 : base + count, :])
        logits = raw * lax.rsqrt(square / model_width + norm_eps)
        largest = jnp.max(jnp.max(logits, axis=1, keepdims=True), axis=0, keepdims=True)
        log_total = largest + jnp.log(whole_sum(jnp.exp(logits - largest)))
        ref_logit = whole_sum(jnp.where(ids == ref_ref[var], logits, 0.0))
        alt_logit = whole_sum(jnp.where(ids == alt_ref[var], logits, 0.0))
        pair = jnp.where(column == 0, ref_logit - log_total, alt_logit - ref_logit)
        scores = jnp.where(row == var, pair, scores)
    return scores


def finish_kernel(chunks, vars_dev, vocab, ref_ref, alt_ref, streams_ref, *refs):
    back_refs, mixed_ref, scores_ref, sums = refs[:chunks], refs[chunks], refs[chunks + 1], refs[chunks + 2]
    tok_rows = streams_ref.shape[1]
    owners, _, width = back_refs[0].shape
    step = pl.program_id(0)
    for owner in range(owners):
        for chunk in range(chunks):
            lanes = pl.ds((owner * chunks + chunk) * width, width)
            gate = streams_ref[0, :, lanes].astype(f32)
            filtered = back_refs[chunk][owner, :tok_rows, :].astype(f32)
            mixed_ref[:, lanes] = (gate * filtered).astype(bf16)
    part = jnp.sum(back_refs[-1][:, tok_rows:, :].astype(f32), axis=0)

    @pl.when(step == 0)
    def _():
        sums[...] = part

    @pl.when(step > 0)
    def _():
        sums[...] += part

    @pl.when(step == pl.num_programs(0) - 1)
    def _():
        model_width = pl.num_programs(0) * owners * chunks * width
        scores_ref[...] = final_scores(sums[...], 2, vars_dev, vocab, model_width, ref_ref, alt_ref)


def finish(streams, backs, ref_ids, alt_ids, vocab):
    _, tok_rows, model_width = streams.shape
    chunks = len(backs)
    n_devices, _, width = backs[0].shape
    vars_dev = ref_ids.shape[0]
    owners = max(1, n_devices // 4)
    while owners * chunks * width % lane_tile:
        owners *= 2
    extra = backs[-1].shape[1] - tok_rows
    return pl.pallas_call(
        functools.partial(finish_kernel, chunks, vars_dev, vocab),
        grid=(n_devices // owners,),
        in_specs=[
            pl.BlockSpec(memory_space=pltpu.SMEM),
            pl.BlockSpec(memory_space=pltpu.SMEM),
            pl.BlockSpec((1, tok_rows, owners * chunks * width), lambda i: (0, 0, i)),
        ]
        + [pl.BlockSpec((owners, back.shape[1], width), lambda i: (i, 0, 0)) for back in backs],
        out_specs=[
            pl.BlockSpec((tok_rows, owners * chunks * width), lambda i: (0, i)),
            pl.BlockSpec((vars_dev, 2), lambda i: (0, 0)),
        ],
        out_shape=[
            jax.ShapeDtypeStruct((tok_rows, model_width), bf16),
            jax.ShapeDtypeStruct((vars_dev, 2), f32),
        ],
        scratch_shapes=[pltpu.VMEM((extra, width), f32)],
        compiler_params=pltpu.CompilerParams(vmem_limit_bytes=24 * MIB),
        name="finish",
    )(ref_ids, alt_ids, streams, *backs)

def stacked_products_kernel(halves, vars_dev, me_ref, offsets_ref, streams_ref, out_ref, *scratch):
    gates, pairs, built, gate_sems, pair_sems, out_sems = scratch
    n_devices = built.shape[0]
    pieces, _, tok_rows, lanes_each = pairs.shape
    body = halves * tok_rows
    width = halves * lane_tile
    owners = lanes_each // width
    me = me_ref[0]
    slot = tok_rows // vars_dev

    def pair_copy(piece):
        lanes = pl.ds(piece * lanes_each, lanes_each)
        return pltpu.make_async_copy(
            streams_ref.at[pl.ds(1, 2), :, lanes], pairs.at[piece], pair_sems.at[piece]
        )

    local_rows = [var * slot + offsets_ref[me * vars_dev + var] for var in range(vars_dev)]

    def out_copy(owner):
        return pltpu.make_async_copy(built.at[owner], out_ref.at[owner], out_sems.at[owner])

    def gate_copy(var):
        start = pl.multiple_of(local_rows[var] // row_tile * row_tile, row_tile)
        return pltpu.make_async_copy(
            streams_ref.at[0, pl.ds(start, row_tile), :], gates.at[var], gate_sems.at[var]
        )

    for var in range(vars_dev):
        gate_copy(var).start()
    for piece in range(pieces):
        pair_copy(piece).start()
    extra = built.shape[1] - body
    row = lax.broadcasted_iota(jnp.int32, gates.shape[1:], 0)
    place = lax.broadcasted_iota(jnp.int32, (extra, lane_tile), 0)
    gate_rows = []
    for var in range(vars_dev):
        gate_copy(var).wait()
        mine = jnp.where(row == local_rows[var] % row_tile, gates[var].astype(f32), 0.0)
        gate_rows.append(jnp.sum(mine, axis=0, keepdims=True))
    for piece in range(pieces):
        pair_copy(piece).wait()
        for member in range(owners):
            owner = piece * owners + member
            tail = jnp.zeros((extra, lane_tile), f32)
            for half in range(halves):
                lanes = slice(member * width + half * lane_tile, member * width + (half + 1) * lane_tile)
                rows = slice(half * tok_rows, (half + 1) * tok_rows)
                built[owner, rows, :] = pairs[piece, 0, :, lanes] * pairs[piece, 1, :, lanes]
                start = owner * width + half * lane_tile
                for var in range(vars_dev):
                    mine = gate_rows[var][:, start : start + lane_tile]
                    tail = jnp.where(place == half * vars_dev + var, mine, tail)
            built[owner, body:, :] = tail.astype(bf16)
            out_copy(owner).start()
    for owner in range(n_devices):
        out_copy(owner).wait()


def stacked_products(me, offsets, streams, vars_dev, n_devices, extra):
    _, tok_rows, model_width = streams.shape
    halves = model_width // n_devices // lane_tile
    rows_out = halves * tok_rows + extra
    pieces = math.gcd(n_devices, 8)
    return pl.pallas_call(
        functools.partial(stacked_products_kernel, halves, vars_dev),
        in_specs=[pl.BlockSpec(memory_space=pltpu.SMEM)] * 2 + [pl.BlockSpec(memory_space=pl.ANY)],
        out_specs=pl.BlockSpec(memory_space=pl.ANY),
        out_shape=jax.ShapeDtypeStruct((n_devices, rows_out, lane_tile), bf16),
        scratch_shapes=[
            pltpu.VMEM((vars_dev, row_tile, model_width), bf16),
            pltpu.VMEM((pieces, 2, tok_rows, model_width // pieces), bf16),
            pltpu.VMEM((n_devices, rows_out, lane_tile), bf16),
            pltpu.SemaphoreType.DMA((vars_dev,)),
            pltpu.SemaphoreType.DMA((pieces,)),
            pltpu.SemaphoreType.DMA((n_devices,)),
        ],
        compiler_params=pltpu.CompilerParams(vmem_limit_bytes=60 * MIB),
        cost_estimate=pl.CostEstimate(
            flops=tok_rows * model_width, bytes_accessed=6 * tok_rows * model_width, transcendentals=0
        ),
        name="stacked_products",
    )(me, offsets, streams)


def stacked_filter_kernel(vars_dev, halves, tok_rows, *refs):
    positions_ref, gain_ref, forward, inverse, unembed, taps, arrived = refs[:7]
    out_ref, packed, leaving, body_sems, tail_sem = refs[7:12]
    points, spectrum, joint = (refs[12 + k * halves : 12 + (k + 1) * halves] for k in range(3))
    n_devices = arrived.shape[0]
    body = halves * tok_rows
    n_blocks, double, _ = points[0].shape
    block = double // 2
    per_block = block // tok_rows
    group = 2 if n_blocks % 2 == 0 else 1
    n_groups = n_blocks // group
    tiles = block // half_tile
    n_steps = math.gcd(n_groups, tiles)
    groups_each, tiles_each = n_groups // n_steps, tiles // n_steps

    def body_copy(device):
        rows = pl.ds(0, body)
        return pltpu.make_async_copy(
            leaving.at[device, rows], out_ref.at[device, rows], body_sems.at[device]
        )

    def transform(half, first):
        channels = slice(half * lane_tile, (half + 1) * lane_tile)
        rows = slice(half * tok_rows, (half + 1) * tok_rows)
        filters = [
            taps[channels, pl.ds(pl.multiple_of((first + m) * block, lane_tile), block)]
            for m in range(group)
        ]
        both = lax.dot_general(
            forward[...],
            jnp.concatenate(filters, axis=0),
            (((1,), (1,)), ((), ())),
            preferred_element_type=f32,
        )
        total = both[:double] + both[double:]
        for m in range(group):
            spectrum[half][first + m] = total[:, m * lane_tile : (m + 1) * lane_tile]
        signal = [
            jnp.concatenate([arrived[(first + m) * per_block + k, rows, :] for k in range(per_block)], axis=0)
            for m in range(group)
        ]
        both = jnp.dot(forward[...], jnp.concatenate(signal, axis=1), preferred_element_type=f32)
        total = both[:double] + both[double:]
        for m in range(group):
            points[half][first + m] = total[:, m * lane_tile : (m + 1) * lane_tile]

    def invert(half, first):
        rows = slice(half * tok_rows, (half + 1) * tok_rows)
        highs, lows = split_bf16(jnp.concatenate([joint[half][first + m] for m in range(group)], axis=1))
        both = jnp.dot(inverse[...], highs, preferred_element_type=f32)
        rest = jnp.dot(inverse[:block, :], lows, preferred_element_type=f32)
        result = (both[:block] + both[block:] + rest).astype(bf16)
        for m in range(group):
            for k in range(per_block):
                leaving[(first + m) * per_block + k, rows, :] = result[
                    k * tok_rows : (k + 1) * tok_rows, m * lane_tile : (m + 1) * lane_tile
                ]
                if half == halves - 1:
                    body_copy((first + m) * per_block + k).start()

    for stage in range(halves + 2):

        def run_step(step, carry, stage=stage):
            if 0 <= stage - 2:
                for index in range(groups_each):
                    invert(stage - 2, (step * groups_each + index) * group)
            if 0 <= stage - 1 < halves:
                for index in range(tiles_each):
                    start = pl.multiple_of((step * tiles_each + index) * half_tile, half_tile)
                    half = stage - 1
                    multiply_tile(points[half], spectrum[half], joint[half], start, slice(None))
            if stage < halves:
                for index in range(groups_each):
                    transform(stage, (step * groups_each + index) * group)
            return carry

        lax.fori_loop(0, n_steps, run_step, 0)

    length = n_devices * tok_rows
    column = lax.broadcasted_iota(jnp.int32, (positions_ref.shape[0], length), 1)
    picker = (column == positions_ref[...]).astype(f32).astype(bf16)
    tails = arrived[:, body:, :].astype(f32)
    place = lax.broadcasted_iota(jnp.int32, tails.shape, 1)
    raw = None
    squares = None
    for half in range(halves):
        lanes = slice(half * lane_tile, (half + 1) * lane_tile)
        picked = [
            jnp.sum(jnp.where(place == half * vars_dev + var, tails, 0.0), axis=1)
            for var in range(vars_dev)
        ]
        gate_rows = picked[0] if vars_dev == 1 else jnp.concatenate(picked, axis=0)
        filtered = leaving[:, half * tok_rows : (half + 1) * tok_rows, :].reshape(length, lane_tile)
        filtered = jnp.dot(picker, filtered, preferred_element_type=f32)
        rows = (gate_rows * filtered).astype(bf16).astype(f32)
        weighted = (rows * gain_ref[:, lanes]).astype(bf16)
        part = jnp.dot(weighted, unembed[lanes, :], preferred_element_type=f32)
        raw = part if raw is None else raw + part
        squares = rows * rows if squares is None else squares + rows * rows
    pack_scores(raw, squares, 2, vars_dev, packed, n_devices)
    extra = packed.shape[0] // n_devices
    leaving[:, body:, :] = packed[...].reshape(n_devices, extra, lane_tile).astype(bf16)
    rows = pl.ds(body, extra)
    tail_copy = pltpu.make_async_copy(leaving.at[:, rows], out_ref.at[:, rows], tail_sem.at[0])
    tail_copy.start()
    for device in range(n_devices):
        body_copy(device).wait()
    tail_copy.wait()


def stacked_filter(positions, gain_row, tables, arrived, vars_dev, tok_rows, extra):
    width, length = tables[3].shape
    n_devices = arrived.shape[0]
    double = tables[0].shape[0] // 2
    n_blocks = 2 * length // double
    halves = width // lane_tile
    rows_out = halves * tok_rows + extra
    flops = 2 * width * n_blocks * (double * double * 5 // 2 + 4 * n_blocks * double)
    return pl.pallas_call(
        functools.partial(stacked_filter_kernel, vars_dev, halves, tok_rows),
        in_specs=[whole_spec()] * 7,
        out_specs=pl.BlockSpec(memory_space=pl.ANY),
        out_shape=jax.ShapeDtypeStruct((n_devices, rows_out, lane_tile), bf16),
        scratch_shapes=[
            pltpu.VMEM((n_devices * extra, lane_tile), f32),
            pltpu.VMEM((n_devices, rows_out, lane_tile), bf16),
            pltpu.SemaphoreType.DMA((n_devices,)),
            pltpu.SemaphoreType.DMA((1,)),
        ]
        + [pltpu.VMEM((n_blocks, double, lane_tile), f32)] * (3 * halves),
        compiler_params=pltpu.CompilerParams(vmem_limit_bytes=24 * MIB),
        cost_estimate=pl.CostEstimate(flops=flops, bytes_accessed=8 * MIB, transcendentals=0),
        name="stacked_filter",
    )(positions, gain_row, *tables, arrived)


def stacked_finish_kernel(halves, vars_dev, vocab, ref_ref, alt_ref, gates_ref, back_ref, *refs):
    mixed_ref, scores_ref, results, scores, out_sems, score_sem = refs
    n_devices, tok_rows, width = results.shape

    def out_copy(owner):
        return pltpu.make_async_copy(
            results.at[owner], mixed_ref.at[:, pl.ds(owner * width, width)], out_sems.at[owner]
        )

    sums = None
    for owner in range(n_devices):
        tail = back_ref[owner, halves * tok_rows :, :].astype(f32)
        sums = tail if sums is None else sums + tail
        for half in range(halves):
            lanes = slice(half * lane_tile, (half + 1) * lane_tile)
            start = owner * width + half * lane_tile
            filtered = back_ref[owner, half * tok_rows : (half + 1) * tok_rows, :]
            results[owner, :, lanes] = gates_ref[:, start : start + lane_tile] * filtered
        out_copy(owner).start()
    model_width = n_devices * width
    scores[...] = final_scores(sums, 2, vars_dev, vocab, model_width, ref_ref, alt_ref)
    score_copy = pltpu.make_async_copy(scores, scores_ref, score_sem.at[0])
    score_copy.start()
    for owner in range(n_devices):
        out_copy(owner).wait()
    score_copy.wait()


def stacked_finish(ref_ids, alt_ids, gates, back, vocab):
    tok_rows, model_width = gates.shape
    n_devices = back.shape[0]
    vars_dev = ref_ids.shape[0]
    width = model_width // n_devices
    return pl.pallas_call(
        functools.partial(stacked_finish_kernel, width // lane_tile, vars_dev, vocab),
        in_specs=[pl.BlockSpec(memory_space=pltpu.SMEM)] * 2 + [whole_spec()] * 2,
        out_specs=[pl.BlockSpec(memory_space=pl.ANY)] * 2,
        out_shape=[
            jax.ShapeDtypeStruct((tok_rows, model_width), bf16),
            jax.ShapeDtypeStruct((vars_dev, 2), f32),
        ],
        scratch_shapes=[
            pltpu.VMEM((n_devices, tok_rows, width), bf16),
            pltpu.VMEM((vars_dev, 2), f32),
            pltpu.SemaphoreType.DMA((n_devices,)),
            pltpu.SemaphoreType.DMA((1,)),
        ],
        compiler_params=pltpu.CompilerParams(vmem_limit_bytes=16 * MIB),
        cost_estimate=pl.CostEstimate(
            flops=tok_rows * model_width, bytes_accessed=6 * tok_rows * model_width, transcendentals=0
        ),
        name="stacked_finish",
    )(ref_ids, alt_ids, gates, back)


def transposed(blocks):
    return lax.all_to_all(blocks, "seq", split_axis=0, concat_axis=0, tiled=True)


def shards(streams, long_filter, gain, unembed, offsets, ref_ids, alt_ids):
    n_devices = lax.axis_size("seq")
    my_index = lax.axis_index("seq")
    _, tok_rows, model_width = streams.shape
    group_width = model_width // n_devices
    vars_dev = ref_ids.shape[0]
    vocab = unembed.shape[1]
    chunks = max(1, group_width // lane_tile)
    width = group_width // chunks
    block = tok_rows * block_devices(n_devices, tok_rows)
    forward_np, inverse_np = block_tables(block)
    forward, inverse = jnp.asarray(forward_np), jnp.asarray(inverse_np)

    slot = tok_rows // vars_dev
    starts = jnp.arange(vars_dev, dtype=jnp.int32) * slot
    local_rows = starts + lax.dynamic_slice_in_dim(offsets, my_index * vars_dev, vars_dev)
    by_device = offsets.reshape(n_devices, vars_dev)
    positions = by_device + starts[None, :]
    positions += jnp.arange(n_devices, dtype=jnp.int32)[:, None] * tok_rows
    positions = positions.T.reshape(n_devices * vars_dev, 1)
    my_gain = lax.dynamic_slice_in_dim(gain, my_index * group_width, group_width).astype(f32)

    if chunks * lane_tile == group_width:
        me = jnp.reshape(my_index, (1,)).astype(jnp.int32)
        gate_extra = round_up(chunks * vars_dev, row_tile)
        score_extra = round_up(2 * vars_dev * (vocab // lane_tile + 1), row_tile)
        arrived = transposed(stacked_products(me, offsets, streams, vars_dev, n_devices, gate_extra))
        tables = (forward, inverse, unembed, long_filter)
        gain_row = my_gain[None, :]
        leaving = stacked_filter(positions, gain_row, tables, arrived, vars_dev, tok_rows, score_extra)
        back = transposed(leaving)
        mixed, scores = stacked_finish(ref_ids, alt_ids, streams[0], back, vocab)
        return (mixed, scores.T)

    gate_extra = round_up(chunks * vars_dev, row_tile)
    score_extra = round_up(vars_dev * 2 * (vocab // width + 1), row_tile)
    products = make_products(streams, local_rows, n_devices, chunks, gate_extra)
    moved = [lax.all_to_all(part, "seq", split_axis=0, concat_axis=0, tiled=True) for part in products]
    carried = ()
    backs = []
    for chunk in range(chunks):
        mine = slice(chunk * width, (chunk + 1) * width)
        spectrum = filter_spectrum(long_filter[mine], forward, block)
        operands = (
            moved[chunk], spectrum, forward, inverse, positions,
            my_gain[None, mine], unembed[mine],
        )
        if chunk > 0:
            carried = (gates,) + tuple(carried)
        results = filter_chunk(chunk, chunks, vars_dev, tok_rows, score_extra, operands, carried)
        carried = results[1:3]
        if chunk == 0 and chunks > 1:
            gates = results[3]
        backs.append(lax.all_to_all(results[0], "seq", split_axis=0, concat_axis=0, tiled=True))
    mixed, scores = finish(streams, backs, ref_ids, alt_ids, vocab)
    return (mixed, scores.T)


def solution(mesh):
    placed = (
        P(None, ("grp", "seq"), None),
        P("seq", None),
        P(),
        P("seq", None),
        P("grp"),
        P(("grp", "seq")),
        P(("grp", "seq")),
    )
    return jax.shard_map(
        shards,
        mesh=mesh,
        in_specs=placed,
        out_specs=(P(("grp", "seq"), None), P(None, ("grp", "seq"))),
        check_vma=False,
    )
```

```python
import functools
import math

import jax
import jax.numpy as jnp
import numpy as np
from jax import lax
from jax.experimental import pallas as pl
from jax.experimental.pallas import tpu as pltpu
from jax.sharding import PartitionSpec as P

norm_eps = 1e-06
f32 = jnp.float32
bf16 = jnp.bfloat16
row_tile = 16
half_tile = 8
lane_tile = 128
MIB = 1 << 20


def round_up(value, step):
    return -(-value // step) * step


def split_bf16(values):
    high = values.astype(bf16)
    low = (values - high.astype(f32)).astype(bf16)
    return high, low


def block_tables(block):
    turns = (4 * np.arange(block)[:, None] + 1) * np.arange(block)[None, :] % (4 * block)
    theta = turns * (math.pi / (2 * block))
    table = np.concatenate([np.cos(theta), np.sin(theta)], axis=0)
    parts = []
    for matrix in (table, table.T / block):
        high = matrix.astype(bf16)
        low = (matrix - high.astype(np.float64)).astype(bf16)
        parts.append(np.concatenate([high, low], axis=0))
    return parts


def block_devices(n_devices, tok_rows):
    target = math.isqrt(32 * n_devices * tok_rows)
    count = 1
    while n_devices % (2 * count) == 0 and 2 * count * tok_rows <= target:
        count *= 2
    return count


def whole_spec():
    return pl.BlockSpec(memory_space=pltpu.VMEM)


def product_kernel(chunks, width, vars_dev, rows_ref, streams_ref, *out_refs):
    tok_rows = streams_ref.shape[1]
    n_owners = out_refs[0].shape[0]
    extra = out_refs[0].shape[1] - tok_rows
    place = lax.broadcasted_iota(jnp.int32, (extra, tok_rows), 0)
    column = lax.broadcasted_iota(jnp.int32, (extra, tok_rows), 1)
    for owner in range(n_owners):
        gates = jnp.zeros((extra, width), f32)
        for chunk in range(chunks):
            lanes = pl.ds((owner * chunks + chunk) * width, width)
            left = streams_ref[1, :, lanes].astype(f32)
            right = streams_ref[2, :, lanes].astype(f32)
            out_refs[chunk][owner, :tok_rows, :] = (left * right).astype(bf16)
            picker = jnp.zeros((extra, tok_rows), jnp.bool_)
            for var in range(vars_dev):
                picker |= (place == chunk * vars_dev + var) & (column == rows_ref[var])
            gates += jnp.dot(
                picker.astype(f32).astype(bf16),
                streams_ref[0, :, lanes],
                preferred_element_type=f32,
            )
        out_refs[0][owner, tok_rows:, :] = gates.astype(bf16)


def make_products(streams, local_rows, n_devices, chunks, extra):
    _, tok_rows, model_width = streams.shape
    vars_dev = local_rows.shape[0]
    group_width = model_width // n_devices
    width = group_width // chunks
    owners = max(1, n_devices // 4)
    while owners * group_width % lane_tile:
        owners *= 2
    steps = n_devices // owners
    rows_out = [tok_rows + extra] + [tok_rows] * (chunks - 1)
    return pl.pallas_call(
        functools.partial(product_kernel, chunks, width, vars_dev),
        grid=(steps,),
        in_specs=[
            pl.BlockSpec(memory_space=pltpu.SMEM),
            pl.BlockSpec((3, tok_rows, owners * group_width), lambda i: (0, 0, i)),
        ],
        out_specs=[pl.BlockSpec((owners, rows, width), lambda i: (i, 0, 0)) for rows in rows_out],
        out_shape=[jax.ShapeDtypeStruct((n_devices, rows, width), bf16) for rows in rows_out],
        compiler_params=pltpu.CompilerParams(vmem_limit_bytes=24 * MIB),
        name="products",
    )(local_rows, streams)


def spectrum_kernel(block, filter_ref, forward_ref, out_ref):
    n_blocks = out_ref.shape[0]
    for index in range(n_blocks):
        taps = filter_ref[:, index * block : (index + 1) * block]
        both = lax.dot_general(
            forward_ref[...], taps, (((1,), (1,)), ((), ())), preferred_element_type=f32
        )
        out_ref[index] = both[: 2 * block] + both[2 * block :]


def filter_spectrum(taps, forward, block):
    width, length = taps.shape
    n_blocks = length // block
    return pl.pallas_call(
        functools.partial(spectrum_kernel, block),
        in_specs=[whole_spec()] * 2,
        out_specs=whole_spec(),
        out_shape=jax.ShapeDtypeStruct((n_blocks, 2 * block, width), f32),
        compiler_params=pltpu.CompilerParams(vmem_limit_bytes=40 * MIB),
        cost_estimate=pl.CostEstimate(
            flops=8 * block * length * width, bytes_accessed=4 * MIB, transcendentals=0
        ),
        name="filter_spectrum",
    )(taps, forward)


def multiply_tile(points, spectrum_ref, joint, start, lanes):
    n_blocks, double, _ = points.shape
    upper = pl.ds(start, half_tile)
    lower = pl.ds(pl.multiple_of(double // 2 + start, half_tile), half_tile)
    signal = [(points[k, upper, lanes], points[k, lower, lanes]) for k in range(n_blocks)]
    taps = [(spectrum_ref[k, upper, lanes], spectrum_ref[k, lower, lanes]) for k in range(n_blocks)]
    before_re = jnp.zeros_like(signal[0][0])
    before_im = before_re
    for total in range(n_blocks):
        sum_re = jnp.zeros_like(before_re)
        sum_im = sum_re
        for delay in range(total + 1):
            a_re, a_im = signal[total - delay]
            b_re, b_im = taps[delay]
            sum_re += a_re * b_re - a_im * b_im
            sum_im += a_re * b_im + a_im * b_re
        joint[total, upper, lanes] = sum_re + before_im
        joint[total, lower, lanes] = sum_im - before_re
        before_re, before_im = sum_re, sum_im


def multiply_points(points, spectrum_ref, joint):
    n_blocks, double, width = points.shape
    lanes_step = min(width, lane_tile)

    def multiply_step(step, carry):
        start = pl.multiple_of(step * half_tile, half_tile)
        for first in range(0, width, lanes_step):
            multiply_tile(points, spectrum_ref, joint, start, slice(first, first + lanes_step))
        return carry

    lax.fori_loop(0, double // 2 // half_tile, multiply_step, 0)


def convolve(chunk_ref, spectrum_ref, forward_ref, inverse_ref, out_ref, points, tok_rows):
    n_blocks, double, width = points.shape
    block = double // 2
    per_block = block // tok_rows
    group = max(1, min(n_blocks, 256 // width)) if width % lane_tile == 0 else 1

    def forward_step(step, carry):
        pieces = []
        for member in range(group):
            start = (step * group + member) * per_block
            rows = chunk_ref[pl.ds(start, per_block), :tok_rows, :]
            pieces.append(rows.reshape(block, width))
        signal = pieces[0] if group == 1 else jnp.concatenate(pieces, axis=1)
        both = jnp.dot(forward_ref[...], signal, preferred_element_type=f32)
        total = both[:double] + both[double:]
        for member in range(group):
            points[step * group + member] = total[:, member * width : (member + 1) * width]
        return carry

    lax.fori_loop(0, n_blocks // group, forward_step, 0)

    multiply_points(points, spectrum_ref, points)

    def inverse_step(step, carry):
        first = step * group
        pieces = [points[first + member] for member in range(group)]
        highs, lows = split_bf16(pieces[0] if group == 1 else jnp.concatenate(pieces, axis=1))
        both = jnp.dot(inverse_ref[...], highs, preferred_element_type=f32)
        rest = jnp.dot(inverse_ref[:block, :], lows, preferred_element_type=f32)
        result = (both[:block] + both[block:] + rest).astype(bf16)
        for member in range(group):
            piece = result[:, member * width : (member + 1) * width]
            out_ref[pl.ds((first + member) * per_block, per_block), :tok_rows, :] = piece.reshape(
                per_block, tok_rows, width
            )
        return carry

    lax.fori_loop(0, n_blocks // group, inverse_step, 0)


def score_rows(index, vars_dev, tok_rows, positions, gate_block, out_ref, gain_row, unembed):
    n_devices, extra, width = gate_block.shape
    gates = gate_block.astype(f32)
    place = lax.broadcasted_iota(jnp.int32, (n_devices, extra, width), 1)
    picked = [
        jnp.sum(jnp.where(place == index * vars_dev + var, gates, 0.0), axis=1)
        for var in range(vars_dev)
    ]
    gate_rows = picked[0] if vars_dev == 1 else jnp.concatenate(picked, axis=0)
    length = n_devices * tok_rows
    column = lax.broadcasted_iota(jnp.int32, (positions.shape[0], length), 1)
    picker = (column == positions).astype(f32).astype(bf16)
    filtered = jnp.dot(
        picker, out_ref[:, :tok_rows, :].reshape(length, width), preferred_element_type=f32
    )
    rows = (gate_rows * filtered).astype(bf16).astype(f32)
    weighted = (rows * gain_row).astype(bf16)
    return jnp.dot(weighted, unembed, preferred_element_type=f32), rows * rows


def pack_scores(raw, squares, raw_parts, vars_dev, packed, n_devices):
    total, width = packed.shape
    extra = total // n_devices
    per_row = raw.shape[1] // width
    count = raw_parts * per_row + 2
    packed[...] = jnp.zeros_like(packed)
    for var in range(vars_dev):
        mine = slice(var * n_devices, (var + 1) * n_devices)
        pieces = [raw[mine, r * width : (r + 1) * width] for r in range(per_row)]
        rounded = [piece.astype(bf16).astype(f32) for piece in pieces]
        rows = rounded + [piece - high for piece, high in zip(pieces, rounded)][: (raw_parts - 1) * per_row]
        high = squares[mine].astype(bf16).astype(f32)
        rows += [high, squares[mine] - high]
        for row, piece in enumerate(rows):
            packed[pl.ds(var * count + row, n_devices, stride=extra), :] = piece


def chunk_kernel(index, chunks, vars_dev, tok_rows, *refs):
    refs = list(refs)
    chunk_ref, spectrum_ref, forward_ref, inverse_ref = refs[:4]
    positions_ref, gain_ref, unembed_ref = refs[4:7]
    refs = refs[7:]
    first, last = index == 0, index == chunks - 1
    gates_ref = None if first else refs.pop(0)
    raw_before, square_before = (None, None) if first else (refs.pop(0), refs.pop(0))
    out_ref = refs.pop(0)
    raw_out, square_out = (None, None) if last else (refs.pop(0), refs.pop(0))
    gates_out = refs.pop(0) if first and not last else None
    points = refs[0]
    convolve(chunk_ref, spectrum_ref, forward_ref, inverse_ref, out_ref, points, tok_rows)
    gate_block = chunk_ref[:, tok_rows:, :] if first else gates_ref[...]
    raw, squares = score_rows(
        index, vars_dev, tok_rows, positions_ref[...], gate_block, out_ref, gain_ref[...], unembed_ref[...]
    )
    if not first:
        raw = raw + raw_before[...]
        squares = squares + square_before[...]
    if gates_out is not None:
        gates_out[...] = gate_block
    if not last:
        raw_out[...] = raw
        square_out[...] = squares
        return
    packed = refs[1]
    n_devices, _, width = out_ref.shape
    extra = out_ref.shape[1] - tok_rows
    pack_scores(raw, squares, 2, vars_dev, packed, n_devices)
    out_ref[:, tok_rows:, :] = packed[...].reshape(n_devices, extra, width).astype(bf16)


def filter_chunk(index, chunks, vars_dev, tok_rows, extra, operands, carried):
    moved, spectrum = operands[:2]
    n_devices, _, width = moved.shape
    n_blocks, double, _ = spectrum.shape
    vocab = operands[6].shape[1]
    n_vars = operands[4].shape[0]
    first, last = index == 0, index == chunks - 1
    rows_out = tok_rows + (extra if last else 0)
    out_shape = [jax.ShapeDtypeStruct((n_devices, rows_out, width), bf16)]
    scratch = [pltpu.VMEM((n_blocks, double, width), f32)]
    if last:
        scratch.append(pltpu.VMEM((n_devices * extra, width), f32))
    else:
        out_shape.append(jax.ShapeDtypeStruct((n_vars, vocab), f32))
        out_shape.append(jax.ShapeDtypeStruct((n_vars, width), f32))
    if first and not last:
        out_shape.append(jax.ShapeDtypeStruct((n_devices, moved.shape[1] - tok_rows, width), bf16))
    flops = 2 * width * n_blocks * (double * double * 5 // 2 + 4 * n_blocks * double)
    return pl.pallas_call(
        functools.partial(chunk_kernel, index, chunks, vars_dev, tok_rows),
        in_specs=[whole_spec()] * (len(operands) + len(carried)),
        out_specs=[whole_spec()] * len(out_shape),
        out_shape=out_shape,
        scratch_shapes=scratch,
        compiler_params=pltpu.CompilerParams(vmem_limit_bytes=(20 if n_blocks <= 8 else 58) * MIB),
        cost_estimate=pl.CostEstimate(flops=flops, bytes_accessed=8 * MIB, transcendentals=0),
        name="filter_chunk",
    )(*operands, *carried)


def final_scores(sums, raw_parts, vars_dev, vocab, model_width, ref_ref, alt_ref):
    width = sums.shape[1]
    per_row = vocab // width
    count = raw_parts * per_row + 2
    ids = lax.broadcasted_iota(jnp.int32, (per_row, width), 0) * width
    ids += lax.broadcasted_iota(jnp.int32, (per_row, width), 1)
    row = lax.broadcasted_iota(jnp.int32, (vars_dev, 2), 0)
    column = lax.broadcasted_iota(jnp.int32, (vars_dev, 2), 1)
    scores = jnp.zeros((vars_dev, 2), f32)

    def whole_sum(values):
        return jnp.sum(jnp.sum(values, axis=1, keepdims=True), axis=0, keepdims=True)

    for var in range(vars_dev):
        base = var * count
        raw = sums[base : base + per_row, :]
        if raw_parts == 2:
            raw = raw + sums[base + per_row : base + 2 * per_row, :]
        square = whole_sum(sums[base + count - 2 : base + count, :])
        logits = raw * lax.rsqrt(square / model_width + norm_eps)
        largest = jnp.max(jnp.max(logits, axis=1, keepdims=True), axis=0, keepdims=True)
        log_total = largest + jnp.log(whole_sum(jnp.exp(logits - largest)))
        ref_logit = whole_sum(jnp.where(ids == ref_ref[var], logits, 0.0))
        alt_logit = whole_sum(jnp.where(ids == alt_ref[var], logits, 0.0))
        pair = jnp.where(column == 0, ref_logit - log_total, alt_logit - ref_logit)
        scores = jnp.where(row == var, pair, scores)
    return scores


def finish_kernel(chunks, vars_dev, vocab, ref_ref, alt_ref, streams_ref, *refs):
    back_refs, mixed_ref, scores_ref, sums = refs[:chunks], refs[chunks], refs[chunks + 1], refs[chunks + 2]
    tok_rows = streams_ref.shape[1]
    owners, _, width = back_refs[0].shape
    step = pl.program_id(0)
    for owner in range(owners):
        for chunk in range(chunks):
            lanes = pl.ds((owner * chunks + chunk) * width, width)
            gate = streams_ref[0, :, lanes].astype(f32)
            filtered = back_refs[chunk][owner, :tok_rows, :].astype(f32)
            mixed_ref[:, lanes] = (gate * filtered).astype(bf16)
    part = jnp.sum(back_refs[-1][:, tok_rows:, :].astype(f32), axis=0)

    @pl.when(step == 0)
    def _():
        sums[...] = part

    @pl.when(step > 0)
    def _():
        sums[...] += part

    @pl.when(step == pl.num_programs(0) - 1)
    def _():
        model_width = pl.num_programs(0) * owners * chunks * width
        scores_ref[...] = final_scores(sums[...], 2, vars_dev, vocab, model_width, ref_ref, alt_ref)


def finish(streams, backs, ref_ids, alt_ids, vocab):
    _, tok_rows, model_width = streams.shape
    chunks = len(backs)
    n_devices, _, width = backs[0].shape
    vars_dev = ref_ids.shape[0]
    owners = max(1, n_devices // 4)
    while owners * chunks * width % lane_tile:
        owners *= 2
    extra = backs[-1].shape[1] - tok_rows
    return pl.pallas_call(
        functools.partial(finish_kernel, chunks, vars_dev, vocab),
        grid=(n_devices // owners,),
        in_specs=[
            pl.BlockSpec(memory_space=pltpu.SMEM),
            pl.BlockSpec(memory_space=pltpu.SMEM),
            pl.BlockSpec((1, tok_rows, owners * chunks * width), lambda i: (0, 0, i)),
        ]
        + [pl.BlockSpec((owners, back.shape[1], width), lambda i: (i, 0, 0)) for back in backs],
        out_specs=[
            pl.BlockSpec((tok_rows, owners * chunks * width), lambda i: (0, i)),
            pl.BlockSpec((vars_dev, 2), lambda i: (0, 0)),
        ],
        out_shape=[
            jax.ShapeDtypeStruct((tok_rows, model_width), bf16),
            jax.ShapeDtypeStruct((vars_dev, 2), f32),
        ],
        scratch_shapes=[pltpu.VMEM((extra, width), f32)],
        compiler_params=pltpu.CompilerParams(vmem_limit_bytes=24 * MIB),
        name="finish",
    )(ref_ids, alt_ids, streams, *backs)

def stacked_products_kernel(halves, vars_dev, offsets_ref, streams_ref, out_ref, *scratch):
    gates, pairs, built, offsets, gate_sems, pair_sems, out_sems, offset_sem = scratch
    n_devices = built.shape[0]
    pieces, _, tok_rows, lanes_each = pairs.shape
    body = halves * tok_rows
    width = halves * lane_tile
    owners = lanes_each // width
    me = lax.axis_index("seq")
    slot = tok_rows // vars_dev

    def pair_copy(piece):
        lanes = pl.ds(piece * lanes_each, lanes_each)
        return pltpu.make_async_copy(
            streams_ref.at[pl.ds(1, 2), :, lanes], pairs.at[piece], pair_sems.at[piece]
        )


    def out_copy(owner):
        return pltpu.make_async_copy(built.at[owner], out_ref.at[owner], out_sems.at[owner])

    def gate_copy(var):
        start = pl.multiple_of(local_rows[var] // row_tile * row_tile, row_tile)
        return pltpu.make_async_copy(
            streams_ref.at[0, pl.ds(start, row_tile), :], gates.at[var], gate_sems.at[var]
        )

    offset_copy = pltpu.make_async_copy(offsets_ref, offsets, offset_sem.at[0])
    offset_copy.start()
    for piece in range(pieces):
        pair_copy(piece).start()
    offset_copy.wait()
    local_rows = [var * slot + offsets[me * vars_dev + var] for var in range(vars_dev)]
    for var in range(vars_dev):
        gate_copy(var).start()
    extra = built.shape[1] - body
    row = lax.broadcasted_iota(jnp.int32, gates.shape[1:], 0)
    place = lax.broadcasted_iota(jnp.int32, (extra, lane_tile), 0)
    gate_rows = []
    for var in range(vars_dev):
        gate_copy(var).wait()
        mine = jnp.where(row == local_rows[var] % row_tile, gates[var].astype(f32), 0.0)
        gate_rows.append(jnp.sum(mine, axis=0, keepdims=True))
    for piece in range(pieces):
        pair_copy(piece).wait()
        for member in range(owners):
            owner = piece * owners + member
            tail = jnp.zeros((extra, lane_tile), f32)
            for half in range(halves):
                lanes = slice(member * width + half * lane_tile, member * width + (half + 1) * lane_tile)
                rows = slice(half * tok_rows, (half + 1) * tok_rows)
                built[owner, rows, :] = pairs[piece, 0, :, lanes] * pairs[piece, 1, :, lanes]
                start = owner * width + half * lane_tile
                for var in range(vars_dev):
                    mine = gate_rows[var][:, start : start + lane_tile]
                    tail = jnp.where(place == half * vars_dev + var, mine, tail)
            built[owner, body:, :] = tail.astype(bf16)
            out_copy(owner).start()
    for owner in range(n_devices):
        out_copy(owner).wait()


def stacked_products(offsets, streams, vars_dev, n_devices, extra):
    _, tok_rows, model_width = streams.shape
    halves = model_width // n_devices // lane_tile
    rows_out = halves * tok_rows + extra
    pieces = math.gcd(n_devices, 8)
    return pl.pallas_call(
        functools.partial(stacked_products_kernel, halves, vars_dev),
        in_specs=[pl.BlockSpec(memory_space=pl.ANY)] * 2,
        out_specs=pl.BlockSpec(memory_space=pl.ANY),
        out_shape=jax.ShapeDtypeStruct((n_devices, rows_out, lane_tile), bf16),
        scratch_shapes=[
            pltpu.VMEM((vars_dev, row_tile, model_width), bf16),
            pltpu.VMEM((pieces, 2, tok_rows, model_width // pieces), bf16),
            pltpu.VMEM((n_devices, rows_out, lane_tile), bf16),
            pltpu.SMEM(offsets.shape, jnp.int32),
            pltpu.SemaphoreType.DMA((vars_dev,)),
            pltpu.SemaphoreType.DMA((pieces,)),
            pltpu.SemaphoreType.DMA((n_devices,)),
            pltpu.SemaphoreType.DMA((1,)),
        ],
        compiler_params=pltpu.CompilerParams(vmem_limit_bytes=60 * MIB),
        cost_estimate=pl.CostEstimate(
            flops=tok_rows * model_width, bytes_accessed=6 * tok_rows * model_width, transcendentals=0
        ),
        name="stacked_products",
    )(offsets, streams)


def stacked_filter_kernel(vars_dev, halves, tok_rows, *refs):
    positions_ref, gain_ref, forward, inverse, unembed, taps, arrived = refs[:7]
    out_ref, points, joint, spectrum, packed, leaving, body_sems, tail_sem = refs[7:]
    n_devices = arrived.shape[0]
    body = halves * tok_rows
    n_blocks, double, width = points.shape
    block = double // 2
    per_block = block // tok_rows
    group = math.gcd(n_blocks, 4)

    def body_copy(rank):
        rows = pl.ds(0, body)
        return pltpu.make_async_copy(leaving.at[rank, rows], out_ref.at[rank, rows], body_sems.at[rank])

    for step in range(0, n_blocks, group):
        filters = [taps[:, index * block : (index + 1) * block] for index in range(step, step + group)]
        both = lax.dot_general(
            forward[...],
            jnp.concatenate(filters, axis=0),
            (((1,), (1,)), ((), ())),
            preferred_element_type=f32,
        )
        total = both[:double] + both[double:]
        for member in range(group):
            spectrum[step + member] = total[:, member * width : (member + 1) * width]

    for step in range(0, n_blocks, group):
        pieces = []
        for index in range(step, step + group):
            for half in range(halves):
                rows = slice(half * tok_rows, (half + 1) * tok_rows)
                parts = [arrived[index * per_block + m, rows, :] for m in range(per_block)]
                pieces.append(jnp.concatenate(parts, axis=0))
        signal = jnp.concatenate(pieces, axis=1)
        both = jnp.dot(forward[...], signal, preferred_element_type=f32)
        total = both[:double] + both[double:]
        for member in range(group):
            points[step + member] = total[:, member * width : (member + 1) * width]
    multiply_points(points, spectrum, joint)

    for step in range(0, n_blocks, group):
        highs, lows = split_bf16(jnp.concatenate([joint[step + m] for m in range(group)], axis=1))
        both = jnp.dot(inverse[...], highs, preferred_element_type=f32)
        rest = jnp.dot(inverse[:block, :], lows, preferred_element_type=f32)
        result = (both[:block] + both[block:] + rest).astype(bf16)
        for index in range(group):
            for member in range(per_block):
                rank = (step + index) * per_block + member
                for half in range(halves):
                    start = index * width + half * lane_tile
                    leaving[rank, half * tok_rows : (half + 1) * tok_rows, :] = result[
                        member * tok_rows : (member + 1) * tok_rows, start : start + lane_tile
                    ]
                body_copy(rank).start()

    length = n_devices * tok_rows
    column = lax.broadcasted_iota(jnp.int32, (positions_ref.shape[0], length), 1)
    picker = (column == positions_ref[...]).astype(f32).astype(bf16)
    tails = arrived[:, body:, :].astype(f32)
    place = lax.broadcasted_iota(jnp.int32, tails.shape, 1)
    raw = None
    squares = None
    for half in range(halves):
        lanes = slice(half * lane_tile, (half + 1) * lane_tile)
        picked = [
            jnp.sum(jnp.where(place == half * vars_dev + var, tails, 0.0), axis=1)
            for var in range(vars_dev)
        ]
        gate_rows = picked[0] if vars_dev == 1 else jnp.concatenate(picked, axis=0)
        filtered = leaving[:, half * tok_rows : (half + 1) * tok_rows, :].reshape(length, lane_tile)
        filtered = jnp.dot(picker, filtered, preferred_element_type=f32)
        rows = (gate_rows * filtered).astype(bf16).astype(f32)
        weighted = (rows * gain_ref[:, lanes]).astype(bf16)
        part = jnp.dot(weighted, unembed[lanes, :], preferred_element_type=f32)
        raw = part if raw is None else raw + part
        squares = rows * rows if squares is None else squares + rows * rows
    pack_scores(raw, squares, 2, vars_dev, packed, n_devices)
    extra = packed.shape[0] // n_devices
    leaving[:, body:, :] = packed[...].reshape(n_devices, extra, lane_tile).astype(bf16)
    rows = pl.ds(body, extra)
    tail_copy = pltpu.make_async_copy(leaving.at[:, rows], out_ref.at[:, rows], tail_sem.at[0])
    tail_copy.start()
    for rank in range(n_devices):
        body_copy(rank).wait()
    tail_copy.wait()


def stacked_filter(positions, gain_row, tables, arrived, vars_dev, tok_rows, extra):
    width, length = tables[3].shape
    n_devices = arrived.shape[0]
    double = tables[0].shape[0] // 2
    n_blocks = 2 * length // double
    halves = width // lane_tile
    rows_out = halves * tok_rows + extra
    flops = 2 * width * n_blocks * (double * double * 5 // 2 + 4 * n_blocks * double)
    return pl.pallas_call(
        functools.partial(stacked_filter_kernel, vars_dev, halves, tok_rows),
        in_specs=[whole_spec()] * 7,
        out_specs=pl.BlockSpec(memory_space=pl.ANY),
        out_shape=jax.ShapeDtypeStruct((n_devices, rows_out, lane_tile), bf16),
        scratch_shapes=[pltpu.VMEM((n_blocks, double, width), f32)] * 3
        + [
            pltpu.VMEM((n_devices * extra, lane_tile), f32),
            pltpu.VMEM((n_devices, rows_out, lane_tile), bf16),
            pltpu.SemaphoreType.DMA((n_devices,)),
            pltpu.SemaphoreType.DMA((1,)),
        ],
        compiler_params=pltpu.CompilerParams(vmem_limit_bytes=24 * MIB),
        cost_estimate=pl.CostEstimate(flops=flops, bytes_accessed=8 * MIB, transcendentals=0),
        name="stacked_filter",
    )(positions, gain_row, *tables, arrived)


def stacked_finish_kernel(halves, vars_dev, vocab, ref_ref, alt_ref, gates_ref, back_ref, *refs):
    mixed_ref, scores_ref, results, scores, out_sems, score_sem = refs
    n_devices, tok_rows, width = results.shape

    def out_copy(owner):
        return pltpu.make_async_copy(
            results.at[owner], mixed_ref.at[:, pl.ds(owner * width, width)], out_sems.at[owner]
        )

    sums = None
    for owner in range(n_devices):
        tail = back_ref[owner, halves * tok_rows :, :].astype(f32)
        sums = tail if sums is None else sums + tail
        for half in range(halves):
            lanes = slice(half * lane_tile, (half + 1) * lane_tile)
            start = owner * width + half * lane_tile
            filtered = back_ref[owner, half * tok_rows : (half + 1) * tok_rows, :]
            results[owner, :, lanes] = gates_ref[:, start : start + lane_tile] * filtered
        out_copy(owner).start()
    model_width = n_devices * width
    scores[...] = final_scores(sums, 2, vars_dev, vocab, model_width, ref_ref, alt_ref)
    score_copy = pltpu.make_async_copy(scores, scores_ref, score_sem.at[0])
    score_copy.start()
    for owner in range(n_devices):
        out_copy(owner).wait()
    score_copy.wait()


def stacked_finish(ref_ids, alt_ids, gates, back, vocab):
    tok_rows, model_width = gates.shape
    n_devices = back.shape[0]
    vars_dev = ref_ids.shape[0]
    width = model_width // n_devices
    return pl.pallas_call(
        functools.partial(stacked_finish_kernel, width // lane_tile, vars_dev, vocab),
        in_specs=[pl.BlockSpec(memory_space=pltpu.SMEM)] * 2 + [whole_spec()] * 2,
        out_specs=[pl.BlockSpec(memory_space=pl.ANY)] * 2,
        out_shape=[
            jax.ShapeDtypeStruct((tok_rows, model_width), bf16),
            jax.ShapeDtypeStruct((vars_dev, 2), f32),
        ],
        scratch_shapes=[
            pltpu.VMEM((n_devices, tok_rows, width), bf16),
            pltpu.VMEM((vars_dev, 2), f32),
            pltpu.SemaphoreType.DMA((n_devices,)),
            pltpu.SemaphoreType.DMA((1,)),
        ],
        compiler_params=pltpu.CompilerParams(vmem_limit_bytes=16 * MIB),
        cost_estimate=pl.CostEstimate(
            flops=tok_rows * model_width, bytes_accessed=6 * tok_rows * model_width, transcendentals=0
        ),
        name="stacked_finish",
    )(ref_ids, alt_ids, gates, back)


def transposed(blocks):
    return lax.all_to_all(blocks, "seq", split_axis=0, concat_axis=0, tiled=True)


def shards(streams, long_filter, gain, unembed, offsets, ref_ids, alt_ids):
    n_devices = lax.axis_size("seq")
    my_index = lax.axis_index("seq")
    _, tok_rows, model_width = streams.shape
    group_width = model_width // n_devices
    vars_dev = ref_ids.shape[0]
    vocab = unembed.shape[1]
    chunks = max(1, group_width // lane_tile)
    width = group_width // chunks
    block = tok_rows * block_devices(n_devices, tok_rows)
    forward_np, inverse_np = block_tables(block)
    forward, inverse = jnp.asarray(forward_np), jnp.asarray(inverse_np)

    slot = tok_rows // vars_dev
    starts = jnp.arange(vars_dev, dtype=jnp.int32) * slot
    local_rows = starts + lax.dynamic_slice_in_dim(offsets, my_index * vars_dev, vars_dev)
    by_device = offsets.reshape(n_devices, vars_dev)
    positions = by_device + starts[None, :]
    positions += jnp.arange(n_devices, dtype=jnp.int32)[:, None] * tok_rows
    positions = positions.T.reshape(n_devices * vars_dev, 1)
    my_gain = lax.dynamic_slice_in_dim(gain, my_index * group_width, group_width).astype(f32)

    if chunks * lane_tile == group_width:
        gate_extra = round_up(chunks * vars_dev, row_tile)
        score_extra = round_up(2 * vars_dev * (vocab // lane_tile + 1), row_tile)
        arrived = transposed(stacked_products(offsets, streams, vars_dev, n_devices, gate_extra))
        tables = (forward, inverse, unembed, long_filter)
        gain_row = my_gain[None, :]
        leaving = stacked_filter(positions, gain_row, tables, arrived, vars_dev, tok_rows, score_extra)
        back = transposed(leaving)
        mixed, scores = stacked_finish(ref_ids, alt_ids, streams[0], back, vocab)
        return (mixed, scores.T)

    gate_extra = round_up(chunks * vars_dev, row_tile)
    score_extra = round_up(vars_dev * 2 * (vocab // width + 1), row_tile)
    products = make_products(streams, local_rows, n_devices, chunks, gate_extra)
    moved = [lax.all_to_all(part, "seq", split_axis=0, concat_axis=0, tiled=True) for part in products]
    carried = ()
    backs = []
    for chunk in range(chunks):
        mine = slice(chunk * width, (chunk + 1) * width)
        spectrum = filter_spectrum(long_filter[mine], forward, block)
        operands = (
            moved[chunk], spectrum, forward, inverse, positions,
            my_gain[None, mine], unembed[mine],
        )
        if chunk > 0:
            carried = (gates,) + tuple(carried)
        results = filter_chunk(chunk, chunks, vars_dev, tok_rows, score_extra, operands, carried)
        carried = results[1:3]
        if chunk == 0 and chunks > 1:
            gates = results[3]
        backs.append(lax.all_to_all(results[0], "seq", split_axis=0, concat_axis=0, tiled=True))
    mixed, scores = finish(streams, backs, ref_ids, alt_ids, vocab)
    return (mixed, scores.T)


def solution(mesh):
    placed = (
        P(None, ("grp", "seq"), None),
        P("seq", None),
        P(),
        P("seq", None),
        P("grp"),
        P(("grp", "seq")),
        P(("grp", "seq")),
    )
    return jax.shard_map(
        shards,
        mesh=mesh,
        in_specs=placed,
        out_specs=(P(("grp", "seq"), None), P(None, ("grp", "seq"))),
        check_vma=False,
    )
```

```python
import functools
import math

import jax
import jax.numpy as jnp
import numpy as np
from jax import lax
from jax.experimental import pallas as pl
from jax.experimental.pallas import tpu as pltpu
from jax.sharding import PartitionSpec as P

norm_eps = 1e-06
f32 = jnp.float32
bf16 = jnp.bfloat16
row_tile = 16
half_tile = 8
lane_tile = 128
MIB = 1 << 20


def round_up(value, step):
    return -(-value // step) * step


def split_bf16(values):
    high = values.astype(bf16)
    low = (values - high.astype(f32)).astype(bf16)
    return high, low


def block_tables(block):
    turns = (4 * np.arange(block)[:, None] + 1) * np.arange(block)[None, :] % (4 * block)
    theta = turns * (math.pi / (2 * block))
    table = np.concatenate([np.cos(theta), np.sin(theta)], axis=0)
    parts = []
    for matrix in (table, table.T / block):
        high = matrix.astype(bf16)
        low = (matrix - high.astype(np.float64)).astype(bf16)
        parts.append(np.concatenate([high, low], axis=0))
    return parts


def block_devices(n_devices, tok_rows):
    target = math.isqrt(32 * n_devices * tok_rows)
    count = 1
    while n_devices % (2 * count) == 0 and 2 * count * tok_rows <= target:
        count *= 2
    return count


def whole_spec():
    return pl.BlockSpec(memory_space=pltpu.VMEM)


def product_kernel(chunks, width, vars_dev, rows_ref, streams_ref, *out_refs):
    tok_rows = streams_ref.shape[1]
    n_owners = out_refs[0].shape[0]
    extra = out_refs[0].shape[1] - tok_rows
    place = lax.broadcasted_iota(jnp.int32, (extra, tok_rows), 0)
    column = lax.broadcasted_iota(jnp.int32, (extra, tok_rows), 1)
    for owner in range(n_owners):
        gates = jnp.zeros((extra, width), f32)
        for chunk in range(chunks):
            lanes = pl.ds((owner * chunks + chunk) * width, width)
            left = streams_ref[1, :, lanes].astype(f32)
            right = streams_ref[2, :, lanes].astype(f32)
            out_refs[chunk][owner, :tok_rows, :] = (left * right).astype(bf16)
            picker = jnp.zeros((extra, tok_rows), jnp.bool_)
            for var in range(vars_dev):
                picker |= (place == chunk * vars_dev + var) & (column == rows_ref[var])
            gates += jnp.dot(
                picker.astype(f32).astype(bf16),
                streams_ref[0, :, lanes],
                preferred_element_type=f32,
            )
        out_refs[0][owner, tok_rows:, :] = gates.astype(bf16)


def make_products(streams, local_rows, n_devices, chunks, extra):
    _, tok_rows, model_width = streams.shape
    vars_dev = local_rows.shape[0]
    group_width = model_width // n_devices
    width = group_width // chunks
    owners = max(1, n_devices // 4)
    while owners * group_width % lane_tile:
        owners *= 2
    steps = n_devices // owners
    rows_out = [tok_rows + extra] + [tok_rows] * (chunks - 1)
    return pl.pallas_call(
        functools.partial(product_kernel, chunks, width, vars_dev),
        grid=(steps,),
        in_specs=[
            pl.BlockSpec(memory_space=pltpu.SMEM),
            pl.BlockSpec((3, tok_rows, owners * group_width), lambda i: (0, 0, i)),
        ],
        out_specs=[pl.BlockSpec((owners, rows, width), lambda i: (i, 0, 0)) for rows in rows_out],
        out_shape=[jax.ShapeDtypeStruct((n_devices, rows, width), bf16) for rows in rows_out],
        compiler_params=pltpu.CompilerParams(vmem_limit_bytes=24 * MIB),
        name="products",
    )(local_rows, streams)


def spectrum_kernel(block, filter_ref, forward_ref, out_ref):
    n_blocks = out_ref.shape[0]
    for index in range(n_blocks):
        taps = filter_ref[:, index * block : (index + 1) * block]
        both = lax.dot_general(
            forward_ref[...], taps, (((1,), (1,)), ((), ())), preferred_element_type=f32
        )
        out_ref[index] = both[: 2 * block] + both[2 * block :]


def filter_spectrum(taps, forward, block):
    width, length = taps.shape
    n_blocks = length // block
    return pl.pallas_call(
        functools.partial(spectrum_kernel, block),
        in_specs=[whole_spec()] * 2,
        out_specs=whole_spec(),
        out_shape=jax.ShapeDtypeStruct((n_blocks, 2 * block, width), f32),
        compiler_params=pltpu.CompilerParams(vmem_limit_bytes=40 * MIB),
        cost_estimate=pl.CostEstimate(
            flops=8 * block * length * width, bytes_accessed=4 * MIB, transcendentals=0
        ),
        name="filter_spectrum",
    )(taps, forward)


def multiply_tile(points, spectrum_ref, joint, start, lanes):
    n_blocks, double, _ = points.shape
    upper = pl.ds(start, half_tile)
    lower = pl.ds(pl.multiple_of(double // 2 + start, half_tile), half_tile)
    signal = [(points[k, upper, lanes], points[k, lower, lanes]) for k in range(n_blocks)]
    signal = [(a_re, a_im, a_re + a_im) for a_re, a_im in signal]
    taps = [(spectrum_ref[k, upper, lanes], spectrum_ref[k, lower, lanes]) for k in range(n_blocks)]
    taps = [(b_re, b_im - b_re, b_re + b_im) for b_re, b_im in taps]
    before_re = jnp.zeros_like(signal[0][0])
    before_im = before_re
    for total in range(n_blocks):
        first = second = third = None
        for delay in range(total + 1):
            a_re, a_im, a_sum = signal[total - delay]
            b_re, b_less, b_sum = taps[delay]
            one, two, three = b_re * a_sum, a_re * b_less, a_im * b_sum
            first = one if first is None else first + one
            second = two if second is None else second + two
            third = three if third is None else third + three
        sum_re, sum_im = first - third, first + second
        joint[total, upper, lanes] = sum_re + before_im
        joint[total, lower, lanes] = sum_im - before_re
        before_re, before_im = sum_re, sum_im


def multiply_points(points, spectrum_ref, joint):
    n_blocks, double, width = points.shape
    lanes_step = min(width, lane_tile)

    def multiply_step(step, carry):
        start = pl.multiple_of(step * half_tile, half_tile)
        for first in range(0, width, lanes_step):
            multiply_tile(points, spectrum_ref, joint, start, slice(first, first + lanes_step))
        return carry

    lax.fori_loop(0, double // 2 // half_tile, multiply_step, 0)


def convolve(chunk_ref, spectrum_ref, forward_ref, inverse_ref, out_ref, points, tok_rows):
    n_blocks, double, width = points.shape
    block = double // 2
    per_block = block // tok_rows
    group = max(1, min(n_blocks, 256 // width)) if width % lane_tile == 0 else 1

    def forward_step(step, carry):
        pieces = []
        for member in range(group):
            start = (step * group + member) * per_block
            rows = chunk_ref[pl.ds(start, per_block), :tok_rows, :]
            pieces.append(rows.reshape(block, width))
        signal = pieces[0] if group == 1 else jnp.concatenate(pieces, axis=1)
        both = jnp.dot(forward_ref[...], signal, preferred_element_type=f32)
        total = both[:double] + both[double:]
        for member in range(group):
            points[step * group + member] = total[:, member * width : (member + 1) * width]
        return carry

    lax.fori_loop(0, n_blocks // group, forward_step, 0)

    multiply_points(points, spectrum_ref, points)

    def inverse_step(step, carry):
        first = step * group
        pieces = [points[first + member] for member in range(group)]
        highs, lows = split_bf16(pieces[0] if group == 1 else jnp.concatenate(pieces, axis=1))
        both = jnp.dot(inverse_ref[...], highs, preferred_element_type=f32)
        rest = jnp.dot(inverse_ref[:block, :], lows, preferred_element_type=f32)
        result = (both[:block] + both[block:] + rest).astype(bf16)
        for member in range(group):
            piece = result[:, member * width : (member + 1) * width]
            out_ref[pl.ds((first + member) * per_block, per_block), :tok_rows, :] = piece.reshape(
                per_block, tok_rows, width
            )
        return carry

    lax.fori_loop(0, n_blocks // group, inverse_step, 0)


def score_rows(index, vars_dev, tok_rows, positions, gate_block, out_ref, gain_row, unembed):
    n_devices, extra, width = gate_block.shape
    gates = gate_block.astype(f32)
    place = lax.broadcasted_iota(jnp.int32, (n_devices, extra, width), 1)
    picked = [
        jnp.sum(jnp.where(place == index * vars_dev + var, gates, 0.0), axis=1)
        for var in range(vars_dev)
    ]
    gate_rows = picked[0] if vars_dev == 1 else jnp.concatenate(picked, axis=0)
    length = n_devices * tok_rows
    column = lax.broadcasted_iota(jnp.int32, (positions.shape[0], length), 1)
    picker = (column == positions).astype(f32).astype(bf16)
    filtered = jnp.dot(
        picker, out_ref[:, :tok_rows, :].reshape(length, width), preferred_element_type=f32
    )
    rows = (gate_rows * filtered).astype(bf16).astype(f32)
    weighted = (rows * gain_row).astype(bf16)
    return jnp.dot(weighted, unembed, preferred_element_type=f32), rows * rows


def pack_scores(raw, squares, raw_parts, vars_dev, packed, n_devices):
    total, width = packed.shape
    extra = total // n_devices
    per_row = raw.shape[1] // width
    count = raw_parts * per_row + 2
    packed[...] = jnp.zeros_like(packed)
    for var in range(vars_dev):
        mine = slice(var * n_devices, (var + 1) * n_devices)
        pieces = [raw[mine, r * width : (r + 1) * width] for r in range(per_row)]
        rounded = [piece.astype(bf16).astype(f32) for piece in pieces]
        rows = rounded + [piece - high for piece, high in zip(pieces, rounded)][: (raw_parts - 1) * per_row]
        high = squares[mine].astype(bf16).astype(f32)
        rows += [high, squares[mine] - high]
        for row, piece in enumerate(rows):
            packed[pl.ds(var * count + row, n_devices, stride=extra), :] = piece


def chunk_kernel(index, chunks, vars_dev, tok_rows, *refs):
    refs = list(refs)
    chunk_ref, spectrum_ref, forward_ref, inverse_ref = refs[:4]
    positions_ref, gain_ref, unembed_ref = refs[4:7]
    refs = refs[7:]
    first, last = index == 0, index == chunks - 1
    gates_ref = None if first else refs.pop(0)
    raw_before, square_before = (None, None) if first else (refs.pop(0), refs.pop(0))
    out_ref = refs.pop(0)
    raw_out, square_out = (None, None) if last else (refs.pop(0), refs.pop(0))
    gates_out = refs.pop(0) if first and not last else None
    points = refs[0]
    convolve(chunk_ref, spectrum_ref, forward_ref, inverse_ref, out_ref, points, tok_rows)
    gate_block = chunk_ref[:, tok_rows:, :] if first else gates_ref[...]
    raw, squares = score_rows(
        index, vars_dev, tok_rows, positions_ref[...], gate_block, out_ref, gain_ref[...], unembed_ref[...]
    )
    if not first:
        raw = raw + raw_before[...]
        squares = squares + square_before[...]
    if gates_out is not None:
        gates_out[...] = gate_block
    if not last:
        raw_out[...] = raw
        square_out[...] = squares
        return
    packed = refs[1]
    n_devices, _, width = out_ref.shape
    extra = out_ref.shape[1] - tok_rows
    pack_scores(raw, squares, 2, vars_dev, packed, n_devices)
    out_ref[:, tok_rows:, :] = packed[...].reshape(n_devices, extra, width).astype(bf16)


def filter_chunk(index, chunks, vars_dev, tok_rows, extra, operands, carried):
    moved, spectrum = operands[:2]
    n_devices, _, width = moved.shape
    n_blocks, double, _ = spectrum.shape
    vocab = operands[6].shape[1]
    n_vars = operands[4].shape[0]
    first, last = index == 0, index == chunks - 1
    rows_out = tok_rows + (extra if last else 0)
    out_shape = [jax.ShapeDtypeStruct((n_devices, rows_out, width), bf16)]
    scratch = [pltpu.VMEM((n_blocks, double, width), f32)]
    if last:
        scratch.append(pltpu.VMEM((n_devices * extra, width), f32))
    else:
        out_shape.append(jax.ShapeDtypeStruct((n_vars, vocab), f32))
        out_shape.append(jax.ShapeDtypeStruct((n_vars, width), f32))
    if first and not last:
        out_shape.append(jax.ShapeDtypeStruct((n_devices, moved.shape[1] - tok_rows, width), bf16))
    flops = 2 * width * n_blocks * (double * double * 5 // 2 + 4 * n_blocks * double)
    return pl.pallas_call(
        functools.partial(chunk_kernel, index, chunks, vars_dev, tok_rows),
        in_specs=[whole_spec()] * (len(operands) + len(carried)),
        out_specs=[whole_spec()] * len(out_shape),
        out_shape=out_shape,
        scratch_shapes=scratch,
        compiler_params=pltpu.CompilerParams(vmem_limit_bytes=(20 if n_blocks <= 8 else 58) * MIB),
        cost_estimate=pl.CostEstimate(flops=flops, bytes_accessed=8 * MIB, transcendentals=0),
        name="filter_chunk",
    )(*operands, *carried)


def final_scores(sums, raw_parts, vars_dev, vocab, model_width, ref_ref, alt_ref):
    width = sums.shape[1]
    per_row = vocab // width
    count = raw_parts * per_row + 2
    ids = lax.broadcasted_iota(jnp.int32, (per_row, width), 0) * width
    ids += lax.broadcasted_iota(jnp.int32, (per_row, width), 1)
    row = lax.broadcasted_iota(jnp.int32, (vars_dev, 2), 0)
    column = lax.broadcasted_iota(jnp.int32, (vars_dev, 2), 1)
    scores = jnp.zeros((vars_dev, 2), f32)

    def whole_sum(values):
        return jnp.sum(jnp.sum(values, axis=1, keepdims=True), axis=0, keepdims=True)

    for var in range(vars_dev):
        base = var * count
        raw = sums[base : base + per_row, :]
        if raw_parts == 2:
            raw = raw + sums[base + per_row : base + 2 * per_row, :]
        square = whole_sum(sums[base + count - 2 : base + count, :])
        logits = raw * lax.rsqrt(square / model_width + norm_eps)
        largest = jnp.max(jnp.max(logits, axis=1, keepdims=True), axis=0, keepdims=True)
        log_total = largest + jnp.log(whole_sum(jnp.exp(logits - largest)))
        ref_logit = whole_sum(jnp.where(ids == ref_ref[var], logits, 0.0))
        alt_logit = whole_sum(jnp.where(ids == alt_ref[var], logits, 0.0))
        pair = jnp.where(column == 0, ref_logit - log_total, alt_logit - ref_logit)
        scores = jnp.where(row == var, pair, scores)
    return scores


def finish_kernel(chunks, vars_dev, vocab, ref_ref, alt_ref, streams_ref, *refs):
    back_refs, mixed_ref, scores_ref, sums = refs[:chunks], refs[chunks], refs[chunks + 1], refs[chunks + 2]
    tok_rows = streams_ref.shape[1]
    owners, _, width = back_refs[0].shape
    step = pl.program_id(0)
    for owner in range(owners):
        for chunk in range(chunks):
            lanes = pl.ds((owner * chunks + chunk) * width, width)
            gate = streams_ref[0, :, lanes].astype(f32)
            filtered = back_refs[chunk][owner, :tok_rows, :].astype(f32)
            mixed_ref[:, lanes] = (gate * filtered).astype(bf16)
    part = jnp.sum(back_refs[-1][:, tok_rows:, :].astype(f32), axis=0)

    @pl.when(step == 0)
    def _():
        sums[...] = part

    @pl.when(step > 0)
    def _():
        sums[...] += part

    @pl.when(step == pl.num_programs(0) - 1)
    def _():
        model_width = pl.num_programs(0) * owners * chunks * width
        scores_ref[...] = final_scores(sums[...], 2, vars_dev, vocab, model_width, ref_ref, alt_ref)


def finish(streams, backs, ref_ids, alt_ids, vocab):
    _, tok_rows, model_width = streams.shape
    chunks = len(backs)
    n_devices, _, width = backs[0].shape
    vars_dev = ref_ids.shape[0]
    owners = max(1, n_devices // 4)
    while owners * chunks * width % lane_tile:
        owners *= 2
    extra = backs[-1].shape[1] - tok_rows
    return pl.pallas_call(
        functools.partial(finish_kernel, chunks, vars_dev, vocab),
        grid=(n_devices // owners,),
        in_specs=[
            pl.BlockSpec(memory_space=pltpu.SMEM),
            pl.BlockSpec(memory_space=pltpu.SMEM),
            pl.BlockSpec((1, tok_rows, owners * chunks * width), lambda i: (0, 0, i)),
        ]
        + [pl.BlockSpec((owners, back.shape[1], width), lambda i: (i, 0, 0)) for back in backs],
        out_specs=[
            pl.BlockSpec((tok_rows, owners * chunks * width), lambda i: (0, i)),
            pl.BlockSpec((vars_dev, 2), lambda i: (0, 0)),
        ],
        out_shape=[
            jax.ShapeDtypeStruct((tok_rows, model_width), bf16),
            jax.ShapeDtypeStruct((vars_dev, 2), f32),
        ],
        scratch_shapes=[pltpu.VMEM((extra, width), f32)],
        compiler_params=pltpu.CompilerParams(vmem_limit_bytes=24 * MIB),
        name="finish",
    )(ref_ids, alt_ids, streams, *backs)

def stacked_products_kernel(halves, vars_dev, offsets_ref, streams_ref, out_ref, *scratch):
    gates, pairs, built, offsets, gate_sems, pair_sems, out_sems, offset_sem = scratch
    n_devices = built.shape[0]
    pieces, _, tok_rows, lanes_each = pairs.shape
    body = halves * tok_rows
    width = halves * lane_tile
    owners = lanes_each // width
    me = lax.axis_index("seq")
    slot = tok_rows // vars_dev

    def pair_copy(piece):
        lanes = pl.ds(piece * lanes_each, lanes_each)
        return pltpu.make_async_copy(
            streams_ref.at[pl.ds(1, 2), :, lanes], pairs.at[piece], pair_sems.at[piece]
        )


    def out_copy(owner):
        return pltpu.make_async_copy(built.at[owner], out_ref.at[owner], out_sems.at[owner])

    def gate_copy(var):
        start = pl.multiple_of(local_rows[var] // row_tile * row_tile, row_tile)
        return pltpu.make_async_copy(
            streams_ref.at[0, pl.ds(start, row_tile), :], gates.at[var], gate_sems.at[var]
        )

    offset_copy = pltpu.make_async_copy(offsets_ref, offsets, offset_sem.at[0])
    offset_copy.start()
    for piece in range(pieces):
        pair_copy(piece).start()
    offset_copy.wait()
    local_rows = [var * slot + offsets[me * vars_dev + var] for var in range(vars_dev)]
    for var in range(vars_dev):
        gate_copy(var).start()
    extra = built.shape[1] - body
    row = lax.broadcasted_iota(jnp.int32, gates.shape[1:], 0)
    place = lax.broadcasted_iota(jnp.int32, (extra, lane_tile), 0)
    gate_rows = []
    for var in range(vars_dev):
        gate_copy(var).wait()
        mine = jnp.where(row == local_rows[var] % row_tile, gates[var].astype(f32), 0.0)
        gate_rows.append(jnp.sum(mine, axis=0, keepdims=True))
    for piece in range(pieces):
        pair_copy(piece).wait()
        for member in range(owners):
            owner = piece * owners + member
            tail = jnp.zeros((extra, lane_tile), f32)
            for half in range(halves):
                lanes = slice(member * width + half * lane_tile, member * width + (half + 1) * lane_tile)
                rows = slice(half * tok_rows, (half + 1) * tok_rows)
                built[owner, rows, :] = pairs[piece, 0, :, lanes] * pairs[piece, 1, :, lanes]
                start = owner * width + half * lane_tile
                for var in range(vars_dev):
                    mine = gate_rows[var][:, start : start + lane_tile]
                    tail = jnp.where(place == half * vars_dev + var, mine, tail)
            built[owner, body:, :] = tail.astype(bf16)
            out_copy(owner).start()
    for owner in range(n_devices):
        out_copy(owner).wait()


def stacked_products(offsets, streams, vars_dev, n_devices, extra):
    _, tok_rows, model_width = streams.shape
    halves = model_width // n_devices // lane_tile
    rows_out = halves * tok_rows + extra
    pieces = math.gcd(n_devices, 8)
    return pl.pallas_call(
        functools.partial(stacked_products_kernel, halves, vars_dev),
        in_specs=[pl.BlockSpec(memory_space=pl.ANY)] * 2,
        out_specs=pl.BlockSpec(memory_space=pl.ANY),
        out_shape=jax.ShapeDtypeStruct((n_devices, rows_out, lane_tile), bf16),
        scratch_shapes=[
            pltpu.VMEM((vars_dev, row_tile, model_width), bf16),
            pltpu.VMEM((pieces, 2, tok_rows, model_width // pieces), bf16),
            pltpu.VMEM((n_devices, rows_out, lane_tile), bf16),
            pltpu.SMEM(offsets.shape, jnp.int32),
            pltpu.SemaphoreType.DMA((vars_dev,)),
            pltpu.SemaphoreType.DMA((pieces,)),
            pltpu.SemaphoreType.DMA((n_devices,)),
            pltpu.SemaphoreType.DMA((1,)),
        ],
        compiler_params=pltpu.CompilerParams(vmem_limit_bytes=60 * MIB),
        cost_estimate=pl.CostEstimate(
            flops=tok_rows * model_width, bytes_accessed=6 * tok_rows * model_width, transcendentals=0
        ),
        name="stacked_products",
    )(offsets, streams)


def stacked_filter_kernel(vars_dev, halves, tok_rows, *refs):
    positions_ref, gain_ref, forward, inverse, unembed, taps, arrived = refs[:7]
    out_ref, points, joint, spectrum, packed, leaving, body_sems, tail_sem = refs[7:]
    n_devices = arrived.shape[0]
    body = halves * tok_rows
    n_blocks, double, width = points.shape
    block = double // 2
    per_block = block // tok_rows
    group = math.gcd(n_blocks, 4)

    def body_copy(rank):
        rows = pl.ds(0, body)
        return pltpu.make_async_copy(leaving.at[rank, rows], out_ref.at[rank, rows], body_sems.at[rank])

    for step in range(0, n_blocks, group):
        filters = [taps[:, index * block : (index + 1) * block] for index in range(step, step + group)]
        both = lax.dot_general(
            forward[...],
            jnp.concatenate(filters, axis=0),
            (((1,), (1,)), ((), ())),
            preferred_element_type=f32,
        )
        total = both[:double] + both[double:]
        for member in range(group):
            spectrum[step + member] = total[:, member * width : (member + 1) * width]

    for step in range(0, n_blocks, group):
        pieces = []
        for index in range(step, step + group):
            for half in range(halves):
                rows = slice(half * tok_rows, (half + 1) * tok_rows)
                parts = [arrived[index * per_block + m, rows, :] for m in range(per_block)]
                pieces.append(jnp.concatenate(parts, axis=0))
        signal = jnp.concatenate(pieces, axis=1)
        both = jnp.dot(forward[...], signal, preferred_element_type=f32)
        total = both[:double] + both[double:]
        for member in range(group):
            points[step + member] = total[:, member * width : (member + 1) * width]
    multiply_points(points, spectrum, joint)

    row = lax.broadcasted_iota(jnp.int32, (tok_rows, width), 0)
    rows_of = [[None] * n_devices for _ in range(vars_dev)]
    group = math.gcd(n_blocks, 2)
    for step in range(0, n_blocks, group):
        highs, lows = split_bf16(jnp.concatenate([joint[step + m] for m in range(group)], axis=1))
        both = jnp.dot(inverse[...], highs, preferred_element_type=f32)
        rest = jnp.dot(inverse[:block, :], lows, preferred_element_type=f32)
        result = (both[:block] + both[block:] + rest).astype(bf16)
        for index in range(group):
            for member in range(per_block):
                device = (step + index) * per_block + member
                piece = result[
                    member * tok_rows : (member + 1) * tok_rows, index * width : (index + 1) * width
                ]
                for half in range(halves):
                    leaving[device, half * tok_rows : (half + 1) * tok_rows, :] = piece[
                        :, half * lane_tile : (half + 1) * lane_tile
                    ]
                body_copy(device).start()
                for var in range(vars_dev):
                    spot = var * n_devices + device
                    local = positions_ref[spot : spot + 1, :] - device * tok_rows
                    mine = jnp.where(row == local, piece.astype(f32), 0.0)
                    rows_of[var][device] = jnp.sum(mine, axis=0, keepdims=True)

    picked_rows = jnp.concatenate([mine for rows in rows_of for mine in rows], axis=0)
    tails = arrived[:, body:, :].astype(f32)
    place = lax.broadcasted_iota(jnp.int32, tails.shape, 1)
    raw = None
    squares = None
    for half in range(halves):
        lanes = slice(half * lane_tile, (half + 1) * lane_tile)
        picked = [
            jnp.sum(jnp.where(place == half * vars_dev + var, tails, 0.0), axis=1)
            for var in range(vars_dev)
        ]
        gate_rows = picked[0] if vars_dev == 1 else jnp.concatenate(picked, axis=0)
        rows = (gate_rows * picked_rows[:, lanes]).astype(bf16).astype(f32)
        weighted = (rows * gain_ref[:, lanes]).astype(bf16)
        part = jnp.dot(weighted, unembed[lanes, :], preferred_element_type=f32)
        raw = part if raw is None else raw + part
        squares = rows * rows if squares is None else squares + rows * rows
    pack_scores(raw, squares, 2, vars_dev, packed, n_devices)
    extra = packed.shape[0] // n_devices
    leaving[:, body:, :] = packed[...].reshape(n_devices, extra, lane_tile).astype(bf16)
    rows = pl.ds(body, extra)
    tail_copy = pltpu.make_async_copy(leaving.at[:, rows], out_ref.at[:, rows], tail_sem.at[0])
    tail_copy.start()
    for rank in range(n_devices):
        body_copy(rank).wait()
    tail_copy.wait()


def stacked_filter(positions, gain_row, tables, arrived, vars_dev, tok_rows, extra):
    width, length = tables[3].shape
    n_devices = arrived.shape[0]
    double = tables[0].shape[0] // 2
    n_blocks = 2 * length // double
    halves = width // lane_tile
    rows_out = halves * tok_rows + extra
    flops = 2 * width * n_blocks * (double * double * 5 // 2 + 4 * n_blocks * double)
    return pl.pallas_call(
        functools.partial(stacked_filter_kernel, vars_dev, halves, tok_rows),
        in_specs=[whole_spec()] * 7,
        out_specs=pl.BlockSpec(memory_space=pl.ANY),
        out_shape=jax.ShapeDtypeStruct((n_devices, rows_out, lane_tile), bf16),
        scratch_shapes=[pltpu.VMEM((n_blocks, double, width), f32)] * 3
        + [
            pltpu.VMEM((n_devices * extra, lane_tile), f32),
            pltpu.VMEM((n_devices, rows_out, lane_tile), bf16),
            pltpu.SemaphoreType.DMA((n_devices,)),
            pltpu.SemaphoreType.DMA((1,)),
        ],
        compiler_params=pltpu.CompilerParams(vmem_limit_bytes=24 * MIB),
        cost_estimate=pl.CostEstimate(flops=flops, bytes_accessed=8 * MIB, transcendentals=0),
        name="stacked_filter",
    )(positions, gain_row, *tables, arrived)


def stacked_finish_kernel(halves, vars_dev, vocab, ref_ref, alt_ref, gates_ref, back_ref, *refs):
    mixed_ref, scores_ref, results, scores, out_sems, score_sem = refs
    n_devices, tok_rows, width = results.shape

    def out_copy(owner):
        return pltpu.make_async_copy(
            results.at[owner], mixed_ref.at[:, pl.ds(owner * width, width)], out_sems.at[owner]
        )

    sums = None
    for owner in range(n_devices):
        tail = back_ref[owner, halves * tok_rows :, :].astype(f32)
        sums = tail if sums is None else sums + tail
        for half in range(halves):
            lanes = slice(half * lane_tile, (half + 1) * lane_tile)
            start = owner * width + half * lane_tile
            filtered = back_ref[owner, half * tok_rows : (half + 1) * tok_rows, :]
            results[owner, :, lanes] = gates_ref[:, start : start + lane_tile] * filtered
        out_copy(owner).start()
    model_width = n_devices * width
    scores[...] = final_scores(sums, 2, vars_dev, vocab, model_width, ref_ref, alt_ref)
    score_copy = pltpu.make_async_copy(scores, scores_ref, score_sem.at[0])
    score_copy.start()
    for owner in range(n_devices):
        out_copy(owner).wait()
    score_copy.wait()


def stacked_finish(ref_ids, alt_ids, gates, back, vocab):
    tok_rows, model_width = gates.shape
    n_devices = back.shape[0]
    vars_dev = ref_ids.shape[0]
    width = model_width // n_devices
    return pl.pallas_call(
        functools.partial(stacked_finish_kernel, width // lane_tile, vars_dev, vocab),
        in_specs=[pl.BlockSpec(memory_space=pltpu.SMEM)] * 2 + [whole_spec()] * 2,
        out_specs=[pl.BlockSpec(memory_space=pl.ANY)] * 2,
        out_shape=[
            jax.ShapeDtypeStruct((tok_rows, model_width), bf16),
            jax.ShapeDtypeStruct((vars_dev, 2), f32),
        ],
        scratch_shapes=[
            pltpu.VMEM((n_devices, tok_rows, width), bf16),
            pltpu.VMEM((vars_dev, 2), f32),
            pltpu.SemaphoreType.DMA((n_devices,)),
            pltpu.SemaphoreType.DMA((1,)),
        ],
        compiler_params=pltpu.CompilerParams(vmem_limit_bytes=16 * MIB),
        cost_estimate=pl.CostEstimate(
            flops=tok_rows * model_width, bytes_accessed=6 * tok_rows * model_width, transcendentals=0
        ),
        name="stacked_finish",
    )(ref_ids, alt_ids, gates, back)


def transposed(blocks):
    return lax.all_to_all(blocks, "seq", split_axis=0, concat_axis=0, tiled=True)


def shards(streams, long_filter, gain, unembed, offsets, ref_ids, alt_ids):
    n_devices = lax.axis_size("seq")
    my_index = lax.axis_index("seq")
    _, tok_rows, model_width = streams.shape
    group_width = model_width // n_devices
    vars_dev = ref_ids.shape[0]
    vocab = unembed.shape[1]
    chunks = max(1, group_width // lane_tile)
    width = group_width // chunks
    block = tok_rows * block_devices(n_devices, tok_rows)
    forward_np, inverse_np = block_tables(block)
    forward, inverse = jnp.asarray(forward_np), jnp.asarray(inverse_np)

    slot = tok_rows // vars_dev
    starts = jnp.arange(vars_dev, dtype=jnp.int32) * slot
    local_rows = starts + lax.dynamic_slice_in_dim(offsets, my_index * vars_dev, vars_dev)
    by_device = offsets.reshape(n_devices, vars_dev)
    positions = by_device + starts[None, :]
    positions += jnp.arange(n_devices, dtype=jnp.int32)[:, None] * tok_rows
    positions = positions.T.reshape(n_devices * vars_dev, 1)
    my_gain = lax.dynamic_slice_in_dim(gain, my_index * group_width, group_width).astype(f32)

    if chunks * lane_tile == group_width:
        gate_extra = round_up(chunks * vars_dev, row_tile)
        score_extra = round_up(2 * vars_dev * (vocab // lane_tile + 1), row_tile)
        arrived = transposed(stacked_products(offsets, streams, vars_dev, n_devices, gate_extra))
        tables = (forward, inverse, unembed, long_filter)
        gain_row = my_gain[None, :]
        leaving = stacked_filter(positions, gain_row, tables, arrived, vars_dev, tok_rows, score_extra)
        back = transposed(leaving)
        mixed, scores = stacked_finish(ref_ids, alt_ids, streams[0], back, vocab)
        return (mixed, scores.T)

    gate_extra = round_up(chunks * vars_dev, row_tile)
    score_extra = round_up(vars_dev * 2 * (vocab // width + 1), row_tile)
    products = make_products(streams, local_rows, n_devices, chunks, gate_extra)
    moved = [lax.all_to_all(part, "seq", split_axis=0, concat_axis=0, tiled=True) for part in products]
    carried = ()
    backs = []
    for chunk in range(chunks):
        mine = slice(chunk * width, (chunk + 1) * width)
        spectrum = filter_spectrum(long_filter[mine], forward, block)
        operands = (
            moved[chunk], spectrum, forward, inverse, positions,
            my_gain[None, mine], unembed[mine],
        )
        if chunk > 0:
            carried = (gates,) + tuple(carried)
        results = filter_chunk(chunk, chunks, vars_dev, tok_rows, score_extra, operands, carried)
        carried = results[1:3]
        if chunk == 0 and chunks > 1:
            gates = results[3]
        backs.append(lax.all_to_all(results[0], "seq", split_axis=0, concat_axis=0, tiled=True))
    mixed, scores = finish(streams, backs, ref_ids, alt_ids, vocab)
    return (mixed, scores.T)


def solution(mesh):
    placed = (
        P(None, ("grp", "seq"), None),
        P("seq", None),
        P(),
        P("seq", None),
        P("grp"),
        P(("grp", "seq")),
        P(("grp", "seq")),
    )
    return jax.shard_map(
        shards,
        mesh=mesh,
        in_specs=placed,
        out_specs=(P(("grp", "seq"), None), P(None, ("grp", "seq"))),
        check_vma=False,
    )
```

```python
import functools
import math

import jax
import jax.numpy as jnp
import numpy as np
from jax import lax
from jax.experimental import pallas as pl
from jax.experimental.pallas import tpu as pltpu
from jax.sharding import PartitionSpec as P

norm_eps = 1e-06
f32 = jnp.float32
bf16 = jnp.bfloat16
row_tile = 16
half_tile = 8
lane_tile = 128
MIB = 1 << 20


def round_up(value, step):
    return -(-value // step) * step


def split_bf16(values):
    high = values.astype(bf16)
    low = (values - high.astype(f32)).astype(bf16)
    return high, low


def block_tables(block):
    turns = (4 * np.arange(block)[:, None] + 1) * np.arange(block)[None, :] % (4 * block)
    theta = turns * (math.pi / (2 * block))
    table = np.concatenate([np.cos(theta), np.sin(theta)], axis=0)
    parts = []
    for matrix in (table, table.T / block):
        high = matrix.astype(bf16)
        low = (matrix - high.astype(np.float64)).astype(bf16)
        parts.append(np.concatenate([high, low], axis=0))
    return parts


def block_devices(n_devices, tok_rows):
    target = math.isqrt(32 * n_devices * tok_rows)
    count = 1
    while n_devices % (2 * count) == 0 and 2 * count * tok_rows <= target:
        count *= 2
    return count


def whole_spec():
    return pl.BlockSpec(memory_space=pltpu.VMEM)


def product_kernel(chunks, width, vars_dev, rows_ref, streams_ref, *out_refs):
    tok_rows = streams_ref.shape[1]
    n_owners = out_refs[0].shape[0]
    extra = out_refs[0].shape[1] - tok_rows
    place = lax.broadcasted_iota(jnp.int32, (extra, tok_rows), 0)
    column = lax.broadcasted_iota(jnp.int32, (extra, tok_rows), 1)
    for owner in range(n_owners):
        gates = jnp.zeros((extra, width), f32)
        for chunk in range(chunks):
            lanes = pl.ds((owner * chunks + chunk) * width, width)
            left = streams_ref[1, :, lanes].astype(f32)
            right = streams_ref[2, :, lanes].astype(f32)
            out_refs[chunk][owner, :tok_rows, :] = (left * right).astype(bf16)
            picker = jnp.zeros((extra, tok_rows), jnp.bool_)
            for var in range(vars_dev):
                picker |= (place == chunk * vars_dev + var) & (column == rows_ref[var])
            gates += jnp.dot(
                picker.astype(f32).astype(bf16),
                streams_ref[0, :, lanes],
                preferred_element_type=f32,
            )
        out_refs[0][owner, tok_rows:, :] = gates.astype(bf16)


def make_products(streams, local_rows, n_devices, chunks, extra):
    _, tok_rows, model_width = streams.shape
    vars_dev = local_rows.shape[0]
    group_width = model_width // n_devices
    width = group_width // chunks
    owners = max(1, n_devices // 4)
    while owners * group_width % lane_tile:
        owners *= 2
    steps = n_devices // owners
    rows_out = [tok_rows + extra] + [tok_rows] * (chunks - 1)
    return pl.pallas_call(
        functools.partial(product_kernel, chunks, width, vars_dev),
        grid=(steps,),
        in_specs=[
            pl.BlockSpec(memory_space=pltpu.SMEM),
            pl.BlockSpec((3, tok_rows, owners * group_width), lambda i: (0, 0, i)),
        ],
        out_specs=[pl.BlockSpec((owners, rows, width), lambda i: (i, 0, 0)) for rows in rows_out],
        out_shape=[jax.ShapeDtypeStruct((n_devices, rows, width), bf16) for rows in rows_out],
        compiler_params=pltpu.CompilerParams(vmem_limit_bytes=24 * MIB),
        name="products",
    )(local_rows, streams)


def spectrum_kernel(block, filter_ref, forward_ref, out_ref):
    n_blocks = out_ref.shape[0]
    for index in range(n_blocks):
        taps = filter_ref[:, index * block : (index + 1) * block]
        both = lax.dot_general(
            forward_ref[...], taps, (((1,), (1,)), ((), ())), preferred_element_type=f32
        )
        out_ref[index] = both[: 2 * block] + both[2 * block :]


def filter_spectrum(taps, forward, block):
    width, length = taps.shape
    n_blocks = length // block
    return pl.pallas_call(
        functools.partial(spectrum_kernel, block),
        in_specs=[whole_spec()] * 2,
        out_specs=whole_spec(),
        out_shape=jax.ShapeDtypeStruct((n_blocks, 2 * block, width), f32),
        compiler_params=pltpu.CompilerParams(vmem_limit_bytes=40 * MIB),
        cost_estimate=pl.CostEstimate(
            flops=8 * block * length * width, bytes_accessed=4 * MIB, transcendentals=0
        ),
        name="filter_spectrum",
    )(taps, forward)


def multiply_tile(points, spectrum_ref, joint, start, lanes):
    n_blocks, double, _ = points.shape
    upper = pl.ds(start, half_tile)
    lower = pl.ds(pl.multiple_of(double // 2 + start, half_tile), half_tile)
    signal = [(points[k, upper, lanes], points[k, lower, lanes]) for k in range(n_blocks)]
    signal = [(a_re, a_im, a_re + a_im) for a_re, a_im in signal]
    taps = [(spectrum_ref[k, upper, lanes], spectrum_ref[k, lower, lanes]) for k in range(n_blocks)]
    taps = [(b_re, b_im - b_re, b_re + b_im) for b_re, b_im in taps]
    before_re = jnp.zeros_like(signal[0][0])
    before_im = before_re
    for total in range(n_blocks):
        first = second = third = None
        for delay in range(total + 1):
            a_re, a_im, a_sum = signal[total - delay]
            b_re, b_less, b_sum = taps[delay]
            one, two, three = b_re * a_sum, a_re * b_less, a_im * b_sum
            first = one if first is None else first + one
            second = two if second is None else second + two
            third = three if third is None else third + three
        sum_re, sum_im = first - third, first + second
        joint[total, upper, lanes] = sum_re + before_im
        joint[total, lower, lanes] = sum_im - before_re
        before_re, before_im = sum_re, sum_im


def multiply_points(points, spectrum_ref, joint):
    n_blocks, double, width = points.shape
    lanes_step = min(width, lane_tile)

    def multiply_step(step, carry):
        start = pl.multiple_of(step * half_tile, half_tile)
        for first in range(0, width, lanes_step):
            multiply_tile(points, spectrum_ref, joint, start, slice(first, first + lanes_step))
        return carry

    lax.fori_loop(0, double // 2 // half_tile, multiply_step, 0)


def convolve(chunk_ref, spectrum_ref, forward_ref, inverse_ref, out_ref, points, tok_rows):
    n_blocks, double, width = points.shape
    block = double // 2
    per_block = block // tok_rows
    group = max(1, min(n_blocks, 256 // width)) if width % lane_tile == 0 else 1

    def forward_step(step, carry):
        pieces = []
        for member in range(group):
            start = (step * group + member) * per_block
            rows = chunk_ref[pl.ds(start, per_block), :tok_rows, :]
            pieces.append(rows.reshape(block, width))
        signal = pieces[0] if group == 1 else jnp.concatenate(pieces, axis=1)
        both = jnp.dot(forward_ref[...], signal, preferred_element_type=f32)
        total = both[:double] + both[double:]
        for member in range(group):
            points[step * group + member] = total[:, member * width : (member + 1) * width]
        return carry

    lax.fori_loop(0, n_blocks // group, forward_step, 0)

    multiply_points(points, spectrum_ref, points)

    def inverse_step(step, carry):
        first = step * group
        pieces = [points[first + member] for member in range(group)]
        highs, lows = split_bf16(pieces[0] if group == 1 else jnp.concatenate(pieces, axis=1))
        both = jnp.dot(inverse_ref[...], highs, preferred_element_type=f32)
        rest = jnp.dot(inverse_ref[:block, :], lows, preferred_element_type=f32)
        result = (both[:block] + both[block:] + rest).astype(bf16)
        for member in range(group):
            piece = result[:, member * width : (member + 1) * width]
            out_ref[pl.ds((first + member) * per_block, per_block), :tok_rows, :] = piece.reshape(
                per_block, tok_rows, width
            )
        return carry

    lax.fori_loop(0, n_blocks // group, inverse_step, 0)


def score_rows(index, vars_dev, tok_rows, positions, gate_block, out_ref, gain_row, unembed):
    n_devices, extra, width = gate_block.shape
    gates = gate_block.astype(f32)
    place = lax.broadcasted_iota(jnp.int32, (n_devices, extra, width), 1)
    picked = [
        jnp.sum(jnp.where(place == index * vars_dev + var, gates, 0.0), axis=1)
        for var in range(vars_dev)
    ]
    gate_rows = picked[0] if vars_dev == 1 else jnp.concatenate(picked, axis=0)
    length = n_devices * tok_rows
    column = lax.broadcasted_iota(jnp.int32, (positions.shape[0], length), 1)
    picker = (column == positions).astype(f32).astype(bf16)
    filtered = jnp.dot(
        picker, out_ref[:, :tok_rows, :].reshape(length, width), preferred_element_type=f32
    )
    rows = (gate_rows * filtered).astype(bf16).astype(f32)
    weighted = (rows * gain_row).astype(bf16)
    return jnp.dot(weighted, unembed, preferred_element_type=f32), rows * rows


def pack_scores(raw, squares, raw_parts, vars_dev, packed, n_devices):
    total, width = packed.shape
    extra = total // n_devices
    per_row = raw.shape[1] // width
    count = raw_parts * per_row + 2
    packed[...] = jnp.zeros_like(packed)
    for var in range(vars_dev):
        mine = slice(var * n_devices, (var + 1) * n_devices)
        pieces = [raw[mine, r * width : (r + 1) * width] for r in range(per_row)]
        rounded = [piece.astype(bf16).astype(f32) for piece in pieces]
        rows = rounded + [piece - high for piece, high in zip(pieces, rounded)][: (raw_parts - 1) * per_row]
        high = squares[mine].astype(bf16).astype(f32)
        rows += [high, squares[mine] - high]
        for row, piece in enumerate(rows):
            packed[pl.ds(var * count + row, n_devices, stride=extra), :] = piece


def chunk_kernel(index, chunks, vars_dev, tok_rows, *refs):
    refs = list(refs)
    chunk_ref, spectrum_ref, forward_ref, inverse_ref = refs[:4]
    positions_ref, gain_ref, unembed_ref = refs[4:7]
    refs = refs[7:]
    first, last = index == 0, index == chunks - 1
    gates_ref = None if first else refs.pop(0)
    raw_before, square_before = (None, None) if first else (refs.pop(0), refs.pop(0))
    out_ref = refs.pop(0)
    raw_out, square_out = (None, None) if last else (refs.pop(0), refs.pop(0))
    gates_out = refs.pop(0) if first and not last else None
    points = refs[0]
    convolve(chunk_ref, spectrum_ref, forward_ref, inverse_ref, out_ref, points, tok_rows)
    gate_block = chunk_ref[:, tok_rows:, :] if first else gates_ref[...]
    raw, squares = score_rows(
        index, vars_dev, tok_rows, positions_ref[...], gate_block, out_ref, gain_ref[...], unembed_ref[...]
    )
    if not first:
        raw = raw + raw_before[...]
        squares = squares + square_before[...]
    if gates_out is not None:
        gates_out[...] = gate_block
    if not last:
        raw_out[...] = raw
        square_out[...] = squares
        return
    packed = refs[1]
    n_devices, _, width = out_ref.shape
    extra = out_ref.shape[1] - tok_rows
    pack_scores(raw, squares, 2, vars_dev, packed, n_devices)
    out_ref[:, tok_rows:, :] = packed[...].reshape(n_devices, extra, width).astype(bf16)


def filter_chunk(index, chunks, vars_dev, tok_rows, extra, operands, carried):
    moved, spectrum = operands[:2]
    n_devices, _, width = moved.shape
    n_blocks, double, _ = spectrum.shape
    vocab = operands[6].shape[1]
    n_vars = operands[4].shape[0]
    first, last = index == 0, index == chunks - 1
    rows_out = tok_rows + (extra if last else 0)
    out_shape = [jax.ShapeDtypeStruct((n_devices, rows_out, width), bf16)]
    scratch = [pltpu.VMEM((n_blocks, double, width), f32)]
    if last:
        scratch.append(pltpu.VMEM((n_devices * extra, width), f32))
    else:
        out_shape.append(jax.ShapeDtypeStruct((n_vars, vocab), f32))
        out_shape.append(jax.ShapeDtypeStruct((n_vars, width), f32))
    if first and not last:
        out_shape.append(jax.ShapeDtypeStruct((n_devices, moved.shape[1] - tok_rows, width), bf16))
    flops = 2 * width * n_blocks * (double * double * 5 // 2 + 4 * n_blocks * double)
    return pl.pallas_call(
        functools.partial(chunk_kernel, index, chunks, vars_dev, tok_rows),
        in_specs=[whole_spec()] * (len(operands) + len(carried)),
        out_specs=[whole_spec()] * len(out_shape),
        out_shape=out_shape,
        scratch_shapes=scratch,
        compiler_params=pltpu.CompilerParams(vmem_limit_bytes=(20 if n_blocks <= 8 else 58) * MIB),
        cost_estimate=pl.CostEstimate(flops=flops, bytes_accessed=8 * MIB, transcendentals=0),
        name="filter_chunk",
    )(*operands, *carried)


def final_scores(sums, raw_parts, vars_dev, vocab, model_width, ref_ref, alt_ref):
    width = sums.shape[1]
    per_row = vocab // width
    count = raw_parts * per_row + 2
    ids = lax.broadcasted_iota(jnp.int32, (per_row, width), 0) * width
    ids += lax.broadcasted_iota(jnp.int32, (per_row, width), 1)
    row = lax.broadcasted_iota(jnp.int32, (vars_dev, 2), 0)
    column = lax.broadcasted_iota(jnp.int32, (vars_dev, 2), 1)
    scores = jnp.zeros((vars_dev, 2), f32)

    def whole_sum(values):
        return jnp.sum(jnp.sum(values, axis=1, keepdims=True), axis=0, keepdims=True)

    for var in range(vars_dev):
        base = var * count
        raw = sums[base : base + per_row, :]
        if raw_parts == 2:
            raw = raw + sums[base + per_row : base + 2 * per_row, :]
        square = whole_sum(sums[base + count - 2 : base + count, :])
        logits = raw * lax.rsqrt(square / model_width + norm_eps)
        largest = jnp.max(jnp.max(logits, axis=1, keepdims=True), axis=0, keepdims=True)
        log_total = largest + jnp.log(whole_sum(jnp.exp(logits - largest)))
        ref_logit = whole_sum(jnp.where(ids == ref_ref[var], logits, 0.0))
        alt_logit = whole_sum(jnp.where(ids == alt_ref[var], logits, 0.0))
        pair = jnp.where(column == 0, ref_logit - log_total, alt_logit - ref_logit)
        scores = jnp.where(row == var, pair, scores)
    return scores


def finish_kernel(chunks, vars_dev, vocab, ref_ref, alt_ref, streams_ref, *refs):
    back_refs, mixed_ref, scores_ref, sums = refs[:chunks], refs[chunks], refs[chunks + 1], refs[chunks + 2]
    tok_rows = streams_ref.shape[1]
    owners, _, width = back_refs[0].shape
    step = pl.program_id(0)
    for owner in range(owners):
        for chunk in range(chunks):
            lanes = pl.ds((owner * chunks + chunk) * width, width)
            gate = streams_ref[0, :, lanes].astype(f32)
            filtered = back_refs[chunk][owner, :tok_rows, :].astype(f32)
            mixed_ref[:, lanes] = (gate * filtered).astype(bf16)
    part = jnp.sum(back_refs[-1][:, tok_rows:, :].astype(f32), axis=0)

    @pl.when(step == 0)
    def _():
        sums[...] = part

    @pl.when(step > 0)
    def _():
        sums[...] += part

    @pl.when(step == pl.num_programs(0) - 1)
    def _():
        model_width = pl.num_programs(0) * owners * chunks * width
        scores_ref[...] = final_scores(sums[...], 2, vars_dev, vocab, model_width, ref_ref, alt_ref)


def finish(streams, backs, ref_ids, alt_ids, vocab):
    _, tok_rows, model_width = streams.shape
    chunks = len(backs)
    n_devices, _, width = backs[0].shape
    vars_dev = ref_ids.shape[0]
    owners = max(1, n_devices // 4)
    while owners * chunks * width % lane_tile:
        owners *= 2
    extra = backs[-1].shape[1] - tok_rows
    return pl.pallas_call(
        functools.partial(finish_kernel, chunks, vars_dev, vocab),
        grid=(n_devices // owners,),
        in_specs=[
            pl.BlockSpec(memory_space=pltpu.SMEM),
            pl.BlockSpec(memory_space=pltpu.SMEM),
            pl.BlockSpec((1, tok_rows, owners * chunks * width), lambda i: (0, 0, i)),
        ]
        + [pl.BlockSpec((owners, back.shape[1], width), lambda i: (i, 0, 0)) for back in backs],
        out_specs=[
            pl.BlockSpec((tok_rows, owners * chunks * width), lambda i: (0, i)),
            pl.BlockSpec((vars_dev, 2), lambda i: (0, 0)),
        ],
        out_shape=[
            jax.ShapeDtypeStruct((tok_rows, model_width), bf16),
            jax.ShapeDtypeStruct((vars_dev, 2), f32),
        ],
        scratch_shapes=[pltpu.VMEM((extra, width), f32)],
        compiler_params=pltpu.CompilerParams(vmem_limit_bytes=24 * MIB),
        name="finish",
    )(ref_ids, alt_ids, streams, *backs)

def group_order(n_devices):
    quarters = math.gcd(n_devices, 4)
    size = n_devices // quarters
    return [quarter * size + index for index in range(size) for quarter in range(quarters)]


def ranks(n_devices):
    return {device: rank for rank, device in enumerate(group_order(n_devices))}


def stacked_products_kernel(halves, vars_dev, offsets_ref, streams_ref, out_ref, *scratch):
    gates, pairs, built, offsets, gate_sems, pair_sems, out_sems, offset_sem = scratch
    n_devices = built.shape[0]
    rank_of = ranks(n_devices)
    pieces, _, tok_rows, lanes_each = pairs.shape
    body = halves * tok_rows
    width = halves * lane_tile
    owners = lanes_each // width
    me = lax.axis_index("seq")
    slot = tok_rows // vars_dev

    def pair_copy(piece):
        lanes = pl.ds(piece * lanes_each, lanes_each)
        return pltpu.make_async_copy(
            streams_ref.at[pl.ds(1, 2), :, lanes], pairs.at[piece], pair_sems.at[piece]
        )


    def out_copy(owner):
        return pltpu.make_async_copy(built.at[owner], out_ref.at[owner], out_sems.at[owner])

    def gate_copy(var):
        start = pl.multiple_of(local_rows[var] // row_tile * row_tile, row_tile)
        return pltpu.make_async_copy(
            streams_ref.at[0, pl.ds(start, row_tile), :], gates.at[var], gate_sems.at[var]
        )

    offset_copy = pltpu.make_async_copy(offsets_ref, offsets, offset_sem.at[0])
    offset_copy.start()
    for piece in range(pieces):
        pair_copy(piece).start()
    offset_copy.wait()
    local_rows = [var * slot + offsets[me * vars_dev + var] for var in range(vars_dev)]
    for var in range(vars_dev):
        gate_copy(var).start()
    extra = built.shape[1] - body
    row = lax.broadcasted_iota(jnp.int32, gates.shape[1:], 0)
    place = lax.broadcasted_iota(jnp.int32, (extra, lane_tile), 0)
    gate_rows = []
    for var in range(vars_dev):
        gate_copy(var).wait()
        mine = jnp.where(row == local_rows[var] % row_tile, gates[var].astype(f32), 0.0)
        gate_rows.append(jnp.sum(mine, axis=0, keepdims=True))
    for piece in range(pieces):
        pair_copy(piece).wait()
        for member in range(owners):
            owner = piece * owners + member
            rank = rank_of[owner]
            tail = jnp.zeros((extra, lane_tile), f32)
            for half in range(halves):
                lanes = slice(member * width + half * lane_tile, member * width + (half + 1) * lane_tile)
                rows = slice(half * tok_rows, (half + 1) * tok_rows)
                built[rank, rows, :] = pairs[piece, 0, :, lanes] * pairs[piece, 1, :, lanes]
                start = owner * width + half * lane_tile
                for var in range(vars_dev):
                    mine = gate_rows[var][:, start : start + lane_tile]
                    tail = jnp.where(place == half * vars_dev + var, mine, tail)
            built[rank, body:, :] = tail.astype(bf16)
            out_copy(rank).start()
    for owner in range(n_devices):
        out_copy(owner).wait()


def stacked_products(offsets, streams, vars_dev, n_devices, extra):
    _, tok_rows, model_width = streams.shape
    halves = model_width // n_devices // lane_tile
    rows_out = halves * tok_rows + extra
    pieces = math.gcd(n_devices, 8)
    return pl.pallas_call(
        functools.partial(stacked_products_kernel, halves, vars_dev),
        in_specs=[pl.BlockSpec(memory_space=pl.ANY)] * 2,
        out_specs=pl.BlockSpec(memory_space=pl.ANY),
        out_shape=jax.ShapeDtypeStruct((n_devices, rows_out, lane_tile), bf16),
        scratch_shapes=[
            pltpu.VMEM((vars_dev, row_tile, model_width), bf16),
            pltpu.VMEM((pieces, 2, tok_rows, model_width // pieces), bf16),
            pltpu.VMEM((n_devices, rows_out, lane_tile), bf16),
            pltpu.SMEM(offsets.shape, jnp.int32),
            pltpu.SemaphoreType.DMA((vars_dev,)),
            pltpu.SemaphoreType.DMA((pieces,)),
            pltpu.SemaphoreType.DMA((n_devices,)),
            pltpu.SemaphoreType.DMA((1,)),
        ],
        compiler_params=pltpu.CompilerParams(vmem_limit_bytes=60 * MIB),
        cost_estimate=pl.CostEstimate(
            flops=tok_rows * model_width, bytes_accessed=6 * tok_rows * model_width, transcendentals=0
        ),
        name="stacked_products",
    )(offsets, streams)


def stacked_filter_kernel(vars_dev, halves, tok_rows, *refs):
    positions_ref, gain_ref, forward, inverse, unembed, taps, arrived = refs[:7]
    out_ref, points, joint, spectrum, packed, leaving, body_sems, tail_sem = refs[7:]
    n_devices = arrived.shape[0]
    rank_of = ranks(n_devices)
    body = halves * tok_rows
    n_blocks, double, width = points.shape
    block = double // 2
    per_block = block // tok_rows
    group = math.gcd(n_blocks, 4)

    def body_copy(rank):
        rows = pl.ds(0, body)
        return pltpu.make_async_copy(leaving.at[rank, rows], out_ref.at[rank, rows], body_sems.at[rank])

    for step in range(0, n_blocks, group):
        filters = [taps[:, index * block : (index + 1) * block] for index in range(step, step + group)]
        both = lax.dot_general(
            forward[...],
            jnp.concatenate(filters, axis=0),
            (((1,), (1,)), ((), ())),
            preferred_element_type=f32,
        )
        total = both[:double] + both[double:]
        for member in range(group):
            spectrum[step + member] = total[:, member * width : (member + 1) * width]

    for step in range(0, n_blocks, group):
        pieces = []
        for index in range(step, step + group):
            for half in range(halves):
                rows = slice(half * tok_rows, (half + 1) * tok_rows)
                parts = [arrived[rank_of[index * per_block + m], rows, :] for m in range(per_block)]
                pieces.append(jnp.concatenate(parts, axis=0))
        signal = jnp.concatenate(pieces, axis=1)
        both = jnp.dot(forward[...], signal, preferred_element_type=f32)
        total = both[:double] + both[double:]
        for member in range(group):
            points[step + member] = total[:, member * width : (member + 1) * width]
    multiply_points(points, spectrum, joint)

    row = lax.broadcasted_iota(jnp.int32, (tok_rows, width), 0)
    rows_of = [[None] * n_devices for _ in range(vars_dev)]
    group = math.gcd(n_blocks, 2)
    for step in range(0, n_blocks, group):
        highs, lows = split_bf16(jnp.concatenate([joint[step + m] for m in range(group)], axis=1))
        both = jnp.dot(inverse[...], highs, preferred_element_type=f32)
        rest = jnp.dot(inverse[:block, :], lows, preferred_element_type=f32)
        result = (both[:block] + both[block:] + rest).astype(bf16)
        for index in range(group):
            for member in range(per_block):
                device = (step + index) * per_block + member
                rank = rank_of[device]
                piece = result[
                    member * tok_rows : (member + 1) * tok_rows, index * width : (index + 1) * width
                ]
                for half in range(halves):
                    leaving[rank, half * tok_rows : (half + 1) * tok_rows, :] = piece[
                        :, half * lane_tile : (half + 1) * lane_tile
                    ]
                body_copy(rank).start()
                for var in range(vars_dev):
                    spot = var * n_devices + device
                    local = positions_ref[spot : spot + 1, :] - device * tok_rows
                    mine = jnp.where(row == local, piece.astype(f32), 0.0)
                    rows_of[var][rank] = jnp.sum(mine, axis=0, keepdims=True)

    picked_rows = jnp.concatenate([mine for rows in rows_of for mine in rows], axis=0)
    tails = arrived[:, body:, :].astype(f32)
    place = lax.broadcasted_iota(jnp.int32, tails.shape, 1)
    raw = None
    squares = None
    for half in range(halves):
        lanes = slice(half * lane_tile, (half + 1) * lane_tile)
        picked = [
            jnp.sum(jnp.where(place == half * vars_dev + var, tails, 0.0), axis=1)
            for var in range(vars_dev)
        ]
        gate_rows = picked[0] if vars_dev == 1 else jnp.concatenate(picked, axis=0)
        rows = (gate_rows * picked_rows[:, lanes]).astype(bf16).astype(f32)
        weighted = (rows * gain_ref[:, lanes]).astype(bf16)
        part = jnp.dot(weighted, unembed[lanes, :], preferred_element_type=f32)
        raw = part if raw is None else raw + part
        squares = rows * rows if squares is None else squares + rows * rows
    pack_scores(raw, squares, 2, vars_dev, packed, n_devices)
    extra = packed.shape[0] // n_devices
    leaving[:, body:, :] = packed[...].reshape(n_devices, extra, lane_tile).astype(bf16)
    rows = pl.ds(body, extra)
    tail_copy = pltpu.make_async_copy(leaving.at[:, rows], out_ref.at[:, rows], tail_sem.at[0])
    tail_copy.start()
    for rank in range(n_devices):
        body_copy(rank).wait()
    tail_copy.wait()


def stacked_filter(positions, gain_row, tables, arrived, vars_dev, tok_rows, extra):
    width, length = tables[3].shape
    n_devices = arrived.shape[0]
    double = tables[0].shape[0] // 2
    n_blocks = 2 * length // double
    halves = width // lane_tile
    rows_out = halves * tok_rows + extra
    flops = 2 * width * n_blocks * (double * double * 5 // 2 + 4 * n_blocks * double)
    return pl.pallas_call(
        functools.partial(stacked_filter_kernel, vars_dev, halves, tok_rows),
        in_specs=[whole_spec()] * 7,
        out_specs=pl.BlockSpec(memory_space=pl.ANY),
        out_shape=jax.ShapeDtypeStruct((n_devices, rows_out, lane_tile), bf16),
        scratch_shapes=[pltpu.VMEM((n_blocks, double, width), f32)] * 3
        + [
            pltpu.VMEM((n_devices * extra, lane_tile), f32),
            pltpu.VMEM((n_devices, rows_out, lane_tile), bf16),
            pltpu.SemaphoreType.DMA((n_devices,)),
            pltpu.SemaphoreType.DMA((1,)),
        ],
        compiler_params=pltpu.CompilerParams(vmem_limit_bytes=24 * MIB),
        cost_estimate=pl.CostEstimate(flops=flops, bytes_accessed=8 * MIB, transcendentals=0),
        name="stacked_filter",
    )(positions, gain_row, *tables, arrived)


def stacked_finish_kernel(halves, vars_dev, vocab, ref_ref, alt_ref, gates_ref, back_ref, *refs):
    mixed_ref, scores_ref, results, scores, out_sems, score_sem = refs
    n_devices, tok_rows, width = results.shape
    rank_of = ranks(n_devices)

    def out_copy(owner):
        return pltpu.make_async_copy(
            results.at[owner], mixed_ref.at[:, pl.ds(owner * width, width)], out_sems.at[owner]
        )

    sums = None
    for owner in range(n_devices):
        tail = back_ref[rank_of[owner], halves * tok_rows :, :].astype(f32)
        sums = tail if sums is None else sums + tail
        for half in range(halves):
            lanes = slice(half * lane_tile, (half + 1) * lane_tile)
            start = owner * width + half * lane_tile
            filtered = back_ref[rank_of[owner], half * tok_rows : (half + 1) * tok_rows, :]
            results[owner, :, lanes] = gates_ref[:, start : start + lane_tile] * filtered
        out_copy(owner).start()
    model_width = n_devices * width
    scores[...] = final_scores(sums, 2, vars_dev, vocab, model_width, ref_ref, alt_ref)
    score_copy = pltpu.make_async_copy(scores, scores_ref, score_sem.at[0])
    score_copy.start()
    for owner in range(n_devices):
        out_copy(owner).wait()
    score_copy.wait()


def stacked_finish(ref_ids, alt_ids, gates, back, vocab):
    tok_rows, model_width = gates.shape
    n_devices = back.shape[0]
    vars_dev = ref_ids.shape[0]
    width = model_width // n_devices
    return pl.pallas_call(
        functools.partial(stacked_finish_kernel, width // lane_tile, vars_dev, vocab),
        in_specs=[pl.BlockSpec(memory_space=pltpu.SMEM)] * 2 + [whole_spec()] * 2,
        out_specs=[pl.BlockSpec(memory_space=pl.ANY)] * 2,
        out_shape=[
            jax.ShapeDtypeStruct((tok_rows, model_width), bf16),
            jax.ShapeDtypeStruct((vars_dev, 2), f32),
        ],
        scratch_shapes=[
            pltpu.VMEM((n_devices, tok_rows, width), bf16),
            pltpu.VMEM((vars_dev, 2), f32),
            pltpu.SemaphoreType.DMA((n_devices,)),
            pltpu.SemaphoreType.DMA((1,)),
        ],
        compiler_params=pltpu.CompilerParams(vmem_limit_bytes=16 * MIB),
        cost_estimate=pl.CostEstimate(
            flops=tok_rows * model_width, bytes_accessed=6 * tok_rows * model_width, transcendentals=0
        ),
        name="stacked_finish",
    )(ref_ids, alt_ids, gates, back)


def transposed(blocks):
    groups = [group_order(blocks.shape[0])]
    return lax.all_to_all(
        blocks, "seq", split_axis=0, concat_axis=0, axis_index_groups=groups, tiled=True
    )


def shards(streams, long_filter, gain, unembed, offsets, ref_ids, alt_ids):
    n_devices = lax.axis_size("seq")
    my_index = lax.axis_index("seq")
    _, tok_rows, model_width = streams.shape
    group_width = model_width // n_devices
    vars_dev = ref_ids.shape[0]
    vocab = unembed.shape[1]
    chunks = max(1, group_width // lane_tile)
    width = group_width // chunks
    block = tok_rows * block_devices(n_devices, tok_rows)
    forward_np, inverse_np = block_tables(block)
    forward, inverse = jnp.asarray(forward_np), jnp.asarray(inverse_np)

    slot = tok_rows // vars_dev
    starts = jnp.arange(vars_dev, dtype=jnp.int32) * slot
    local_rows = starts + lax.dynamic_slice_in_dim(offsets, my_index * vars_dev, vars_dev)
    by_device = offsets.reshape(n_devices, vars_dev)
    positions = by_device + starts[None, :]
    positions += jnp.arange(n_devices, dtype=jnp.int32)[:, None] * tok_rows
    positions = positions.T.reshape(n_devices * vars_dev, 1)
    my_gain = lax.dynamic_slice_in_dim(gain, my_index * group_width, group_width).astype(f32)

    if chunks * lane_tile == group_width:
        gate_extra = round_up(chunks * vars_dev, row_tile)
        score_extra = round_up(2 * vars_dev * (vocab // lane_tile + 1), row_tile)
        arrived = transposed(stacked_products(offsets, streams, vars_dev, n_devices, gate_extra))
        tables = (forward, inverse, unembed, long_filter)
        gain_row = my_gain[None, :]
        leaving = stacked_filter(positions, gain_row, tables, arrived, vars_dev, tok_rows, score_extra)
        back = transposed(leaving)
        mixed, scores = stacked_finish(ref_ids, alt_ids, streams[0], back, vocab)
        return (mixed, scores.T)

    gate_extra = round_up(chunks * vars_dev, row_tile)
    score_extra = round_up(vars_dev * 2 * (vocab // width + 1), row_tile)
    products = make_products(streams, local_rows, n_devices, chunks, gate_extra)
    moved = [lax.all_to_all(part, "seq", split_axis=0, concat_axis=0, tiled=True) for part in products]
    carried = ()
    backs = []
    for chunk in range(chunks):
        mine = slice(chunk * width, (chunk + 1) * width)
        spectrum = filter_spectrum(long_filter[mine], forward, block)
        operands = (
            moved[chunk], spectrum, forward, inverse, positions,
            my_gain[None, mine], unembed[mine],
        )
        if chunk > 0:
            carried = (gates,) + tuple(carried)
        results = filter_chunk(chunk, chunks, vars_dev, tok_rows, score_extra, operands, carried)
        carried = results[1:3]
        if chunk == 0 and chunks > 1:
            gates = results[3]
        backs.append(lax.all_to_all(results[0], "seq", split_axis=0, concat_axis=0, tiled=True))
    mixed, scores = finish(streams, backs, ref_ids, alt_ids, vocab)
    return (mixed, scores.T)


def solution(mesh):
    placed = (
        P(None, ("grp", "seq"), None),
        P("seq", None),
        P(),
        P("seq", None),
        P("grp"),
        P(("grp", "seq")),
        P(("grp", "seq")),
    )
    return jax.shard_map(
        shards,
        mesh=mesh,
        in_specs=placed,
        out_specs=(P(("grp", "seq"), None), P(None, ("grp", "seq"))),
        check_vma=False,
    )
```

```python
import functools
import math

import jax
import jax.numpy as jnp
import numpy as np
from jax import lax
from jax.experimental import pallas as pl
from jax.experimental.pallas import tpu as pltpu
from jax.sharding import PartitionSpec as P

norm_eps = 1e-06
f32 = jnp.float32
bf16 = jnp.bfloat16
row_tile = 16
half_tile = 8
lane_tile = 128
MIB = 1 << 20


def round_up(value, step):
    return -(-value // step) * step


def split_bf16(values):
    high = values.astype(bf16)
    low = (values - high.astype(f32)).astype(bf16)
    return high, low


def block_tables(block):
    turns = (4 * np.arange(block)[:, None] + 1) * np.arange(block)[None, :] % (4 * block)
    theta = turns * (math.pi / (2 * block))
    table = np.concatenate([np.cos(theta), np.sin(theta)], axis=0)
    parts = []
    for matrix in (table, table.T / block):
        high = matrix.astype(bf16)
        low = (matrix - high.astype(np.float64)).astype(bf16)
        parts.append(np.concatenate([high, low], axis=0))
    return parts


def block_devices(n_devices, tok_rows):
    target = math.isqrt(32 * n_devices * tok_rows)
    count = 1
    while n_devices % (2 * count) == 0 and 2 * count * tok_rows <= target:
        count *= 2
    return count


def whole_spec():
    return pl.BlockSpec(memory_space=pltpu.VMEM)


def product_kernel(chunks, width, vars_dev, rows_ref, streams_ref, *out_refs):
    tok_rows = streams_ref.shape[1]
    n_owners = out_refs[0].shape[0]
    extra = out_refs[0].shape[1] - tok_rows
    place = lax.broadcasted_iota(jnp.int32, (extra, tok_rows), 0)
    column = lax.broadcasted_iota(jnp.int32, (extra, tok_rows), 1)
    for owner in range(n_owners):
        gates = jnp.zeros((extra, width), f32)
        for chunk in range(chunks):
            lanes = pl.ds((owner * chunks + chunk) * width, width)
            left = streams_ref[1, :, lanes].astype(f32)
            right = streams_ref[2, :, lanes].astype(f32)
            out_refs[chunk][owner, :tok_rows, :] = (left * right).astype(bf16)
            picker = jnp.zeros((extra, tok_rows), jnp.bool_)
            for var in range(vars_dev):
                picker |= (place == chunk * vars_dev + var) & (column == rows_ref[var])
            gates += jnp.dot(
                picker.astype(f32).astype(bf16),
                streams_ref[0, :, lanes],
                preferred_element_type=f32,
            )
        out_refs[0][owner, tok_rows:, :] = gates.astype(bf16)


def make_products(streams, local_rows, n_devices, chunks, extra):
    _, tok_rows, model_width = streams.shape
    vars_dev = local_rows.shape[0]
    group_width = model_width // n_devices
    width = group_width // chunks
    owners = max(1, n_devices // 4)
    while owners * group_width % lane_tile:
        owners *= 2
    steps = n_devices // owners
    rows_out = [tok_rows + extra] + [tok_rows] * (chunks - 1)
    return pl.pallas_call(
        functools.partial(product_kernel, chunks, width, vars_dev),
        grid=(steps,),
        in_specs=[
            pl.BlockSpec(memory_space=pltpu.SMEM),
            pl.BlockSpec((3, tok_rows, owners * group_width), lambda i: (0, 0, i)),
        ],
        out_specs=[pl.BlockSpec((owners, rows, width), lambda i: (i, 0, 0)) for rows in rows_out],
        out_shape=[jax.ShapeDtypeStruct((n_devices, rows, width), bf16) for rows in rows_out],
        compiler_params=pltpu.CompilerParams(vmem_limit_bytes=24 * MIB),
        name="products",
    )(local_rows, streams)


def spectrum_kernel(block, filter_ref, forward_ref, out_ref):
    n_blocks = out_ref.shape[0]
    for index in range(n_blocks):
        taps = filter_ref[:, index * block : (index + 1) * block]
        both = lax.dot_general(
            forward_ref[...], taps, (((1,), (1,)), ((), ())), preferred_element_type=f32
        )
        out_ref[index] = both[: 2 * block] + both[2 * block :]


def filter_spectrum(taps, forward, block):
    width, length = taps.shape
    n_blocks = length // block
    return pl.pallas_call(
        functools.partial(spectrum_kernel, block),
        in_specs=[whole_spec()] * 2,
        out_specs=whole_spec(),
        out_shape=jax.ShapeDtypeStruct((n_blocks, 2 * block, width), f32),
        compiler_params=pltpu.CompilerParams(vmem_limit_bytes=40 * MIB),
        cost_estimate=pl.CostEstimate(
            flops=8 * block * length * width, bytes_accessed=4 * MIB, transcendentals=0
        ),
        name="filter_spectrum",
    )(taps, forward)


def multiply_tile(points, spectrum_ref, joint, start, lanes):
    n_blocks, double, _ = points.shape
    upper = pl.ds(start, half_tile)
    lower = pl.ds(pl.multiple_of(double // 2 + start, half_tile), half_tile)
    signal = [(points[k, upper, lanes], points[k, lower, lanes]) for k in range(n_blocks)]
    signal = [(a_re, a_im, a_re + a_im) for a_re, a_im in signal]
    taps = [(spectrum_ref[k, upper, lanes], spectrum_ref[k, lower, lanes]) for k in range(n_blocks)]
    taps = [(b_re, b_im - b_re, b_re + b_im) for b_re, b_im in taps]
    before_re = jnp.zeros_like(signal[0][0])
    before_im = before_re
    for total in range(n_blocks):
        first = second = third = None
        for delay in range(total + 1):
            a_re, a_im, a_sum = signal[total - delay]
            b_re, b_less, b_sum = taps[delay]
            one, two, three = b_re * a_sum, a_re * b_less, a_im * b_sum
            first = one if first is None else first + one
            second = two if second is None else second + two
            third = three if third is None else third + three
        sum_re, sum_im = first - third, first + second
        joint[total, upper, lanes] = sum_re + before_im
        joint[total, lower, lanes] = sum_im - before_re
        before_re, before_im = sum_re, sum_im


def multiply_points(points, spectrum_ref, joint):
    n_blocks, double, width = points.shape
    lanes_step = min(width, lane_tile)

    def multiply_step(step, carry):
        start = pl.multiple_of(step * half_tile, half_tile)
        for first in range(0, width, lanes_step):
            multiply_tile(points, spectrum_ref, joint, start, slice(first, first + lanes_step))
        return carry

    lax.fori_loop(0, double // 2 // half_tile, multiply_step, 0)


def convolve(chunk_ref, spectrum_ref, forward_ref, inverse_ref, out_ref, points, tok_rows):
    n_blocks, double, width = points.shape
    block = double // 2
    per_block = block // tok_rows
    group = max(1, min(n_blocks, 256 // width)) if width % lane_tile == 0 else 1

    def forward_step(step, carry):
        pieces = []
        for member in range(group):
            start = (step * group + member) * per_block
            rows = chunk_ref[pl.ds(start, per_block), :tok_rows, :]
            pieces.append(rows.reshape(block, width))
        signal = pieces[0] if group == 1 else jnp.concatenate(pieces, axis=1)
        both = jnp.dot(forward_ref[...], signal, preferred_element_type=f32)
        total = both[:double] + both[double:]
        for member in range(group):
            points[step * group + member] = total[:, member * width : (member + 1) * width]
        return carry

    lax.fori_loop(0, n_blocks // group, forward_step, 0)

    multiply_points(points, spectrum_ref, points)

    def inverse_step(step, carry):
        first = step * group
        pieces = [points[first + member] for member in range(group)]
        highs, lows = split_bf16(pieces[0] if group == 1 else jnp.concatenate(pieces, axis=1))
        both = jnp.dot(inverse_ref[...], highs, preferred_element_type=f32)
        rest = jnp.dot(inverse_ref[:block, :], lows, preferred_element_type=f32)
        result = (both[:block] + both[block:] + rest).astype(bf16)
        for member in range(group):
            piece = result[:, member * width : (member + 1) * width]
            out_ref[pl.ds((first + member) * per_block, per_block), :tok_rows, :] = piece.reshape(
                per_block, tok_rows, width
            )
        return carry

    lax.fori_loop(0, n_blocks // group, inverse_step, 0)


def score_rows(index, vars_dev, tok_rows, positions, gate_block, out_ref, gain_row, unembed):
    n_devices, extra, width = gate_block.shape
    gates = gate_block.astype(f32)
    place = lax.broadcasted_iota(jnp.int32, (n_devices, extra, width), 1)
    picked = [
        jnp.sum(jnp.where(place == index * vars_dev + var, gates, 0.0), axis=1)
        for var in range(vars_dev)
    ]
    gate_rows = picked[0] if vars_dev == 1 else jnp.concatenate(picked, axis=0)
    length = n_devices * tok_rows
    column = lax.broadcasted_iota(jnp.int32, (positions.shape[0], length), 1)
    picker = (column == positions).astype(f32).astype(bf16)
    filtered = jnp.dot(
        picker, out_ref[:, :tok_rows, :].reshape(length, width), preferred_element_type=f32
    )
    rows = (gate_rows * filtered).astype(bf16).astype(f32)
    weighted = (rows * gain_row).astype(bf16)
    return jnp.dot(weighted, unembed, preferred_element_type=f32), rows * rows


def pack_scores(raw, squares, raw_parts, vars_dev, packed, n_devices):
    total, width = packed.shape
    extra = total // n_devices
    per_row = raw.shape[1] // width
    count = raw_parts * per_row + 2
    packed[...] = jnp.zeros_like(packed)
    for var in range(vars_dev):
        mine = slice(var * n_devices, (var + 1) * n_devices)
        pieces = [raw[mine, r * width : (r + 1) * width] for r in range(per_row)]
        rounded = [piece.astype(bf16).astype(f32) for piece in pieces]
        rows = rounded + [piece - high for piece, high in zip(pieces, rounded)][: (raw_parts - 1) * per_row]
        high = squares[mine].astype(bf16).astype(f32)
        rows += [high, squares[mine] - high]
        for row, piece in enumerate(rows):
            packed[pl.ds(var * count + row, n_devices, stride=extra), :] = piece


def chunk_kernel(index, chunks, vars_dev, tok_rows, *refs):
    refs = list(refs)
    chunk_ref, spectrum_ref, forward_ref, inverse_ref = refs[:4]
    positions_ref, gain_ref, unembed_ref = refs[4:7]
    refs = refs[7:]
    first, last = index == 0, index == chunks - 1
    gates_ref = None if first else refs.pop(0)
    raw_before, square_before = (None, None) if first else (refs.pop(0), refs.pop(0))
    out_ref = refs.pop(0)
    raw_out, square_out = (None, None) if last else (refs.pop(0), refs.pop(0))
    gates_out = refs.pop(0) if first and not last else None
    points = refs[0]
    convolve(chunk_ref, spectrum_ref, forward_ref, inverse_ref, out_ref, points, tok_rows)
    gate_block = chunk_ref[:, tok_rows:, :] if first else gates_ref[...]
    raw, squares = score_rows(
        index, vars_dev, tok_rows, positions_ref[...], gate_block, out_ref, gain_ref[...], unembed_ref[...]
    )
    if not first:
        raw = raw + raw_before[...]
        squares = squares + square_before[...]
    if gates_out is not None:
        gates_out[...] = gate_block
    if not last:
        raw_out[...] = raw
        square_out[...] = squares
        return
    packed = refs[1]
    n_devices, _, width = out_ref.shape
    extra = out_ref.shape[1] - tok_rows
    pack_scores(raw, squares, 2, vars_dev, packed, n_devices)
    out_ref[:, tok_rows:, :] = packed[...].reshape(n_devices, extra, width).astype(bf16)


def filter_chunk(index, chunks, vars_dev, tok_rows, extra, operands, carried):
    moved, spectrum = operands[:2]
    n_devices, _, width = moved.shape
    n_blocks, double, _ = spectrum.shape
    vocab = operands[6].shape[1]
    n_vars = operands[4].shape[0]
    first, last = index == 0, index == chunks - 1
    rows_out = tok_rows + (extra if last else 0)
    out_shape = [jax.ShapeDtypeStruct((n_devices, rows_out, width), bf16)]
    scratch = [pltpu.VMEM((n_blocks, double, width), f32)]
    if last:
        scratch.append(pltpu.VMEM((n_devices * extra, width), f32))
    else:
        out_shape.append(jax.ShapeDtypeStruct((n_vars, vocab), f32))
        out_shape.append(jax.ShapeDtypeStruct((n_vars, width), f32))
    if first and not last:
        out_shape.append(jax.ShapeDtypeStruct((n_devices, moved.shape[1] - tok_rows, width), bf16))
    flops = 2 * width * n_blocks * (double * double * 5 // 2 + 4 * n_blocks * double)
    return pl.pallas_call(
        functools.partial(chunk_kernel, index, chunks, vars_dev, tok_rows),
        in_specs=[whole_spec()] * (len(operands) + len(carried)),
        out_specs=[whole_spec()] * len(out_shape),
        out_shape=out_shape,
        scratch_shapes=scratch,
        compiler_params=pltpu.CompilerParams(vmem_limit_bytes=(20 if n_blocks <= 8 else 58) * MIB),
        cost_estimate=pl.CostEstimate(flops=flops, bytes_accessed=8 * MIB, transcendentals=0),
        name="filter_chunk",
    )(*operands, *carried)


def final_scores(sums, raw_parts, vars_dev, vocab, model_width, ref_ref, alt_ref):
    width = sums.shape[1]
    per_row = vocab // width
    count = raw_parts * per_row + 2
    ids = lax.broadcasted_iota(jnp.int32, (per_row, width), 0) * width
    ids += lax.broadcasted_iota(jnp.int32, (per_row, width), 1)
    row = lax.broadcasted_iota(jnp.int32, (vars_dev, 2), 0)
    column = lax.broadcasted_iota(jnp.int32, (vars_dev, 2), 1)
    scores = jnp.zeros((vars_dev, 2), f32)

    def whole_sum(values):
        return jnp.sum(jnp.sum(values, axis=1, keepdims=True), axis=0, keepdims=True)

    for var in range(vars_dev):
        base = var * count
        raw = sums[base : base + per_row, :]
        if raw_parts == 2:
            raw = raw + sums[base + per_row : base + 2 * per_row, :]
        square = whole_sum(sums[base + count - 2 : base + count, :])
        logits = raw * lax.rsqrt(square / model_width + norm_eps)
        largest = jnp.max(jnp.max(logits, axis=1, keepdims=True), axis=0, keepdims=True)
        log_total = largest + jnp.log(whole_sum(jnp.exp(logits - largest)))
        ref_logit = whole_sum(jnp.where(ids == ref_ref[var], logits, 0.0))
        alt_logit = whole_sum(jnp.where(ids == alt_ref[var], logits, 0.0))
        pair = jnp.where(column == 0, ref_logit - log_total, alt_logit - ref_logit)
        scores = jnp.where(row == var, pair, scores)
    return scores


def finish_kernel(chunks, vars_dev, vocab, ref_ref, alt_ref, streams_ref, *refs):
    back_refs, mixed_ref, scores_ref, sums = refs[:chunks], refs[chunks], refs[chunks + 1], refs[chunks + 2]
    tok_rows = streams_ref.shape[1]
    owners, _, width = back_refs[0].shape
    step = pl.program_id(0)
    for owner in range(owners):
        for chunk in range(chunks):
            lanes = pl.ds((owner * chunks + chunk) * width, width)
            gate = streams_ref[0, :, lanes].astype(f32)
            filtered = back_refs[chunk][owner, :tok_rows, :].astype(f32)
            mixed_ref[:, lanes] = (gate * filtered).astype(bf16)
    part = jnp.sum(back_refs[-1][:, tok_rows:, :].astype(f32), axis=0)

    @pl.when(step == 0)
    def _():
        sums[...] = part

    @pl.when(step > 0)
    def _():
        sums[...] += part

    @pl.when(step == pl.num_programs(0) - 1)
    def _():
        model_width = pl.num_programs(0) * owners * chunks * width
        scores_ref[...] = final_scores(sums[...], 2, vars_dev, vocab, model_width, ref_ref, alt_ref)


def finish(streams, backs, ref_ids, alt_ids, vocab):
    _, tok_rows, model_width = streams.shape
    chunks = len(backs)
    n_devices, _, width = backs[0].shape
    vars_dev = ref_ids.shape[0]
    owners = max(1, n_devices // 4)
    while owners * chunks * width % lane_tile:
        owners *= 2
    extra = backs[-1].shape[1] - tok_rows
    return pl.pallas_call(
        functools.partial(finish_kernel, chunks, vars_dev, vocab),
        grid=(n_devices // owners,),
        in_specs=[
            pl.BlockSpec(memory_space=pltpu.SMEM),
            pl.BlockSpec(memory_space=pltpu.SMEM),
            pl.BlockSpec((1, tok_rows, owners * chunks * width), lambda i: (0, 0, i)),
        ]
        + [pl.BlockSpec((owners, back.shape[1], width), lambda i: (i, 0, 0)) for back in backs],
        out_specs=[
            pl.BlockSpec((tok_rows, owners * chunks * width), lambda i: (0, i)),
            pl.BlockSpec((vars_dev, 2), lambda i: (0, 0)),
        ],
        out_shape=[
            jax.ShapeDtypeStruct((tok_rows, model_width), bf16),
            jax.ShapeDtypeStruct((vars_dev, 2), f32),
        ],
        scratch_shapes=[pltpu.VMEM((extra, width), f32)],
        compiler_params=pltpu.CompilerParams(vmem_limit_bytes=24 * MIB),
        name="finish",
    )(ref_ids, alt_ids, streams, *backs)

def stacked_products_kernel(halves, vars_dev, offsets_ref, streams_ref, out_ref, *scratch):
    gates, pairs, built, offsets, gate_sems, pair_sems, out_sems, offset_sem, tail_sem = scratch
    n_devices = built.shape[0]
    pieces, _, tok_rows, lanes_each = pairs.shape
    body = halves * tok_rows
    width = halves * lane_tile
    owners = lanes_each // width
    me = lax.axis_index("seq")
    slot = tok_rows // vars_dev

    def pair_copy(piece):
        lanes = pl.ds(piece * lanes_each, lanes_each)
        return pltpu.make_async_copy(
            streams_ref.at[pl.ds(1, 2), :, lanes], pairs.at[piece], pair_sems.at[piece]
        )


    def body_copy(owner):
        rows = pl.ds(0, body)
        return pltpu.make_async_copy(built.at[owner, rows], out_ref.at[owner, rows], out_sems.at[owner])

    def gate_copy(var):
        start = pl.multiple_of(local_rows[var] // row_tile * row_tile, row_tile)
        return pltpu.make_async_copy(
            streams_ref.at[0, pl.ds(start, row_tile), :], gates.at[var], gate_sems.at[var]
        )

    offset_copy = pltpu.make_async_copy(offsets_ref, offsets, offset_sem.at[0])
    offset_copy.start()
    for piece in range(pieces):
        pair_copy(piece).start()
    offset_copy.wait()
    local_rows = [var * slot + offsets[me * vars_dev + var] for var in range(vars_dev)]
    for var in range(vars_dev):
        gate_copy(var).start()
    for piece in range(pieces):
        pair_copy(piece).wait()
        for member in range(owners):
            owner = piece * owners + member
            for half in range(halves):
                lanes = slice(member * width + half * lane_tile, member * width + (half + 1) * lane_tile)
                rows = slice(half * tok_rows, (half + 1) * tok_rows)
                built[owner, rows, :] = pairs[piece, 0, :, lanes] * pairs[piece, 1, :, lanes]
            body_copy(owner).start()

    extra = built.shape[1] - body
    row = lax.broadcasted_iota(jnp.int32, gates.shape[1:], 0)
    place = lax.broadcasted_iota(jnp.int32, (extra, lane_tile), 0)
    gate_rows = []
    for var in range(vars_dev):
        gate_copy(var).wait()
        mine = jnp.where(row == local_rows[var] % row_tile, gates[var].astype(f32), 0.0)
        gate_rows.append(jnp.sum(mine, axis=0, keepdims=True))
    for owner in range(n_devices):
        tail = jnp.zeros((extra, lane_tile), f32)
        for half in range(halves):
            start = owner * width + half * lane_tile
            for var in range(vars_dev):
                mine = gate_rows[var][:, start : start + lane_tile]
                tail = jnp.where(place == half * vars_dev + var, mine, tail)
        built[owner, body:, :] = tail.astype(bf16)
    rows = pl.ds(body, extra)
    tail_copy = pltpu.make_async_copy(built.at[:, rows], out_ref.at[:, rows], tail_sem.at[0])
    tail_copy.start()
    for owner in range(n_devices):
        body_copy(owner).wait()
    tail_copy.wait()


def stacked_products(offsets, streams, vars_dev, n_devices, extra):
    _, tok_rows, model_width = streams.shape
    halves = model_width // n_devices // lane_tile
    rows_out = halves * tok_rows + extra
    pieces = math.gcd(n_devices, 8)
    return pl.pallas_call(
        functools.partial(stacked_products_kernel, halves, vars_dev),
        in_specs=[pl.BlockSpec(memory_space=pl.ANY)] * 2,
        out_specs=pl.BlockSpec(memory_space=pl.ANY),
        out_shape=jax.ShapeDtypeStruct((n_devices, rows_out, lane_tile), bf16),
        scratch_shapes=[
            pltpu.VMEM((vars_dev, row_tile, model_width), bf16),
            pltpu.VMEM((pieces, 2, tok_rows, model_width // pieces), bf16),
            pltpu.VMEM((n_devices, rows_out, lane_tile), bf16),
            pltpu.SMEM(offsets.shape, jnp.int32),
            pltpu.SemaphoreType.DMA((vars_dev,)),
            pltpu.SemaphoreType.DMA((pieces,)),
            pltpu.SemaphoreType.DMA((n_devices,)),
            pltpu.SemaphoreType.DMA((1,)),
            pltpu.SemaphoreType.DMA((1,)),
        ],
        compiler_params=pltpu.CompilerParams(vmem_limit_bytes=60 * MIB),
        cost_estimate=pl.CostEstimate(
            flops=tok_rows * model_width, bytes_accessed=6 * tok_rows * model_width, transcendentals=0
        ),
        name="stacked_products",
    )(offsets, streams)


def stacked_filter_kernel(vars_dev, halves, tok_rows, *refs):
    positions_ref, gain_ref, forward, inverse, unembed, taps, arrived = refs[:7]
    out_ref, points, joint, spectrum, packed, leaving, body_sems, tail_sem = refs[7:]
    n_devices = arrived.shape[0]
    body = halves * tok_rows
    n_blocks, double, width = points.shape
    block = double // 2
    per_block = block // tok_rows
    group = math.gcd(n_blocks, 4)

    def body_copy(rank):
        rows = pl.ds(0, body)
        return pltpu.make_async_copy(leaving.at[rank, rows], out_ref.at[rank, rows], body_sems.at[rank])

    for step in range(0, n_blocks, group):
        filters = [taps[:, index * block : (index + 1) * block] for index in range(step, step + group)]
        both = lax.dot_general(
            forward[...],
            jnp.concatenate(filters, axis=0),
            (((1,), (1,)), ((), ())),
            preferred_element_type=f32,
        )
        total = both[:double] + both[double:]
        for member in range(group):
            spectrum[step + member] = total[:, member * width : (member + 1) * width]

    for step in range(0, n_blocks, group):
        pieces = []
        for index in range(step, step + group):
            for half in range(halves):
                rows = slice(half * tok_rows, (half + 1) * tok_rows)
                parts = [arrived[index * per_block + m, rows, :] for m in range(per_block)]
                pieces.append(jnp.concatenate(parts, axis=0))
        signal = jnp.concatenate(pieces, axis=1)
        both = jnp.dot(forward[...], signal, preferred_element_type=f32)
        total = both[:double] + both[double:]
        for member in range(group):
            points[step + member] = total[:, member * width : (member + 1) * width]
    multiply_points(points, spectrum, joint)

    row = lax.broadcasted_iota(jnp.int32, (tok_rows, width), 0)
    rows_of = [[None] * n_devices for _ in range(vars_dev)]
    group = math.gcd(n_blocks, 2)
    for step in range(0, n_blocks, group):
        highs, lows = split_bf16(jnp.concatenate([joint[step + m] for m in range(group)], axis=1))
        both = jnp.dot(inverse[...], highs, preferred_element_type=f32)
        rest = jnp.dot(inverse[:block, :], lows, preferred_element_type=f32)
        result = (both[:block] + both[block:] + rest).astype(bf16)
        for index in range(group):
            for member in range(per_block):
                device = (step + index) * per_block + member
                piece = result[
                    member * tok_rows : (member + 1) * tok_rows, index * width : (index + 1) * width
                ]
                for half in range(halves):
                    leaving[device, half * tok_rows : (half + 1) * tok_rows, :] = piece[
                        :, half * lane_tile : (half + 1) * lane_tile
                    ]
                body_copy(device).start()
                for var in range(vars_dev):
                    spot = var * n_devices + device
                    local = positions_ref[spot : spot + 1, :] - device * tok_rows
                    mine = jnp.where(row == local, piece.astype(f32), 0.0)
                    rows_of[var][device] = jnp.sum(mine, axis=0, keepdims=True)

    picked_rows = jnp.concatenate([mine for rows in rows_of for mine in rows], axis=0)
    tails = arrived[:, body:, :].astype(f32)
    place = lax.broadcasted_iota(jnp.int32, tails.shape, 1)
    raw = None
    squares = None
    for half in range(halves):
        lanes = slice(half * lane_tile, (half + 1) * lane_tile)
        picked = [
            jnp.sum(jnp.where(place == half * vars_dev + var, tails, 0.0), axis=1)
            for var in range(vars_dev)
        ]
        gate_rows = picked[0] if vars_dev == 1 else jnp.concatenate(picked, axis=0)
        rows = (gate_rows * picked_rows[:, lanes]).astype(bf16).astype(f32)
        weighted = (rows * gain_ref[:, lanes]).astype(bf16)
        part = jnp.dot(weighted, unembed[lanes, :], preferred_element_type=f32)
        raw = part if raw is None else raw + part
        squares = rows * rows if squares is None else squares + rows * rows
    pack_scores(raw, squares, 2, vars_dev, packed, n_devices)
    extra = packed.shape[0] // n_devices
    leaving[:, body:, :] = packed[...].reshape(n_devices, extra, lane_tile).astype(bf16)
    rows = pl.ds(body, extra)
    tail_copy = pltpu.make_async_copy(leaving.at[:, rows], out_ref.at[:, rows], tail_sem.at[0])
    tail_copy.start()
    for rank in range(n_devices):
        body_copy(rank).wait()
    tail_copy.wait()


def stacked_filter(positions, gain_row, tables, arrived, vars_dev, tok_rows, extra):
    width, length = tables[3].shape
    n_devices = arrived.shape[0]
    double = tables[0].shape[0] // 2
    n_blocks = 2 * length // double
    halves = width // lane_tile
    rows_out = halves * tok_rows + extra
    flops = 2 * width * n_blocks * (double * double * 5 // 2 + 4 * n_blocks * double)
    return pl.pallas_call(
        functools.partial(stacked_filter_kernel, vars_dev, halves, tok_rows),
        in_specs=[whole_spec()] * 7,
        out_specs=pl.BlockSpec(memory_space=pl.ANY),
        out_shape=jax.ShapeDtypeStruct((n_devices, rows_out, lane_tile), bf16),
        scratch_shapes=[pltpu.VMEM((n_blocks, double, width), f32)] * 3
        + [
            pltpu.VMEM((n_devices * extra, lane_tile), f32),
            pltpu.VMEM((n_devices, rows_out, lane_tile), bf16),
            pltpu.SemaphoreType.DMA((n_devices,)),
            pltpu.SemaphoreType.DMA((1,)),
        ],
        compiler_params=pltpu.CompilerParams(vmem_limit_bytes=24 * MIB),
        cost_estimate=pl.CostEstimate(flops=flops, bytes_accessed=8 * MIB, transcendentals=0),
        name="stacked_filter",
    )(positions, gain_row, *tables, arrived)


def stacked_finish_kernel(halves, vars_dev, vocab, ref_ref, alt_ref, gates_ref, back_ref, *refs):
    mixed_ref, scores_ref, results, scores, out_sems, score_sem = refs
    n_devices, tok_rows, width = results.shape

    def out_copy(owner):
        return pltpu.make_async_copy(
            results.at[owner], mixed_ref.at[:, pl.ds(owner * width, width)], out_sems.at[owner]
        )

    sums = None
    for owner in range(n_devices):
        tail = back_ref[owner, halves * tok_rows :, :].astype(f32)
        sums = tail if sums is None else sums + tail
        for half in range(halves):
            lanes = slice(half * lane_tile, (half + 1) * lane_tile)
            start = owner * width + half * lane_tile
            filtered = back_ref[owner, half * tok_rows : (half + 1) * tok_rows, :]
            results[owner, :, lanes] = gates_ref[:, start : start + lane_tile] * filtered
        out_copy(owner).start()
    model_width = n_devices * width
    scores[...] = final_scores(sums, 2, vars_dev, vocab, model_width, ref_ref, alt_ref)
    score_copy = pltpu.make_async_copy(scores, scores_ref, score_sem.at[0])
    score_copy.start()
    for owner in range(n_devices):
        out_copy(owner).wait()
    score_copy.wait()


def stacked_finish(ref_ids, alt_ids, gates, back, vocab):
    tok_rows, model_width = gates.shape
    n_devices = back.shape[0]
    vars_dev = ref_ids.shape[0]
    width = model_width // n_devices
    return pl.pallas_call(
        functools.partial(stacked_finish_kernel, width // lane_tile, vars_dev, vocab),
        in_specs=[pl.BlockSpec(memory_space=pltpu.SMEM)] * 2 + [whole_spec()] * 2,
        out_specs=[pl.BlockSpec(memory_space=pl.ANY)] * 2,
        out_shape=[
            jax.ShapeDtypeStruct((tok_rows, model_width), bf16),
            jax.ShapeDtypeStruct((vars_dev, 2), f32),
        ],
        scratch_shapes=[
            pltpu.VMEM((n_devices, tok_rows, width), bf16),
            pltpu.VMEM((vars_dev, 2), f32),
            pltpu.SemaphoreType.DMA((n_devices,)),
            pltpu.SemaphoreType.DMA((1,)),
        ],
        compiler_params=pltpu.CompilerParams(vmem_limit_bytes=16 * MIB),
        cost_estimate=pl.CostEstimate(
            flops=tok_rows * model_width, bytes_accessed=6 * tok_rows * model_width, transcendentals=0
        ),
        name="stacked_finish",
    )(ref_ids, alt_ids, gates, back)


def transposed(blocks):
    return lax.all_to_all(blocks, "seq", split_axis=0, concat_axis=0, tiled=True)


def shards(streams, long_filter, gain, unembed, offsets, ref_ids, alt_ids):
    n_devices = lax.axis_size("seq")
    my_index = lax.axis_index("seq")
    _, tok_rows, model_width = streams.shape
    group_width = model_width // n_devices
    vars_dev = ref_ids.shape[0]
    vocab = unembed.shape[1]
    chunks = max(1, group_width // lane_tile)
    width = group_width // chunks
    block = tok_rows * block_devices(n_devices, tok_rows)
    forward_np, inverse_np = block_tables(block)
    forward, inverse = jnp.asarray(forward_np), jnp.asarray(inverse_np)

    slot = tok_rows // vars_dev
    starts = jnp.arange(vars_dev, dtype=jnp.int32) * slot
    local_rows = starts + lax.dynamic_slice_in_dim(offsets, my_index * vars_dev, vars_dev)
    by_device = offsets.reshape(n_devices, vars_dev)
    positions = by_device + starts[None, :]
    positions += jnp.arange(n_devices, dtype=jnp.int32)[:, None] * tok_rows
    positions = positions.T.reshape(n_devices * vars_dev, 1)
    my_gain = lax.dynamic_slice_in_dim(gain, my_index * group_width, group_width).astype(f32)

    if chunks * lane_tile == group_width:
        gate_extra = round_up(chunks * vars_dev, row_tile)
        score_extra = round_up(2 * vars_dev * (vocab // lane_tile + 1), row_tile)
        arrived = transposed(stacked_products(offsets, streams, vars_dev, n_devices, gate_extra))
        tables = (forward, inverse, unembed, long_filter)
        gain_row = my_gain[None, :]
        leaving = stacked_filter(positions, gain_row, tables, arrived, vars_dev, tok_rows, score_extra)
        back = transposed(leaving)
        mixed, scores = stacked_finish(ref_ids, alt_ids, streams[0], back, vocab)
        return (mixed, scores.T)

    gate_extra = round_up(chunks * vars_dev, row_tile)
    score_extra = round_up(vars_dev * 2 * (vocab // width + 1), row_tile)
    products = make_products(streams, local_rows, n_devices, chunks, gate_extra)
    moved = [lax.all_to_all(part, "seq", split_axis=0, concat_axis=0, tiled=True) for part in products]
    carried = ()
    backs = []
    for chunk in range(chunks):
        mine = slice(chunk * width, (chunk + 1) * width)
        spectrum = filter_spectrum(long_filter[mine], forward, block)
        operands = (
            moved[chunk], spectrum, forward, inverse, positions,
            my_gain[None, mine], unembed[mine],
        )
        if chunk > 0:
            carried = (gates,) + tuple(carried)
        results = filter_chunk(chunk, chunks, vars_dev, tok_rows, score_extra, operands, carried)
        carried = results[1:3]
        if chunk == 0 and chunks > 1:
            gates = results[3]
        backs.append(lax.all_to_all(results[0], "seq", split_axis=0, concat_axis=0, tiled=True))
    mixed, scores = finish(streams, backs, ref_ids, alt_ids, vocab)
    return (mixed, scores.T)


def solution(mesh):
    placed = (
        P(None, ("grp", "seq"), None),
        P("seq", None),
        P(),
        P("seq", None),
        P("grp"),
        P(("grp", "seq")),
        P(("grp", "seq")),
    )
    return jax.shard_map(
        shards,
        mesh=mesh,
        in_specs=placed,
        out_specs=(P(("grp", "seq"), None), P(None, ("grp", "seq"))),
        check_vma=False,
    )
```
